32 devices in a mesh: seq: 8 (over z, x), stream: 4 (over y, core).
Axes of the slice: x: 2, y: 2, z: 4, core: 2. Of those that a mesh axis runs over, the one named last changes fastest.
Arguments:
- enc_in: bfloat16 [4, 4, 1024, 512], P(None, 'stream', 'seq'), may hold values from -6 to 6
- dec_in: bfloat16 [4, 4, 1024, 512], P(None, 'stream', 'seq'), may hold values from -6 to 6
- cotangent: bfloat16 [4, 4, 1024, 512], P(None, 'stream', 'seq'), may hold values from -6 to 6
- lengths: int32 [4, 4, 16], P(None, 'stream'), may hold values from 1 to 256, 1024 in all within a row
- attn_master: float32 [6144, 512], P(('seq', 'stream')), may hold values from -0.25 to 0.25
- ffn_in_master: float32 [1024, 2048], P(('seq', 'stream')), may hold values from -0.25 to 0.25
- ffn_out_master: float32 [4096, 512], P(('seq', 'stream')), may hold values from -0.125 to 0.125
- norm_master: float32 [5120], P(('seq', 'stream')), may hold values from -0.5 to 3.9
- attn_first: float32 [6144, 512], P(('seq', 'stream')), may hold values from -256 to 256
- ffn_in_first: float32 [1024, 2048], P(('seq', 'stream')), may hold values from -256 to 256
- ffn_out_first: float32 [4096, 512], P(('seq', 'stream')), may hold values from -256 to 256
- norm_first: float32 [5120], P(('seq', 'stream')), may hold values from -256 to 256
- attn_second: float32 [6144, 512], P(('seq', 'stream')), may hold values from 819.2 to 13107.2
- ffn_in_second: float32 [1024, 2048], P(('seq', 'stream')), may hold values from 819.2 to 13107.2
- ffn_out_second: float32 [4096, 512], P(('seq', 'stream')), may hold values from 819.2 to 13107.2
- norm_second: float32 [5120], P(('seq', 'stream')), may hold values from 819.2 to 13107.2
Outputs:
- enc_out: bfloat16 [4, 4, 1024, 512], P(None, 'stream', 'seq')
- dec_out: bfloat16 [4, 4, 1024, 512], P(None, 'stream', 'seq')
- enc_in_grad: float32 [4, 4, 1024, 512], P(None, 'stream', 'seq')
- dec_in_grad: float32 [4, 4, 1024, 512], P(None, 'stream', 'seq')
- attn_grad: float32 [6144, 512], P(('seq', 'stream'))
- ffn_in_grad: float32 [1024, 2048], P(('seq', 'stream'))
- ffn_out_grad: float32 [4096, 512], P(('seq', 'stream'))
- norm_grad: float32 [5120], P(('seq', 'stream'))
- attn_new: float32 [6144, 512], P(('seq', 'stream'))
- ffn_in_new: float32 [1024, 2048], P(('seq', 'stream'))
- ffn_out_new: float32 [4096, 512], P(('seq', 'stream'))
- norm_new: float32 [5120], P(('seq', 'stream'))
- attn_first_new: float32 [6144, 512], P(('seq', 'stream'))
- ffn_in_first_new: float32 [1024, 2048], P(('seq', 'stream'))
- ffn_out_first_new: float32 [4096, 512], P(('seq', 'stream'))
- norm_first_new: float32 [5120], P(('seq', 'stream'))
- attn_second_new: float32 [6144, 512], P(('seq', 'stream'))
- ffn_in_second_new: float32 [1024, 2048], P(('seq', 'stream'))
- ffn_out_second_new: float32 [4096, 512], P(('seq', 'stream'))
- norm_second_new: float32 [5120], P(('seq', 'stream'))
- attn_copy: bfloat16 [6144, 512], P(('seq', 'stream'))
- ffn_in_copy: bfloat16 [1024, 2048], P(('seq', 'stream'))
- ffn_out_copy: bfloat16 [4096, 512], P(('seq', 'stream'))
- norm_copy: bfloat16 [5120], P(('seq', 'stream'))
- norms: float32 [2, 26], replicated
- trust: float32 [26], replicated
The draws below stay inside these ranges and needn't reach their ends.
Inputs may be any that keep to these rules, and one draw needn't show every extreme that they name: Each stream's 16 lengths sum to 1024, and the longest of each stream is exactly 256.
All inputs are finite; a program needn't handle non-finite values.
Results may differ from the reference program's by a relative error of at most 0.038.
The reference program's roundings to bfloat16 on the way count: a program that leaves them out, or rounds other values in their place, can miss the bound.
Values may be sent and summed in bfloat16 or wider, within the bound.
No kernel may reach another device: no remote copies, remote signals or barrier semaphores. Data moves between devices by JAX's collectives and lax.ppermute only.
A program may use at most 256 MiB of HBM per device.

```python
import math
import jax
import jax.numpy as jnp
import numpy as np
from jax import lax

D = 512
FF = 2048
HEADS = 8
TOK_DEV = 128
MICRO = 4
STEP = 5
LENGTH = 1024
STREAMS = 4
NSENT = 16
NTOK = 16384


def draw_norm_master(key, part):
    key = jax.random.fold_in(key, 7)
    gain_key, bias_key = jax.random.split(key)
    places = jnp.arange(10 * D, dtype=jnp.int32)
    column = (places % D).astype(jnp.float32)
    row_index = places // D
    rising = 1.0 + 2.0 * column / (D - 1)
    gain_vals = rising * jax.random.uniform(gain_key, (10 * D,), jnp.float32, 0.7, 1.3)
    bias_vals = jax.random.uniform(bias_key, (10 * D,), jnp.float32, -0.5, 0.5)
    return jnp.where(row_index % 2 == 0, gain_vals, bias_vals).astype(jnp.float32)


def level_of(own_key, dims, cuts, smallest, high):
    def one(dim, blocks):
        heights = jax.random.uniform(jax.random.fold_in(jax.random.fold_in(own_key, 6), dim), (blocks,), jnp.float32, smallest / len(cuts), high / len(cuts))
        return jnp.repeat(jnp.exp(heights), dims[dim] // blocks).reshape((-1,) + (1,) * (len(dims) - dim - 1))

    gain = one(*cuts[0])
    for cut in cuts[1:]:
        gain = gain * one(*cut)
    return gain


def split_up(amount, total, limit, skew):
    portions = [(1 << 20) // math.isqrt(standing ** skew) + 1 for standing in range(2, amount + 1)]
    surplus, given = total - limit - (amount - 1), [1] * (amount - 1)
    while surplus > 0:
        free = [i for i in range(amount - 1) if given[i] < limit]
        whole, remaining = sum([portions[i] for i in free]), surplus
        for i in free:
            addition = min(limit - given[i], max(1, remaining * portions[i] // whole), surplus)
            given[i] = given[i] + addition
            surplus = surplus - addition
    return np.array([limit] + given)


def uneven_parts(stream_key, number_of, total, bound, slope):
    if number_of == 2:
        one = jax.random.randint(stream_key, (), max(1, total - bound), min(bound, total - 1) + 1)
        return jnp.stack([one, total - one])
    sizes = jnp.asarray(split_up(number_of, total, bound, slope), jnp.int32)
    pairs = (number_of - 1) // 2
    donor, taker = sizes[1:1 + 2 * pairs:2], sizes[2:2 + 2 * pairs:2]
    slack = jnp.minimum(donor - 1, bound - taker)
    shifted = jax.random.randint(jax.random.fold_in(stream_key, 1), (pairs,), 0, 1 << 20) % (slack + 1)
    sizes = sizes.at[1:1 + 2 * pairs:2].set(donor - shifted).at[2:2 + 2 * pairs:2].set(taker + shifted)
    return sizes[jax.random.permutation(jax.random.fold_in(stream_key, 2), number_of)]


def bell_draw(stream_key, shape, scale, limit, pieces=(), kind=jnp.bfloat16):
    gain = level_of(stream_key, shape, pieces, -0.22, 0.18) if pieces else 1.0
    drawn = jax.random.normal(stream_key, shape, jnp.float32) * scale * gain
    return jnp.minimum(jnp.maximum(drawn, -limit), limit).astype(kind)


def setup_inputs(seed: int = 0) -> dict:
    key_list = jax.random.split(jax.random.key(seed), 17)
    enc_in = bell_draw(key_list[0], (MICRO, STREAMS, LENGTH, D), 1.0, 6.0, ((1, 4), (2, 8)))
    dec_in = bell_draw(key_list[1], (MICRO, STREAMS, LENGTH, D), 1.0, 6.0, ((1, 4), (2, 8)))
    cotangent = bell_draw(key_list[2], (MICRO, STREAMS, LENGTH, D), 1.0, 6.0, ((1, 4), (2, 8)))
    lengths = jax.vmap(lambda own: uneven_parts(own, NSENT, LENGTH, 2 * TOK_DEV, 2))(jax.random.split(key_list[3], MICRO * STREAMS)).reshape((MICRO, STREAMS, NSENT)).astype(jnp.int32)
    attn_master = bell_draw(key_list[4], (12 * D, D), D ** -0.5, 0.25, ((0, 32),), jnp.float32)
    ffn_in_master = bell_draw(key_list[5], (2 * D, FF), D ** -0.5, 0.25, ((0, 32),), jnp.float32)
    ffn_out_master = bell_draw(key_list[6], (2 * FF, D), FF ** -0.5, 0.125, ((0, 32),), jnp.float32)
    norm_master = draw_norm_master(jax.random.fold_in(key_list[16], 71), 0)
    attn_first = bell_draw(key_list[8], (12 * D, D), ((0.1 * NTOK) ** 0.5), 256.0, ((0, 32),), jnp.float32)
    ffn_in_first = bell_draw(key_list[9], (2 * D, FF), ((0.1 * NTOK) ** 0.5), 256.0, ((0, 32),), jnp.float32)
    ffn_out_first = bell_draw(key_list[10], (2 * FF, D), ((0.1 * NTOK) ** 0.5), 256.0, ((0, 32),), jnp.float32)
    norm_first = bell_draw(key_list[11], (10 * D,), ((0.1 * NTOK) ** 0.5), 256.0, ((0, 32),), jnp.float32)
    attn_second = jnp.clip(jnp.exp(math.log(13107.2) - 2.7725887 * jax.random.uniform(key_list[12], (12 * D, D), jnp.float32) ** level_of(key_list[12], (12 * D, D), ((0, 32),), -0.2, 0.2)), 819.2, 13107.2)
    ffn_in_second = jnp.clip(jnp.exp(math.log(13107.2) - 2.7725887 * jax.random.uniform(key_list[13], (2 * D, FF), jnp.float32) ** level_of(key_list[13], (2 * D, FF), ((0, 32),), -0.2, 0.2)), 819.2, 13107.2)
    ffn_out_second = jnp.clip(jnp.exp(math.log(13107.2) - 2.7725887 * jax.random.uniform(key_list[14], (2 * FF, D), jnp.float32) ** level_of(key_list[14], (2 * FF, D), ((0, 32),), -0.2, 0.2)), 819.2, 13107.2)
    norm_second = jnp.clip(jnp.exp(math.log(13107.2) - 2.7725887 * jax.random.uniform(key_list[15], (10 * D,), jnp.float32) ** level_of(key_list[15], (10 * D,), ((0, 32),), -0.2, 0.2)), 819.2, 13107.2)
    return {"enc_in": enc_in, "dec_in": dec_in, "cotangent": cotangent, "lengths": lengths, "attn_master": attn_master, "ffn_in_master": ffn_in_master, "ffn_out_master": ffn_out_master, "norm_master": norm_master, "attn_first": attn_first, "ffn_in_first": ffn_in_first, "ffn_out_first": ffn_out_first, "norm_first": norm_first, "attn_second": attn_second, "ffn_in_second": ffn_in_second, "ffn_out_second": ffn_out_second, "norm_second": norm_second}


@jax.custom_vjp
def low(v):
    return lax.optimization_barrier(v.astype(jnp.bfloat16)).astype(jnp.float32)

@jax.custom_vjp
def low_back(v):
    return v

def low_keep(v):
    return (low(v), None)

def low_pass(kept, grad):
    return (grad,)

def back_keep(v):
    return (v, None)

def back_low(kept, grad):
    return (low(grad),)
low.defvjp(low_keep, low_pass)
low_back.defvjp(back_keep, back_low)
exact = lax.Precision.HIGHEST
norm_eps = 1e-05
beta_one = 0.5
beta_two = 0.5
lamb_eps = 1e-06
weight_decay = 0.01
learn_rate = 0.5
masked_score = -1e+30

def round_both(values):
    return low_back(low(values))

def matmul(left, right):
    return jnp.dot(left, right, precision=exact, preferred_element_type=jnp.float32)

def layer_norm(residual, gain_row, bias_row):
    centre = residual - lax.optimization_barrier(jnp.mean(residual, axis=-1, keepdims=True))
    spread = lax.optimization_barrier(jnp.mean(centre * centre, axis=-1, keepdims=True))
    return centre * lax.rsqrt(spread + norm_eps) * gain_row + bias_row

def smooth(values):
    return jax.nn.gelu(values, approximate=True)

def segment_ids(sent_lengths):
    bounds = jnp.cumsum(sent_lengths).astype(jnp.int32)
    places = jnp.arange(LENGTH, dtype=jnp.int32)
    return lax.optimization_barrier(jnp.sum((bounds[None, :] <= places[:, None]).astype(jnp.int32), axis=1)).astype(jnp.int32)

def attend(queries, key_rows, value_rows, segment, causal):
    reach_rows = 2 * TOK_DEV
    block_rows = min(512, LENGTH)
    head_size = D // HEADS
    score_scale = 1.0 / math.sqrt(head_size)
    keys_pad = jnp.pad(key_rows, ((reach_rows, reach_rows), (0, 0)))
    values_pad = jnp.pad(value_rows, ((reach_rows, reach_rows), (0, 0)))
    segment_pad = jnp.pad(segment, (reach_rows, reach_rows), constant_values=-1)
    window_rows = block_rows + 2 * reach_rows

    def one_block(offset):
        query_blk = lax.dynamic_slice_in_dim(queries, offset, block_rows, 0).reshape(block_rows, HEADS, head_size)
        key_blk = lax.dynamic_slice_in_dim(keys_pad, offset, window_rows, 0).reshape(window_rows, HEADS, head_size)
        value_blk = lax.dynamic_slice_in_dim(values_pad, offset, window_rows, 0).reshape(window_rows, HEADS, head_size)
        query_seg = lax.dynamic_slice_in_dim(segment, offset, block_rows, 0)
        key_seg = lax.dynamic_slice_in_dim(segment_pad, offset, window_rows, 0)
        query_pos = offset + jnp.arange(block_rows, dtype=jnp.int32)
        key_pos = offset - reach_rows + jnp.arange(window_rows, dtype=jnp.int32)
        scores = low_back(jnp.einsum('qhd,khd->hqk', query_blk, key_blk, precision=exact) * score_scale)
        allowed = query_seg[:, None] == key_seg[None, :]
        if causal:
            allowed = allowed & (key_pos[None, :] <= query_pos[:, None])
        scores = jnp.where(allowed[None], scores, masked_score)
        exp_scores = jnp.exp(scores - lax.optimization_barrier(jnp.max(scores, axis=-1, keepdims=True)))
        probs = low(exp_scores / lax.optimization_barrier(jnp.sum(exp_scores, axis=-1, keepdims=True)))
        mixed = jnp.einsum('hqk,khd->qhd', probs, value_blk, precision=exact)
        return mixed.reshape(block_rows, D)
    starts = jnp.arange(LENGTH // block_rows, dtype=jnp.int32) * block_rows
    return lax.map(jax.checkpoint(one_block), starts).reshape(LENGTH, D)

def feed_forward(hidden, w_up, w_down):
    pre_act = low_back(matmul(low(hidden), w_up))
    activ = round_both(smooth(pre_act))
    return low_back(matmul(activ, w_down))

def encoder_layer(source, attn_w, ffn_up, ffn_down, gains, segment):
    queries = round_both(matmul(source, attn_w[0]))
    key_rows = round_both(matmul(source, attn_w[1]))
    value_rows = round_both(matmul(source, attn_w[2]))
    mixed = round_both(attend(queries, key_rows, value_rows, segment, False))
    branch = low_back(matmul(mixed, attn_w[3]))
    hidden = layer_norm(source + branch, gains[0], gains[1])
    ffn_rows = feed_forward(hidden, ffn_up[0], ffn_down[0])
    return layer_norm(ffn_rows + hidden + source, gains[2], gains[3])

def decoder_layer(source, enc_low, attn_w, ffn_up, ffn_down, gains, segment):
    queries = round_both(matmul(source, attn_w[4]))
    key_rows = round_both(matmul(source, attn_w[5]))
    value_rows = round_both(matmul(source, attn_w[6]))
    mixed = round_both(attend(queries, key_rows, value_rows, segment, True))
    branch = low_back(matmul(mixed, attn_w[7]))
    first = layer_norm(source + branch, gains[4], gains[5])
    cross_q = round_both(matmul(low(first), attn_w[8]))
    cross_k = round_both(matmul(enc_low, attn_w[9]))
    cross_v = round_both(matmul(enc_low, attn_w[10]))
    mixed_two = round_both(attend(cross_q, cross_k, cross_v, segment, False))
    branch_two = low_back(matmul(mixed_two, attn_w[11]))
    second = layer_norm(first + branch_two, gains[6], gains[7])
    ffn_rows = feed_forward(second, ffn_up[1], ffn_down[1])
    return layer_norm(ffn_rows + second + source, gains[8], gains[9])

def forward(enc_rows, dec_rows, attn_w, ffn_up, ffn_down, gains, segment):
    encoded = encoder_layer(enc_rows, attn_w, ffn_up, ffn_down, gains, segment)
    enc_low = low(encoded)
    decoded = decoder_layer(dec_rows, enc_low, attn_w, ffn_up, ffn_down, gains, segment)
    return (decoded, enc_low)

def lamb(master, grad_all, first, second, count):
    first_new = beta_one * first + (1.0 - beta_one) * grad_all
    second_new = beta_two * second + (1.0 - beta_two) * grad_all * grad_all
    update = first_new / (1.0 - beta_one ** STEP) / (jnp.sqrt(second_new / (1.0 - beta_two ** STEP)) + lamb_eps) + weight_decay * master
    grouped_w = master.reshape(count, -1)
    grouped_u = update.reshape(count, -1)
    weight_norm = jnp.sqrt(lax.optimization_barrier(jnp.sum(grouped_w * grouped_w, axis=1)))
    update_norm = jnp.sqrt(lax.optimization_barrier(jnp.sum(grouped_u * grouped_u, axis=1)))
    ratio = weight_norm / update_norm
    new_w = (grouped_w - learn_rate * ratio[:, None] * grouped_u).reshape(master.shape)
    return (first_new, second_new, new_w, weight_norm, update_norm, ratio)

def reference(enc_in, dec_in, cotangent, lengths, attn_master, ffn_in_master, ffn_out_master, norm_master, attn_first, ffn_in_first, ffn_out_first, norm_first, attn_second, ffn_in_second, ffn_out_second, norm_second):
    attn_w = low(attn_master).reshape(12, D, D)
    ffn_up = low(ffn_in_master).reshape(2, D, FF)
    ffn_down = low(ffn_out_master).reshape(2, FF, D)
    gains = low(norm_master).reshape(10, D)
    count = MICRO * STREAMS
    enc_rows = enc_in.astype(jnp.float32).reshape(count, LENGTH, D)
    dec_rows = dec_in.astype(jnp.float32).reshape(count, LENGTH, D)
    cot_rows = cotangent.astype(jnp.float32).reshape(count, LENGTH, D)
    len_rows = lengths.reshape(count, NSENT)

    def per_stream(totals, item):
        enc_one, dec_one, cot_one, len_one = item
        segment = segment_ids(len_one)

        def run(enc_arg, dec_arg, attn_arg, up_arg, down_arg, gain_arg):
            return forward(enc_arg, dec_arg, attn_arg, up_arg, down_arg, gain_arg, segment)
        decoded, pull, enc_low = jax.vjp(run, enc_one, dec_one, attn_w, ffn_up, ffn_down, gains, has_aux=True)
        grads = pull(cot_one)
        new_totals = (totals[0] + grads[2], totals[1] + grads[3], totals[2] + grads[4], totals[3] + grads[5])
        return (new_totals, (enc_low.astype(jnp.bfloat16), decoded.astype(jnp.bfloat16), grads[0], grads[1]))
    start_totals = (jnp.zeros((12, D, D), jnp.float32), jnp.zeros((2, D, FF), jnp.float32), jnp.zeros((2, FF, D), jnp.float32), jnp.zeros((10, D), jnp.float32))
    totals, outs = lax.scan(per_stream, start_totals, (enc_rows, dec_rows, cot_rows, len_rows))
    shape_out = (MICRO, STREAMS, LENGTH, D)
    enc_out = outs[0].reshape(shape_out)
    dec_out = outs[1].reshape(shape_out)
    enc_in_grad = outs[2].reshape(shape_out)
    dec_in_grad = outs[3].reshape(shape_out)
    attn_grad = totals[0].reshape(12 * D, D)
    ffn_in_grad = totals[1].reshape(2 * D, FF)
    ffn_out_grad = totals[2].reshape(2 * FF, D)
    norm_grad = totals[3].reshape(10 * D)
    attn_res = lamb(attn_master, attn_grad, attn_first, attn_second, 12)
    up_res = lamb(ffn_in_master, ffn_in_grad, ffn_in_first, ffn_in_second, 2)
    down_res = lamb(ffn_out_master, ffn_out_grad, ffn_out_first, ffn_out_second, 2)
    norm_res = lamb(norm_master, norm_grad, norm_first, norm_second, 10)
    results = (attn_res, up_res, down_res, norm_res)
    norms = jnp.stack((jnp.concatenate([item[3] for item in results]), jnp.concatenate([item[4] for item in results])))
    trust = jnp.concatenate([item[5] for item in results])
    return (enc_out, dec_out, enc_in_grad, dec_in_grad, attn_grad, ffn_in_grad, ffn_out_grad, norm_grad, attn_res[2], up_res[2], down_res[2], norm_res[2], attn_res[0], up_res[0], down_res[0], norm_res[0], attn_res[1], up_res[1], down_res[1], norm_res[1], attn_res[2].astype(jnp.bfloat16), up_res[2].astype(jnp.bfloat16), down_res[2].astype(jnp.bfloat16), norm_res[2].astype(jnp.bfloat16), norms, trust)
```

```python
import functools
import math

import jax
import jax.numpy as jnp
from jax import lax
from jax.experimental import pallas as pl
from jax.experimental.pallas import tpu as pltpu
from jax.sharding import Mesh
from jax.sharding import PartitionSpec as P

HEADS = 8
STEP = 5
HALO = 256
TILE = 256

norm_eps = 1e-05
beta_one = 0.5
beta_two = 0.5
lamb_eps = 1e-06
weight_decay = 0.01
learn_rate = 0.5
masked_score = -1e30

BF = jnp.bfloat16
F32 = jnp.float32
MIB = 1024 * 1024


def dot_nn(a, b):
    return lax.dot_general(a, b, (((1,), (0,)), ((), ())), preferred_element_type=F32)


def dot_nt(a, b):
    return lax.dot_general(a, b, (((1,), (1,)), ((), ())), preferred_element_type=F32)


def dot_tn(a, b):
    return lax.dot_general(a, b, (((0,), (0,)), ((), ())), preferred_element_type=F32)


def norm_parts(rows):
    centre = rows - jnp.mean(rows, axis=-1, keepdims=True)
    inv = lax.rsqrt(jnp.mean(centre * centre, axis=-1, keepdims=True) + norm_eps)
    return centre * inv, inv


def norm_rows(rows, gain, bias):
    return norm_parts(rows)[0] * gain + bias


def norm_back(rows, gain, grad):
    unit, inv = norm_parts(rows)
    lead = grad * gain
    back = inv * (
        lead
        - jnp.mean(lead, axis=-1, keepdims=True)
        - unit * jnp.mean(lead * unit, axis=-1, keepdims=True)
    )
    return (
        back,
        jnp.sum(grad * unit, axis=0, keepdims=True),
        jnp.sum(grad, axis=0, keepdims=True),
    )


gelu_a = 0.7978845608028654
gelu_b = 0.044715


def gelu(v):
    return 0.5 * v * (1.0 + jnp.tanh(gelu_a * (v + gelu_b * (v * v * v))))


def gelu_both(v):
    sq = v * v
    t = jnp.tanh(gelu_a * (v + gelu_b * (sq * v)))
    half = 0.5 * (1.0 + t)
    slope = half + 0.5 * v * (1.0 - t * t) * (gelu_a * (1.0 + 3.0 * gelu_b * sq))
    return v * half, slope


def matrix(ref, index, width):
    shards = ref.shape[0]
    per = 6 * width // shards
    pieces = []
    row, end = index * width, (index + 1) * width
    while row < end:
        shard, place = divmod(row, per)
        take = min(per - place, end - row)
        pieces.append(ref[shard, place : place + take, :])
        row += take
    return pieces[0] if len(pieces) == 1 else jnp.concatenate(pieces, axis=0)


def lane_low(shape):
    return lax.broadcasted_iota(jnp.int32, shape, 1) < 64


def attn_fwd_body(cfg, *refs):
    causal, normed, picks, gain_at = cfg
    q_src, kv_src, blk0, blk1, gains, qcol, krow, q_out, k_out, v_out, o_out, lse_out, res_out = refs
    blocks = (blk0, blk1)
    rows, width = q_src.shape

    def weight(slot):
        return matrix(blocks[picks[slot] // 6], picks[slot] % 6, width)

    if normed:
        base = norm_rows(q_src[...], gains[gain_at : gain_at + 1, :], gains[gain_at + 1 : gain_at + 2, :])
        low_src = base.astype(BF)
    else:
        base = None
        low_src = q_src[...]
    queries = dot_nn(low_src, weight(0))
    q_out[...] = (queries.astype(BF).astype(F32) * 0.125).astype(BF)
    k_out[...] = dot_nn(kv_src[...], weight(1)).astype(BF)
    v_out[...] = dot_nn(kv_src[...], weight(2)).astype(BF)
    window = k_out.shape[0]
    kseg = krow[0:1, :]
    kpos = krow[1:2, :]

    def tile_step(index, carry):
        spot = pl.ds(pl.multiple_of(index * TILE, TILE), TILE)
        allowed = qcol[spot, 0:1] == kseg
        if causal:
            allowed = allowed & (kpos <= qcol[spot, 1:2])
        low = lane_low((TILE, 128))
        low_w = lane_low((window, 128))
        totals = []
        for pair in range(HEADS // 2):
            lanes = slice(pair * 128, pair * 128 + 128)
            q2 = q_out[spot, lanes]
            k2 = k_out[:, lanes]
            v2 = v_out[:, lanes]
            mixed = None
            for half in range(2):
                keep = low if half == 0 else ~low
                keep_w = low_w if half == 0 else ~low_w
                scores = dot_nt(jnp.where(keep, q2, jnp.zeros_like(q2)), k2)
                scores = jnp.where(allowed, scores, masked_score)
                top = jnp.max(scores, axis=-1, keepdims=True)
                weights = jnp.exp(scores - top)
                total = jnp.sum(weights, axis=-1, keepdims=True)
                probs = (weights * (1.0 / total)).astype(BF)
                part = dot_nn(probs, jnp.where(keep_w, v2, jnp.zeros_like(v2)))
                mixed = part if mixed is None else mixed + part
                totals.append(top + jnp.log(total))
            o_out[spot, lanes] = mixed.astype(BF)
        lane = lax.broadcasted_iota(jnp.int32, (TILE, 128), 1)
        packed = jnp.zeros((TILE, 128), F32)
        for head in range(HEADS):
            packed = jnp.where(lane == head, totals[head], packed)
        lse_out[:, spot] = jnp.transpose(packed)[0:HEADS, :]
        return carry

    lax.fori_loop(0, rows // TILE, tile_step, 0)
    branch = dot_nn(o_out[...], weight(3))
    if base is None:
        base = q_src[...].astype(F32)
    else:
        base = norm_rows(q_src[...], gains[gain_at : gain_at + 1, :], gains[gain_at + 1 : gain_at + 2, :])
    res_out[...] = base + branch


def params(limit=40):
    return pltpu.CompilerParams(vmem_limit_bytes=limit * MIB)


def attn_forward(q_src, kv_src, blocks, gains, places, causal, picks, gain_at):
    rows, width = q_src.shape
    window = kv_src.shape[0]
    shapes = (
        jax.ShapeDtypeStruct((rows, width), BF),
        jax.ShapeDtypeStruct((window, width), BF),
        jax.ShapeDtypeStruct((window, width), BF),
        jax.ShapeDtypeStruct((rows, width), BF),
        jax.ShapeDtypeStruct((HEADS, rows), F32),
        jax.ShapeDtypeStruct((rows, width), F32),
    )
    cfg = (causal, gain_at is not None, picks, gain_at)
    return pl.pallas_call(
        functools.partial(attn_fwd_body, cfg),
        out_shape=shapes,
        compiler_params=params(),
        cost_estimate=pl.CostEstimate(
            flops=12 * rows * width * width + 8 * rows * window * width,
            bytes_accessed=12 * MIB,
            transcendentals=0,
        ),
        name="attn_fwd",
    )(q_src, kv_src, blocks[0], blocks[1], gains, places["qcol"], places["krow"])


def attn_bwd_body(cfg, *refs):
    causal, picks, gain_at, src_gain = cfg
    (
        grad_in, resid, src, q_in, k_in, v_in, o_in, lse_in, blk0, blk1, gains, qrow, kcol,
        gq_out, dwq_out, dwo_out, own_out, halo_out, ng_out, do_scr, dq_scr, dk_scr, dv_scr,
    ) = refs
    blocks = (blk0, blk1)
    rows, width = q_in.shape
    window = k_in.shape[0]

    def weight(slot):
        return matrix(blocks[picks[slot] // 6], picks[slot] % 6, width)

    back, dgain, dbias = norm_back(resid[...], gains[gain_at : gain_at + 1, :], grad_in[...].astype(F32))
    gq_out[...] = back
    ng_out[0:1, :] = dgain
    ng_out[1:2, :] = dbias
    branch = back.astype(BF)
    dwo_out[...] = dot_tn(o_in[...], branch).astype(BF)
    do_scr[...] = dot_nt(branch, weight(3)).astype(BF)
    dk_scr[...] = jnp.zeros_like(dk_scr)
    dv_scr[...] = jnp.zeros_like(dv_scr)
    kseg = kcol[:, 0:1]
    kpos = kcol[:, 1:2]

    def tile_step(index, carry):
        spot = pl.ds(pl.multiple_of(index * TILE, TILE), TILE)
        allowed = kseg == qrow[0:1, spot]
        if causal:
            allowed = allowed & (kpos <= qrow[1:2, spot])
        low = lane_low((TILE, 128))
        low_w = lane_low((window, 128))
        for pair in range(HEADS // 2):
            lanes = slice(pair * 128, pair * 128 + 128)
            q2 = q_in[spot, lanes]
            do2 = do_scr[spot, lanes]
            k2 = k_in[:, lanes]
            v2 = v_in[:, lanes]
            dq2 = None
            dk2 = None
            dv2 = None
            for half in range(2):
                keep = low if half == 0 else ~low
                keep_w = low_w if half == 0 else ~low_w
                head = 2 * pair + half
                qh = jnp.where(keep, q2, jnp.zeros_like(q2))
                doh = jnp.where(keep, do2, jnp.zeros_like(do2))
                scores = jnp.where(allowed, dot_nt(k2, qh), masked_score)
                probs = jnp.exp(scores - lse_in[head : head + 1, spot])
                gprobs = dot_nt(v2, doh)
                delta = jnp.sum(gprobs * probs, axis=0, keepdims=True)
                gscores = (probs * (gprobs - delta)).astype(BF)
                part_v = dot_nn(probs.astype(BF), doh)
                part_k = dot_nn(gscores, qh)
                part_q = dot_tn(gscores, jnp.where(keep_w, k2, jnp.zeros_like(k2)))
                dv2 = part_v if dv2 is None else dv2 + part_v
                dk2 = part_k if dk2 is None else dk2 + part_k
                dq2 = part_q if dq2 is None else dq2 + part_q
            dq_scr[spot, lanes] = (dq2 * 0.125).astype(BF)
            dk_scr[:, lanes] += dk2
            dv_scr[:, lanes] += dv2
        return carry

    lax.fori_loop(0, rows // TILE, tile_step, 0)
    own_out[0] = dk_scr[0:rows, :]
    own_out[1] = dv_scr[0:rows, :]
    halo_out[0] = dk_scr[rows:window, :].astype(BF)
    halo_out[1] = dv_scr[rows:window, :].astype(BF)
    if src_gain is None:
        low_src = src[...]
    else:
        low_src = norm_rows(src[...], gains[src_gain : src_gain + 1, :], gains[src_gain + 1 : src_gain + 2, :]).astype(BF)
    dwq_out[...] = dot_tn(low_src, dq_scr[...]).astype(BF)
    gq_out[...] += dot_nt(dq_scr[...], weight(0))


def attn_backward(grad_in, resid, src, kept, blocks, gains, places, causal, picks, gain_at, src_gain):
    q, k, v, o, lse = kept
    rows, width = q.shape
    window = k.shape[0]
    shapes = (
        jax.ShapeDtypeStruct((rows, width), F32),
        jax.ShapeDtypeStruct((width, width), BF),
        jax.ShapeDtypeStruct((width, width), BF),
        jax.ShapeDtypeStruct((2, rows, width), F32),
        jax.ShapeDtypeStruct((2, window - rows, width), BF),
        jax.ShapeDtypeStruct((2, width), F32),
    )
    return pl.pallas_call(
        functools.partial(attn_bwd_body, (causal, picks, gain_at, src_gain)),
        out_shape=shapes,
        scratch_shapes=[
            pltpu.VMEM((rows, width), BF),
            pltpu.VMEM((rows, width), BF),
            pltpu.VMEM((window, width), F32),
            pltpu.VMEM((window, width), F32),
        ],
        compiler_params=params(),
        cost_estimate=pl.CostEstimate(
            flops=8 * rows * width * width + 20 * rows * window * width,
            bytes_accessed=16 * MIB,
            transcendentals=0,
        ),
        name="attn_bwd",
    )(grad_in, resid, src, q, k, v, o, lse, blocks[0], blocks[1], gains, places["qrow"], places["kcol"])


def kv_bwd_body(cfg, *refs):
    picks, offsets, n_add = cfg
    spot_ref, src, own, halo, blk0, blk1 = refs[:6]
    adds = refs[6 : 6 + n_add]
    g_out, dwk_out, dwv_out, scr = refs[6 + n_add :]
    blocks = (blk0, blk1)
    rows, width = src.shape

    def weight(slot):
        return matrix(blocks[picks[slot] // 6], picks[slot] % 6, width)

    scr[...] = own[...]
    if offsets is None:
        spot = pl.ds(pl.multiple_of(spot_ref[0], HALO), HALO)
        scr[:, spot, :] += halo[...].astype(F32)
    else:
        for index, offset in enumerate(offsets):
            scr[:, offset : offset + HALO, :] += halo[:, index * HALO : index * HALO + HALO, :].astype(F32)
    dk = scr[0].astype(BF)
    dv = scr[1].astype(BF)
    dwk_out[...] = dot_tn(src[...], dk).astype(BF)
    dwv_out[...] = dot_tn(src[...], dv).astype(BF)
    total = dot_nt(dk, weight(1)) + dot_nt(dv, weight(2))
    for ref in adds:
        total = total + ref[...]
    g_out[...] = total.astype(g_out.dtype)


def kv_backward(src, own, halo, blocks, adds, places, picks, out_type):
    rows, width = src.shape
    vmem = pl.BlockSpec(memory_space=pltpu.VMEM)
    return pl.pallas_call(
        functools.partial(kv_bwd_body, (picks, places["offsets"], len(adds))),
        out_shape=(
            jax.ShapeDtypeStruct((rows, width), out_type),
            jax.ShapeDtypeStruct((width, width), BF),
            jax.ShapeDtypeStruct((width, width), BF),
        ),
        in_specs=[pl.BlockSpec(memory_space=pltpu.SMEM)] + [vmem] * (5 + len(adds)),
        out_specs=(vmem, vmem, vmem),
        scratch_shapes=[pltpu.VMEM((2, rows, width), F32)],
        compiler_params=params(),
        cost_estimate=pl.CostEstimate(
            flops=8 * rows * width * width, bytes_accessed=14 * MIB, transcendentals=0
        ),
        name="kv_bwd",
    )(places["spot"], src, own, halo, blocks[0], blocks[1], *adds)


def ffn_fwd_body(cfg, resid, base, gains, w_up, w_down, res_out, low_out, hid, hid_low, acc):
    gain_in, gain_out = cfg
    step = pl.program_id(0)

    @pl.when(step == 0)
    def start():
        rows = norm_rows(resid[...], gains[gain_in : gain_in + 1, :], gains[gain_in + 1 : gain_in + 2, :])
        hid[...] = rows
        hid_low[...] = rows.astype(BF)
        acc[...] = jnp.zeros_like(acc)

    activ = gelu(dot_nn(hid_low[...], w_up[...])).astype(BF)
    acc[...] += dot_nn(activ, w_down[...])

    @pl.when(step == pl.num_programs(0) - 1)
    def end():
        total = acc[...] + hid[...] + base[...].astype(F32)
        res_out[...] = total
        low_out[...] = norm_rows(
            total, gains[gain_out : gain_out + 1, :], gains[gain_out + 1 : gain_out + 2, :]
        ).astype(BF)


def ffn_forward(resid, base, gains, w_up, w_down, gain_in, gain_out):
    rows, width = resid.shape
    units = w_up.shape[1]
    tile = 512
    full = pl.BlockSpec((rows, width), lambda t: (0, 0))
    return pl.pallas_call(
        functools.partial(ffn_fwd_body, (gain_in, gain_out)),
        grid=(units // tile,),
        in_specs=[
            full,
            full,
            pl.BlockSpec(gains.shape, lambda t: (0, 0)),
            pl.BlockSpec((width, tile), lambda t: (0, t)),
            pl.BlockSpec((tile, width), lambda t: (t, 0)),
        ],
        out_specs=(full, full),
        out_shape=(jax.ShapeDtypeStruct((rows, width), F32), jax.ShapeDtypeStruct((rows, width), BF)),
        scratch_shapes=[
            pltpu.VMEM((rows, width), F32),
            pltpu.VMEM((rows, width), BF),
            pltpu.VMEM((rows, width), F32),
        ],
        compiler_params=params(),
        cost_estimate=pl.CostEstimate(
            flops=4 * rows * width * units, bytes_accessed=7 * MIB, transcendentals=rows * units
        ),
        name="ffn_fwd",
    )(resid, base, gains, w_up, w_down)


def ffn_bwd_body(
    cfg, grad_in, res_late, resid, gains, w_up, w_down, gh_out, late_out, dup_out, ddown_out, ng_out,
    hid_low, late_low,
):
    gain_in, gain_out = cfg
    step = pl.program_id(0)

    @pl.when(step == 0)
    def start():
        back, dgain, dbias = norm_back(
            res_late[...], gains[gain_out : gain_out + 1, :], grad_in[...].astype(F32)
        )
        late_out[...] = back
        gh_out[...] = back
        late_low[...] = back.astype(BF)
        ng_out[0:1, :] = dgain
        ng_out[1:2, :] = dbias
        hid_low[...] = norm_rows(
            resid[...], gains[gain_in : gain_in + 1, :], gains[gain_in + 1 : gain_in + 2, :]
        ).astype(BF)

    activ, slope = gelu_both(dot_nn(hid_low[...], w_up[...]))
    ddown_out[...] = dot_tn(activ.astype(BF), late_low[...]).astype(BF)
    grad_act = dot_nt(late_low[...], w_down[...]).astype(BF).astype(F32)
    grad_pre = (grad_act * slope).astype(BF)
    dup_out[...] = dot_tn(hid_low[...], grad_pre).astype(BF)
    gh_out[...] += dot_nt(grad_pre, w_up[...])


def ffn_backward(grad_in, res_late, resid, gains, w_up, w_down, gain_in, gain_out):
    rows, width = resid.shape
    units = w_up.shape[1]
    tile = 512
    full = pl.BlockSpec((rows, width), lambda t: (0, 0))
    up = pl.BlockSpec((width, tile), lambda t: (0, t))
    down = pl.BlockSpec((tile, width), lambda t: (t, 0))
    return pl.pallas_call(
        functools.partial(ffn_bwd_body, (gain_in, gain_out)),
        grid=(units // tile,),
        in_specs=[full, full, full, pl.BlockSpec(gains.shape, lambda t: (0, 0)), up, down],
        out_specs=(full, full, up, down, pl.BlockSpec((2, width), lambda t: (0, 0))),
        out_shape=(
            jax.ShapeDtypeStruct((rows, width), F32),
            jax.ShapeDtypeStruct((rows, width), F32),
            jax.ShapeDtypeStruct((width, units), BF),
            jax.ShapeDtypeStruct((units, width), BF),
            jax.ShapeDtypeStruct((2, width), F32),
        ),
        scratch_shapes=[pltpu.VMEM((rows, width), BF), pltpu.VMEM((rows, width), BF)],
        compiler_params=params(),
        cost_estimate=pl.CostEstimate(
            flops=10 * rows * width * units, bytes_accessed=14 * MIB, transcendentals=rows * units
        ),
        name="ffn_bwd",
    )(grad_in, res_late, resid, gains, w_up, w_down)


def segments_at(bounds, places, total_len):
    found = jnp.sum((bounds[None, :] <= places[:, None]).astype(jnp.int32), axis=-1)
    return jnp.where((places >= 0) & (places < total_len), found, -1)


def row_squares(values):
    if values.ndim == 2:
        return jnp.sum(values * values, axis=1)
    return values * values


def owner_groups(rows_local, owner, per_group, count):
    group_ids = (owner * rows_local + jnp.arange(rows_local, dtype=jnp.int32)) // per_group
    return group_ids[:, None] == jnp.arange(count, dtype=jnp.int32)[None, :]


def group_sum(onehot, row_values):
    return jnp.sum(jnp.where(onehot, row_values[:, None], 0.0), axis=0)


def lamb_moments(master, grad_rows, first, second):
    first_new = beta_one * first + (1.0 - beta_one) * grad_rows
    second_new = beta_two * second + (1.0 - beta_two) * grad_rows * grad_rows
    update = (
        first_new
        / (1.0 - beta_one**STEP)
        / (jnp.sqrt(second_new / (1.0 - beta_two**STEP)) + lamb_eps)
        + weight_decay * master
    )
    return (first_new, second_new, update)


GROUP = ("lo", "stream")
EVERY = ("hi", "lo", "stream")


def swap_hi(array):
    return lax.ppermute(array, "hi", [(0, 1), (1, 0)])


def shift_hi(array, distance):
    count = lax.axis_size("hi")
    route = [(i - distance, i) for i in range(count) if i - distance in range(count)]
    return lax.ppermute(array, "hi", route)


def halo_rows(rows_array):
    high = lax.axis_index("hi")
    rows = rows_array.shape[-2]
    axis = rows_array.ndim - 2
    if lax.axis_size("hi") == 2:
        sent = jnp.where(
            high == 0,
            lax.slice_in_dim(rows_array, rows - HALO, rows, axis=axis),
            lax.slice_in_dim(rows_array, 0, HALO, axis=axis),
        )
        return swap_hi(sent)
    left = shift_hi(lax.slice_in_dim(rows_array, rows - HALO, rows, axis=axis), 1)
    right = shift_hi(lax.slice_in_dim(rows_array, 0, HALO, axis=axis), -1)
    return jnp.concatenate((left, right), axis=axis)


def halo_return(grads):
    if lax.axis_size("hi") == 2:
        return swap_hi(grads)
    to_left = shift_hi(grads[:, :HALO], -1)
    to_right = shift_hi(grads[:, HALO:], 1)
    return jnp.concatenate((to_left, to_right), axis=1)


def spread_blocks(shard):
    count = lax.axis_size("hi")
    if count == 2:
        other = swap_hi(shard)
        first = lax.axis_index("hi") == 0
        return (jnp.where(first, shard, other)[None], jnp.where(first, other, shard)[None])
    gathered = lax.all_gather(shard, "hi", axis=0, tiled=False)
    return (gathered[: count // 2], gathered[count // 2 :])


def gather_block(rows):
    owners, per, width = rows.shape
    full = lax.all_gather(rows, GROUP, axis=0, tiled=False)
    if owners == 1:
        return full[:, 0]
    return full.swapaxes(0, 1).reshape(1, -1, width)


def scatter_block(grads, owners):
    group = lax.axis_size("lo") * lax.axis_size("stream")
    rows, width = grads.shape
    if owners > 1:
        grads = grads.reshape(owners, group, rows // (owners * group), width).swapaxes(0, 1)
        grads = grads.reshape(rows, width)
    part = lax.psum_scatter(grads, GROUP, scatter_dimension=0, tiled=True)
    return part.reshape(owners, -1, width)


def finish_blocks(parts):
    if lax.axis_size("hi") == 2:
        first = lax.axis_index("hi") == 0
        mine = jnp.where(first, parts[0][0], parts[1][0])
        sent = jnp.where(first, parts[1][0], parts[0][0])
        return mine.astype(F32) + swap_hi(sent).astype(F32)
    whole = jnp.concatenate(parts, axis=0)
    return lax.psum_scatter(whole, "hi", scatter_dimension=0, tiled=False).astype(F32)


def shards(
    enc_in,
    dec_in,
    cotangent,
    lengths,
    attn_master,
    ffn_in_master,
    ffn_out_master,
    norm_master,
    attn_first,
    ffn_in_first,
    ffn_out_first,
    norm_first,
    attn_second,
    ffn_in_second,
    ffn_out_second,
    norm_second,
):
    micro, _, length_dev, width = enc_in.shape
    rows = micro * length_dev
    hidden_units = ffn_in_master.shape[1]
    high, low, stream = lax.axis_index("hi"), lax.axis_index("lo"), lax.axis_index("stream")
    n_high = lax.axis_size("hi")
    group = micro * lax.axis_size("stream")
    place = low * lax.axis_size("stream") + stream
    owner = high * group + place
    owners = n_high // 2
    masters = (attn_master, ffn_in_master, ffn_out_master, norm_master)
    group_info = ((width, 12), (width, 2), (hidden_units, 2), (width, 10))
    onehots = [
        owner_groups(master.shape[0], owner, info[0], info[1])
        for master, info in zip(masters, group_info)
    ]
    weight_local = jnp.concatenate(
        [group_sum(onehot, row_squares(master)) for onehot, master in zip(onehots, masters)]
    )

    attn_rows = attn_master.shape[0]
    norm_count = norm_master.shape[0]
    norm_pad = max(16, n_high)
    norm_shard = jnp.pad(norm_master.astype(BF)[None, :], ((0, 15), (0, width - norm_count)))
    attn_part = jnp.concatenate((attn_master.astype(BF), norm_shard), axis=0)
    attn_spread = spread_blocks(attn_part)
    norm_spread = jnp.concatenate([part[:, attn_rows] for part in attn_spread], axis=0)
    norm_spread = jnp.pad(norm_spread, ((0, norm_pad - n_high), (0, 0)))
    up_spread = spread_blocks(ffn_in_master.astype(BF))
    down_spread = spread_blocks(ffn_out_master.astype(BF))
    if owners == 1:
        with_norm = jnp.concatenate((attn_spread[0][:, :attn_rows], norm_spread[None]), axis=1)
        block0 = gather_block(with_norm)
        norm_all = block0[:, attn_rows:]
    else:
        block0 = gather_block(attn_spread[0][:, :attn_rows])
        norm_all = lax.all_gather(norm_spread, GROUP, axis=0, tiled=False)
    gains = norm_all[:, :n_high, :norm_count].swapaxes(0, 1).reshape(10, width).astype(F32)
    up0 = gather_block(up_spread[0]).reshape(width, hidden_units)
    down0 = gather_block(down_spread[0]).reshape(hidden_units, width)
    block1 = gather_block(attn_spread[1][:, :attn_rows])
    up1 = gather_block(up_spread[1]).reshape(width, hidden_units)
    down1 = gather_block(down_spread[1]).reshape(hidden_units, width)
    blocks = (block0, block1)

    packed = jnp.stack((enc_in[:, 0], dec_in[:, 0], cotangent[:, 0]), axis=1)
    packed = lax.all_to_all(packed, "lo", split_axis=0, concat_axis=0, tiled=True)
    packed = packed.swapaxes(0, 1).reshape(3, rows, width)
    enc_rows, dec_rows, cot_rows = packed[0], packed[1], packed[2]
    halos = halo_rows(packed[:2])
    enc_window = jnp.concatenate((enc_rows, halos[0]), axis=0)
    dec_window = jnp.concatenate((dec_rows, halos[1]), axis=0)

    total_len = rows * n_high
    bounds = jnp.cumsum(lengths[:, 0, :], axis=-1)
    bounds = lax.dynamic_index_in_dim(bounds, low, 0, keepdims=False)
    base = high * rows
    own_pos = base + jnp.arange(rows, dtype=jnp.int32)
    step = jnp.arange(HALO, dtype=jnp.int32)
    if n_high == 2:
        halo_pos = jnp.where(high == 0, rows, rows - HALO) + step
    else:
        halo_pos = jnp.concatenate((base - HALO + step, base + rows + step))
    key_pos = jnp.concatenate((own_pos, halo_pos))
    key_seg = segments_at(bounds, key_pos, total_len)
    krow = jnp.stack((key_seg, key_pos), axis=0)
    kcol = jnp.stack((key_seg, key_pos), axis=1)
    places = {
        "krow": krow,
        "kcol": kcol,
        "qrow": krow[:, :rows],
        "qcol": kcol[:rows],
        "offsets": None if n_high == 2 else (0, rows - HALO),
        "spot": jnp.where(high == 0, rows - HALO, 0).astype(jnp.int32).reshape(1),
    }

    enc_picks, self_picks, cross_picks = (0, 1, 2, 3), (4, 5, 6, 7), (8, 9, 10, 11)
    *enc_kept, resid_one = attn_forward(
        enc_rows, enc_window, (block0, block0), gains, places, False, enc_picks, None
    )
    resid_two, enc_low = ffn_forward(resid_one, enc_rows, gains, up0, down0, 0, 2)
    low_window = jnp.concatenate((enc_low, halo_rows(enc_low)), axis=0)
    *self_kept, resid_three = attn_forward(
        dec_rows, dec_window, blocks, gains, places, True, self_picks, None
    )
    *cross_kept, resid_four = attn_forward(
        resid_three, low_window, (block1, block1), gains, places, False, cross_picks, 4
    )
    resid_five, dec_low = ffn_forward(resid_four, dec_rows, gains, up1, down1, 6, 8)

    grad_second, grad_five, dup1, ddown1, ng8 = ffn_backward(
        cot_rows, resid_five, resid_four, gains, up1, down1, 6, 8
    )
    up_part1 = scatter_block(dup1, owners)
    down_part1 = scatter_block(ddown1, owners)
    grad_first, dwq_c, dwo_c, own_c, halo_c, ng6 = attn_backward(
        grad_second, resid_four, resid_three, cross_kept, (block1, block1), gains, places, False, cross_picks, 6, 4
    )
    back_c = halo_return(halo_c)
    grad_dec_q, dwq_s, dwo_s, own_s, halo_s, ng4 = attn_backward(
        grad_first, resid_three, dec_rows, self_kept, blocks, gains, places, True, self_picks, 4, None
    )
    back_s = halo_return(halo_s)
    enc_rows_low = enc_low
    grad_encoded, dwk_c, dwv_c = kv_backward(
        enc_rows_low, own_c, back_c, (block1, block1), (), places, cross_picks, F32
    )
    dec_grad, dwk_s, dwv_s = kv_backward(
        dec_rows, own_s, back_s, blocks, (grad_five, grad_dec_q), places, self_picks, BF
    )
    attn_part1 = scatter_block(
        jnp.concatenate((dwv_s, dwo_s, dwq_c, dwk_c, dwv_c, dwo_c), axis=0), owners
    )
    grad_hidden, grad_two, dup0, ddown0, ng2 = ffn_backward(
        grad_encoded, resid_two, resid_one, gains, up0, down0, 0, 2
    )
    up_part0 = scatter_block(dup0, owners)
    down_part0 = scatter_block(ddown0, owners)
    grad_enc_q, dwq_e, dwo_e, own_e, halo_e, ng0 = attn_backward(
        grad_hidden, resid_one, enc_rows, enc_kept, (block0, block0), gains, places, False, enc_picks, 0, None
    )
    back_e = halo_return(halo_e)
    enc_grad, dwk_e, dwv_e = kv_backward(
        enc_rows, own_e, back_e, (block0, block0), (grad_two, grad_enc_q), places, enc_picks, BF
    )
    attn_local0 = jnp.concatenate((dwq_e, dwk_e, dwv_e, dwo_e, dwq_s, dwk_s), axis=0)
    norm_local = jnp.concatenate((ng0, ng2, ng4, ng6, ng8), axis=0)
    norm_local = norm_local.reshape(n_high, group, norm_count).swapaxes(0, 1).astype(BF)
    norm_local = jnp.pad(norm_local, ((0, 0), (0, norm_pad - n_high), (0, width - norm_count)))
    if owners == 1:
        local = jnp.concatenate((attn_local0.reshape(group, attn_rows, width), norm_local), axis=1)
        part = scatter_block(local.reshape(-1, width), 1)
        attn_part0, norm_part = part[:, :attn_rows], part[0, attn_rows:]
        first = high == 0
        mine = jnp.concatenate((jnp.where(first, attn_part0[0], attn_part1[0]), norm_part), axis=0)
        sent = jnp.concatenate((jnp.where(first, attn_part1[0], attn_part0[0]), norm_part), axis=0)
        both = mine.astype(F32) + swap_hi(sent).astype(F32)
        attn_own = both[:attn_rows]
        norm_own = lax.dynamic_index_in_dim(both[attn_rows:], high, 0, keepdims=False)[:norm_count]
    else:
        attn_part0 = scatter_block(attn_local0, owners)
        norm_part = lax.psum_scatter(norm_local, GROUP, scatter_dimension=0, tiled=True)[0]
        attn_own = finish_blocks((attn_part0, attn_part1))
        norm_own = lax.psum(norm_part.astype(F32), "hi")
        norm_own = lax.dynamic_index_in_dim(norm_own, high, 0, keepdims=False)[:norm_count]
    up_own = finish_blocks((up_part0, up_part1))
    down_own = finish_blocks((down_part0, down_part1))

    outs = jnp.stack((enc_low, dec_low, enc_grad, dec_grad), axis=0)
    outs = outs.reshape(4, micro, length_dev, width).swapaxes(0, 1)
    outs = lax.all_to_all(outs, "lo", split_axis=0, concat_axis=0, tiled=True)

    owned = (attn_own, up_own, down_own, norm_own)
    firsts = (attn_first, ffn_in_first, ffn_out_first, norm_first)
    seconds = (attn_second, ffn_in_second, ffn_out_second, norm_second)
    moments = [
        lamb_moments(masters[index], owned[index], firsts[index], seconds[index])
        for index in range(4)
    ]
    update_local = jnp.concatenate(
        [group_sum(onehots[index], row_squares(moments[index][2])) for index in range(4)]
    )
    squares = jnp.stack((weight_local, update_local))
    squares = jnp.pad(squares, ((0, 6), (0, 128 - squares.shape[1])))
    squares = jnp.sum(lax.all_gather(squares, EVERY, axis=0, tiled=False), axis=0)
    norms = jnp.sqrt(squares[:2, :26])
    ratio = norms[0] / norms[1]
    bounds_at = (0, 12, 14, 16, 26)
    new_weights = []
    for index in range(4):
        row_ratio = jnp.sum(
            jnp.where(onehots[index], ratio[None, bounds_at[index] : bounds_at[index + 1]], 0.0), axis=1
        )
        if masters[index].ndim == 2:
            row_ratio = row_ratio[:, None]
        new_weights.append(masters[index] - learn_rate * row_ratio * moments[index][2])
    return (
        outs[:, 0][:, None],
        outs[:, 1][:, None],
        outs[:, 2][:, None].astype(F32),
        outs[:, 3][:, None].astype(F32),
        *owned,
        *new_weights,
        *[item[0] for item in moments],
        *[item[1] for item in moments],
        *[item.astype(BF) for item in new_weights],
        norms,
        ratio,
    )


def solution(mesh):
    count_seq, count_stream = mesh.shape["seq"], mesh.shape["stream"]

    def run(*args):
        micro = args[0].shape[0]
        split = Mesh(
            mesh.devices.reshape(count_seq // micro, micro, count_stream), ("hi", "lo", "stream")
        )
        tokens = P(None, "stream", ("hi", "lo"), None)
        wide = P(("hi", "lo", "stream"), None)
        flat = P(("hi", "lo", "stream"))
        owned = (wide, wide, wide, flat)
        return jax.shard_map(
            shards,
            mesh=split,
            in_specs=(tokens, tokens, tokens, P(None, "stream", None), *owned, *owned, *owned),
            out_specs=(tokens, tokens, tokens, tokens, *owned, *owned, *owned, *owned, *owned, P(), P()),
            check_vma=False,
        )(*args)

    return run
```

```python
import functools
import math

import jax
import jax.numpy as jnp
from jax import lax
from jax.experimental import pallas as pl
from jax.experimental.pallas import tpu as pltpu
from jax.sharding import Mesh
from jax.sharding import PartitionSpec as P

HEADS = 8
STEP = 5
HALO = 256
TILE = 256

norm_eps = 1e-05
beta_one = 0.5
beta_two = 0.5
lamb_eps = 1e-06
weight_decay = 0.01
learn_rate = 0.5
masked_score = -1e30

BF = jnp.bfloat16
F32 = jnp.float32
MIB = 1024 * 1024


def dot_nn(a, b):
    return lax.dot_general(a, b, (((1,), (0,)), ((), ())), preferred_element_type=F32)


def dot_nt(a, b):
    return lax.dot_general(a, b, (((1,), (1,)), ((), ())), preferred_element_type=F32)


def dot_tn(a, b):
    return lax.dot_general(a, b, (((0,), (0,)), ((), ())), preferred_element_type=F32)


def norm_parts(rows):
    centre = rows - jnp.mean(rows, axis=-1, keepdims=True)
    inv = lax.rsqrt(jnp.mean(centre * centre, axis=-1, keepdims=True) + norm_eps)
    return centre * inv, inv


def norm_rows(rows, gain, bias):
    return norm_parts(rows)[0] * gain + bias


def norm_back(rows, gain, grad):
    unit, inv = norm_parts(rows)
    lead = grad * gain
    back = inv * (
        lead
        - jnp.mean(lead, axis=-1, keepdims=True)
        - unit * jnp.mean(lead * unit, axis=-1, keepdims=True)
    )
    return (
        back,
        jnp.sum(grad * unit, axis=0, keepdims=True),
        jnp.sum(grad, axis=0, keepdims=True),
    )


gelu_a = 0.7978845608028654
gelu_b = 0.044715


def gelu(v):
    return 0.5 * v * (1.0 + jnp.tanh(gelu_a * (v + gelu_b * (v * v * v))))


def gelu_both(v):
    sq = v * v
    t = jnp.tanh(gelu_a * (v + gelu_b * (sq * v)))
    half = 0.5 * (1.0 + t)
    slope = half + 0.5 * v * (1.0 - t * t) * (gelu_a * (1.0 + 3.0 * gelu_b * sq))
    return v * half, slope


def matrix(ref, index, width):
    shards = ref.shape[0]
    per = 6 * width // shards
    pieces = []
    row, end = index * width, (index + 1) * width
    while row < end:
        shard, place = divmod(row, per)
        take = min(per - place, end - row)
        pieces.append(ref[shard, place : place + take, :])
        row += take
    return pieces[0] if len(pieces) == 1 else jnp.concatenate(pieces, axis=0)


def lane_low(shape):
    return lax.broadcasted_iota(jnp.int32, shape, 1) < 64


def attn_fwd_body(cfg, *refs):
    causal, normed, picks, gain_at = cfg
    q_src, kv_src, blk0, blk1, gains, qcol, krow, q_out, k_out, v_out, o_out, lse_out, res_out = refs
    blocks = (blk0, blk1)
    rows, width = q_src.shape

    def weight(slot):
        return matrix(blocks[picks[slot] // 6], picks[slot] % 6, width)

    if normed:
        base = norm_rows(q_src[...], gains[gain_at : gain_at + 1, :], gains[gain_at + 1 : gain_at + 2, :])
        low_src = base.astype(BF)
    else:
        base = None
        low_src = q_src[...]
    queries = dot_nn(low_src, weight(0))
    q_out[...] = (queries.astype(BF).astype(F32) * 0.125).astype(BF)
    k_out[...] = dot_nn(kv_src[...], weight(1)).astype(BF)
    v_out[...] = dot_nn(kv_src[...], weight(2)).astype(BF)
    window = k_out.shape[0]
    kseg = krow[0:1, :]
    kpos = krow[1:2, :]

    def tile_step(index, carry):
        spot = pl.ds(pl.multiple_of(index * TILE, TILE), TILE)
        allowed = qcol[spot, 0:1] == kseg
        if causal:
            allowed = allowed & (kpos <= qcol[spot, 1:2])
        low = lane_low((TILE, 128))
        low_w = lane_low((window, 128))
        totals = []
        for pair in range(HEADS // 2):
            lanes = slice(pair * 128, pair * 128 + 128)
            q2 = q_out[spot, lanes]
            k2 = k_out[:, lanes]
            v2 = v_out[:, lanes]
            mixed = None
            for half in range(2):
                keep = low if half == 0 else ~low
                keep_w = low_w if half == 0 else ~low_w
                scores = dot_nt(jnp.where(keep, q2, jnp.zeros_like(q2)), k2)
                scores = jnp.where(allowed, scores, masked_score)
                top = jnp.max(scores, axis=-1, keepdims=True)
                weights = jnp.exp(scores - top)
                total = jnp.sum(weights, axis=-1, keepdims=True)
                probs = (weights * (1.0 / total)).astype(BF)
                part = dot_nn(probs, jnp.where(keep_w, v2, jnp.zeros_like(v2)))
                mixed = part if mixed is None else mixed + part
                totals.append(top + jnp.log(total))
            o_out[spot, lanes] = mixed.astype(BF)
        lane = lax.broadcasted_iota(jnp.int32, (TILE, 128), 1)
        packed = jnp.zeros((TILE, 128), F32)
        for head in range(HEADS):
            packed = jnp.where(lane == head, totals[head], packed)
        lse_out[:, spot] = jnp.transpose(packed)[0:HEADS, :]
        return carry

    lax.fori_loop(0, rows // TILE, tile_step, 0)
    branch = dot_nn(o_out[...], weight(3))
    if base is None:
        base = q_src[...].astype(F32)
    else:
        base = norm_rows(q_src[...], gains[gain_at : gain_at + 1, :], gains[gain_at + 1 : gain_at + 2, :])
    res_out[...] = base + branch


def params(limit):
    return pltpu.CompilerParams(vmem_limit_bytes=limit * MIB)


def attn_forward(q_src, kv_src, blocks, gains, places, causal, picks, gain_at):
    rows, width = q_src.shape
    window = kv_src.shape[0]
    shapes = (
        jax.ShapeDtypeStruct((rows, width), BF),
        jax.ShapeDtypeStruct((window, width), BF),
        jax.ShapeDtypeStruct((window, width), BF),
        jax.ShapeDtypeStruct((rows, width), BF),
        jax.ShapeDtypeStruct((HEADS, rows), F32),
        jax.ShapeDtypeStruct((rows, width), F32),
    )
    cfg = (causal, gain_at is not None, picks, gain_at)
    return pl.pallas_call(
        functools.partial(attn_fwd_body, cfg),
        out_shape=shapes,
        compiler_params=params(12),
        cost_estimate=pl.CostEstimate(
            flops=12 * rows * width * width + 8 * rows * window * width,
            bytes_accessed=12 * MIB,
            transcendentals=0,
        ),
        name="attn_fwd",
    )(q_src, kv_src, blocks[0], blocks[1], gains, places["qcol"], places["krow"])


def attn_bwd_body(cfg, *refs):
    causal, picks, gain_at, src_gain = cfg
    (
        grad_in, resid, src, q_in, k_in, v_in, o_in, lse_in, blk0, blk1, gains, qrow, kcol,
        gq_out, dwq_out, dwo_out, own_out, halo_out, ng_out, do_scr, dq_scr, dk_scr, dv_scr,
    ) = refs
    blocks = (blk0, blk1)
    rows, width = q_in.shape
    window = k_in.shape[0]

    def weight(slot):
        return matrix(blocks[picks[slot] // 6], picks[slot] % 6, width)

    back, dgain, dbias = norm_back(resid[...], gains[gain_at : gain_at + 1, :], grad_in[...].astype(F32))
    gq_out[...] = back
    ng_out[0:1, :] = dgain
    ng_out[1:2, :] = dbias
    branch = back.astype(BF)
    dwo_out[...] = dot_tn(o_in[...], branch).astype(BF)
    do_scr[...] = dot_nt(branch, weight(3)).astype(BF)
    dk_scr[...] = jnp.zeros_like(dk_scr)
    dv_scr[...] = jnp.zeros_like(dv_scr)
    kseg = kcol[:, 0:1]
    kpos = kcol[:, 1:2]

    def tile_step(index, carry):
        spot = pl.ds(pl.multiple_of(index * TILE, TILE), TILE)
        allowed = kseg == qrow[0:1, spot]
        if causal:
            allowed = allowed & (kpos <= qrow[1:2, spot])
        low = lane_low((TILE, 128))
        low_w = lane_low((window, 128))
        for pair in range(HEADS // 2):
            lanes = slice(pair * 128, pair * 128 + 128)
            q2 = q_in[spot, lanes]
            do2 = do_scr[spot, lanes]
            k2 = k_in[:, lanes]
            v2 = v_in[:, lanes]
            dq2 = None
            dk2 = None
            dv2 = None
            for half in range(2):
                keep = low if half == 0 else ~low
                keep_w = low_w if half == 0 else ~low_w
                head = 2 * pair + half
                qh = jnp.where(keep, q2, jnp.zeros_like(q2))
                doh = jnp.where(keep, do2, jnp.zeros_like(do2))
                scores = jnp.where(allowed, dot_nt(k2, qh), masked_score)
                probs = jnp.exp(scores - lse_in[head : head + 1, spot])
                gprobs = dot_nt(v2, doh)
                delta = jnp.sum(gprobs * probs, axis=0, keepdims=True)
                gscores = (probs * (gprobs - delta)).astype(BF)
                part_v = dot_nn(probs.astype(BF), doh)
                part_k = dot_nn(gscores, qh)
                part_q = dot_tn(gscores, jnp.where(keep_w, k2, jnp.zeros_like(k2)))
                dv2 = part_v if dv2 is None else dv2 + part_v
                dk2 = part_k if dk2 is None else dk2 + part_k
                dq2 = part_q if dq2 is None else dq2 + part_q
            dq_scr[spot, lanes] = (dq2 * 0.125).astype(BF)
            dk_scr[:, lanes] += dk2
            dv_scr[:, lanes] += dv2
        return carry

    lax.fori_loop(0, rows // TILE, tile_step, 0)
    own_out[0] = dk_scr[0:rows, :]
    own_out[1] = dv_scr[0:rows, :]
    halo_out[0] = dk_scr[rows:window, :].astype(BF)
    halo_out[1] = dv_scr[rows:window, :].astype(BF)
    if src_gain is None:
        low_src = src[...]
    else:
        low_src = norm_rows(src[...], gains[src_gain : src_gain + 1, :], gains[src_gain + 1 : src_gain + 2, :]).astype(BF)
    dwq_out[...] = dot_tn(low_src, dq_scr[...]).astype(BF)
    gq_out[...] += dot_nt(dq_scr[...], weight(0))


def attn_backward(grad_in, resid, src, kept, blocks, gains, places, causal, picks, gain_at, src_gain):
    q, k, v, o, lse = kept
    rows, width = q.shape
    window = k.shape[0]
    shapes = (
        jax.ShapeDtypeStruct((rows, width), F32),
        jax.ShapeDtypeStruct((width, width), BF),
        jax.ShapeDtypeStruct((width, width), BF),
        jax.ShapeDtypeStruct((2, rows, width), F32),
        jax.ShapeDtypeStruct((2, window - rows, width), BF),
        jax.ShapeDtypeStruct((2, width), F32),
    )
    return pl.pallas_call(
        functools.partial(attn_bwd_body, (causal, picks, gain_at, src_gain)),
        out_shape=shapes,
        scratch_shapes=[
            pltpu.VMEM((rows, width), BF),
            pltpu.VMEM((rows, width), BF),
            pltpu.VMEM((window, width), F32),
            pltpu.VMEM((window, width), F32),
        ],
        compiler_params=params(20),
        cost_estimate=pl.CostEstimate(
            flops=8 * rows * width * width + 20 * rows * window * width,
            bytes_accessed=16 * MIB,
            transcendentals=0,
        ),
        name="attn_bwd",
    )(grad_in, resid, src, q, k, v, o, lse, blocks[0], blocks[1], gains, places["qrow"], places["kcol"])


def kv_bwd_body(cfg, *refs):
    picks, offsets, n_add = cfg
    spot_ref, src, own, halo, blk0, blk1 = refs[:6]
    adds = refs[6 : 6 + n_add]
    g_out, dwk_out, dwv_out, scr = refs[7 + n_add :]
    blocks = (blk0, blk1)
    rows, width = src.shape

    def weight(slot):
        return matrix(blocks[picks[slot] // 6], picks[slot] % 6, width)

    scr[...] = own[...]
    if offsets is None:
        spot = pl.ds(pl.multiple_of(spot_ref[0], HALO), HALO)
        scr[:, spot, :] += halo[...].astype(F32)
    else:
        for index, offset in enumerate(offsets):
            scr[:, offset : offset + HALO, :] += halo[:, index * HALO : index * HALO + HALO, :].astype(F32)
    dk = scr[0].astype(BF)
    dv = scr[1].astype(BF)
    dwk_out[...] = dot_tn(src[...], dk).astype(BF)
    dwv_out[...] = dot_tn(src[...], dv).astype(BF)
    total = dot_nt(dk, weight(1)) + dot_nt(dv, weight(2))
    for ref in adds:
        total = total + ref[...]
    g_out[...] = total.astype(g_out.dtype)


def kv_backward(src, own, halo, blocks, adds, after, places, picks, out_type):
    rows, width = src.shape
    vmem = pl.BlockSpec(memory_space=pltpu.VMEM)
    return pl.pallas_call(
        functools.partial(kv_bwd_body, (picks, places["offsets"], len(adds))),
        out_shape=(
            jax.ShapeDtypeStruct((rows, width), out_type),
            jax.ShapeDtypeStruct((width, width), BF),
            jax.ShapeDtypeStruct((width, width), BF),
        ),
        in_specs=[pl.BlockSpec(memory_space=pltpu.SMEM)] + [vmem] * (6 + len(adds)),
        out_specs=(vmem, vmem, vmem),
        scratch_shapes=[pltpu.VMEM((2, rows, width), F32)],
        compiler_params=params(12),
        cost_estimate=pl.CostEstimate(
            flops=8 * rows * width * width, bytes_accessed=14 * MIB, transcendentals=0
        ),
        name="kv_bwd",
    )(places["spot"], src, own, halo, blocks[0], blocks[1], *adds, after)


def up_tile(pack, tile):
    places, rows, width = pack.shape
    part = pack[:, 128 + 32 * tile : 160 + 32 * tile, :]
    return part.reshape(places * 32, width)


def down_tile(pack, tile):
    return pack[4 * tile : 4 * tile + 4, 0:128, :].reshape(512, pack.shape[2])


def ffn_fwd_body(cfg, resid, base, gains, pack, res_out, low_out):
    gain_in, gain_out = cfg
    hidden = norm_rows(resid[...], gains[gain_in : gain_in + 1, :], gains[gain_in + 1 : gain_in + 2, :])
    low = hidden.astype(BF)
    res_out[...] = hidden + base[...].astype(F32)
    for tile in range(4):
        activ = gelu(dot_nn(low, up_tile(pack, tile))).astype(BF)
        res_out[...] += dot_nn(activ, down_tile(pack, tile))
    low_out[...] = norm_rows(
        res_out[...], gains[gain_out : gain_out + 1, :], gains[gain_out + 1 : gain_out + 2, :]
    ).astype(BF)


def ffn_forward(resid, base, gains, pack, gain_in, gain_out):
    rows, width = resid.shape
    units = 4 * width
    return pl.pallas_call(
        functools.partial(ffn_fwd_body, (gain_in, gain_out)),
        out_shape=(jax.ShapeDtypeStruct((rows, width), F32), jax.ShapeDtypeStruct((rows, width), BF)),
        compiler_params=params(14),
        cost_estimate=pl.CostEstimate(
            flops=4 * rows * width * units, bytes_accessed=7 * MIB, transcendentals=rows * units
        ),
        name="ffn_fwd",
    )(resid, base, gains, pack)


def ffn_bwd_body(
    cfg, grad_in, res_late, resid, gains, pack, after, gh_out, late_out, dpack_out, ng_out, hid_low, late_low
):
    gain_in, gain_out = cfg
    back, dgain, dbias = norm_back(
        res_late[...], gains[gain_out : gain_out + 1, :], grad_in[...].astype(F32)
    )
    late_out[...] = back
    gh_out[...] = back
    late_low[...] = back.astype(BF)
    ng_out[0:1, :] = dgain
    ng_out[1:2, :] = dbias
    hid_low[...] = norm_rows(
        resid[...], gains[gain_in : gain_in + 1, :], gains[gain_in + 1 : gain_in + 2, :]
    ).astype(BF)
    places, _, width = pack.shape
    for tile in range(4):
        activ, slope = gelu_both(dot_nn(hid_low[...], up_tile(pack, tile)))
        grad_down = dot_tn(activ.astype(BF), late_low[...]).astype(BF)
        dpack_out[4 * tile : 4 * tile + 4, 0:128, :] = grad_down.reshape(4, 128, width)
        grad_act = dot_nt(late_low[...], down_tile(pack, tile)).astype(BF).astype(F32)
        grad_pre = (grad_act * slope).astype(BF)
        grad_up = dot_tn(hid_low[...], grad_pre).astype(BF)
        dpack_out[:, 128 + 32 * tile : 160 + 32 * tile, :] = grad_up.reshape(places, 32, width)
        gh_out[...] += dot_nt(grad_pre, up_tile(pack, tile))


def ffn_backward(grad_in, res_late, resid, gains, pack, after, gain_in, gain_out):
    rows, width = resid.shape
    units = 4 * width
    return pl.pallas_call(
        functools.partial(ffn_bwd_body, (gain_in, gain_out)),
        out_shape=(
            jax.ShapeDtypeStruct((rows, width), F32),
            jax.ShapeDtypeStruct((rows, width), F32),
            jax.ShapeDtypeStruct(pack.shape, BF),
            jax.ShapeDtypeStruct((2, width), F32),
        ),
        scratch_shapes=[pltpu.VMEM((rows, width), BF), pltpu.VMEM((rows, width), BF)],
        compiler_params=params(20),
        cost_estimate=pl.CostEstimate(
            flops=10 * rows * width * units, bytes_accessed=14 * MIB, transcendentals=rows * units
        ),
        name="ffn_bwd",
    )(grad_in, res_late, resid, gains, pack, after)


def segments_at(bounds, places, total_len):
    found = jnp.sum((bounds[None, :] <= places[:, None]).astype(jnp.int32), axis=-1)
    return jnp.where((places >= 0) & (places < total_len), found, -1)


def row_squares(values):
    if values.ndim == 2:
        return jnp.sum(values * values, axis=1)
    return values * values


def owner_groups(rows_local, owner, per_group, count):
    group_ids = (owner * rows_local + jnp.arange(rows_local, dtype=jnp.int32)) // per_group
    return group_ids[:, None] == jnp.arange(count, dtype=jnp.int32)[None, :]


def group_sum(onehot, row_values):
    return jnp.sum(jnp.where(onehot, row_values[:, None], 0.0), axis=0)


def lamb_moments(master, grad_rows, first, second):
    first_new = beta_one * first + (1.0 - beta_one) * grad_rows
    second_new = beta_two * second + (1.0 - beta_two) * grad_rows * grad_rows
    update = (
        first_new
        / (1.0 - beta_one**STEP)
        / (jnp.sqrt(second_new / (1.0 - beta_two**STEP)) + lamb_eps)
        + weight_decay * master
    )
    return (first_new, second_new, update)


GROUP = ("lo", "y", "c")
CHIPS = ("lo", "y")
EVERY = ("hi", "lo", "y", "c")


def swap_hi(array):
    return lax.ppermute(array, "hi", [(0, 1), (1, 0)])


def shift_hi(array, distance):
    count = lax.axis_size("hi")
    route = [(i - distance, i) for i in range(count) if i - distance in range(count)]
    return lax.ppermute(array, "hi", route)


def halo_rows(rows_array):
    high = lax.axis_index("hi")
    rows = rows_array.shape[-2]
    axis = rows_array.ndim - 2
    if lax.axis_size("hi") == 2:
        sent = jnp.where(
            high == 0,
            lax.slice_in_dim(rows_array, rows - HALO, rows, axis=axis),
            lax.slice_in_dim(rows_array, 0, HALO, axis=axis),
        )
        return swap_hi(sent)
    left = shift_hi(lax.slice_in_dim(rows_array, rows - HALO, rows, axis=axis), 1)
    right = shift_hi(lax.slice_in_dim(rows_array, 0, HALO, axis=axis), -1)
    return jnp.concatenate((left, right), axis=axis)


def halo_return(grads):
    if lax.axis_size("hi") == 2:
        return swap_hi(grads)
    to_left = shift_hi(grads[:, :HALO], -1)
    to_right = shift_hi(grads[:, HALO:], 1)
    return jnp.concatenate((to_left, to_right), axis=1)


def pack_up(rows):
    count, units = rows.shape
    return rows.reshape(count, 4, units // 4).swapaxes(0, 1).reshape(4 * count, units // 4)


def unpack_up(packed):
    count, width = packed.shape
    return packed.reshape(4, count // 4, width).swapaxes(0, 1).reshape(count // 4, 4 * width)


def gather_packs(attn_shard, up_shard, down_shard, norm_shard):
    n_high = lax.axis_size("hi")
    high = lax.axis_index("hi")
    width = attn_shard.shape[1]
    norm_count = norm_shard.shape[0]
    norm_row = jnp.pad(norm_shard[None, :], ((0, 0), (0, width - norm_count)))
    if n_high == 2:
        attn_rows = attn_shard.shape[0]
        mine = jnp.concatenate(
            (attn_shard, down_shard, pack_up(up_shard), jnp.pad(norm_row, ((0, 15), (0, 0)))), axis=0
        )
        other = swap_hi(mine)
        zero = jnp.where(high == 0, mine, other)
        one = jnp.where(high == 0, other, mine)
        ffn_end = mine.shape[0] - 16
        early = jnp.concatenate(
            (
                zero[:attn_rows],
                one[:attn_rows],
                zero[attn_rows:ffn_end],
                zero[ffn_end : ffn_end + 1],
                one[ffn_end:-1],
            ),
            axis=0,
        )
        full = lax.all_gather(early, GROUP, axis=0, tiled=False)
        late = lax.all_gather(one[attn_rows:ffn_end], GROUP, axis=0, tiled=False)
        attn0 = full[:, :attn_rows]
        attn1 = full[:, attn_rows : 2 * attn_rows]
        ffn0 = full[:, 2 * attn_rows : attn_rows + ffn_end]
        norms = full[:, attn_rows + ffn_end : attn_rows + ffn_end + 2, :norm_count].swapaxes(0, 1)
        return attn0, attn1, ffn0, late, norms.reshape(10, width).astype(F32)
    group = lax.axis_size("lo") * lax.axis_size("y") * lax.axis_size("c")
    attn = lax.all_gather(attn_shard, EVERY, axis=0, tiled=True).reshape(2, group, -1, width)
    down = lax.all_gather(down_shard, EVERY, axis=0, tiled=True).reshape(2, group, -1, width)
    up = lax.all_gather(up_shard, EVERY, axis=0, tiled=True)
    up = up.reshape(2, group, -1, 4, width).swapaxes(2, 3).reshape(2, group, -1, width)
    norms = lax.all_gather(norm_row, EVERY, axis=0, tiled=True)[:, :norm_count]
    ffn = jnp.concatenate((down, up), axis=2)
    return attn[0], attn[1], ffn[0], ffn[1], norms.reshape(10, width).astype(F32)


def reduce_places(chunk):
    places, rows, width = chunk.shape
    core = lax.axis_index("c")
    view = chunk.reshape(places // 2, 2, rows, width)
    kept = jnp.where(core == 0, view[:, 0], view[:, 1])
    sent = jnp.where(core == 0, view[:, 1], view[:, 0])
    got = lax.ppermute(sent, "c", [(0, 1), (1, 0)])
    pair = (kept.astype(F32) + got.astype(F32)).astype(BF)
    parts = lax.all_to_all(pair, CHIPS, split_axis=0, concat_axis=0, tiled=True)
    return jnp.sum(parts.astype(F32), axis=0)


def join_halves(zero, one):
    first = lax.axis_index("hi") == 0
    mine = jnp.where(first, zero, one)
    sent = jnp.where(first, one, zero).astype(BF)
    return mine + swap_hi(sent).astype(F32)


def reduce_grads(attn0, attn1, ffn0, ffn1, norm_local, attn_rows):
    n_high = lax.axis_size("hi")
    high = lax.axis_index("hi")
    group, _, width = ffn0.shape
    norm_count = norm_local.size // (n_high * group)
    norm_local = norm_local.reshape(n_high, group, norm_count)
    if n_high == 2:
        part1 = reduce_places(ffn1)
        attn_part1 = reduce_places(attn1)
        part0 = reduce_places(ffn0)
        ffn_own = join_halves(part0, part1)
        norm_rows_local = jnp.pad(
            norm_local.swapaxes(0, 1).astype(BF), ((0, 0), (0, 16 - n_high), (0, width - norm_count))
        )
        both = reduce_places(jnp.concatenate((attn0, norm_rows_local), axis=1))
        norm_part = both[attn_rows:]
        own = join_halves(
            both, jnp.concatenate((attn_part1, norm_part), axis=0)
        )
        norm_own = lax.dynamic_index_in_dim(own[attn_rows:], high, 0, keepdims=False)[:norm_count]
        return own[:attn_rows], unpack_up(ffn_own[128:]), ffn_own[:128], norm_own

    def scatter(rows):
        return lax.psum_scatter(rows, EVERY, scatter_dimension=0, tiled=True).astype(F32)

    attn = jnp.concatenate((attn0, attn1), axis=0).reshape(-1, width)
    ffn = jnp.stack((ffn0, ffn1)).reshape(2 * group, -1, width)
    up = ffn[:, 128:].reshape(2 * group, 4, 32, width).swapaxes(1, 2).reshape(-1, 4 * width)
    norms = lax.psum_scatter(
        norm_local.reshape(n_high * group, norm_count), EVERY, scatter_dimension=0, tiled=True
    )
    return scatter(attn), scatter(up), scatter(ffn[:, :128].reshape(-1, width)), norms[0]


def shards(
    enc_in,
    dec_in,
    cotangent,
    lengths,
    attn_master,
    ffn_in_master,
    ffn_out_master,
    norm_master,
    attn_first,
    ffn_in_first,
    ffn_out_first,
    norm_first,
    attn_second,
    ffn_in_second,
    ffn_out_second,
    norm_second,
):
    micro, _, length_dev, width = enc_in.shape
    rows = micro * length_dev
    hidden_units = ffn_in_master.shape[1]
    high, low = lax.axis_index("hi"), lax.axis_index("lo")
    n_high = lax.axis_size("hi")
    owner = lax.axis_index(EVERY)
    masters = (attn_master, ffn_in_master, ffn_out_master, norm_master)
    group_info = ((width, 12), (width, 2), (hidden_units, 2), (width, 10))
    onehots = [
        owner_groups(master.shape[0], owner, info[0], info[1])
        for master, info in zip(masters, group_info)
    ]
    weight_local = jnp.concatenate(
        [group_sum(onehot, row_squares(master)) for onehot, master in zip(onehots, masters)]
    )

    attn_rows = attn_master.shape[0]
    block0, block1, pack0, pack1, gains = gather_packs(
        attn_master.astype(BF), ffn_in_master.astype(BF), ffn_out_master.astype(BF), norm_master.astype(BF)
    )
    blocks = (block0, block1)

    packed = jnp.stack((enc_in[:, 0], dec_in[:, 0], cotangent[:, 0]), axis=1)
    packed = lax.all_to_all(packed, "lo", split_axis=0, concat_axis=0, tiled=True)
    packed = packed.swapaxes(0, 1).reshape(3, rows, width)
    enc_rows, dec_rows, cot_rows = packed[0], packed[1], packed[2]
    halos = halo_rows(packed[:2])
    enc_window = jnp.concatenate((enc_rows, halos[0]), axis=0)
    dec_window = jnp.concatenate((dec_rows, halos[1]), axis=0)

    total_len = rows * n_high
    bounds = jnp.cumsum(lengths[:, 0, :], axis=-1)
    bounds = lax.dynamic_index_in_dim(bounds, low, 0, keepdims=False)
    base = high * rows
    own_pos = base + jnp.arange(rows, dtype=jnp.int32)
    step = jnp.arange(HALO, dtype=jnp.int32)
    if n_high == 2:
        halo_pos = jnp.where(high == 0, rows, rows - HALO) + step
    else:
        halo_pos = jnp.concatenate((base - HALO + step, base + rows + step))
    key_pos = jnp.concatenate((own_pos, halo_pos))
    key_seg = segments_at(bounds, key_pos, total_len)
    krow = jnp.stack((key_seg, key_pos), axis=0)
    kcol = jnp.stack((key_seg, key_pos), axis=1)
    places = {
        "krow": krow,
        "kcol": kcol,
        "qrow": krow[:, :rows],
        "qcol": kcol[:rows],
        "offsets": None if n_high == 2 else (0, rows - HALO),
        "spot": jnp.where(high == 0, rows - HALO, 0).astype(jnp.int32).reshape(1),
    }

    enc_picks, self_picks, cross_picks = (0, 1, 2, 3), (4, 5, 6, 7), (8, 9, 10, 11)
    *enc_kept, resid_one = attn_forward(
        enc_rows, enc_window, (block0, block0), gains, places, False, enc_picks, None
    )
    resid_two, enc_low = ffn_forward(resid_one, enc_rows, gains, pack0, 0, 2)
    low_window = jnp.concatenate((enc_low, halo_rows(enc_low)), axis=0)
    *self_kept, resid_three = attn_forward(
        dec_rows, dec_window, blocks, gains, places, True, self_picks, None
    )
    *cross_kept, resid_four = attn_forward(
        resid_three, low_window, (block1, block1), gains, places, False, cross_picks, 4
    )
    resid_five, dec_low = ffn_forward(resid_four, dec_rows, gains, pack1, 6, 8)

    grad_second, grad_five, dpack1, ng8 = ffn_backward(
        cot_rows, resid_five, resid_four, gains, pack1, gains, 6, 8
    )
    grad_first, dwq_c, dwo_c, own_c, halo_c, ng6 = attn_backward(
        grad_second, resid_four, resid_three, cross_kept, (block1, block1), gains, places, False, cross_picks, 6, 4
    )
    back_c = halo_return(halo_c)
    grad_dec_q, dwq_s, dwo_s, own_s, halo_s, ng4 = attn_backward(
        grad_first, resid_three, dec_rows, self_kept, blocks, gains, places, True, self_picks, 4, None
    )
    back_s = halo_return(halo_s)
    grad_encoded, dwk_c, dwv_c = kv_backward(
        enc_low, own_c, back_c, (block1, block1), (), ng4, places, cross_picks, F32
    )
    dec_grad, dwk_s, dwv_s = kv_backward(
        dec_rows, own_s, back_s, blocks, (grad_five, grad_dec_q), ng4, places, self_picks, BF
    )
    grad_hidden, grad_two, dpack0, ng2 = ffn_backward(
        grad_encoded, resid_two, resid_one, gains, pack0, ng4, 0, 2
    )
    grad_enc_q, dwq_e, dwo_e, own_e, halo_e, ng0 = attn_backward(
        grad_hidden, resid_one, enc_rows, enc_kept, (block0, block0), gains, places, False, enc_picks, 0, None
    )
    back_e = halo_return(halo_e)
    enc_grad, dwk_e, dwv_e = kv_backward(
        enc_rows, own_e, back_e, (block0, block0), (grad_two, grad_enc_q), ng0, places, enc_picks, BF
    )
    attn_local0 = jnp.concatenate((dwq_e, dwk_e, dwv_e, dwo_e, dwq_s, dwk_s), axis=0)
    attn_local1 = jnp.concatenate((dwv_s, dwo_s, dwq_c, dwk_c, dwv_c, dwo_c), axis=0)
    group = pack0.shape[0]
    attn_own, up_own, down_own, norm_own = reduce_grads(
        attn_local0.reshape(group, -1, width),
        attn_local1.reshape(group, -1, width),
        dpack0,
        dpack1,
        jnp.concatenate((ng0, ng2, ng4, ng6, ng8), axis=0),
        attn_rows,
    )

    def restore(*arrays):
        outs = jnp.stack(arrays, axis=0).reshape(len(arrays), micro, length_dev, width).swapaxes(0, 1)
        return lax.all_to_all(outs, "lo", split_axis=0, concat_axis=0, tiled=True)

    lows = restore(enc_low, dec_low)
    grads = restore(enc_grad, dec_grad)

    owned = (attn_own, up_own, down_own, norm_own)
    firsts = (attn_first, ffn_in_first, ffn_out_first, norm_first)
    seconds = (attn_second, ffn_in_second, ffn_out_second, norm_second)
    moments = [
        lamb_moments(masters[index], owned[index], firsts[index], seconds[index])
        for index in range(4)
    ]
    update_local = jnp.concatenate(
        [group_sum(onehots[index], row_squares(moments[index][2])) for index in range(4)]
    )
    squares = jnp.stack((weight_local, update_local))
    squares = jnp.pad(squares, ((0, 6), (0, 128 - squares.shape[1])))
    count = lax.axis_size(EVERY)
    squares = jnp.broadcast_to(squares[None], (count,) + squares.shape)
    squares = jnp.sum(lax.all_to_all(squares, EVERY, split_axis=0, concat_axis=0, tiled=True), axis=0)
    norms = jnp.sqrt(squares[:2, :26])
    ratio = norms[0] / norms[1]
    bounds_at = (0, 12, 14, 16, 26)
    new_weights = []
    for index in range(4):
        row_ratio = jnp.sum(
            jnp.where(onehots[index], ratio[None, bounds_at[index] : bounds_at[index + 1]], 0.0), axis=1
        )
        if masters[index].ndim == 2:
            row_ratio = row_ratio[:, None]
        new_weights.append(masters[index] - learn_rate * row_ratio * moments[index][2])
    return (
        lows[:, 0][:, None],
        lows[:, 1][:, None],
        grads[:, 0][:, None].astype(F32),
        grads[:, 1][:, None].astype(F32),
        *owned,
        *new_weights,
        *[item[0] for item in moments],
        *[item[1] for item in moments],
        *[item.astype(BF) for item in new_weights],
        norms,
        ratio,
    )


def solution(mesh):
    count_seq, count_stream = mesh.shape["seq"], mesh.shape["stream"]

    def run(*args):
        micro = args[0].shape[0]
        split = Mesh(
            mesh.devices.reshape(count_seq // micro, micro, count_stream // 2, 2), ("hi", "lo", "y", "c")
        )
        tokens = P(None, ("y", "c"), ("hi", "lo"), None)
        wide = P(EVERY, None)
        flat = P(EVERY)
        owned = (wide, wide, wide, flat)
        return jax.shard_map(
            shards,
            mesh=split,
            in_specs=(tokens, tokens, tokens, P(None, ("y", "c"), None), *owned, *owned, *owned),
            out_specs=(tokens, tokens, tokens, tokens, *owned, *owned, *owned, *owned, *owned, P(), P()),
            check_vma=False,
        )(*args)

    return run
```

```python
import functools
import math

import jax
import jax.numpy as jnp
from jax import lax
from jax.experimental import pallas as pl
from jax.experimental.pallas import tpu as pltpu
from jax.sharding import Mesh
from jax.sharding import PartitionSpec as P

HEADS = 8
STEP = 5
HALO = 256
TILE = 256

norm_eps = 1e-05
beta_one = 0.5
beta_two = 0.5
lamb_eps = 1e-06
weight_decay = 0.01
learn_rate = 0.5
masked_score = -1e30

BF = jnp.bfloat16
F32 = jnp.float32
MIB = 1024 * 1024


def dot_nn(a, b):
    return lax.dot_general(a, b, (((1,), (0,)), ((), ())), preferred_element_type=F32)


def dot_nt(a, b):
    return lax.dot_general(a, b, (((1,), (1,)), ((), ())), preferred_element_type=F32)


def dot_tn(a, b):
    return lax.dot_general(a, b, (((0,), (0,)), ((), ())), preferred_element_type=F32)


def norm_parts(rows):
    centre = rows - jnp.mean(rows, axis=-1, keepdims=True)
    inv = lax.rsqrt(jnp.mean(centre * centre, axis=-1, keepdims=True) + norm_eps)
    return centre * inv, inv


def norm_rows(rows, gain, bias):
    return norm_parts(rows)[0] * gain + bias


def norm_back(rows, gain, grad):
    unit, inv = norm_parts(rows)
    lead = grad * gain
    back = inv * (
        lead
        - jnp.mean(lead, axis=-1, keepdims=True)
        - unit * jnp.mean(lead * unit, axis=-1, keepdims=True)
    )
    return (
        back,
        jnp.sum(grad * unit, axis=0, keepdims=True),
        jnp.sum(grad, axis=0, keepdims=True),
    )


gelu_a = 0.7978845608028654
gelu_b = 0.044715


def gelu(v):
    return 0.5 * v * (1.0 + jnp.tanh(gelu_a * (v + gelu_b * (v * v * v))))


def gelu_both(v):
    sq = v * v
    t = jnp.tanh(gelu_a * (v + gelu_b * (sq * v)))
    half = 0.5 * (1.0 + t)
    slope = half + 0.5 * v * (1.0 - t * t) * (gelu_a * (1.0 + 3.0 * gelu_b * sq))
    return v * half, slope


def pick(pack, place, rows):
    mine, other, core = pack
    parity = core[0] == place % 2
    chip = place // 2
    return jnp.where(parity, mine[chip, rows, :], other[chip, rows, :])


def matrix(pack, index, width):
    places = 2 * pack[0].shape[0]
    per = 6 * width // places
    pieces = []
    row, end = index * width, (index + 1) * width
    while row < end:
        place, start = divmod(row, per)
        take = min(per - start, end - row)
        pieces.append(pick(pack, place, slice(start, start + take)))
        row += take
    return pieces[0] if len(pieces) == 1 else jnp.concatenate(pieces, axis=0)


def lane_low(shape):
    return lax.broadcasted_iota(jnp.int32, shape, 1) < 64


def attn_fwd_body(cfg, *refs):
    causal, normed, picks, gain_at = cfg
    core, q_src, kv_src, mine0, other0, mine1, other1, gains, qcol, krow = refs[:10]
    q_out, k_out, v_out, o_out, lse_out, res_out = refs[10:]
    blocks = ((mine0, other0, core), (mine1, other1, core))
    rows, width = q_src.shape

    def weight(slot):
        return matrix(blocks[picks[slot] // 6], picks[slot] % 6, width)

    if normed:
        base = norm_rows(q_src[...], gains[gain_at : gain_at + 1, :], gains[gain_at + 1 : gain_at + 2, :])
        low_src = base.astype(BF)
    else:
        base = None
        low_src = q_src[...]
    queries = dot_nn(low_src, weight(0))
    q_out[...] = (queries.astype(BF).astype(F32) * 0.125).astype(BF)
    k_out[...] = dot_nn(kv_src[...], weight(1)).astype(BF)
    v_out[...] = dot_nn(kv_src[...], weight(2)).astype(BF)
    window = k_out.shape[0]
    kseg = krow[0:1, :]
    kpos = krow[1:2, :]

    def tile_step(index, carry):
        spot = pl.ds(pl.multiple_of(index * TILE, TILE), TILE)
        allowed = qcol[spot, 0:1] == kseg
        if causal:
            allowed = allowed & (kpos <= qcol[spot, 1:2])
        low = lane_low((TILE, 128))
        low_w = lane_low((window, 128))
        totals = []
        for pair in range(HEADS // 2):
            lanes = slice(pair * 128, pair * 128 + 128)
            q2 = q_out[spot, lanes]
            k2 = k_out[:, lanes]
            v2 = v_out[:, lanes]
            mixed = None
            for half in range(2):
                keep = low if half == 0 else ~low
                keep_w = low_w if half == 0 else ~low_w
                scores = dot_nt(jnp.where(keep, q2, jnp.zeros_like(q2)), k2)
                scores = jnp.where(allowed, scores, masked_score)
                top = jnp.max(scores, axis=-1, keepdims=True)
                weights = jnp.exp(scores - top)
                total = jnp.sum(weights, axis=-1, keepdims=True)
                probs = (weights * (1.0 / total)).astype(BF)
                part = dot_nn(probs, jnp.where(keep_w, v2, jnp.zeros_like(v2)))
                mixed = part if mixed is None else mixed + part
                totals.append(top + jnp.log(total))
            o_out[spot, lanes] = mixed.astype(BF)
        lane = lax.broadcasted_iota(jnp.int32, (TILE, 128), 1)
        packed = jnp.zeros((TILE, 128), F32)
        for head in range(HEADS):
            packed = jnp.where(lane == head, totals[head], packed)
        lse_out[:, spot] = jnp.transpose(packed)[0:HEADS, :]
        return carry

    lax.fori_loop(0, rows // TILE, tile_step, 0)
    branch = dot_nn(o_out[...], weight(3))
    if base is None:
        base = q_src[...].astype(F32)
    else:
        base = norm_rows(q_src[...], gains[gain_at : gain_at + 1, :], gains[gain_at + 1 : gain_at + 2, :])
    res_out[...] = base + branch


def specs(in_vmem, order_only=0):
    vmem = pl.BlockSpec(memory_space=pltpu.VMEM)
    anywhere = pl.BlockSpec(memory_space=pl.ANY)
    return [pl.BlockSpec(memory_space=pltpu.SMEM)] + [vmem] * in_vmem + [anywhere] * order_only


def params(limit):
    return pltpu.CompilerParams(vmem_limit_bytes=limit * MIB)


def attn_forward(q_src, kv_src, blocks, gains, places, causal, picks, gain_at):
    rows, width = q_src.shape
    window = kv_src.shape[0]
    shapes = (
        jax.ShapeDtypeStruct((rows, width), BF),
        jax.ShapeDtypeStruct((window, width), BF),
        jax.ShapeDtypeStruct((window, width), BF),
        jax.ShapeDtypeStruct((rows, width), BF),
        jax.ShapeDtypeStruct((HEADS, rows), F32),
        jax.ShapeDtypeStruct((rows, width), F32),
    )
    cfg = (causal, gain_at is not None, picks, gain_at)
    return pl.pallas_call(
        functools.partial(attn_fwd_body, cfg),
        out_shape=shapes,
        in_specs=specs(9),
        compiler_params=params(12),
        cost_estimate=pl.CostEstimate(
            flops=12 * rows * width * width + 8 * rows * window * width,
            bytes_accessed=12 * MIB,
            transcendentals=0,
        ),
        name="attn_fwd",
    )(places["core"], q_src, kv_src, *blocks[0], *blocks[1], gains, places["qcol"], places["krow"])


def attn_bwd_body(cfg, *refs):
    causal, picks, gain_at, src_gain = cfg
    core, grad_in, resid, src, q_in, k_in, v_in, o_in, lse_in = refs[:9]
    mine0, other0, mine1, other1, gains, qrow, kcol, _ = refs[9:17]
    gq_out, dwq_out, dwo_out, own_out, halo_out, ng_out, do_scr, dq_scr, dk_scr, dv_scr = refs[17:]
    blocks = ((mine0, other0, core), (mine1, other1, core))
    rows, width = q_in.shape
    window = k_in.shape[0]

    def weight(slot):
        return matrix(blocks[picks[slot] // 6], picks[slot] % 6, width)

    back, dgain, dbias = norm_back(resid[...], gains[gain_at : gain_at + 1, :], grad_in[...].astype(F32))
    gq_out[...] = back
    ng_out[0:1, :] = dgain
    ng_out[1:2, :] = dbias
    branch = back.astype(BF)
    dwo_out[...] = dot_tn(o_in[...], branch).astype(BF)
    do_scr[...] = dot_nt(branch, weight(3)).astype(BF)
    dk_scr[...] = jnp.zeros_like(dk_scr)
    dv_scr[...] = jnp.zeros_like(dv_scr)
    kseg = kcol[:, 0:1]
    kpos = kcol[:, 1:2]

    def tile_step(index, carry):
        spot = pl.ds(pl.multiple_of(index * TILE, TILE), TILE)
        allowed = kseg == qrow[0:1, spot]
        if causal:
            allowed = allowed & (kpos <= qrow[1:2, spot])
        low = lane_low((TILE, 128))
        low_w = lane_low((window, 128))
        for pair in range(HEADS // 2):
            lanes = slice(pair * 128, pair * 128 + 128)
            q2 = q_in[spot, lanes]
            do2 = do_scr[spot, lanes]
            k2 = k_in[:, lanes]
            v2 = v_in[:, lanes]
            dq2 = None
            dk2 = None
            dv2 = None
            for half in range(2):
                keep = low if half == 0 else ~low
                keep_w = low_w if half == 0 else ~low_w
                head = 2 * pair + half
                qh = jnp.where(keep, q2, jnp.zeros_like(q2))
                doh = jnp.where(keep, do2, jnp.zeros_like(do2))
                scores = jnp.where(allowed, dot_nt(k2, qh), masked_score)
                probs = jnp.exp(scores - lse_in[head : head + 1, spot])
                gprobs = dot_nt(v2, doh)
                delta = jnp.sum(gprobs * probs, axis=0, keepdims=True)
                gscores = (probs * (gprobs - delta)).astype(BF)
                part_v = dot_nn(probs.astype(BF), doh)
                part_k = dot_nn(gscores, qh)
                part_q = dot_tn(gscores, jnp.where(keep_w, k2, jnp.zeros_like(k2)))
                dv2 = part_v if dv2 is None else dv2 + part_v
                dk2 = part_k if dk2 is None else dk2 + part_k
                dq2 = part_q if dq2 is None else dq2 + part_q
            dq_scr[spot, lanes] = (dq2 * 0.125).astype(BF)
            dk_scr[:, lanes] += dk2
            dv_scr[:, lanes] += dv2
        return carry

    lax.fori_loop(0, rows // TILE, tile_step, 0)
    own_out[0] = dk_scr[0:rows, :]
    own_out[1] = dv_scr[0:rows, :]
    halo_out[0] = dk_scr[rows:window, :].astype(BF)
    halo_out[1] = dv_scr[rows:window, :].astype(BF)
    if src_gain is None:
        low_src = src[...]
    else:
        low_src = norm_rows(src[...], gains[src_gain : src_gain + 1, :], gains[src_gain + 1 : src_gain + 2, :]).astype(BF)
    dwq_out[...] = dot_tn(low_src, dq_scr[...]).astype(BF)
    gq_out[...] += dot_nt(dq_scr[...], weight(0))


def attn_backward(grad_in, resid, src, kept, blocks, gains, after, places, causal, picks, gain_at, src_gain):
    q, k, v, o, lse = kept
    rows, width = q.shape
    window = k.shape[0]
    shapes = (
        jax.ShapeDtypeStruct((rows, width), F32),
        jax.ShapeDtypeStruct((width, width), BF),
        jax.ShapeDtypeStruct((width, width), BF),
        jax.ShapeDtypeStruct((2, rows, width), F32),
        jax.ShapeDtypeStruct((2, window - rows, width), BF),
        jax.ShapeDtypeStruct((2, width), F32),
    )
    return pl.pallas_call(
        functools.partial(attn_bwd_body, (causal, picks, gain_at, src_gain)),
        in_specs=specs(15, 1),
        out_shape=shapes,
        scratch_shapes=[
            pltpu.VMEM((rows, width), BF),
            pltpu.VMEM((rows, width), BF),
            pltpu.VMEM((window, width), F32),
            pltpu.VMEM((window, width), F32),
        ],
        compiler_params=params(20),
        cost_estimate=pl.CostEstimate(
            flops=8 * rows * width * width + 20 * rows * window * width,
            bytes_accessed=16 * MIB,
            transcendentals=0,
        ),
        name="attn_bwd",
    )(
        places["core"], grad_in, resid, src, q, k, v, o, lse, *blocks[0], *blocks[1], gains,
        places["qrow"], places["kcol"], after,
    )


def kv_bwd_body(cfg, *refs):
    picks, offsets, n_add = cfg
    core, src, own, halo, mine0, other0, mine1, other1 = refs[:8]
    adds = refs[8 : 8 + n_add]
    g_out, dwk_out, dwv_out, scr = refs[9 + n_add :]
    blocks = ((mine0, other0, core), (mine1, other1, core))
    rows, width = src.shape

    def weight(slot):
        return matrix(blocks[picks[slot] // 6], picks[slot] % 6, width)

    scr[...] = own[...]
    if offsets is None:
        spot = pl.ds(pl.multiple_of(core[1], HALO), HALO)
        scr[:, spot, :] += halo[...].astype(F32)
    else:
        for index, offset in enumerate(offsets):
            scr[:, offset : offset + HALO, :] += halo[:, index * HALO : index * HALO + HALO, :].astype(F32)
    dk = scr[0].astype(BF)
    dv = scr[1].astype(BF)
    dwk_out[...] = dot_tn(src[...], dk).astype(BF)
    dwv_out[...] = dot_tn(src[...], dv).astype(BF)
    total = dot_nt(dk, weight(1)) + dot_nt(dv, weight(2))
    for ref in adds:
        total = total + ref[...]
    g_out[...] = total.astype(g_out.dtype)


def kv_backward(src, own, halo, blocks, adds, after, places, picks, out_type):
    rows, width = src.shape
    vmem = pl.BlockSpec(memory_space=pltpu.VMEM)
    return pl.pallas_call(
        functools.partial(kv_bwd_body, (picks, places["offsets"], len(adds))),
        out_shape=(
            jax.ShapeDtypeStruct((rows, width), out_type),
            jax.ShapeDtypeStruct((width, width), BF),
            jax.ShapeDtypeStruct((width, width), BF),
        ),
        in_specs=specs(7 + len(adds), 1),
        out_specs=(vmem, vmem, vmem),
        scratch_shapes=[pltpu.VMEM((2, rows, width), F32)],
        compiler_params=params(12),
        cost_estimate=pl.CostEstimate(
            flops=8 * rows * width * width, bytes_accessed=14 * MIB, transcendentals=0
        ),
        name="kv_bwd",
    )(places["core"], src, own, halo, *blocks[0], *blocks[1], *adds, after)


def up_tile(pack, tile):
    spot = slice(128 + 32 * tile, 160 + 32 * tile)
    return jnp.concatenate([pick(pack, place, spot) for place in range(2 * pack[0].shape[0])], axis=0)


def down_tile(pack, tile):
    return jnp.concatenate([pick(pack, 4 * tile + step, slice(0, 128)) for step in range(4)], axis=0)


def ffn_fwd_body(cfg, core, resid, base, gains, mine, other, res_out, low_out):
    gain_in, gain_out = cfg
    pack = (mine, other, core)
    hidden = norm_rows(resid[...], gains[gain_in : gain_in + 1, :], gains[gain_in + 1 : gain_in + 2, :])
    low = hidden.astype(BF)
    res_out[...] = hidden + base[...].astype(F32)
    for tile in range(4):
        activ = gelu(dot_nn(low, up_tile(pack, tile))).astype(BF)
        res_out[...] += dot_nn(activ, down_tile(pack, tile))
    low_out[...] = norm_rows(
        res_out[...], gains[gain_out : gain_out + 1, :], gains[gain_out + 1 : gain_out + 2, :]
    ).astype(BF)


def ffn_forward(resid, base, gains, pack, places, gain_in, gain_out):
    rows, width = resid.shape
    units = 4 * width
    return pl.pallas_call(
        functools.partial(ffn_fwd_body, (gain_in, gain_out)),
        out_shape=(jax.ShapeDtypeStruct((rows, width), F32), jax.ShapeDtypeStruct((rows, width), BF)),
        in_specs=specs(5),
        compiler_params=params(14),
        cost_estimate=pl.CostEstimate(
            flops=4 * rows * width * units, bytes_accessed=7 * MIB, transcendentals=rows * units
        ),
        name="ffn_fwd",
    )(places["core"], resid, base, gains, *pack)


def ffn_bwd_body(
    cfg, core, grad_in, res_late, resid, gains, mine, other, after, gh_out, late_out, dpack_out, ng_out,
    hid_low, late_low,
):
    gain_in, gain_out = cfg
    pack = (mine, other, core)
    back, dgain, dbias = norm_back(
        res_late[...], gains[gain_out : gain_out + 1, :], grad_in[...].astype(F32)
    )
    late_out[...] = back
    gh_out[...] = back
    late_low[...] = back.astype(BF)
    ng_out[0:1, :] = dgain
    ng_out[1:2, :] = dbias
    hid_low[...] = norm_rows(
        resid[...], gains[gain_in : gain_in + 1, :], gains[gain_in + 1 : gain_in + 2, :]
    ).astype(BF)
    places, _, width = dpack_out.shape
    for tile in range(4):
        activ, slope = gelu_both(dot_nn(hid_low[...], up_tile(pack, tile)))
        grad_down = dot_tn(activ.astype(BF), late_low[...]).astype(BF)
        dpack_out[4 * tile : 4 * tile + 4, 0:128, :] = grad_down.reshape(4, 128, width)
        grad_act = dot_nt(late_low[...], down_tile(pack, tile)).astype(BF).astype(F32)
        grad_pre = (grad_act * slope).astype(BF)
        grad_up = dot_tn(hid_low[...], grad_pre).astype(BF)
        dpack_out[:, 128 + 32 * tile : 160 + 32 * tile, :] = grad_up.reshape(places, 32, width)
        gh_out[...] += dot_nt(grad_pre, up_tile(pack, tile))


def ffn_backward(grad_in, res_late, resid, gains, pack, after, places, gain_in, gain_out):
    rows, width = resid.shape
    units = 4 * width
    return pl.pallas_call(
        functools.partial(ffn_bwd_body, (gain_in, gain_out)),
        in_specs=specs(6, 1),
        out_shape=(
            jax.ShapeDtypeStruct((rows, width), F32),
            jax.ShapeDtypeStruct((rows, width), F32),
            jax.ShapeDtypeStruct((2 * pack[0].shape[0],) + pack[0].shape[1:], BF),
            jax.ShapeDtypeStruct((2, width), F32),
        ),
        scratch_shapes=[pltpu.VMEM((rows, width), BF), pltpu.VMEM((rows, width), BF)],
        compiler_params=params(20),
        cost_estimate=pl.CostEstimate(
            flops=10 * rows * width * units, bytes_accessed=14 * MIB, transcendentals=rows * units
        ),
        name="ffn_bwd",
    )(places["core"], grad_in, res_late, resid, gains, *pack, after)


def segments_at(bounds, places, total_len):
    found = jnp.sum((bounds[None, :] <= places[:, None]).astype(jnp.int32), axis=-1)
    return jnp.where((places >= 0) & (places < total_len), found, -1)


def row_squares(values):
    if values.ndim == 2:
        return jnp.sum(values * values, axis=1)
    return values * values


def owner_groups(rows_local, owner, per_group, count):
    group_ids = (owner * rows_local + jnp.arange(rows_local, dtype=jnp.int32)) // per_group
    return group_ids[:, None] == jnp.arange(count, dtype=jnp.int32)[None, :]


def group_sum(onehot, row_values):
    return jnp.sum(jnp.where(onehot, row_values[:, None], 0.0), axis=0)


def lamb_moments(master, grad_rows, first, second):
    first_new = beta_one * first + (1.0 - beta_one) * grad_rows
    second_new = beta_two * second + (1.0 - beta_two) * grad_rows * grad_rows
    update = (
        first_new
        / (1.0 - beta_one**STEP)
        / (jnp.sqrt(second_new / (1.0 - beta_two**STEP)) + lamb_eps)
        + weight_decay * master
    )
    return (first_new, second_new, update)


GROUP = ("lo", "y", "c")
CHIPS = ("lo", "y")
EVERY = ("hi", "lo", "y", "c")


def swap_hi(array):
    return lax.ppermute(array, "hi", [(0, 1), (1, 0)])


def shift_hi(array, distance):
    count = lax.axis_size("hi")
    route = [(i - distance, i) for i in range(count) if i - distance in range(count)]
    return lax.ppermute(array, "hi", route)


def halo_rows(rows_array):
    high = lax.axis_index("hi")
    rows = rows_array.shape[-2]
    axis = rows_array.ndim - 2
    if lax.axis_size("hi") == 2:
        sent = jnp.where(
            high == 0,
            lax.slice_in_dim(rows_array, rows - HALO, rows, axis=axis),
            lax.slice_in_dim(rows_array, 0, HALO, axis=axis),
        )
        return swap_hi(sent)
    left = shift_hi(lax.slice_in_dim(rows_array, rows - HALO, rows, axis=axis), 1)
    right = shift_hi(lax.slice_in_dim(rows_array, 0, HALO, axis=axis), -1)
    return jnp.concatenate((left, right), axis=axis)


def halo_return(grads):
    if lax.axis_size("hi") == 2:
        return swap_hi(grads)
    to_left = shift_hi(grads[:, :HALO], -1)
    to_right = shift_hi(grads[:, HALO:], 1)
    return jnp.concatenate((to_left, to_right), axis=1)


def pack_up(rows):
    count, units = rows.shape
    return rows.reshape(count, 4, units // 4).swapaxes(0, 1).reshape(4 * count, units // 4)


def unpack_up(packed):
    count, width = packed.shape
    return packed.reshape(4, count // 4, width).swapaxes(0, 1).reshape(count // 4, 4 * width)


def swap_core(array):
    return lax.ppermute(array, "c", [(0, 1), (1, 0)])


def gather_chips(shard):
    count = lax.axis_size(CHIPS)
    sent = jnp.broadcast_to(shard[None], (count,) + shard.shape)
    mine = lax.all_to_all(sent, CHIPS, split_axis=0, concat_axis=0, tiled=True)
    return mine, swap_core(mine)


def by_parity(full):
    even = lax.axis_index("c") == 0
    view = full.reshape(full.shape[0] // 2, 2, *full.shape[1:])
    return jnp.where(even, view[:, 0], view[:, 1]), jnp.where(even, view[:, 1], view[:, 0])


def gather_packs(attn_shard, up_shard, down_shard, norm_shard):
    n_high = lax.axis_size("hi")
    high = lax.axis_index("hi")
    width = attn_shard.shape[1]
    norm_count = norm_shard.shape[0]
    norm_row = jnp.pad(norm_shard[None, :], ((0, 0), (0, width - norm_count)))
    if n_high == 2:
        attn_rows = attn_shard.shape[0]
        first = high == 0
        mine = jnp.concatenate((attn_shard, jnp.pad(norm_row, ((0, 15), (0, 0)))), axis=0)
        other = swap_hi(mine)
        zero = jnp.where(first, mine, other)
        one = jnp.where(first, other, mine)
        early = jnp.concatenate((zero[: attn_rows + 1], one[attn_rows:-1]), axis=0)
        attn0 = gather_chips(early)
        norms = [half[:, attn_rows : attn_rows + 2, :norm_count] for half in attn0]
        even = lax.axis_index("c") == 0
        norms = (jnp.where(even, norms[0], norms[1]), jnp.where(even, norms[1], norms[0]))
        norms = jnp.stack(norms, axis=1).reshape(-1, 2, norm_count).swapaxes(0, 1)
        ffn_mine = jnp.concatenate((down_shard, pack_up(up_shard)), axis=0)
        ffn_other = swap_hi(ffn_mine)
        ffn_zero = jnp.where(first, ffn_mine, ffn_other)
        ffn_one = jnp.where(first, ffn_other, ffn_mine)
        next_rows = ffn_mine.shape[0]
        both = gather_chips(jnp.concatenate((ffn_zero, one[:attn_rows]), axis=0))
        ffn0 = tuple(half[:, :next_rows] for half in both)
        attn1 = tuple(half[:, next_rows:] for half in both)
        ffn1 = gather_chips(ffn_one)
        return attn0, attn1, ffn0, ffn1, norms.reshape(10, width).astype(F32)
    group = lax.axis_size(GROUP)
    attn = lax.all_gather(attn_shard, EVERY, axis=0, tiled=True).reshape(2, group, -1, width)
    down = lax.all_gather(down_shard, EVERY, axis=0, tiled=True).reshape(2, group, -1, width)
    up = lax.all_gather(up_shard, EVERY, axis=0, tiled=True)
    up = up.reshape(2, group, -1, 4, width).swapaxes(2, 3).reshape(2, group, -1, width)
    norms = lax.all_gather(norm_row, EVERY, axis=0, tiled=True)[:, :norm_count]
    ffn = jnp.concatenate((down, up), axis=2)
    parts = [by_parity(part) for part in (attn[0], attn[1], ffn[0], ffn[1])]
    return *parts, norms.reshape(10, width).astype(F32)


def reduce_cores(chunk):
    kept, sent = by_parity(chunk)
    return (kept.astype(F32) + swap_core(sent).astype(F32)).astype(BF)


def reduce_chips(pair):
    parts = lax.all_to_all(pair, CHIPS, split_axis=0, concat_axis=0, tiled=True)
    return jnp.sum(parts.astype(F32), axis=0)


def join_halves(zero, one):
    first = lax.axis_index("hi") == 0
    mine = jnp.where(first, zero, one)
    sent = jnp.where(first, one, zero).astype(BF)
    return mine + swap_hi(sent).astype(F32)


def reduce_plain(attn0, attn1, ffn0, ffn1, norm_local):
    group, _, width = ffn0.shape

    def scatter(rows):
        return lax.psum_scatter(rows, EVERY, scatter_dimension=0, tiled=True).astype(F32)

    attn = jnp.concatenate((attn0, attn1), axis=0).reshape(-1, width)
    ffn = jnp.stack((ffn0, ffn1)).reshape(2 * group, -1, width)
    up = ffn[:, 128:].reshape(2 * group, 4, 32, width).swapaxes(1, 2).reshape(-1, 4 * width)
    norms = lax.psum_scatter(
        norm_local.reshape(lax.axis_size(EVERY), -1), EVERY, scatter_dimension=0, tiled=True
    )
    return scatter(attn), scatter(up), scatter(ffn[:, :128].reshape(-1, width)), norms[0]


def shards(
    enc_in,
    dec_in,
    cotangent,
    lengths,
    attn_master,
    ffn_in_master,
    ffn_out_master,
    norm_master,
    attn_first,
    ffn_in_first,
    ffn_out_first,
    norm_first,
    attn_second,
    ffn_in_second,
    ffn_out_second,
    norm_second,
):
    micro, _, length_dev, width = enc_in.shape
    rows = micro * length_dev
    hidden_units = ffn_in_master.shape[1]
    high, low = lax.axis_index("hi"), lax.axis_index("lo")
    n_high = lax.axis_size("hi")
    owner = lax.axis_index(EVERY)
    masters = (attn_master, ffn_in_master, ffn_out_master, norm_master)
    group_info = ((width, 12), (width, 2), (hidden_units, 2), (width, 10))
    onehots = [
        owner_groups(master.shape[0], owner, info[0], info[1])
        for master, info in zip(masters, group_info)
    ]
    weight_local = jnp.concatenate(
        [group_sum(onehot, row_squares(master)) for onehot, master in zip(onehots, masters)]
    )

    attn_rows = attn_master.shape[0]
    block0, block1, pack0, pack1, gains = gather_packs(
        attn_master.astype(BF), ffn_in_master.astype(BF), ffn_out_master.astype(BF), norm_master.astype(BF)
    )
    blocks = (block0, block1)

    def regroup(*arrays):
        packed = jnp.stack([array[:, 0] for array in arrays], axis=1)
        packed = lax.all_to_all(packed, "lo", split_axis=0, concat_axis=0, tiled=True)
        return packed.swapaxes(0, 1).reshape(len(arrays), rows, width)

    enc_rows = regroup(enc_in)[0]
    dec_rows, cot_rows = regroup(dec_in, cotangent)
    enc_window = jnp.concatenate((enc_rows, halo_rows(enc_rows)), axis=0)
    dec_window = jnp.concatenate((dec_rows, halo_rows(dec_rows)), axis=0)

    total_len = rows * n_high
    bounds = jnp.cumsum(lengths[:, 0, :], axis=-1)
    bounds = lax.dynamic_index_in_dim(bounds, low, 0, keepdims=False)
    base = high * rows
    own_pos = base + jnp.arange(rows, dtype=jnp.int32)
    step = jnp.arange(HALO, dtype=jnp.int32)
    if n_high == 2:
        halo_pos = jnp.where(high == 0, rows, rows - HALO) + step
    else:
        halo_pos = jnp.concatenate((base - HALO + step, base + rows + step))
    key_pos = jnp.concatenate((own_pos, halo_pos))
    key_seg = segments_at(bounds, key_pos, total_len)
    krow = jnp.stack((key_seg, key_pos), axis=0)
    kcol = jnp.stack((key_seg, key_pos), axis=1)
    places = {
        "krow": krow,
        "kcol": kcol,
        "qrow": krow[:, :rows],
        "qcol": kcol[:rows],
        "offsets": None if n_high == 2 else (0, rows - HALO),
        "core": jnp.stack((lax.axis_index("c"), jnp.where(high == 0, rows - HALO, 0))).astype(jnp.int32),
    }

    enc_picks, self_picks, cross_picks = (0, 1, 2, 3), (4, 5, 6, 7), (8, 9, 10, 11)
    *enc_kept, resid_one = attn_forward(
        enc_rows, enc_window, (block0, block0), gains, places, False, enc_picks, None
    )
    resid_two, enc_low = ffn_forward(resid_one, enc_rows, gains, pack0, places, 0, 2)
    low_window = jnp.concatenate((enc_low, halo_rows(enc_low)), axis=0)
    *self_kept, resid_three = attn_forward(
        dec_rows, dec_window, blocks, gains, places, True, self_picks, None
    )
    *cross_kept, resid_four = attn_forward(
        resid_three, low_window, (block1, block1), gains, places, False, cross_picks, 4
    )
    resid_five, dec_low = ffn_forward(resid_four, dec_rows, gains, pack1, places, 6, 8)

    plain = n_high != 2
    group = 2 * pack0[0].shape[0]
    grad_second, grad_five, dpack1, ng8 = ffn_backward(
        cot_rows, resid_five, resid_four, gains, pack1, gains, places, 6, 8
    )
    grad_first, dwq_c, dwo_c, own_c, halo_c, ng6 = attn_backward(
        grad_second, resid_four, resid_three, cross_kept, (block1, block1), gains, ng8, places, False, cross_picks, 6, 4
    )
    back_c = halo_return(halo_c)
    pair_f1 = ng6 if plain else reduce_cores(dpack1)
    grad_dec_q, dwq_s, dwo_s, own_s, halo_s, ng4 = attn_backward(
        grad_first, resid_three, dec_rows, self_kept, blocks, gains, pair_f1, places, True, self_picks, 4, None
    )
    back_s = halo_return(halo_s)
    grad_encoded, dwk_c, dwv_c = kv_backward(
        enc_low, own_c, back_c, (block1, block1), (), ng4, places, cross_picks, F32
    )
    part_f1 = ng4 if plain else reduce_chips(pair_f1)
    grad_hidden, grad_two, dpack0, ng2 = ffn_backward(
        grad_encoded, resid_two, resid_one, gains, pack0, ng4, places, 0, 2
    )
    dec_grad, dwk_s, dwv_s = kv_backward(
        dec_rows, own_s, back_s, blocks, (grad_five, grad_dec_q), part_f1, places, self_picks, BF
    )
    attn_local1 = jnp.concatenate((dwv_s, dwo_s, dwq_c, dwk_c, dwv_c, dwo_c), axis=0).reshape(group, -1, width)
    pair_a1 = ng2 if plain else reduce_cores(attn_local1)
    grad_enc_q, dwq_e, dwo_e, own_e, halo_e, ng0 = attn_backward(
        grad_hidden, resid_one, enc_rows, enc_kept, (block0, block0), gains, pair_a1, places, False, enc_picks, 0, None
    )
    back_e = halo_return(halo_e)
    pair_f0 = ng0 if plain else reduce_cores(dpack0)
    enc_grad, dwk_e, dwv_e = kv_backward(
        enc_rows, own_e, back_e, (block0, block0), (grad_two, grad_enc_q), pair_f0, places, enc_picks, BF
    )
    attn_local0 = jnp.concatenate((dwq_e, dwk_e, dwv_e, dwo_e, dwq_s, dwk_s), axis=0).reshape(group, -1, width)
    norm_local = jnp.concatenate((ng0, ng2, ng4, ng6, ng8), axis=0)
    if plain:
        attn_own, up_own, down_own, norm_own = reduce_plain(attn_local0, attn_local1, dpack0, dpack1, norm_local)
    else:
        norm_count = norm_master.shape[0]
        norm_local = norm_local.reshape(n_high, group, norm_count).swapaxes(0, 1).astype(BF)
        norm_local = jnp.pad(norm_local, ((0, 0), (0, 16 - n_high), (0, width - norm_count)))
        part_a1 = reduce_chips(pair_a1)
        part_f0 = reduce_chips(pair_f0)
        part_a0 = reduce_chips(reduce_cores(jnp.concatenate((attn_local0, norm_local), axis=1)))
        ffn_own = join_halves(part_f0, part_f1)
        both = join_halves(part_a0, jnp.concatenate((part_a1, part_a0[attn_rows:]), axis=0))
        attn_own, up_own, down_own = both[:attn_rows], unpack_up(ffn_own[128:]), ffn_own[:128]
        norm_own = lax.dynamic_index_in_dim(both[attn_rows:], high, 0, keepdims=False)[:norm_count]

    def restore(*arrays):
        outs = jnp.stack(arrays, axis=0).reshape(len(arrays), micro, length_dev, width).swapaxes(0, 1)
        return lax.all_to_all(outs, "lo", split_axis=0, concat_axis=0, tiled=True)

    lows = restore(enc_low, dec_low)
    grads = restore(enc_grad, dec_grad)

    owned = (attn_own, up_own, down_own, norm_own)
    firsts = (attn_first, ffn_in_first, ffn_out_first, norm_first)
    seconds = (attn_second, ffn_in_second, ffn_out_second, norm_second)
    moments = [
        lamb_moments(masters[index], owned[index], firsts[index], seconds[index])
        for index in range(4)
    ]
    update_local = jnp.concatenate(
        [group_sum(onehots[index], row_squares(moments[index][2])) for index in range(4)]
    )
    squares = jnp.stack((weight_local, update_local))
    squares = jnp.pad(squares, ((0, 6), (0, 128 - squares.shape[1])))
    count = lax.axis_size(EVERY)
    squares = jnp.broadcast_to(squares[None], (count,) + squares.shape)
    squares = jnp.sum(lax.all_to_all(squares, EVERY, split_axis=0, concat_axis=0, tiled=True), axis=0)
    norms = jnp.sqrt(squares[:2, :26])
    ratio = norms[0] / norms[1]
    bounds_at = (0, 12, 14, 16, 26)
    new_weights = []
    for index in range(4):
        row_ratio = jnp.sum(
            jnp.where(onehots[index], ratio[None, bounds_at[index] : bounds_at[index + 1]], 0.0), axis=1
        )
        if masters[index].ndim == 2:
            row_ratio = row_ratio[:, None]
        new_weights.append(masters[index] - learn_rate * row_ratio * moments[index][2])
    return (
        lows[:, 0][:, None],
        lows[:, 1][:, None],
        grads[:, 0][:, None].astype(F32),
        grads[:, 1][:, None].astype(F32),
        *owned,
        *new_weights,
        *[item[0] for item in moments],
        *[item[1] for item in moments],
        *[item.astype(BF) for item in new_weights],
        norms,
        ratio,
    )


def solution(mesh):
    count_seq, count_stream = mesh.shape["seq"], mesh.shape["stream"]

    def run(*args):
        micro = args[0].shape[0]
        split = Mesh(
            mesh.devices.reshape(count_seq // micro, micro, count_stream // 2, 2), ("hi", "lo", "y", "c")
        )
        tokens = P(None, ("y", "c"), ("hi", "lo"), None)
        wide = P(EVERY, None)
        flat = P(EVERY)
        owned = (wide, wide, wide, flat)
        return jax.shard_map(
            shards,
            mesh=split,
            in_specs=(tokens, tokens, tokens, P(None, ("y", "c"), None), *owned, *owned, *owned),
            out_specs=(tokens, tokens, tokens, tokens, *owned, *owned, *owned, *owned, *owned, P(), P()),
            check_vma=False,
        )(*args)

    return run
```

```python
import functools
import math

import jax
import jax.numpy as jnp
from jax import lax
from jax.experimental import pallas as pl
from jax.experimental.pallas import tpu as pltpu
from jax.sharding import Mesh
from jax.sharding import PartitionSpec as P

HEADS = 8
STEP = 5
HALO = 256
TILE = 256

norm_eps = 1e-05
beta_one = 0.5
beta_two = 0.5
lamb_eps = 1e-06
weight_decay = 0.01
learn_rate = 0.5
masked_score = -1e30

BF = jnp.bfloat16
F32 = jnp.float32
MIB = 1024 * 1024


def dot_nn(a, b):
    return lax.dot_general(a, b, (((1,), (0,)), ((), ())), preferred_element_type=F32)


def dot_nt(a, b):
    return lax.dot_general(a, b, (((1,), (1,)), ((), ())), preferred_element_type=F32)


def dot_tn(a, b):
    return lax.dot_general(a, b, (((0,), (0,)), ((), ())), preferred_element_type=F32)


def norm_parts(rows):
    centre = rows - jnp.mean(rows, axis=-1, keepdims=True)
    inv = lax.rsqrt(jnp.mean(centre * centre, axis=-1, keepdims=True) + norm_eps)
    return centre * inv, inv


def norm_rows(rows, gain, bias):
    return norm_parts(rows)[0] * gain + bias


def norm_back(rows, gain, grad):
    unit, inv = norm_parts(rows)
    lead = grad * gain
    back = inv * (
        lead
        - jnp.mean(lead, axis=-1, keepdims=True)
        - unit * jnp.mean(lead * unit, axis=-1, keepdims=True)
    )
    return (
        back,
        jnp.sum(grad * unit, axis=0, keepdims=True),
        jnp.sum(grad, axis=0, keepdims=True),
    )


gelu_a = 0.7978845608028654
gelu_b = 0.044715


def gelu(v):
    return 0.5 * v * (1.0 + jnp.tanh(gelu_a * (v + gelu_b * (v * v * v))))


def gelu_both(v):
    sq = v * v
    t = jnp.tanh(gelu_a * (v + gelu_b * (sq * v)))
    half = 0.5 * (1.0 + t)
    slope = half + 0.5 * v * (1.0 - t * t) * (gelu_a * (1.0 + 3.0 * gelu_b * sq))
    return v * half, slope


def lane_low(shape):
    return lax.broadcasted_iota(jnp.int32, shape, 1) < 64


def call(body, name, scalars, ins, outs, flops, scratch=(), order=None):
    arrays, blocks = [], [pl.BlockSpec(memory_space=pltpu.SMEM)]
    for item in ins:
        array, block, index = item if isinstance(item, tuple) else (item, item.shape, (0,) * item.ndim)
        arrays.append(array)
        blocks.append(pl.BlockSpec(block, functools.partial(lambda spot, step: spot, index)))
    if order is not None:
        arrays.append(order)
        blocks.append(pl.BlockSpec(memory_space=pl.ANY))
    size = sum(math.prod(block.block_shape) * 2 for block in blocks if block.block_shape is not None)
    return pl.pallas_call(
        body,
        grid=(1,),
        in_specs=blocks,
        out_specs=tuple(
            pl.BlockSpec(out.shape, functools.partial(lambda rank, step: (0,) * rank, len(out.shape)))
            for out in outs
        ),
        out_shape=tuple(outs),
        scratch_shapes=list(scratch),
        compiler_params=pltpu.CompilerParams(vmem_limit_bytes=56 * MIB),
        cost_estimate=pl.CostEstimate(flops=flops, bytes_accessed=2 * size, transcendentals=0),
        name=name,
    )(scalars, *arrays)


def shape_of(dtype, *dims):
    return jax.ShapeDtypeStruct(dims, dtype)


def square(array, index):
    width = array.shape[1]
    return (array, (width, width), (index, 0))


def tiles_of(core, rows, window):
    if window == rows + HALO:
        near = pl.multiple_of(core[1], HALO)
        return ((near, 0), (pl.multiple_of(rows - TILE - core[1], HALO), None))
    return ((0, 0), (rows - TILE, 1))


def key_rows(ref, lanes, rows, halo):
    if halo is None:
        return ref[0:rows, lanes]
    if halo == 0:
        return ref[0 : rows + HALO, lanes]
    return jnp.concatenate((ref[0:rows, lanes], ref[rows + HALO : rows + 2 * HALO, lanes]), axis=0)


def key_lanes(ref, row, rows, halo):
    if halo is None:
        return ref[row : row + 1, 0:rows]
    if halo == 0:
        return ref[row : row + 1, 0 : rows + HALO]
    return jnp.concatenate(
        (ref[row : row + 1, 0:rows], ref[row : row + 1, rows + HALO : rows + 2 * HALO]), axis=1
    )


def halves(shape):
    low = lane_low(shape)
    return low, ~low


def keep(mask, values):
    return jnp.where(mask, values, jnp.zeros_like(values))


def attn_fwd_body(cfg, *refs):
    causal, gain_at = cfg
    core, q_src, kv_src, w_q, w_k, w_v, w_o, gains, qcol, krow = refs[:10]
    q_out, k_out, v_out, o_out, lse_out, res_out = refs[10:]
    rows, _ = q_src.shape
    window = k_out.shape[0]

    def base_rows():
        if gain_at is None:
            return q_src[...].astype(F32)
        return norm_rows(q_src[...], gains[gain_at : gain_at + 1, :], gains[gain_at + 1 : gain_at + 2, :])

    queries = dot_nn(base_rows().astype(BF), w_q[...])
    q_out[...] = (queries.astype(BF).astype(F32) * 0.125).astype(BF)
    k_out[...] = dot_nn(kv_src[...], w_k[...]).astype(BF)
    v_out[...] = dot_nn(kv_src[...], w_v[...]).astype(BF)
    for offset, halo in tiles_of(core, rows, window):
        spot = pl.ds(offset, TILE)
        allowed = qcol[spot, 0:1] == key_lanes(krow, 0, rows, halo)
        if causal:
            allowed = allowed & (key_lanes(krow, 1, rows, halo) <= qcol[spot, 1:2])
        lane = lax.broadcasted_iota(jnp.int32, (TILE, 128), 1)
        packed = jnp.zeros((TILE, 128), F32)
        for pair in range(HEADS // 2):
            lanes = slice(pair * 128, pair * 128 + 128)
            q2 = q_out[spot, lanes]
            k2 = key_rows(k_out, lanes, rows, halo)
            v2 = key_rows(v_out, lanes, rows, halo)
            mixed = None
            for half in range(2):
                scores = dot_nt(keep(halves(q2.shape)[half], q2), k2)
                scores = jnp.where(allowed, scores, masked_score)
                top = jnp.max(scores, axis=-1, keepdims=True)
                weights = jnp.exp(scores - top)
                total = jnp.sum(weights, axis=-1, keepdims=True)
                probs = (weights * (1.0 / total)).astype(BF)
                part = dot_nn(probs, keep(halves(v2.shape)[half], v2))
                mixed = part if mixed is None else mixed + part
                packed = jnp.where(lane == 2 * pair + half, top + jnp.log(total), packed)
            o_out[spot, lanes] = mixed.astype(BF)
        lse_out[:, spot] = jnp.transpose(packed)[0:HEADS, :]
    res_out[...] = base_rows() + dot_nn(o_out[...], w_o[...])


def attn_forward(q_src, kv_src, mats, gains, places, causal, gain_at):
    rows, width = q_src.shape
    window = kv_src.shape[0]
    outs = (
        shape_of(BF, rows, width),
        shape_of(BF, window, width),
        shape_of(BF, window, width),
        shape_of(BF, rows, width),
        shape_of(F32, HEADS, rows),
        shape_of(F32, rows, width),
    )
    return call(
        functools.partial(attn_fwd_body, (causal, gain_at)),
        "attn_fwd",
        places["core"],
        (q_src, kv_src, *mats, gains, places["qcol"], places["krow"]),
        outs,
        12 * rows * width * width + 8 * rows * window * width,
    )


def score_grads(q2, do2, k2, v2, allowed, lse, delta):
    sums = None
    for half in range(2):
        qh = keep(halves(q2.shape)[half], q2)
        doh = keep(halves(do2.shape)[half], do2)
        scores = jnp.where(allowed, dot_nt(k2, qh), masked_score)
        probs = jnp.exp(scores - lse[half])
        gscores = (probs * (dot_nt(v2, doh) - delta[half])).astype(BF)
        parts = (
            dot_tn(gscores, keep(halves(k2.shape)[half], k2)),
            dot_nn(gscores, qh),
            dot_nn(probs.astype(BF), doh),
        )
        sums = parts if sums is None else tuple(a + b for a, b in zip(sums, parts))
    return sums


def attn_head_body(cfg, *refs):
    causal, gain_at, ordered = cfg
    core, grad_in, resid, o_in, q_in, k_in, v_in, lse_in, w_o, gains, qrow, kcol = refs[:12]
    back_out, do_out, delta_out, dwo_out, halo_out, dqh_out, ng_out = refs[12 + ordered :]
    rows, width = q_in.shape
    window = k_in.shape[0]
    back, dgain, dbias = norm_back(resid[...], gains[gain_at : gain_at + 1, :], grad_in[...].astype(F32))
    back_out[...] = back
    ng_out[0:1, :] = dgain
    ng_out[1:2, :] = dbias
    branch = back.astype(BF)
    do_out[...] = dot_nt(branch, w_o[...]).astype(BF)
    mixed = do_out[...].astype(F32) * o_in[...].astype(F32)
    high = mixed.astype(BF)
    rest = (mixed - high.astype(F32)).astype(BF)
    head = lax.broadcasted_iota(jnp.int32, (16, width), 1) // (width // HEADS)
    which = (head == lax.broadcasted_iota(jnp.int32, (16, width), 0)).astype(F32).astype(BF)
    delta_out[...] = (dot_nt(which, high) + dot_nt(which, rest))[0:HEADS, :]
    for offset, halo in tiles_of(core, rows, window):
        if halo is None:
            continue
        spot = pl.ds(offset, TILE)
        keys = slice(rows + halo * HALO, rows + halo * HALO + HALO)
        here = slice(halo * HALO, halo * HALO + HALO)
        allowed = kcol[keys, 0:1] == qrow[0:1, spot]
        if causal:
            allowed = allowed & (kcol[keys, 1:2] <= qrow[1:2, spot])
        for pair in range(HEADS // 2):
            lanes = slice(pair * 128, pair * 128 + 128)
            heads = (2 * pair, 2 * pair + 1)
            dq2, dk2, dv2 = score_grads(
                q_in[spot, lanes],
                do_out[spot, lanes],
                k_in[keys, lanes],
                v_in[keys, lanes],
                allowed,
                [lse_in[h : h + 1, spot] for h in heads],
                [delta_out[h : h + 1, spot] for h in heads],
            )
            dqh_out[here, lanes] = dq2
            halo_out[0, here, lanes] = dk2.astype(BF)
            halo_out[1, here, lanes] = dv2.astype(BF)
    dwo_out[...] = dot_tn(o_in[...], branch).astype(BF)


def attn_head(grad_in, resid, kept, w_o, gains, places, causal, gain_at, order):
    q, k, v, o, lse = kept
    rows, width = q.shape
    window = k.shape[0]
    outs = (
        shape_of(F32, rows, width),
        shape_of(BF, rows, width),
        shape_of(F32, HEADS, rows),
        shape_of(BF, width, width),
        shape_of(BF, 2, window - rows, width),
        shape_of(F32, window - rows, width),
        shape_of(F32, 2, width),
    )
    return call(
        functools.partial(attn_head_body, (causal, gain_at, order is not None)),
        "attn_head",
        places["core"],
        (grad_in, resid, o, q, k, v, lse, w_o, gains, places["qrow"], places["kcol"]),
        outs,
        4 * rows * width * width + 10 * TILE * (window - rows) * width,
        order=order,
    )


def attn_body_body(cfg, *refs):
    causal, src_gain, ordered, window = cfg
    core, back, do_in, delta, dqh, src, q_in, k_in, v_in, lse_in, w_q, gains, qrow, kcol = refs[:14]
    gq_out, dwq_out, own_out, dq_scr = refs[14 + ordered :]
    rows, width = q_in.shape
    for tile in range(rows // TILE):
        spot = slice(tile * TILE, tile * TILE + TILE)
        allowed = kcol[0:rows, 0:1] == qrow[0:1, spot]
        if causal:
            allowed = allowed & (kcol[0:rows, 1:2] <= qrow[1:2, spot])
        for pair in range(HEADS // 2):
            lanes = slice(pair * 128, pair * 128 + 128)
            heads = (2 * pair, 2 * pair + 1)
            dq2, dk2, dv2 = score_grads(
                q_in[spot, lanes],
                do_in[spot, lanes],
                k_in[:, lanes],
                v_in[:, lanes],
                allowed,
                [lse_in[h : h + 1, spot] for h in heads],
                [delta[h : h + 1, spot] for h in heads],
            )
            dq_scr[spot, lanes] = dq2
            if tile == 0:
                own_out[0, :, lanes] = dk2
                own_out[1, :, lanes] = dv2
            else:
                own_out[0, :, lanes] += dk2
                own_out[1, :, lanes] += dv2
    for offset, halo in tiles_of(core, rows, window):
        if halo is not None:
            dq_scr[pl.ds(offset, TILE), :] += dqh[halo * HALO : halo * HALO + HALO, :]
    grad_q = (dq_scr[...] * 0.125).astype(BF)
    if src_gain is None:
        low_src = src[...]
    else:
        low_src = norm_rows(
            src[...], gains[src_gain : src_gain + 1, :], gains[src_gain + 1 : src_gain + 2, :]
        ).astype(BF)
    dwq_out[...] = dot_tn(low_src, grad_q).astype(BF)
    gq_out[...] = back[...] + dot_nt(grad_q, w_q[...])


def attn_body(back, grad_o, delta, dqh, src, kept, w_q, gains, places, causal, src_gain, order):
    q, k, v, _, lse = kept
    rows, width = q.shape
    outs = (shape_of(F32, rows, width), shape_of(BF, width, width), shape_of(F32, 2, rows, width))
    own = ((rows, width), (0, 0))
    return call(
        functools.partial(attn_body_body, (causal, src_gain, order is not None, k.shape[0])),
        "attn_body",
        places["core"],
        (back, grad_o, delta, dqh, src, q, (k, *own), (v, *own), lse, w_q, gains, places["qrow"], places["kcol"]),
        outs,
        4 * rows * width * width + 10 * rows * rows * width,
        scratch=[pltpu.VMEM((rows, width), F32)],
        order=order,
    )


def split_places(core, source, kept, sent):
    for parity in range(2):

        @pl.when(core[0] == parity)
        def store():
            for chip in range(kept.shape[0]):
                kept[chip] = source[2 * chip + parity]
                sent[chip] = source[2 * chip + 1 - parity]


def join_body(starts, *refs):
    core, mine, other = refs[:3]
    for parity in range(2):

        @pl.when(core[0] == parity)
        def store():
            for out, start in zip(refs[3:], starts):
                for chip in range(mine.shape[0]):
                    out[2 * chip + parity] = mine[chip, start : start + out.shape[1], :]
                    out[2 * chip + 1 - parity] = other[chip, start : start + out.shape[1], :]


def join_places(core, mine, other, *counts):
    chips, _, width = mine.shape
    starts = [sum(counts[:index]) for index in range(len(counts))]
    outs = [shape_of(BF, 2 * chips, count, width) for count in counts]
    return call(functools.partial(join_body, starts), "join_places", core, (mine, other), outs, 0)


def kv_bwd_body(cfg, *refs):
    n_add, layout, offsets, n_mats, with_norm, ordered = cfg
    core, src, own, halo, w_k, w_v = refs[:6]
    adds = refs[6 : 6 + n_add]
    mats = refs[6 + n_add : 6 + n_add + n_mats]
    refs = refs[6 + n_add + n_mats :]
    norm_in = refs[0] if with_norm else None
    refs = refs[with_norm + ordered :]
    rows, width = src.shape
    g_out, dwk_out = refs[:2]
    if layout is None:
        dwv_out, scr = refs[2:]
    else:
        kept, sent, scr, stack = refs[2:]
    scr[...] = own[...]
    for index in range(halo.shape[1] // HALO):
        spot = pl.ds(pl.multiple_of(core[1], HALO) if offsets is None else offsets[index], HALO)
        scr[:, spot, :] += halo[:, index * HALO : index * HALO + HALO, :].astype(F32)
    dk = scr[0].astype(BF)
    dv = scr[1].astype(BF)
    dwk = dot_tn(src[...], dk).astype(BF)
    dwv = dot_tn(src[...], dv).astype(BF)
    dwk_out[...] = dwk
    if layout is None:
        dwv_out[...] = dwv
    total = dot_nt(dk, w_k[...]) + dot_nt(dv, w_v[...])
    for ref in adds:
        total = total + ref[...]
    g_out[...] = total.astype(g_out.dtype)
    if layout is not None:
        places = stack.shape[0]
        per = 6 * width // places
        for slot, item in enumerate(layout):
            row, end = slot * width, slot * width + width
            while row < end:
                place, start = divmod(row, per)
                take = min(per - start, end - row)
                at = row - slot * width
                if item == "k":
                    piece = dwk[at : at + take]
                elif item == "v":
                    piece = dwv[at : at + take]
                else:
                    piece = mats[item][at : at + take, :]
                stack[place, start : start + take, :] = piece
                row += take
        if with_norm:
            stack[:, per:, :] = norm_in[...]
        split_places(core, stack, kept, sent)


def kv_backward(src, own, halo, w_k, w_v, adds, places, out_type, group, layout=None, mats=(), norm=None, order=None):
    rows, width = src.shape
    outs = [shape_of(out_type, rows, width), shape_of(BF, width, width)]
    scratch = [pltpu.VMEM((2, rows, width), F32)]
    if layout is None:
        outs.append(shape_of(BF, width, width))
    else:
        block = 6 * width // group + (0 if norm is None else norm.shape[1])
        outs += [shape_of(BF, group // 2, block, width)] * 2
        scratch.append(pltpu.VMEM((group, block, width), BF))
    cfg = (len(adds), layout, places["offsets"], len(mats), norm is not None, order is not None)
    return call(
        functools.partial(kv_bwd_body, cfg),
        "kv_bwd",
        places["core"],
        (src, own, halo, w_k, w_v, *adds, *mats, *(() if norm is None else (norm,))),
        outs,
        8 * rows * width * width,
        scratch=scratch,
        order=order,
    )


def up_tile(pack, tile):
    places, _, width = pack.shape
    return pack[:, 128 + 32 * tile : 160 + 32 * tile, :].reshape(places * 32, width)


def down_tile(pack, tile):
    return pack[4 * tile : 4 * tile + 4, 0:128, :].reshape(512, pack.shape[2])


def ffn_fwd_body(cfg, core, resid, base, gains, pack, res_out, low_out):
    gain_in, gain_out = cfg
    hidden = norm_rows(resid[...], gains[gain_in : gain_in + 1, :], gains[gain_in + 1 : gain_in + 2, :])
    low = hidden.astype(BF)
    res_out[...] = hidden + base[...].astype(F32)
    for tile in range(4):
        activ = gelu(dot_nn(low, up_tile(pack, tile))).astype(BF)
        res_out[...] += dot_nn(activ, down_tile(pack, tile))
    low_out[...] = norm_rows(
        res_out[...], gains[gain_out : gain_out + 1, :], gains[gain_out + 1 : gain_out + 2, :]
    ).astype(BF)


def ffn_forward(resid, base, gains, pack, places, gain_in, gain_out):
    rows, width = resid.shape
    return call(
        functools.partial(ffn_fwd_body, (gain_in, gain_out)),
        "ffn_fwd",
        places["core"],
        (resid, base, gains, pack),
        (shape_of(F32, rows, width), shape_of(BF, rows, width)),
        16 * rows * width * width,
    )


def ffn_bwd_body(cfg, *refs):
    gain_in, gain_out, split, ordered = cfg
    core, grad_in, res_late, resid, gains, pack = refs[:6]
    gh_out, late_out, ng_out = refs[6 + ordered : 9 + ordered]
    if split:
        kept, sent, hid_low, late_low, dpack = refs[9 + ordered :]
    else:
        dpack, hid_low, late_low = refs[9 + ordered :]
    back, dgain, dbias = norm_back(
        res_late[...], gains[gain_out : gain_out + 1, :], grad_in[...].astype(F32)
    )
    late_out[...] = back
    gh_out[...] = back
    late_low[...] = back.astype(BF)
    ng_out[0:1, :] = dgain
    ng_out[1:2, :] = dbias
    hid_low[...] = norm_rows(
        resid[...], gains[gain_in : gain_in + 1, :], gains[gain_in + 1 : gain_in + 2, :]
    ).astype(BF)
    places, _, width = pack.shape
    for tile in range(4):
        activ, slope = gelu_both(dot_nn(hid_low[...], up_tile(pack, tile)))
        grad_down = dot_tn(activ.astype(BF), late_low[...]).astype(BF)
        dpack[4 * tile : 4 * tile + 4, 0:128, :] = grad_down.reshape(4, 128, width)
        grad_act = dot_nt(late_low[...], down_tile(pack, tile)).astype(BF).astype(F32)
        grad_pre = (grad_act * slope).astype(BF)
        grad_up = dot_tn(hid_low[...], grad_pre).astype(BF)
        dpack[:, 128 + 32 * tile : 160 + 32 * tile, :] = grad_up.reshape(places, 32, width)
        gh_out[...] += dot_nt(grad_pre, up_tile(pack, tile))
    if split:
        split_places(core, dpack, kept, sent)


def ffn_backward(grad_in, res_late, resid, gains, pack, places, gain_in, gain_out, split, order=None):
    rows, width = resid.shape
    count, block, _ = pack.shape
    outs = [shape_of(F32, rows, width), shape_of(F32, rows, width), shape_of(F32, 2, width)]
    scratch = [pltpu.VMEM((rows, width), BF), pltpu.VMEM((rows, width), BF)]
    if split:
        outs += [shape_of(BF, count // 2, block, width)] * 2
        scratch.append(pltpu.VMEM(pack.shape, BF))
    else:
        outs.append(shape_of(BF, *pack.shape))
    return call(
        functools.partial(ffn_bwd_body, (gain_in, gain_out, split, order is not None)),
        "ffn_bwd",
        places["core"],
        (grad_in, res_late, resid, gains, pack),
        outs,
        40 * rows * width * width,
        scratch=scratch,
        order=order,
    )


def segments_at(bounds, places, total_len):
    found = jnp.sum((bounds[None, :] <= places[:, None]).astype(jnp.int32), axis=-1)
    return jnp.where((places >= 0) & (places < total_len), found, -1)


def row_squares(values):
    if values.ndim == 2:
        return jnp.sum(values * values, axis=1)
    return values * values


def owner_groups(rows_local, owner, per_group, count):
    group_ids = (owner * rows_local + jnp.arange(rows_local, dtype=jnp.int32)) // per_group
    return group_ids[:, None] == jnp.arange(count, dtype=jnp.int32)[None, :]


def group_sum(onehot, row_values):
    return jnp.sum(jnp.where(onehot, row_values[:, None], 0.0), axis=0)


def lamb_moments(master, grad_rows, first, second):
    first_new = beta_one * first + (1.0 - beta_one) * grad_rows
    second_new = beta_two * second + (1.0 - beta_two) * grad_rows * grad_rows
    update = (
        first_new
        / (1.0 - beta_one**STEP)
        / (jnp.sqrt(second_new / (1.0 - beta_two**STEP)) + lamb_eps)
        + weight_decay * master
    )
    return (first_new, second_new, update)


GROUP = ("lo", "y", "c")
CHIPS = ("lo", "y")
EVERY = ("hi", "lo", "y", "c")


def swap_hi(array):
    return lax.ppermute(array, "hi", [(0, 1), (1, 0)])


def shift_hi(array, distance):
    count = lax.axis_size("hi")
    route = [(i - distance, i) for i in range(count) if i - distance in range(count)]
    return lax.ppermute(array, "hi", route)


def halo_rows(rows_array):
    high = lax.axis_index("hi")
    rows = rows_array.shape[-2]
    axis = rows_array.ndim - 2
    if lax.axis_size("hi") == 2:
        sent = jnp.where(
            high == 0,
            lax.slice_in_dim(rows_array, rows - HALO, rows, axis=axis),
            lax.slice_in_dim(rows_array, 0, HALO, axis=axis),
        )
        return swap_hi(sent)
    left = shift_hi(lax.slice_in_dim(rows_array, rows - HALO, rows, axis=axis), 1)
    right = shift_hi(lax.slice_in_dim(rows_array, 0, HALO, axis=axis), -1)
    return jnp.concatenate((left, right), axis=axis)


def halo_return(grads):
    if lax.axis_size("hi") == 2:
        return swap_hi(grads)
    to_left = shift_hi(grads[:, :HALO], -1)
    to_right = shift_hi(grads[:, HALO:], 1)
    return jnp.concatenate((to_left, to_right), axis=1)


def pack_up(rows):
    count, units = rows.shape
    return rows.reshape(count, 4, units // 4).swapaxes(0, 1).reshape(4 * count, units // 4)


def unpack_up(packed):
    count, width = packed.shape
    return packed.reshape(4, count // 4, width).swapaxes(0, 1).reshape(count // 4, 4 * width)


def swap_core(array):
    return lax.ppermute(array, "c", [(0, 1), (1, 0)])


def tie(array, other):
    bit = lax.slice(other, (0,) * other.ndim, (1,) * other.ndim).reshape(()) * 0
    return array + bit.astype(array.dtype)


def spread_chips(shard):
    count = lax.axis_size(CHIPS)
    sent = jnp.broadcast_to(shard[None], (count,) + shard.shape)
    return lax.all_to_all(sent, CHIPS, split_axis=0, concat_axis=0, tiled=True)


def from_parity(mine, other):
    even = lax.axis_index("c") == 0
    full = jnp.stack((jnp.where(even, mine, other), jnp.where(even, other, mine)), axis=1)
    return full.reshape(-1, *mine.shape[1:])


def gather_plain(attn_shard, up_shard, down_shard, norm_shard):
    width = attn_shard.shape[1]
    group = lax.axis_size(GROUP)
    norm_count = norm_shard.shape[0]
    attn = lax.all_gather(attn_shard, EVERY, axis=0, tiled=True)
    down = lax.all_gather(down_shard, EVERY, axis=0, tiled=True).reshape(2, group, -1, width)
    up = lax.all_gather(up_shard, EVERY, axis=0, tiled=True)
    up = up.reshape(2, group, -1, 4, width).swapaxes(2, 3).reshape(2, group, -1, width)
    norms = jnp.pad(norm_shard[None, :], ((0, 0), (0, width - norm_count)))
    norms = lax.all_gather(norms, EVERY, axis=0, tiled=True)[:, :norm_count]
    ffn = jnp.concatenate((down, up), axis=2)
    half = attn.shape[0] // 2
    return attn[:half], attn[half:], ffn[0], ffn[1], norms.reshape(10, width).astype(F32)


def reduce_cores(kept, sent):
    return (kept.astype(F32) + swap_core(sent).astype(F32)).astype(BF)


def reduce_chips(pair):
    parts = lax.all_to_all(pair, CHIPS, split_axis=0, concat_axis=0, tiled=True)
    return jnp.sum(parts.astype(F32), axis=0)


def join_halves(zero, one):
    first = lax.axis_index("hi") == 0
    mine = jnp.where(first, zero, one)
    sent = jnp.where(first, one, zero).astype(BF)
    return mine + swap_hi(sent).astype(F32)


def reduce_plain(attn0, attn1, ffn0, ffn1, norm_local):
    group, _, width = ffn0.shape

    def scatter(rows):
        return lax.psum_scatter(rows, EVERY, scatter_dimension=0, tiled=True).astype(F32)

    attn = jnp.concatenate((attn0, attn1), axis=0).reshape(-1, width)
    ffn = jnp.stack((ffn0, ffn1)).reshape(2 * group, -1, width)
    up = ffn[:, 128:].reshape(2 * group, 4, 32, width).swapaxes(1, 2).reshape(-1, 4 * width)
    norms = lax.psum_scatter(
        norm_local.reshape(lax.axis_size(EVERY), -1), EVERY, scatter_dimension=0, tiled=True
    )
    return scatter(attn), scatter(up), scatter(ffn[:, :128].reshape(-1, width)), norms[0]


def shards(
    enc_in,
    dec_in,
    cotangent,
    lengths,
    attn_master,
    ffn_in_master,
    ffn_out_master,
    norm_master,
    attn_first,
    ffn_in_first,
    ffn_out_first,
    norm_first,
    attn_second,
    ffn_in_second,
    ffn_out_second,
    norm_second,
):
    micro, _, length_dev, width = enc_in.shape
    rows = micro * length_dev
    hidden_units = ffn_in_master.shape[1]
    high, low = lax.axis_index("hi"), lax.axis_index("lo")
    n_high = lax.axis_size("hi")
    owner = lax.axis_index(EVERY)
    masters = (attn_master, ffn_in_master, ffn_out_master, norm_master)
    group_info = ((width, 12), (width, 2), (hidden_units, 2), (width, 10))
    onehots = [
        owner_groups(master.shape[0], owner, info[0], info[1])
        for master, info in zip(masters, group_info)
    ]
    weight_local = jnp.concatenate(
        [group_sum(onehot, row_squares(master)) for onehot, master in zip(onehots, masters)]
    )

    def regroup(*arrays):
        packed = jnp.stack([array[:, 0] for array in arrays], axis=1)
        packed = lax.all_to_all(packed, "lo", split_axis=0, concat_axis=0, tiled=True)
        return packed.swapaxes(0, 1).reshape(len(arrays), rows, width)

    core = jnp.stack((lax.axis_index("c"), jnp.where(high == 0, rows - HALO, 0))).astype(jnp.int32)
    attn_rows = attn_master.shape[0]
    norm_count = norm_master.shape[0]
    plain = n_high != 2
    attn_low, up_low, down_low, norm_low = [master.astype(BF) for master in masters]
    if plain:
        block0, block1, pack0, pack1, gains = gather_plain(attn_low, up_low, down_low, norm_low)
        enc_rows = regroup(enc_in)[0]
        dec_rows, cot_rows = regroup(dec_in, cotangent)
        enc_halo = halo_rows(enc_rows)
    else:
        first = high == 0
        norm_pad = jnp.pad(norm_low[None, :], ((0, 15), (0, width - norm_count)))
        mine = jnp.concatenate((attn_low, norm_pad), axis=0)
        other = swap_hi(mine)
        enc_rows = regroup(enc_in)[0]
        enc_halo = halo_rows(enc_rows)
        zero = jnp.where(first, mine, other)
        one = jnp.where(first, other, mine)
        early = spread_chips(jnp.concatenate((zero[: attn_rows + 1], one[attn_rows:-1]), axis=0))
        early_other = swap_core(early)
        ffn_mine = tie(jnp.concatenate((down_low, pack_up(up_low)), axis=0), other)
        ffn_other = swap_hi(ffn_mine)
        ffn_zero = jnp.where(first, ffn_mine, ffn_other)
        ffn_one = jnp.where(first, ffn_other, ffn_mine)
        dec_rows, cot_rows = regroup(tie(dec_in, early), cotangent)
        middle = spread_chips(tie(jnp.concatenate((ffn_zero, one[:attn_rows]), axis=0), early))
        middle_other = swap_core(middle)
        late = spread_chips(tie(ffn_one, middle))
        next_rows = ffn_mine.shape[0]
        (pack1,) = join_places(core, late, swap_core(late), next_rows)
        block0, norm_all = join_places(core, early, early_other, attn_rows, 16)
        gains = norm_all[:, :2, :norm_count].swapaxes(0, 1).reshape(10, width).astype(F32)
        pack0, block1 = join_places(core, middle, middle_other, next_rows, attn_rows)
        block0, block1 = block0.reshape(-1, width), block1.reshape(-1, width)
    enc_window = jnp.concatenate((enc_rows, enc_halo), axis=0)
    dec_window = jnp.concatenate((dec_rows, halo_rows(dec_rows)), axis=0)
    group = pack0.shape[0]

    total_len = rows * n_high
    bounds = jnp.cumsum(lengths[:, 0, :], axis=-1)
    bounds = lax.dynamic_index_in_dim(bounds, low, 0, keepdims=False)
    base = high * rows
    own_pos = base + jnp.arange(rows, dtype=jnp.int32)
    step = jnp.arange(HALO, dtype=jnp.int32)
    if n_high == 2:
        halo_pos = jnp.where(high == 0, rows, rows - HALO) + step
    else:
        halo_pos = jnp.concatenate((base - HALO + step, base + rows + step))
    key_pos = jnp.concatenate((own_pos, halo_pos))
    key_seg = segments_at(bounds, key_pos, total_len)
    krow = jnp.stack((key_seg, key_pos), axis=0)
    kcol = jnp.stack((key_seg, key_pos), axis=1)
    places = {
        "krow": krow,
        "kcol": kcol,
        "qrow": krow[:, :rows],
        "qcol": kcol[:rows],
        "offsets": None if n_high == 2 else (0, rows - HALO),
        "core": core,
    }

    mats = [square(block0, index) for index in range(6)] + [square(block1, index) for index in range(6)]
    *enc_kept, resid_one = attn_forward(enc_rows, enc_window, mats[0:4], gains, places, False, None)
    resid_two, enc_low = ffn_forward(resid_one, enc_rows, gains, pack0, places, 0, 2)
    low_window = jnp.concatenate((enc_low, halo_rows(enc_low)), axis=0)
    *self_kept, resid_three = attn_forward(dec_rows, dec_window, mats[4:8], gains, places, True, None)
    *cross_kept, resid_four = attn_forward(resid_three, low_window, mats[8:12], gains, places, False, 4)
    resid_five, dec_low = ffn_forward(resid_four, dec_rows, gains, pack1, places, 6, 8)

    grad_second, grad_five, ng8, dpack1 = ffn_backward(
        cot_rows, resid_five, resid_four, gains, pack1, places, 6, 8, False
    )
    back, grad_o, delta, dwo_c, halo_c, dqh, ng6 = attn_head(
        grad_second, resid_four, cross_kept, mats[11], gains, places, False, 6, None
    )
    back_c = halo_return(halo_c)
    grad_first, dwq_c, own_c = attn_body(
        back, grad_o, delta, dqh, resid_three, cross_kept, mats[8], gains, places, False, 4, None
    )
    back, grad_o, delta, dwo_s, halo_s, dqh, ng4 = attn_head(
        grad_first, resid_three, self_kept, mats[7], gains, places, True, 4, None
    )
    back_s = halo_return(halo_s)
    grad_dec_q, dwq_s, own_s = attn_body(
        back, grad_o, delta, dqh, dec_rows, self_kept, mats[4], gains, places, True, None, None
    )
    grad_encoded, dwk_c, dwv_c = kv_backward(
        enc_low, own_c, back_c, mats[9], mats[10], (), places, F32, group, order=own_s
    )
    dec_grad, dwk_s, *pair = kv_backward(
        dec_rows, own_s, back_s, mats[5], mats[6], (grad_five, grad_dec_q), places, BF, group,
        layout=("v", 0, 1, 2, 3, 4), mats=(dwo_s, dwq_c, dwk_c, dwv_c, dwo_c), order=dwk_c,
    )
    pair_a1 = pair[0] if plain else reduce_cores(*pair)
    grad_hidden, grad_two, ng2, *pair_f = ffn_backward(
        grad_encoded, resid_two, resid_one, gains, pack0, places, 0, 2, True, order=dwk_s
    )
    back, grad_o, delta, dwo_e, halo_e, dqh, ng0 = attn_head(
        grad_hidden, resid_one, enc_kept, mats[3], gains, places, False, 0, pair_a1
    )
    back_e = halo_return(halo_e)
    pair_f0 = pair_f[0] if plain else reduce_cores(*pair_f)
    grad_enc_q, dwq_e, own_e = attn_body(
        back, grad_o, delta, dqh, enc_rows, enc_kept, mats[0], gains, places, False, None, pair_f0
    )
    norm_local = jnp.concatenate((ng0, ng2, ng4, ng6, ng8), axis=0).reshape(n_high, group, norm_count)
    norm_block = jnp.pad(
        norm_local.swapaxes(0, 1).astype(BF), ((0, 0), (0, 16 - n_high), (0, width - norm_count))
    )
    enc_grad, _, *pair_e = kv_backward(
        enc_rows, own_e, back_e, mats[1], mats[2], (grad_two, grad_enc_q), places, BF, group,
        layout=(0, "k", "v", 1, 2, 3), mats=(dwq_e, dwo_e, dwq_s, dwk_s), norm=norm_block,
    )
    if plain:
        attn_own, up_own, down_own, norm_own = reduce_plain(
            from_parity(*pair_e)[:, : 6 * width // group], from_parity(*pair), from_parity(*pair_f), dpack1, norm_local
        )
    else:
        part_f1 = lax.psum_scatter(
            dpack1.reshape(-1, width), GROUP, scatter_dimension=0, tiled=True
        ).astype(F32)
        part_a1 = reduce_chips(pair_a1)
        part_f0 = reduce_chips(pair_f0)
        part_a0 = reduce_chips(reduce_cores(*pair_e))
        ffn_own = join_halves(part_f0, part_f1)
        both = join_halves(part_a0, jnp.concatenate((part_a1, part_a0[attn_rows:]), axis=0))
        attn_own, up_own, down_own = both[:attn_rows], unpack_up(ffn_own[128:]), ffn_own[:128]
        norm_own = lax.dynamic_index_in_dim(both[attn_rows:], high, 0, keepdims=False)[:norm_count]

    def restore(*arrays):
        outs = jnp.stack(arrays, axis=0).reshape(len(arrays), micro, length_dev, width).swapaxes(0, 1)
        return lax.all_to_all(outs, "lo", split_axis=0, concat_axis=0, tiled=True)

    lows = restore(enc_low, dec_low)
    grads = restore(enc_grad, dec_grad)

    owned = (attn_own, up_own, down_own, norm_own)
    firsts = (attn_first, ffn_in_first, ffn_out_first, norm_first)
    seconds = (attn_second, ffn_in_second, ffn_out_second, norm_second)
    moments = [
        lamb_moments(masters[index], owned[index], firsts[index], seconds[index])
        for index in range(4)
    ]
    update_local = jnp.concatenate(
        [group_sum(onehots[index], row_squares(moments[index][2])) for index in range(4)]
    )
    squares = jnp.stack((weight_local, update_local))
    squares = jnp.pad(squares, ((0, 6), (0, 128 - squares.shape[1])))
    count = lax.axis_size(EVERY)
    squares = jnp.broadcast_to(squares[None], (count,) + squares.shape)
    squares = jnp.sum(lax.all_to_all(squares, EVERY, split_axis=0, concat_axis=0, tiled=True), axis=0)
    norms = jnp.sqrt(squares[:2, :26])
    ratio = norms[0] / norms[1]
    bounds_at = (0, 12, 14, 16, 26)
    new_weights = []
    for index in range(4):
        row_ratio = jnp.sum(
            jnp.where(onehots[index], ratio[None, bounds_at[index] : bounds_at[index + 1]], 0.0), axis=1
        )
        if masters[index].ndim == 2:
            row_ratio = row_ratio[:, None]
        new_weights.append(masters[index] - learn_rate * row_ratio * moments[index][2])
    return (
        lows[:, 0][:, None],
        lows[:, 1][:, None],
        grads[:, 0][:, None].astype(F32),
        grads[:, 1][:, None].astype(F32),
        *owned,
        *new_weights,
        *[item[0] for item in moments],
        *[item[1] for item in moments],
        *[item.astype(BF) for item in new_weights],
        norms,
        ratio,
    )


def solution(mesh):
    count_seq, count_stream = mesh.shape["seq"], mesh.shape["stream"]

    def run(*args):
        micro = args[0].shape[0]
        split = Mesh(
            mesh.devices.reshape(count_seq // micro, micro, count_stream // 2, 2), ("hi", "lo", "y", "c")
        )
        tokens = P(None, ("y", "c"), ("hi", "lo"), None)
        wide = P(EVERY, None)
        flat = P(EVERY)
        owned = (wide, wide, wide, flat)
        return jax.shard_map(
            shards,
            mesh=split,
            in_specs=(tokens, tokens, tokens, P(None, ("y", "c"), None), *owned, *owned, *owned),
            out_specs=(tokens, tokens, tokens, tokens, *owned, *owned, *owned, *owned, *owned, P(), P()),
            check_vma=False,
        )(*args)

    return run
```

```python
import functools
import math

import jax
import jax.numpy as jnp
from jax import lax
from jax.experimental import pallas as pl
from jax.experimental.pallas import tpu as pltpu
from jax.sharding import Mesh
from jax.sharding import PartitionSpec as P

HEADS = 8
STEP = 5
HALO = 256
TILE = 256

norm_eps = 1e-05
beta_one = 0.5
beta_two = 0.5
lamb_eps = 1e-06
weight_decay = 0.01
learn_rate = 0.5
masked_score = -1e30

BF = jnp.bfloat16
F32 = jnp.float32
MIB = 1024 * 1024


def dot_nn(a, b):
    return lax.dot_general(a, b, (((1,), (0,)), ((), ())), preferred_element_type=F32)


def dot_nt(a, b):
    return lax.dot_general(a, b, (((1,), (1,)), ((), ())), preferred_element_type=F32)


def dot_tn(a, b):
    return lax.dot_general(a, b, (((0,), (0,)), ((), ())), preferred_element_type=F32)


def norm_parts(rows):
    centre = rows - jnp.mean(rows, axis=-1, keepdims=True)
    inv = lax.rsqrt(jnp.mean(centre * centre, axis=-1, keepdims=True) + norm_eps)
    return centre * inv, inv


def norm_rows(rows, gain, bias):
    return norm_parts(rows)[0] * gain + bias


def norm_back(rows, gain, grad):
    unit, inv = norm_parts(rows)
    lead = grad * gain
    back = inv * (
        lead
        - jnp.mean(lead, axis=-1, keepdims=True)
        - unit * jnp.mean(lead * unit, axis=-1, keepdims=True)
    )
    return (
        back,
        jnp.sum(grad * unit, axis=0, keepdims=True),
        jnp.sum(grad, axis=0, keepdims=True),
    )


gelu_a = 0.7978845608028654
gelu_b = 0.044715


def gelu(v):
    return 0.5 * v * (1.0 + jnp.tanh(gelu_a * (v + gelu_b * (v * v * v))))


def gelu_both(v):
    sq = v * v
    t = jnp.tanh(gelu_a * (v + gelu_b * (sq * v)))
    half = 0.5 * (1.0 + t)
    slope = half + 0.5 * v * (1.0 - t * t) * (gelu_a * (1.0 + 3.0 * gelu_b * sq))
    return v * half, slope


def lane_low(shape):
    return lax.broadcasted_iota(jnp.int32, shape, 1) < 64


def shape_of(dtype, *dims):
    return jax.ShapeDtypeStruct(dims, dtype)


class Fetched:
    def __init__(self, ref, copies):
        self.ref, self.copies, self.shape = ref, copies, ref.shape

    def __getitem__(self, index):
        for copy in self.copies:
            copy.wait()
        self.copies = ()
        return self.ref[index]


def square(array, start, index):
    places, _, width = array.shape
    per = 6 * width // places
    pieces = []
    row, end = index * width, index * width + width
    while row < end:
        place, at = divmod(row, per)
        take = min(per - at, end - row)
        spot = slice(row - index * width, row - index * width + take)
        pieces.append(((place, slice(start + at, start + at + take)), spot))
        row += take
    return (array, (width, width), tuple(pieces))


def rows_of(array, start, count):
    places, _, width = array.shape
    every = slice(0, places)
    return (array, (places, count, width), (((every, slice(start, start + count)), every),))


def fused(name, program, core, small, ins, outs, flops, scratch=(), order=None):
    big, sources = [], []
    for item in ins.values():
        array = item[0] if isinstance(item, tuple) else item
        known = [index for index, other in enumerate(big) if other is array]
        sources.append(known[0] if known else len(big))
        if not known:
            big.append(array)
    shapes = [item[1] if isinstance(item, tuple) else item.shape for item in ins.values()]
    pieces = [item[2] if isinstance(item, tuple) else None for item in ins.values()]
    types = [big[source].dtype for source in sources]
    counts = [len(item) if item else 1 for item in pieces]
    n_small, n_big, n_out, extra = len(small), len(big), len(outs), 0 if order is None else 1

    def body(core_ref, *refs):
        small_refs, refs = refs[:n_small], refs[n_small:]
        big_refs, refs = refs[:n_big], refs[n_big + extra :]
        out_refs, refs = refs[:n_out], refs[n_out:]
        in_bufs, refs = refs[: len(ins)], refs[len(ins) :]
        out_bufs, refs = refs[:n_out], refs[n_out:]
        user, (in_sem, out_sem) = refs[:-2], refs[-2:]
        env = dict(zip(small, small_refs))
        used = 0
        for key, source, piece, buf in zip(ins, sources, pieces, in_bufs):
            src = big_refs[source]
            copies = []
            for item in piece or (None,):
                if item is None:
                    copy = pltpu.make_async_copy(src, buf, in_sem.at[used])
                else:
                    copy = pltpu.make_async_copy(src.at[item[0]], buf.at[item[1]], in_sem.at[used])
                copy.start()
                copies.append(copy)
                used += 1
            env[key] = Fetched(buf, copies)
        env.update(zip(outs, out_bufs))
        leaving = {}

        def store(*keys):
            for key in keys:
                index = list(outs).index(key)
                leaving[key] = pltpu.make_async_copy(out_bufs[index], out_refs[index], out_sem.at[index])
                leaving[key].start()

        program(env, core_ref, store, *user)
        store(*[key for key in outs if key not in leaving])
        for copy in leaving.values():
            copy.wait()
        for key in ins:
            for copy in env[key].copies:
                copy.wait()

    vmem = pl.BlockSpec(memory_space=pltpu.VMEM)
    anywhere = pl.BlockSpec(memory_space=pl.ANY)
    size = sum(array.size * array.dtype.itemsize for array in big)
    results = pl.pallas_call(
        body,
        in_specs=[pl.BlockSpec(memory_space=pltpu.SMEM)] + [vmem] * n_small + [anywhere] * (n_big + extra),
        out_specs=tuple([anywhere] * n_out),
        out_shape=tuple(outs.values()),
        scratch_shapes=[pltpu.VMEM(shape, dtype) for shape, dtype in zip(shapes, types)]
        + [pltpu.VMEM(out.shape, out.dtype) for out in outs.values()]
        + list(scratch)
        + [pltpu.SemaphoreType.DMA((sum(counts),)), pltpu.SemaphoreType.DMA((n_out,))],
        compiler_params=pltpu.CompilerParams(vmem_limit_bytes=56 * MIB),
        cost_estimate=pl.CostEstimate(flops=flops, bytes_accessed=size, transcendentals=0),
        name=name,
    )(core, *small.values(), *big, *(() if order is None else (order,)))
    return dict(zip(outs, results))


def tiles_of(core, rows, window):
    if window == rows + HALO:
        near = pl.multiple_of(core[1], HALO)
        return ((near, 0), (pl.multiple_of(rows - TILE - core[1], HALO), None))
    return ((0, 0), (rows - TILE, 1))


def key_rows(ref, lanes, rows, halo):
    if halo is None:
        return ref[0:rows, lanes]
    if halo == 0:
        return ref[0 : rows + HALO, lanes]
    return jnp.concatenate((ref[0:rows, lanes], ref[rows + HALO : rows + 2 * HALO, lanes]), axis=0)


def key_lanes(ref, row, rows, halo):
    if halo is None:
        return ref[row : row + 1, 0:rows]
    if halo == 0:
        return ref[row : row + 1, 0 : rows + HALO]
    return jnp.concatenate(
        (ref[row : row + 1, 0:rows], ref[row : row + 1, rows + HALO : rows + 2 * HALO]), axis=1
    )


def halves(shape):
    low = lane_low(shape)
    return low, ~low


def keep(mask, values):
    return jnp.where(mask, values, jnp.zeros_like(values))


def gain_rows(gains, index):
    return gains[index : index + 1, :], gains[index + 1 : index + 2, :]


def attn_fwd(core, causal, low_src, base, kv_src, weights, qcol, krow, q_out, k_out, v_out, o_out, lse_out, res_out):
    rows, _ = q_out.shape
    window = k_out.shape[0]
    w_q, w_k, w_v, w_o = weights
    queries = dot_nn(low_src(), w_q[...])
    q_out[...] = (queries.astype(BF).astype(F32) * 0.125).astype(BF)
    k_out[...] = dot_nn(kv_src[...], w_k[...]).astype(BF)
    v_out[...] = dot_nn(kv_src[...], w_v[...]).astype(BF)
    for offset, halo in tiles_of(core, rows, window):
        spot = pl.ds(offset, TILE)
        allowed = qcol[spot, 0:1] == key_lanes(krow, 0, rows, halo)
        if causal:
            allowed = allowed & (key_lanes(krow, 1, rows, halo) <= qcol[spot, 1:2])
        lane = lax.broadcasted_iota(jnp.int32, (TILE, 128), 1)
        packed = jnp.zeros((TILE, 128), F32)
        for pair in range(HEADS // 2):
            lanes = slice(pair * 128, pair * 128 + 128)
            q2 = q_out[spot, lanes]
            k2 = key_rows(k_out, lanes, rows, halo)
            v2 = key_rows(v_out, lanes, rows, halo)
            mixed = None
            for half in range(2):
                scores = dot_nt(keep(halves(q2.shape)[half], q2), k2)
                scores = jnp.where(allowed, scores, masked_score)
                top = jnp.max(scores, axis=-1, keepdims=True)
                weights = jnp.exp(scores - top)
                total = jnp.sum(weights, axis=-1, keepdims=True)
                probs = (weights * (1.0 / total)).astype(BF)
                part = dot_nn(probs, keep(halves(v2.shape)[half], v2))
                mixed = part if mixed is None else mixed + part
                packed = jnp.where(lane == 2 * pair + half, top + jnp.log(total), packed)
            o_out[spot, lanes] = mixed.astype(BF)
        lse_out[:, spot] = jnp.transpose(packed)[0:HEADS, :]
    res_out[...] = base() + dot_nn(o_out[...], w_o[...])


def score_grads(q2, do2, k2, v2, allowed, lse, delta):
    sums = None
    for half in range(2):
        qh = keep(halves(q2.shape)[half], q2)
        doh = keep(halves(do2.shape)[half], do2)
        scores = jnp.where(allowed, dot_nt(k2, qh), masked_score)
        probs = jnp.exp(scores - lse[half])
        gscores = (probs * (dot_nt(v2, doh) - delta[half])).astype(BF)
        parts = (
            dot_tn(gscores, keep(halves(k2.shape)[half], k2)),
            dot_nn(gscores, qh),
            dot_nn(probs.astype(BF), doh),
        )
        sums = parts if sums is None else tuple(a + b for a, b in zip(sums, parts))
    return sums


def attn_head(
    core, causal, grad, resid, o_in, q_in, k_in, v_in, lse_in, w_o, gains, gain_at, qrow, kcol,
    back_out, do_out, delta_out, dwo_out, halo_out, dqh_out, ng_out,
):
    rows, width = do_out.shape
    window = k_in.shape[0]
    back, dgain, dbias = norm_back(resid[...], gain_rows(gains, gain_at)[0], grad)
    back_out[...] = back
    ng_out[0:1, :] = dgain
    ng_out[1:2, :] = dbias
    branch = back.astype(BF)
    do_out[...] = dot_nt(branch, w_o[...]).astype(BF)
    mixed = do_out[...].astype(F32) * o_in[...].astype(F32)
    high = mixed.astype(BF)
    rest = (mixed - high.astype(F32)).astype(BF)
    head = lax.broadcasted_iota(jnp.int32, (16, width), 1) // (width // HEADS)
    which = (head == lax.broadcasted_iota(jnp.int32, (16, width), 0)).astype(F32).astype(BF)
    delta_out[...] = (dot_nt(which, high) + dot_nt(which, rest))[0:HEADS, :]
    for offset, halo in tiles_of(core, rows, window):
        if halo is None:
            continue
        spot = pl.ds(offset, TILE)
        keys = slice(rows + halo * HALO, rows + halo * HALO + HALO)
        here = slice(halo * HALO, halo * HALO + HALO)
        allowed = kcol[keys, 0:1] == qrow[0:1, spot]
        if causal:
            allowed = allowed & (kcol[keys, 1:2] <= qrow[1:2, spot])
        for pair in range(HEADS // 2):
            lanes = slice(pair * 128, pair * 128 + 128)
            heads = (2 * pair, 2 * pair + 1)
            dq2, dk2, dv2 = score_grads(
                q_in[spot, lanes],
                do_out[spot, lanes],
                k_in[keys, lanes],
                v_in[keys, lanes],
                allowed,
                [lse_in[h : h + 1, spot] for h in heads],
                [delta_out[h : h + 1, spot] for h in heads],
            )
            dqh_out[here, lanes] = dq2
            halo_out[0, here, lanes] = dk2.astype(BF)
            halo_out[1, here, lanes] = dv2.astype(BF)
    dwo_out[...] = dot_tn(o_in[...], branch).astype(BF)


def attn_body(
    core, causal, window, back, do_in, delta, dqh, low_src, q_in, k_in, v_in, lse_in, w_q, qrow, kcol,
    gq_out, dwq_out, own_out, dq_scr,
):
    rows, width = gq_out.shape
    for tile in range(rows // TILE):
        spot = slice(tile * TILE, tile * TILE + TILE)
        allowed = kcol[0:rows, 0:1] == qrow[0:1, spot]
        if causal:
            allowed = allowed & (kcol[0:rows, 1:2] <= qrow[1:2, spot])
        for pair in range(HEADS // 2):
            lanes = slice(pair * 128, pair * 128 + 128)
            heads = (2 * pair, 2 * pair + 1)
            dq2, dk2, dv2 = score_grads(
                q_in[spot, lanes],
                do_in[spot, lanes],
                k_in[0:rows, lanes],
                v_in[0:rows, lanes],
                allowed,
                [lse_in[h : h + 1, spot] for h in heads],
                [delta[h : h + 1, spot] for h in heads],
            )
            dq_scr[spot, lanes] = dq2
            if tile == 0:
                own_out[0, :, lanes] = dk2
                own_out[1, :, lanes] = dv2
            else:
                own_out[0, :, lanes] += dk2
                own_out[1, :, lanes] += dv2
    for offset, halo in tiles_of(core, rows, window):
        if halo is not None:
            dq_scr[pl.ds(offset, TILE), :] += dqh[halo * HALO : halo * HALO + HALO, :]
    grad_q = (dq_scr[...] * 0.125).astype(BF)
    gq_out[...] = back[...] + dot_nt(grad_q, w_q[...])
    dwq_out[...] = dot_tn(low_src(), grad_q).astype(BF)


def split_places(core, source, kept, sent):
    for parity in range(2):

        @pl.when(core[0] == parity)
        def place():
            for chip in range(kept.shape[0]):
                kept[chip] = source[2 * chip + parity]
                sent[chip] = source[2 * chip + 1 - parity]


def kv_bwd(core, offsets, src, own, halo, w_k, w_v, adds, scr):
    scr[...] = own[...]
    for index in range(halo.shape[1] // HALO):
        spot = pl.ds(pl.multiple_of(core[1], HALO) if offsets is None else offsets[index], HALO)
        scr[:, spot, :] += halo[:, index * HALO : index * HALO + HALO, :].astype(F32)
    dk = scr[0].astype(BF)
    dv = scr[1].astype(BF)
    total = dot_nt(dk, w_k[...]) + dot_nt(dv, w_v[...])
    for ref in adds:
        total = total + ref[...]
    return total, dot_tn(src[...], dk).astype(BF), dot_tn(src[...], dv).astype(BF)


def lay_out(stack, mats):
    places, _, width = stack.shape
    per = 6 * width // places
    for slot, matrix in enumerate(mats):
        row, end = slot * width, slot * width + width
        while row < end:
            place, start = divmod(row, per)
            take = min(per - start, end - row)
            at = row - slot * width
            stack[place, start : start + take, :] = matrix[at : at + take, :]
            row += take


def up_tile(pack, tile):
    places, _, width = pack.shape
    return pack[:, 128 + 32 * tile : 160 + 32 * tile, :].reshape(places * 32, width)


def down_tile(pack, tile):
    return pack[4 * tile : 4 * tile + 4, 0:128, :].reshape(512, pack.shape[2])


def ffn_fwd(resid, base, gains, gain_in, gain_out, pack, res_out, low_out, hid_low=None, pre=None):
    hidden = norm_rows(resid[...], *gain_rows(gains, gain_in))
    low = hidden.astype(BF)
    if hid_low is not None:
        hid_low[...] = low
    res_out[...] = hidden + base[...].astype(F32)
    for tile in range(4):
        values = dot_nn(low, up_tile(pack, tile))
        if pre is not None:
            pre[tile] = values
        res_out[...] += dot_nn(gelu(values).astype(BF), down_tile(pack, tile))
    low_out[...] = norm_rows(res_out[...], *gain_rows(gains, gain_out)).astype(BF)


def ffn_bwd(grad, res_late, gains, gain_out, pack, gh_out, late_out, ng_out, hid_low, late_low, dpack, pre=None):
    back, dgain, dbias = norm_back(res_late[...], gain_rows(gains, gain_out)[0], grad)
    late_out[...] = back
    gh_out[...] = back
    late_low[...] = back.astype(BF)
    ng_out[0:1, :] = dgain
    ng_out[1:2, :] = dbias
    places, _, width = dpack.shape
    for tile in range(4):
        activ, slope = gelu_both(dot_nn(hid_low[...], up_tile(pack, tile)) if pre is None else pre[tile])
        grad_down = dot_tn(activ.astype(BF), late_low[...]).astype(BF)
        dpack[4 * tile : 4 * tile + 4, 0:128, :] = grad_down.reshape(4, 128, width)
        grad_act = dot_nt(late_low[...], down_tile(pack, tile)).astype(BF).astype(F32)
        grad_pre = (grad_act * slope).astype(BF)
        grad_up = dot_tn(hid_low[...], grad_pre).astype(BF)
        dpack[:, 128 + 32 * tile : 160 + 32 * tile, :] = grad_up.reshape(places, 32, width)
        gh_out[...] += dot_nt(grad_pre, up_tile(pack, tile))


def kept_shapes(rows, window, width, with_o=True):
    outs = {
        "q": shape_of(BF, rows, width),
        "k": shape_of(BF, window, width),
        "v": shape_of(BF, window, width),
        "lse": shape_of(F32, HEADS, rows),
    }
    if with_o:
        outs["o"] = shape_of(BF, rows, width)
    return outs


def head_shapes(rows, window, width):
    return {
        "back": shape_of(F32, rows, width),
        "do": shape_of(BF, rows, width),
        "delta": shape_of(F32, HEADS, rows),
        "dwo": shape_of(BF, width, width),
        "halo": shape_of(BF, 2, window - rows, width),
        "dqh": shape_of(F32, window - rows, width),
        "ng": shape_of(F32, 2, width),
    }


def weights_of(env):
    return [env["w" + name] for name in "qkvo"]


def named_mats(mats):
    return {"w" + name: mat for name, mat in zip("qkvo", mats)}


def enc_forward(x, window_rows, mats, pack, gains, places):
    rows, width = x.shape
    window = window_rows.shape[0]

    def program(e, core, store):
        attn_fwd(
            core, False, lambda: e["x"][...], lambda: e["x"][...].astype(F32), e["window"], weights_of(e),
            e["qcol"], e["krow"], e["q"], e["k"], e["v"], e["o"], e["lse"], e["one"],
        )
        store("q", "k", "v", "o", "lse", "one")
        ffn_fwd(e["one"], e["x"], e["gains"], 0, 2, e["pack"], e["two"], e["low"])

    return fused(
        "enc_forward",
        program,
        places["core"],
        {"qcol": places["qcol"], "krow": places["krow"], "gains": gains},
        {"x": x, "window": window_rows, **named_mats(mats), "pack": pack},
        {
            **kept_shapes(rows, window, width),
            "one": shape_of(F32, rows, width),
            "two": shape_of(F32, rows, width),
            "low": shape_of(BF, rows, width),
        },
        28 * rows * width * width + 8 * rows * window * width,
    )


def self_forward(z, window_rows, mats, places):
    rows, width = z.shape
    window = window_rows.shape[0]

    def program(e, core, store):
        attn_fwd(
            core, True, lambda: e["z"][...], lambda: e["z"][...].astype(F32), e["window"], weights_of(e),
            e["qcol"], e["krow"], e["q"], e["k"], e["v"], e["o"], e["lse"], e["three"],
        )

    return fused(
        "self_forward",
        program,
        places["core"],
        {"qcol": places["qcol"], "krow": places["krow"]},
        {"z": z, "window": window_rows, **named_mats(mats)},
        {**kept_shapes(rows, window, width), "three": shape_of(F32, rows, width)},
        12 * rows * width * width + 8 * rows * window * width,
    )


def cross_and_ffn(three, window_rows, mats, pack, z, cot, gains, places):
    rows, width = three.shape
    window = window_rows.shape[0]
    count, block = pack[0].shape[0], pack[1][1]
    f32_rows, low_rows = pltpu.VMEM((rows, width), F32), pltpu.VMEM((rows, width), BF)

    def program(e, core, store, o, four, five, gh, hid_low, late_low, pre, dpack):
        def first():
            return norm_rows(e["three"][...], *gain_rows(e["gains"], 4))

        attn_fwd(
            core, False, lambda: first().astype(BF), first, e["window"], weights_of(e),
            e["qcol"], e["krow"], e["q"], e["k"], e["v"], o, e["lse"], four,
        )
        store("q", "k", "v", "lse")
        ffn_fwd(four, e["z"], e["gains"], 6, 8, e["pack"], five, e["low"], hid_low, pre)
        store("low")
        ffn_bwd(
            e["cot"][...].astype(F32), five, e["gains"], 8, e["pack"], gh, e["five"], e["ng8"],
            hid_low, late_low, dpack, pre,
        )
        split_places(core, dpack, e["kept"], e["sent"])
        store("sent", "kept", "five", "ng8")
        attn_head(
            core, False, gh[...], four, o, e["q"], e["k"], e["v"], e["lse"], e["wo"], e["gains"], 6,
            e["qrow"], e["kcol"], e["back"], e["do"], e["delta"], e["dwo"], e["halo"], e["dqh"], e["ng"],
        )

    return fused(
        "cross_and_ffn",
        program,
        places["core"],
        {**{name: places[name] for name in ("qcol", "krow", "qrow", "kcol")}, "gains": gains},
        {"three": three, "wq": mats[0], "window": window_rows, **named_mats(mats), "z": z, "pack": pack, "cot": cot},
        {
            **kept_shapes(rows, window, width, False),
            "low": shape_of(BF, rows, width),
            "kept": shape_of(BF, count // 2, block, width),
            "sent": shape_of(BF, count // 2, block, width),
            "five": shape_of(F32, rows, width),
            "ng8": shape_of(F32, 2, width),
            **head_shapes(rows, window, width),
        },
        68 * rows * width * width + 8 * rows * window * width,
        scratch=[
            low_rows, f32_rows, f32_rows, f32_rows, low_rows, low_rows,
            pltpu.VMEM((4, rows, width), F32), pltpu.VMEM((count, block, width), BF),
        ],
    )


def cross_body_self_head(c, three, s, mat_q, mat_o, gains, places):
    rows, width = three.shape
    window = c["k"].shape[0]
    own = (slice(0, rows),)

    def program(e, core, store, grad, dq):
        def first():
            return norm_rows(e["three"][...], *gain_rows(e["gains"], 4)).astype(BF)

        attn_body(
            core, False, window, e["back_c"], e["do_c"], e["delta_c"], e["dqh_c"], first, e["q_c"], e["k_c"],
            e["v_c"], e["lse_c"], e["wq"], e["qrow"], e["kcol"], grad, e["dwq"], e["own"], dq,
        )
        store("own", "dwq")
        attn_head(
            core, True, grad[...], e["three"], e["o"], e["q"], e["k"], e["v"], e["lse"], e["wo"], e["gains"], 4,
            e["qrow"], e["kcol"], e["back"], e["do"], e["delta"], e["dwo"], e["halo"], e["dqh"], e["ng"],
        )

    return fused(
        "cross_body_self_head",
        program,
        places["core"],
        {"qrow": places["qrow"], "kcol": places["kcol"], "gains": gains},
        {
            "q_c": c["q"],
            "do_c": c["do"],
            "k_c": (c["k"], (rows, width), ((own, own),)),
            "v_c": (c["v"], (rows, width), ((own, own),)),
            "lse_c": c["lse"],
            "delta_c": c["delta"],
            "dqh_c": c["dqh"],
            "back_c": c["back"],
            "wq": mat_q,
            "three": three,
            "wo": mat_o,
            "o": s["o"],
            "q": s["q"],
            "k": s["k"],
            "v": s["v"],
            "lse": s["lse"],
        },
        {
            "own": shape_of(F32, 2, rows, width),
            "dwq": shape_of(BF, width, width),
            **head_shapes(rows, window, width),
        },
        8 * rows * width * width + 10 * rows * window * width,
        scratch=[pltpu.VMEM((rows, width), F32), pltpu.VMEM((rows, width), F32)],
    )


def own_body(name, kept, head, src, mat_q, causal, places, order):
    rows, width = src.shape
    window = kept["k"].shape[0]
    own = (slice(0, rows),)

    def program(e, core, store, dq):
        attn_body(
            core, causal, window, e["back"], e["do"], e["delta"], e["dqh"], lambda: e["src"][...], e["q"], e["k"],
            e["v"], e["lse"], e["wq"], e["qrow"], e["kcol"], e["gq"], e["dwq"], e["own"], dq,
        )

    return fused(
        name,
        program,
        places["core"],
        {"qrow": places["qrow"], "kcol": places["kcol"]},
        {
            "q": kept["q"],
            "do": head["do"],
            "k": (kept["k"], (rows, width), ((own, own),)),
            "v": (kept["v"], (rows, width), ((own, own),)),
            "lse": kept["lse"],
            "delta": head["delta"],
            "dqh": head["dqh"],
            "back": head["back"],
            "wq": mat_q,
            "src": src,
        },
        {
            "own": shape_of(F32, 2, rows, width),
            "gq": shape_of(F32, rows, width),
            "dwq": shape_of(BF, width, width),
        },
        4 * rows * width * width + 10 * rows * rows * width,
        scratch=[pltpu.VMEM((rows, width), F32)],
        order=order,
    )


def both_kv(low, own_c, halo_c, mats_c, z, own_s, halo_s, mats_s, adds, grads, group, places):
    rows, width = low.shape
    per = 6 * width // group

    def program(e, core, store, scr, stack):
        total, dwk, dwv = kv_bwd(core, places["offsets"], e["low"], e["own_c"], e["halo_c"], e["wk_c"], e["wv_c"], (), scr)
        e["encoded"][...] = total
        store("encoded")
        total, e["dwk"][...], dwv_s = kv_bwd(
            core, places["offsets"], e["z"], e["own_s"], e["halo_s"], e["wk_s"], e["wv_s"], (e["add0"], e["add1"]), scr
        )
        e["grad"][...] = total.astype(BF)
        store("grad", "dwk")
        lay_out(stack, (dwv_s, e["dwo_s"], e["dwq_c"], dwk, dwv, e["dwo_c"]))
        split_places(core, stack, e["kept"], e["sent"])

    return fused(
        "both_kv",
        program,
        places["core"],
        {},
        {
            "own_c": own_c,
            "halo_c": halo_c,
            "wk_c": mats_c[0],
            "wv_c": mats_c[1],
            "low": low,
            "own_s": own_s,
            "halo_s": halo_s,
            "wk_s": mats_s[0],
            "wv_s": mats_s[1],
            "add0": adds[0],
            "add1": adds[1],
            "z": z,
            "dwo_s": grads[0],
            "dwq_c": grads[1],
            "dwo_c": grads[2],
        },
        {
            "encoded": shape_of(F32, rows, width),
            "grad": shape_of(BF, rows, width),
            "dwk": shape_of(BF, width, width),
            "sent": shape_of(BF, group // 2, per, width),
            "kept": shape_of(BF, group // 2, per, width),
        },
        16 * rows * width * width,
        scratch=[pltpu.VMEM((2, rows, width), F32), pltpu.VMEM((group, per, width), BF)],
    )


def enc_ffn_head(grad, one, two, kept, pack, mat_o, gains, places):
    rows, width = one.shape
    window = kept["k"].shape[0]
    count, block = pack[0].shape[0], pack[1][1]

    def program(e, core, store, gh, hid_low, late_low, dpack):
        hid_low[...] = norm_rows(e["one"][...], *gain_rows(e["gains"], 0)).astype(BF)
        ffn_bwd(
            e["grad"][...], e["two"], e["gains"], 2, e["pack"], gh, e["late"], e["ng2"], hid_low, late_low, dpack
        )
        split_places(core, dpack, e["kept"], e["sent"])
        store("sent", "kept", "late", "ng2")
        attn_head(
            core, False, gh[...], e["one"], e["o"], e["q"], e["k"], e["v"], e["lse"], e["wo"], e["gains"], 0,
            e["qrow"], e["kcol"], e["back"], e["do"], e["delta"], e["dwo"], e["halo"], e["dqh"], e["ng"],
        )

    return fused(
        "enc_ffn_head",
        program,
        places["core"],
        {"qrow": places["qrow"], "kcol": places["kcol"], "gains": gains},
        {
            "one": one,
            "two": two,
            "grad": grad,
            "pack": pack,
            "wo": mat_o,
            "o": kept["o"],
            "q": kept["q"],
            "k": kept["k"],
            "v": kept["v"],
            "lse": kept["lse"],
        },
        {
            "sent": shape_of(BF, count // 2, block, width),
            "kept": shape_of(BF, count // 2, block, width),
            "late": shape_of(F32, rows, width),
            "ng2": shape_of(F32, 2, width),
            **head_shapes(rows, window, width),
        },
        44 * rows * width * width + 10 * TILE * TILE * width,
        scratch=[
            pltpu.VMEM((rows, width), F32), pltpu.VMEM((rows, width), BF), pltpu.VMEM((rows, width), BF),
            pltpu.VMEM((count, block, width), BF),
        ],
    )


def enc_kv(x, own, halo, mats, adds, grads, norm, group, places, order):
    rows, width = x.shape
    per = 6 * width // group
    block = per + norm.shape[1]

    def program(e, core, store, scr, stack):
        total, dwk, dwv = kv_bwd(
            core, places["offsets"], e["x"], e["own"], e["halo"], e["wk"], e["wv"], (e["add0"], e["add1"]), scr
        )
        lay_out(stack, (e["dwq_e"], dwk, dwv, e["dwo_e"], e["dwq_s"], e["dwk_s"]))
        stack[:, per:, :] = e["norm"][...]
        split_places(core, stack, e["kept"], e["sent"])
        store("sent", "kept")
        e["grad"][...] = total.astype(BF)

    return fused(
        "enc_kv",
        program,
        places["core"],
        {},
        {
            "own": own,
            "halo": halo,
            "wk": mats[0],
            "wv": mats[1],
            "x": x,
            "dwq_e": grads[0],
            "dwo_e": grads[1],
            "dwq_s": grads[2],
            "dwk_s": grads[3],
            "norm": norm,
            "add0": adds[0],
            "add1": adds[1],
        },
        {
            "sent": shape_of(BF, group // 2, block, width),
            "kept": shape_of(BF, group // 2, block, width),
            "grad": shape_of(BF, rows, width),
        },
        8 * rows * width * width,
        scratch=[pltpu.VMEM((2, rows, width), F32), pltpu.VMEM((group, block, width), BF)],
        order=order,
    )


def segments_at(bounds, places, total_len):
    found = jnp.sum((bounds[None, :] <= places[:, None]).astype(jnp.int32), axis=-1)
    return jnp.where((places >= 0) & (places < total_len), found, -1)


def row_squares(values):
    if values.ndim == 2:
        return jnp.sum(values * values, axis=1)
    return values * values


def owner_groups(rows_local, owner, per_group, count):
    group_ids = (owner * rows_local + jnp.arange(rows_local, dtype=jnp.int32)) // per_group
    return group_ids[:, None] == jnp.arange(count, dtype=jnp.int32)[None, :]


def group_sum(onehot, row_values):
    return jnp.sum(jnp.where(onehot, row_values[:, None], 0.0), axis=0)


def lamb_moments(master, grad_rows, first, second):
    first_new = beta_one * first + (1.0 - beta_one) * grad_rows
    second_new = beta_two * second + (1.0 - beta_two) * grad_rows * grad_rows
    update = (
        first_new
        / (1.0 - beta_one**STEP)
        / (jnp.sqrt(second_new / (1.0 - beta_two**STEP)) + lamb_eps)
        + weight_decay * master
    )
    return (first_new, second_new, update)


GROUP = ("lo", "y", "c")
CHIPS = ("lo", "y")
EVERY = ("hi", "lo", "y", "c")


def swap_hi(array):
    return lax.ppermute(array, "hi", [(0, 1), (1, 0)])


def shift_hi(array, distance):
    count = lax.axis_size("hi")
    route = [(i - distance, i) for i in range(count) if i - distance in range(count)]
    return lax.ppermute(array, "hi", route)


def halo_rows(rows_array):
    high = lax.axis_index("hi")
    rows = rows_array.shape[-2]
    axis = rows_array.ndim - 2
    if lax.axis_size("hi") == 2:
        sent = jnp.where(
            high == 0,
            lax.slice_in_dim(rows_array, rows - HALO, rows, axis=axis),
            lax.slice_in_dim(rows_array, 0, HALO, axis=axis),
        )
        return swap_hi(sent)
    left = shift_hi(lax.slice_in_dim(rows_array, rows - HALO, rows, axis=axis), 1)
    right = shift_hi(lax.slice_in_dim(rows_array, 0, HALO, axis=axis), -1)
    return jnp.concatenate((left, right), axis=axis)


def halo_return(grads):
    if lax.axis_size("hi") == 2:
        return swap_hi(grads)
    to_left = shift_hi(grads[:, :HALO], -1)
    to_right = shift_hi(grads[:, HALO:], 1)
    return jnp.concatenate((to_left, to_right), axis=1)


def pack_up(rows):
    count, units = rows.shape
    return rows.reshape(count, 4, units // 4).swapaxes(0, 1).reshape(4 * count, units // 4)


def unpack_up(packed):
    count, width = packed.shape
    return packed.reshape(4, count // 4, width).swapaxes(0, 1).reshape(count // 4, 4 * width)


def swap_core(array):
    return lax.ppermute(array, "c", [(0, 1), (1, 0)])


def tie(array, other):
    bit = lax.slice(other, (0,) * other.ndim, (1,) * other.ndim).reshape(()) * 0
    return array + bit.astype(array.dtype)


def from_parity(mine, other):
    even = lax.axis_index("c") == 0
    full = jnp.stack((jnp.where(even, mine, other), jnp.where(even, other, mine)), axis=1)
    return full.reshape(-1, *mine.shape[1:])


def gather_plain(attn_shard, up_shard, down_shard, norm_shard):
    width = attn_shard.shape[1]
    group = lax.axis_size(GROUP)
    norm_count = norm_shard.shape[0]
    attn = lax.all_gather(attn_shard, EVERY, axis=0, tiled=True)
    down = lax.all_gather(down_shard, EVERY, axis=0, tiled=True).reshape(2, group, -1, width)
    up = lax.all_gather(up_shard, EVERY, axis=0, tiled=True)
    up = up.reshape(2, group, -1, 4, width).swapaxes(2, 3).reshape(2, group, -1, width)
    norms = jnp.pad(norm_shard[None, :], ((0, 0), (0, width - norm_count)))
    norms = lax.all_gather(norms, EVERY, axis=0, tiled=True)[:, :norm_count]
    ffn = jnp.concatenate((down, up), axis=2)
    attn = attn.reshape(2, group, -1, width)
    rest = jnp.zeros((group, 16, width), BF)
    full = jnp.concatenate((attn[0], attn[1], ffn[0], rest), axis=1)
    return full, ffn[1], norms.reshape(10, width).astype(F32)


def reduce_cores(kept, sent):
    return (kept.astype(F32) + swap_core(sent).astype(F32)).astype(BF)


def reduce_chips(pair):
    parts = lax.all_to_all(pair, CHIPS, split_axis=0, concat_axis=0, tiled=True)
    return jnp.sum(parts.astype(F32), axis=0)


def join_halves(zero, one):
    first = lax.axis_index("hi") == 0
    mine = jnp.where(first, zero, one)
    sent = jnp.where(first, one, zero).astype(BF)
    return mine + swap_hi(sent).astype(F32)


def reduce_plain(attn0, attn1, ffn0, ffn1, norm_local):
    group, _, width = ffn0.shape

    def scatter(rows):
        return lax.psum_scatter(rows, EVERY, scatter_dimension=0, tiled=True).astype(F32)

    attn = jnp.concatenate((attn0, attn1), axis=0).reshape(-1, width)
    ffn = jnp.stack((ffn0, ffn1)).reshape(2 * group, -1, width)
    up = ffn[:, 128:].reshape(2 * group, 4, 32, width).swapaxes(1, 2).reshape(-1, 4 * width)
    norms = lax.psum_scatter(
        norm_local.reshape(lax.axis_size(EVERY), -1), EVERY, scatter_dimension=0, tiled=True
    )
    return scatter(attn), scatter(up), scatter(ffn[:, :128].reshape(-1, width)), norms[0]


def shards(
    enc_in,
    dec_in,
    cotangent,
    lengths,
    attn_master,
    ffn_in_master,
    ffn_out_master,
    norm_master,
    attn_first,
    ffn_in_first,
    ffn_out_first,
    norm_first,
    attn_second,
    ffn_in_second,
    ffn_out_second,
    norm_second,
):
    micro, _, length_dev, width = enc_in.shape
    rows = micro * length_dev
    hidden_units = ffn_in_master.shape[1]
    high, low = lax.axis_index("hi"), lax.axis_index("lo")
    n_high = lax.axis_size("hi")
    owner = lax.axis_index(EVERY)
    masters = (attn_master, ffn_in_master, ffn_out_master, norm_master)
    group_info = ((width, 12), (width, 2), (hidden_units, 2), (width, 10))
    onehots = [
        owner_groups(master.shape[0], owner, info[0], info[1])
        for master, info in zip(masters, group_info)
    ]
    weight_local = jnp.concatenate(
        [group_sum(onehot, row_squares(master)) for onehot, master in zip(onehots, masters)]
    )

    def regroup(*arrays):
        packed = jnp.stack([array[:, 0] for array in arrays], axis=1)
        packed = lax.all_to_all(packed, "lo", split_axis=0, concat_axis=0, tiled=True)
        return packed.swapaxes(0, 1).reshape(len(arrays), rows, width)

    core = jnp.stack((lax.axis_index("c"), jnp.where(high == 0, rows - HALO, 0))).astype(jnp.int32)
    attn_rows = attn_master.shape[0]
    norm_count = norm_master.shape[0]
    plain = n_high != 2
    attn_low, up_low, down_low, norm_low = [master.astype(BF) for master in masters]
    if plain:
        full, late, gains = gather_plain(attn_low, up_low, down_low, norm_low)
        enc_rows, dec_rows, cot_rows = regroup(enc_in, dec_in, cotangent)
    else:
        first = high == 0
        norm_pad = jnp.pad(norm_low[None, :], ((0, 15), (0, width - norm_count)))
        mine = jnp.concatenate((attn_low, down_low, pack_up(up_low), norm_pad), axis=0)
        other = swap_hi(mine)
        enc_rows, dec_rows, cot_rows = regroup(enc_in, dec_in, cotangent)
        zero = jnp.where(first, mine, other)
        one = jnp.where(first, other, mine)
        last = mine.shape[0] - 16
        early = (one[:attn_rows], zero[attn_rows : last + 1], one[last:-1])
        early = jnp.concatenate((tie(zero[:attn_rows], enc_rows), *early), axis=0)
        full = lax.all_gather(early, GROUP, axis=0, tiled=False)
        late = lax.all_gather(one[attn_rows:last], GROUP, axis=0, tiled=False)
        gains = full[:, attn_rows + last : attn_rows + last + 2, :norm_count].swapaxes(0, 1)
        gains = gains.reshape(10, width).astype(F32)
    enc_window = jnp.concatenate((enc_rows, halo_rows(enc_rows)), axis=0)
    dec_window = jnp.concatenate((dec_rows, halo_rows(dec_rows)), axis=0)
    group = full.shape[0]

    total_len = rows * n_high
    bounds = jnp.cumsum(lengths[:, 0, :], axis=-1)
    bounds = lax.dynamic_index_in_dim(bounds, low, 0, keepdims=False)
    base = high * rows
    own_pos = base + jnp.arange(rows, dtype=jnp.int32)
    step = jnp.arange(HALO, dtype=jnp.int32)
    if n_high == 2:
        halo_pos = jnp.where(high == 0, rows, rows - HALO) + step
    else:
        halo_pos = jnp.concatenate((base - HALO + step, base + rows + step))
    key_pos = jnp.concatenate((own_pos, halo_pos))
    key_seg = segments_at(bounds, key_pos, total_len)
    krow = jnp.stack((key_seg, key_pos), axis=0)
    kcol = jnp.stack((key_seg, key_pos), axis=1)
    places = {
        "krow": krow,
        "kcol": kcol,
        "qrow": krow[:, :rows],
        "qcol": kcol[:rows],
        "offsets": None if n_high == 2 else (0, rows - HALO),
        "core": core,
    }

    per = 6 * width // group
    mats = [square(full, 0, index) for index in range(6)] + [square(full, per, index) for index in range(6)]
    pack0 = rows_of(full, 2 * per, late.shape[1])
    pack1 = rows_of(late, 0, late.shape[1])
    e = enc_forward(enc_rows, enc_window, mats[0:4], pack0, gains, places)
    low_window = jnp.concatenate((e["low"], halo_rows(e["low"])), axis=0)
    s = self_forward(dec_rows, dec_window, mats[4:8], places)
    c = cross_and_ffn(s["three"], low_window, mats[8:12], pack1, dec_rows, cot_rows, gains, places)

    back_c = halo_return(c["halo"])
    sh = cross_body_self_head(c, s["three"], s, mats[8], mats[7], gains, places)
    back_s = halo_return(sh["halo"])
    pair_f1 = c["kept"] if plain else reduce_cores(c["kept"], c["sent"])
    sb = own_body("self_body", s, sh, dec_rows, mats[4], True, places, pair_f1)
    kv = both_kv(
        e["low"], sh["own"], back_c, mats[9:11], dec_rows, sb["own"], back_s, mats[5:7], (c["five"], sb["gq"]),
        (sh["dwo"], sh["dwq"], c["dwo"]), group, places,
    )
    eh = enc_ffn_head(kv["encoded"], e["one"], e["two"], e, pack0, mats[3], gains, places)
    back_e = halo_return(eh["halo"])
    pair_a1 = kv["kept"] if plain else reduce_cores(kv["kept"], kv["sent"])
    eb = own_body("enc_body", e, eh, enc_rows, mats[0], False, places, pair_a1)
    if not plain:
        part_a1 = reduce_chips(pair_a1)
        pair_f0 = reduce_cores(tie(eh["kept"], part_a1), eh["sent"])
    norm_local = jnp.concatenate((eh["ng"], eh["ng2"], sh["ng"], c["ng"], c["ng8"]), axis=0)
    norm_local = norm_local.reshape(n_high, group, norm_count)
    norm_block = jnp.pad(
        norm_local.swapaxes(0, 1).astype(BF), ((0, 0), (0, 16 - n_high), (0, width - norm_count))
    )
    ek = enc_kv(
        enc_rows, eb["own"], back_e, mats[1:3], (eh["late"], eb["gq"]), (eb["dwq"], eh["dwo"], sb["dwq"], kv["dwk"]),
        norm_block, group, places, None,
    )
    if plain:
        attn_own, up_own, down_own, norm_own = reduce_plain(
            from_parity(ek["kept"], ek["sent"])[:, :per],
            from_parity(kv["kept"], kv["sent"]),
            from_parity(eh["kept"], eh["sent"]),
            from_parity(c["kept"], c["sent"]),
            norm_local,
        )
        lows, grads = (e["low"], c["low"]), (ek["grad"], kv["grad"])
    else:
        part_f1 = reduce_chips(pair_f1)
        lows = (tie(e["low"], part_f1), c["low"])
        part_f0 = reduce_chips(pair_f0)
        part_a0 = reduce_chips(reduce_cores(ek["kept"], ek["sent"]))
        grads = (tie(ek["grad"], part_a0), kv["grad"])
        ffn_own = join_halves(part_f0, part_f1)
        both = join_halves(part_a0, jnp.concatenate((part_a1, part_a0[attn_rows:]), axis=0))
        attn_own, up_own, down_own = both[:attn_rows], unpack_up(ffn_own[128:]), ffn_own[:128]
        norm_own = lax.dynamic_index_in_dim(both[attn_rows:], high, 0, keepdims=False)[:norm_count]

    def restore(*arrays):
        outs = jnp.stack(arrays, axis=0).reshape(len(arrays), micro, length_dev, width).swapaxes(0, 1)
        return lax.all_to_all(outs, "lo", split_axis=0, concat_axis=0, tiled=True)

    lows = restore(*lows)
    grads = restore(*grads)

    owned = (attn_own, up_own, down_own, norm_own)
    firsts = (attn_first, ffn_in_first, ffn_out_first, norm_first)
    seconds = (attn_second, ffn_in_second, ffn_out_second, norm_second)
    moments = [
        lamb_moments(masters[index], owned[index], firsts[index], seconds[index])
        for index in range(4)
    ]
    update_local = jnp.concatenate(
        [group_sum(onehots[index], row_squares(moments[index][2])) for index in range(4)]
    )
    squares = jnp.stack((weight_local, update_local))
    squares = jnp.pad(squares, ((0, 6), (0, 128 - squares.shape[1])))
    count = lax.axis_size(EVERY)
    squares = jnp.broadcast_to(squares[None], (count,) + squares.shape)
    squares = jnp.sum(lax.all_to_all(squares, EVERY, split_axis=0, concat_axis=0, tiled=True), axis=0)
    norms = jnp.sqrt(squares[:2, :26])
    ratio = norms[0] / norms[1]
    bounds_at = (0, 12, 14, 16, 26)
    new_weights = []
    for index in range(4):
        row_ratio = jnp.sum(
            jnp.where(onehots[index], ratio[None, bounds_at[index] : bounds_at[index + 1]], 0.0), axis=1
        )
        if masters[index].ndim == 2:
            row_ratio = row_ratio[:, None]
        new_weights.append(masters[index] - learn_rate * row_ratio * moments[index][2])
    return (
        lows[:, 0][:, None],
        lows[:, 1][:, None],
        grads[:, 0][:, None].astype(F32),
        grads[:, 1][:, None].astype(F32),
        *owned,
        *new_weights,
        *[item[0] for item in moments],
        *[item[1] for item in moments],
        *[item.astype(BF) for item in new_weights],
        norms,
        ratio,
    )


def solution(mesh):
    count_seq, count_stream = mesh.shape["seq"], mesh.shape["stream"]

    def run(*args):
        micro = args[0].shape[0]
        split = Mesh(
            mesh.devices.reshape(count_seq // micro, micro, count_stream // 2, 2), ("hi", "lo", "y", "c")
        )
        tokens = P(None, ("y", "c"), ("hi", "lo"), None)
        wide = P(EVERY, None)
        flat = P(EVERY)
        owned = (wide, wide, wide, flat)
        return jax.shard_map(
            shards,
            mesh=split,
            in_specs=(tokens, tokens, tokens, P(None, ("y", "c"), None), *owned, *owned, *owned),
            out_specs=(tokens, tokens, tokens, tokens, *owned, *owned, *owned, *owned, *owned, P(), P()),
            check_vma=False,
        )(*args)

    return run
```

```python
import types

import jax
import jax.numpy as jnp
from jax import lax
from jax.experimental import pallas as pl
from jax.experimental.pallas import tpu as pltpu
from jax.sharding import Mesh
from jax.sharding import PartitionSpec as P

HEADS = 8
STEP = 5
HALO = 256
TILE = 256

norm_eps = 1e-05
beta_one = 0.5
beta_two = 0.5
lamb_eps = 1e-06
weight_decay = 0.01
learn_rate = 0.5
masked_score = -1e30

BF = jnp.bfloat16
F32 = jnp.float32
MIB = 1024 * 1024


def dot_nn(a, b):
    return lax.dot_general(a, b, (((1,), (0,)), ((), ())), preferred_element_type=F32)


def dot_nt(a, b):
    return lax.dot_general(a, b, (((1,), (1,)), ((), ())), preferred_element_type=F32)


def dot_tn(a, b):
    return lax.dot_general(a, b, (((0,), (0,)), ((), ())), preferred_element_type=F32)


def norm_parts(rows):
    centre = rows - jnp.mean(rows, axis=-1, keepdims=True)
    inv = lax.rsqrt(jnp.mean(centre * centre, axis=-1, keepdims=True) + norm_eps)
    return centre * inv, inv


def norm_rows(rows, gain, bias):
    return norm_parts(rows)[0] * gain + bias


def norm_back(rows, gain, grad):
    unit, inv = norm_parts(rows)
    lead = grad * gain
    back = inv * (
        lead
        - jnp.mean(lead, axis=-1, keepdims=True)
        - unit * jnp.mean(lead * unit, axis=-1, keepdims=True)
    )
    return (
        back,
        jnp.sum(grad * unit, axis=0, keepdims=True),
        jnp.sum(grad, axis=0, keepdims=True),
    )


gelu_a = 0.7978845608028654
gelu_b = 0.044715


def gelu(v):
    return 0.5 * v * (1.0 + jnp.tanh(gelu_a * (v + gelu_b * (v * v * v))))


def gelu_both(v):
    sq = v * v
    t = jnp.tanh(gelu_a * (v + gelu_b * (sq * v)))
    half = 0.5 * (1.0 + t)
    slope = half + 0.5 * v * (1.0 - t * t) * (gelu_a * (1.0 + 3.0 * gelu_b * sq))
    return v * half, slope


def lane_low(shape):
    return lax.broadcasted_iota(jnp.int32, shape, 1) < 64


def shape_of(dtype, *dims):
    return jax.ShapeDtypeStruct(dims, dtype)


class Fetched:
    def __init__(self, ref, copies):
        self.ref, self.copies, self.shape = ref, copies, ref.shape

    def __getitem__(self, index):
        for copy in self.copies:
            copy.wait()
        self.copies = ()
        return self.ref[index]


def square(array, start, index):
    places, _, width = array.shape
    per = 6 * width // places
    pieces = []
    row, end = index * width, index * width + width
    while row < end:
        place, at = divmod(row, per)
        take = min(per - at, end - row)
        spot = slice(row - index * width, row - index * width + take)
        pieces.append(((place, slice(start + at, start + at + take)), spot))
        row += take
    return (array, (width, width), tuple(pieces))


def rows_of(array, start, count):
    places, _, width = array.shape
    every = slice(0, places)
    return (array, (places, count, width), (((every, slice(start, start + count)), every),))


def fused(name, program, core, small, ins, outs, flops, scratch=(), order=None):
    big, sources = [], []
    for item in ins.values():
        array = item[0] if isinstance(item, tuple) else item
        known = [index for index, other in enumerate(big) if other is array]
        sources.append(known[0] if known else len(big))
        if not known:
            big.append(array)
    shapes = [item[1] if isinstance(item, tuple) else item.shape for item in ins.values()]
    pieces = [item[2] if isinstance(item, tuple) else None for item in ins.values()]
    kinds = [big[source].dtype for source in sources]
    counts = [len(item) if item else 1 for item in pieces]
    n_small, n_big, n_out, extra = len(small), len(big), len(outs), 0 if order is None else 1

    def body(core_ref, *refs):
        small_refs, refs = refs[:n_small], refs[n_small:]
        big_refs, refs = refs[:n_big], refs[n_big + extra :]
        out_refs, refs = refs[:n_out], refs[n_out:]
        in_bufs, refs = refs[: len(ins)], refs[len(ins) :]
        out_bufs, refs = refs[:n_out], refs[n_out:]
        user, (in_sem, out_sem) = refs[:-2], refs[-2:]
        env = types.SimpleNamespace(**dict(zip(small, small_refs)))
        used, fetched = 0, []
        for key, source, piece, buf in zip(ins, sources, pieces, in_bufs):
            src = big_refs[source]
            copies = []
            for item in piece or (None,):
                if item is None:
                    copy = pltpu.make_async_copy(src, buf, in_sem.at[used])
                else:
                    copy = pltpu.make_async_copy(src.at[item[0]], buf.at[item[1]], in_sem.at[used])
                copy.start()
                copies.append(copy)
                used += 1
            setattr(env, key, Fetched(buf, copies))
            fetched.append(getattr(env, key))
        for key, buf in zip(outs, out_bufs):
            setattr(env, key, buf)
        leaving = [None] * n_out

        def store(*bufs):
            for buf in bufs:
                (index,) = [place for place in range(n_out) if out_bufs[place] is buf]
                leaving[index] = pltpu.make_async_copy(buf, out_refs[index], out_sem.at[index])
                leaving[index].start()

        program(env, core_ref, store, *user)
        store(*[buf for buf, copy in zip(out_bufs, leaving) if copy is None])
        for copy in leaving:
            copy.wait()
        for item in fetched:
            for copy in item.copies:
                copy.wait()

    vmem = pl.BlockSpec(memory_space=pltpu.VMEM)
    anywhere = pl.BlockSpec(memory_space=pl.ANY)
    size = sum(array.size * array.dtype.itemsize for array in big)
    results = pl.pallas_call(
        body,
        in_specs=[pl.BlockSpec(memory_space=pltpu.SMEM)] + [vmem] * n_small + [anywhere] * (n_big + extra),
        out_specs=tuple([anywhere] * n_out),
        out_shape=tuple(outs.values()),
        scratch_shapes=[pltpu.VMEM(shape, dtype) for shape, dtype in zip(shapes, kinds)]
        + [pltpu.VMEM(out.shape, out.dtype) for out in outs.values()]
        + list(scratch)
        + [pltpu.SemaphoreType.DMA((sum(counts),)), pltpu.SemaphoreType.DMA((n_out,))],
        compiler_params=pltpu.CompilerParams(vmem_limit_bytes=56 * MIB),
        cost_estimate=pl.CostEstimate(flops=flops, bytes_accessed=size, transcendentals=0),
        name=name,
    )(core, *small.values(), *big, *(() if order is None else (order,)))
    return types.SimpleNamespace(**dict(zip(outs, results)))


def tiles_of(core, rows, window):
    if window == rows + HALO:
        near = pl.multiple_of(core[1], HALO)
        return ((near, 0), (pl.multiple_of(rows - TILE - core[1], HALO), None))
    return ((0, 0), (rows - TILE, 1))


def key_rows(ref, lanes, rows, halo):
    if halo is None:
        return ref[0:rows, lanes]
    if halo == 0:
        return ref[0 : rows + HALO, lanes]
    return jnp.concatenate((ref[0:rows, lanes], ref[rows + HALO : rows + 2 * HALO, lanes]), axis=0)


def key_lanes(ref, row, rows, halo):
    if halo is None:
        return ref[row : row + 1, 0:rows]
    if halo == 0:
        return ref[row : row + 1, 0 : rows + HALO]
    return jnp.concatenate(
        (ref[row : row + 1, 0:rows], ref[row : row + 1, rows + HALO : rows + 2 * HALO]), axis=1
    )


def halves(shape):
    low = lane_low(shape)
    return low, ~low


def keep(mask, values):
    return jnp.where(mask, values, jnp.zeros_like(values))


def gain_rows(gains, index):
    return gains[index : index + 1, :], gains[index + 1 : index + 2, :]


def attn_fwd(core, causal, low_src, base, kv_src, weights, qcol, krow, q_out, k_out, v_out, o_out, lse_out, res_out):
    rows, _ = q_out.shape
    window = k_out.shape[0]
    w_q, w_k, w_v, w_o = weights
    queries = dot_nn(low_src(), w_q[...])
    q_out[...] = (queries.astype(BF).astype(F32) * 0.125).astype(BF)
    k_out[...] = dot_nn(kv_src[...], w_k[...]).astype(BF)
    v_out[...] = dot_nn(kv_src[...], w_v[...]).astype(BF)
    for offset, halo in tiles_of(core, rows, window):
        spot = pl.ds(offset, TILE)
        allowed = qcol[spot, 0:1] == key_lanes(krow, 0, rows, halo)
        if causal:
            allowed = allowed & (key_lanes(krow, 1, rows, halo) <= qcol[spot, 1:2])
        lane = lax.broadcasted_iota(jnp.int32, (TILE, 128), 1)
        packed = jnp.zeros((TILE, 128), F32)
        for pair in range(HEADS // 2):
            lanes = slice(pair * 128, pair * 128 + 128)
            q2 = q_out[spot, lanes]
            k2 = key_rows(k_out, lanes, rows, halo)
            v2 = key_rows(v_out, lanes, rows, halo)
            mixed = None
            for half in range(2):
                scores = dot_nt(keep(halves(q2.shape)[half], q2), k2)
                scores = jnp.where(allowed, scores, masked_score)
                top = jnp.max(scores, axis=-1, keepdims=True)
                weights = jnp.exp(scores - top)
                total = jnp.sum(weights, axis=-1, keepdims=True)
                probs = (weights * (1.0 / total)).astype(BF)
                part = dot_nn(probs, keep(halves(v2.shape)[half], v2))
                mixed = part if mixed is None else mixed + part
                packed = jnp.where(lane == 2 * pair + half, top + jnp.log(total), packed)
            o_out[spot, lanes] = mixed.astype(BF)
        lse_out[:, spot] = jnp.transpose(packed)[0:HEADS, :]
    res_out[...] = base() + dot_nn(o_out[...], w_o[...])


def score_grads(q2, do2, k2, v2, allowed, lse, delta):
    sums = None
    for half in range(2):
        qh = keep(halves(q2.shape)[half], q2)
        doh = keep(halves(do2.shape)[half], do2)
        scores = jnp.where(allowed, dot_nt(k2, qh), masked_score)
        probs = jnp.exp(scores - lse[half])
        gscores = (probs * (dot_nt(v2, doh) - delta[half])).astype(BF)
        parts = (
            dot_tn(gscores, keep(halves(k2.shape)[half], k2)),
            dot_nn(gscores, qh),
            dot_nn(probs.astype(BF), doh),
        )
        sums = parts if sums is None else tuple(a + b for a, b in zip(sums, parts))
    return sums


def attn_head(
    core, causal, grad, resid, o_in, q_in, k_in, v_in, lse_in, w_o, gains, gain_at, qrow, kcol,
    back_out, do_out, delta_out, dwo_out, halo_out, dqh_out, ng_out,
):
    rows, width = do_out.shape
    window = k_in.shape[0]
    back, dgain, dbias = norm_back(resid[...], gain_rows(gains, gain_at)[0], grad)
    back_out[...] = back
    ng_out[0:1, :] = dgain
    ng_out[1:2, :] = dbias
    branch = back.astype(BF)
    do_out[...] = dot_nt(branch, w_o[...]).astype(BF)
    mixed = do_out[...].astype(F32) * o_in[...].astype(F32)
    high = mixed.astype(BF)
    rest = (mixed - high.astype(F32)).astype(BF)
    head = lax.broadcasted_iota(jnp.int32, (16, width), 1) // (width // HEADS)
    which = (head == lax.broadcasted_iota(jnp.int32, (16, width), 0)).astype(F32).astype(BF)
    delta_out[...] = (dot_nt(which, high) + dot_nt(which, rest))[0:HEADS, :]
    for offset, halo in tiles_of(core, rows, window):
        if halo is None:
            continue
        spot = pl.ds(offset, TILE)
        keys = slice(rows + halo * HALO, rows + halo * HALO + HALO)
        here = slice(halo * HALO, halo * HALO + HALO)
        allowed = kcol[keys, 0:1] == qrow[0:1, spot]
        if causal:
            allowed = allowed & (kcol[keys, 1:2] <= qrow[1:2, spot])
        for pair in range(HEADS // 2):
            lanes = slice(pair * 128, pair * 128 + 128)
            heads = (2 * pair, 2 * pair + 1)
            dq2, dk2, dv2 = score_grads(
                q_in[spot, lanes],
                do_out[spot, lanes],
                k_in[keys, lanes],
                v_in[keys, lanes],
                allowed,
                [lse_in[h : h + 1, spot] for h in heads],
                [delta_out[h : h + 1, spot] for h in heads],
            )
            dqh_out[here, lanes] = dq2
            halo_out[0, here, lanes] = dk2.astype(BF)
            halo_out[1, here, lanes] = dv2.astype(BF)
    dwo_out[...] = dot_tn(o_in[...], branch).astype(BF)


def attn_body(
    core, causal, window, back, do_in, delta, dqh, low_src, q_in, k_in, v_in, lse_in, w_q, qrow, kcol,
    gq_out, dwq_out, own_out, dq_scr,
):
    rows, width = gq_out.shape
    for tile in range(rows // TILE):
        spot = slice(tile * TILE, tile * TILE + TILE)
        allowed = kcol[0:rows, 0:1] == qrow[0:1, spot]
        if causal:
            allowed = allowed & (kcol[0:rows, 1:2] <= qrow[1:2, spot])
        for pair in range(HEADS // 2):
            lanes = slice(pair * 128, pair * 128 + 128)
            heads = (2 * pair, 2 * pair + 1)
            dq2, dk2, dv2 = score_grads(
                q_in[spot, lanes],
                do_in[spot, lanes],
                k_in[0:rows, lanes],
                v_in[0:rows, lanes],
                allowed,
                [lse_in[h : h + 1, spot] for h in heads],
                [delta[h : h + 1, spot] for h in heads],
            )
            dq_scr[spot, lanes] = dq2
            if tile == 0:
                own_out[0, :, lanes] = dk2
                own_out[1, :, lanes] = dv2
            else:
                own_out[0, :, lanes] += dk2
                own_out[1, :, lanes] += dv2
    for offset, halo in tiles_of(core, rows, window):
        if halo is not None:
            dq_scr[pl.ds(offset, TILE), :] += dqh[halo * HALO : halo * HALO + HALO, :]
    grad_q = (dq_scr[...] * 0.125).astype(BF)
    gq_out[...] = back[...] + dot_nt(grad_q, w_q[...])
    dwq_out[...] = dot_tn(low_src(), grad_q).astype(BF)


def split_places(core, source, kept, sent):
    for parity in range(2):

        @pl.when(core[0] == parity)
        def place():
            for chip in range(kept.shape[0]):
                kept[chip] = source[2 * chip + parity]
                sent[chip] = source[2 * chip + 1 - parity]


def kv_bwd(core, offsets, src, own, halo, w_k, w_v, adds, scr):
    scr[...] = own[...]
    for index in range(halo.shape[1] // HALO):
        spot = pl.ds(pl.multiple_of(core[1], HALO) if offsets is None else offsets[index], HALO)
        scr[:, spot, :] += halo[:, index * HALO : index * HALO + HALO, :].astype(F32)
    dk = scr[0].astype(BF)
    dv = scr[1].astype(BF)
    total = dot_nt(dk, w_k[...]) + dot_nt(dv, w_v[...])
    for ref in adds:
        total = total + ref[...]
    return total, dot_tn(src[...], dk).astype(BF), dot_tn(src[...], dv).astype(BF)


def lay_out(stack, mats):
    places, _, width = stack.shape
    per = 6 * width // places
    for slot, matrix in enumerate(mats):
        row, end = slot * width, slot * width + width
        while row < end:
            place, start = divmod(row, per)
            take = min(per - start, end - row)
            at = row - slot * width
            stack[place, start : start + take, :] = matrix[at : at + take, :]
            row += take


def up_tile(pack, tile):
    places, _, width = pack.shape
    return pack[:, 128 + 32 * tile : 160 + 32 * tile, :].reshape(places * 32, width)


def down_tile(pack, tile):
    return pack[4 * tile : 4 * tile + 4, 0:128, :].reshape(512, pack.shape[2])


def ffn_fwd(resid, base, gains, gain_in, gain_out, pack, res_out, low_out, hid_low=None, pre=None):
    hidden = norm_rows(resid[...], *gain_rows(gains, gain_in))
    low = hidden.astype(BF)
    if hid_low is not None:
        hid_low[...] = low
    res_out[...] = hidden + base[...].astype(F32)
    for tile in range(4):
        values = dot_nn(low, up_tile(pack, tile))
        if pre is not None:
            pre[tile] = values
        res_out[...] += dot_nn(gelu(values).astype(BF), down_tile(pack, tile))
    low_out[...] = norm_rows(res_out[...], *gain_rows(gains, gain_out)).astype(BF)


def ffn_bwd(grad, res_late, gains, gain_out, pack, gh_out, late_out, ng_out, hid_low, late_low, dpack, pre=None):
    back, dgain, dbias = norm_back(res_late[...], gain_rows(gains, gain_out)[0], grad)
    late_out[...] = back
    gh_out[...] = back
    late_low[...] = back.astype(BF)
    ng_out[0:1, :] = dgain
    ng_out[1:2, :] = dbias
    places, _, width = dpack.shape
    for tile in range(4):
        activ, slope = gelu_both(dot_nn(hid_low[...], up_tile(pack, tile)) if pre is None else pre[tile])
        grad_down = dot_tn(activ.astype(BF), late_low[...]).astype(BF)
        dpack[4 * tile : 4 * tile + 4, 0:128, :] = grad_down.reshape(4, 128, width)
        grad_act = dot_nt(late_low[...], down_tile(pack, tile)).astype(BF).astype(F32)
        grad_pre = (grad_act * slope).astype(BF)
        grad_up = dot_tn(hid_low[...], grad_pre).astype(BF)
        dpack[:, 128 + 32 * tile : 160 + 32 * tile, :] = grad_up.reshape(places, 32, width)
        gh_out[...] += dot_nt(grad_pre, up_tile(pack, tile))


def kept_shapes(rows, window, width, with_o=True):
    outs = dict(
        q=shape_of(BF, rows, width),
        k=shape_of(BF, window, width),
        v=shape_of(BF, window, width),
        lse=shape_of(F32, HEADS, rows),
    )
    return dict(outs, o=shape_of(BF, rows, width)) if with_o else outs


def head_shapes(rows, window, width):
    return dict(
        back=shape_of(F32, rows, width),
        do=shape_of(BF, rows, width),
        delta=shape_of(F32, HEADS, rows),
        dwo=shape_of(BF, width, width),
        halo=shape_of(BF, 2, window - rows, width),
        dqh=shape_of(F32, window - rows, width),
        ng=shape_of(F32, 2, width),
    )


def weights_of(env):
    return env.wq, env.wk, env.wv, env.wo


def named_mats(mats):
    return dict(wq=mats[0], wk=mats[1], wv=mats[2], wo=mats[3])


def input_attention(name, x, window_rows, mats, causal, places):
    rows, width = x.shape
    window = window_rows.shape[0]

    def program(e, core, store):
        attn_fwd(
            core, causal, lambda: e.x[...], lambda: e.x[...].astype(F32), e.window, weights_of(e),
            e.qcol, e.krow, e.q, e.k, e.v, e.o, e.lse, e.resid,
        )

    return fused(
        name,
        program,
        places.core,
        dict(qcol=places.qcol, krow=places.krow),
        dict(x=x, window=window_rows, **named_mats(mats)),
        dict(kept_shapes(rows, window, width), resid=shape_of(F32, rows, width)),
        12 * rows * width * width + 8 * rows * window * width,
    )


def enc_ffn(one, x, pack, gains, places):
    rows, width = x.shape

    def program(e, core, store):
        ffn_fwd(e.one, e.x, e.gains, 0, 2, e.pack, e.two, e.low)

    outs = fused(
        "enc_ffn",
        program,
        places.core,
        dict(gains=gains),
        dict(one=one, x=x, pack=pack),
        dict(low=shape_of(BF, rows, width), two=shape_of(F32, rows, width)),
        16 * rows * width * width,
    )
    return outs.two, outs.low


def cross_and_ffn(three, window_rows, mats, pack, z, cot, gains, places):
    rows, width = three.shape
    window = window_rows.shape[0]
    count, block = pack[0].shape[0], pack[1][1]
    f32_rows, low_rows = pltpu.VMEM((rows, width), F32), pltpu.VMEM((rows, width), BF)

    def program(e, core, store, o, four, five, gh, hid_low, late_low, pre, dpack):
        def first():
            return norm_rows(e.three[...], *gain_rows(e.gains, 4))

        attn_fwd(
            core, False, lambda: first().astype(BF), first, e.window, weights_of(e),
            e.qcol, e.krow, e.q, e.k, e.v, o, e.lse, four,
        )
        store(e.q, e.k, e.v, e.lse)
        ffn_fwd(four, e.z, e.gains, 6, 8, e.pack, five, e.low, hid_low, pre)
        store(e.low)
        ffn_bwd(
            e.cot[...].astype(F32), five, e.gains, 8, e.pack, gh, e.five, e.ng8,
            hid_low, late_low, dpack, pre,
        )
        split_places(core, dpack, e.kept, e.sent)
        store(e.sent, e.kept, e.five, e.ng8)
        attn_head(
            core, False, gh[...], four, o, e.q, e.k, e.v, e.lse, e.wo, e.gains, 6,
            e.qrow, e.kcol, e.back, e.do, e.delta, e.dwo, e.halo, e.dqh, e.ng,
        )

    return fused(
        "cross_and_ffn",
        program,
        places.core,
        dict(qcol=places.qcol, krow=places.krow, qrow=places.qrow, kcol=places.kcol, gains=gains),
        dict(three=three, wq=mats[0], window=window_rows, wk=mats[1], wv=mats[2], wo=mats[3], z=z, pack=pack, cot=cot),
        dict(
            **kept_shapes(rows, window, width, False),
            low=shape_of(BF, rows, width),
            kept=shape_of(BF, count // 2, block, width),
            sent=shape_of(BF, count // 2, block, width),
            five=shape_of(F32, rows, width),
            ng8=shape_of(F32, 2, width),
            **head_shapes(rows, window, width),
        ),
        68 * rows * width * width + 8 * rows * window * width,
        scratch=[
            low_rows, f32_rows, f32_rows, f32_rows, low_rows, low_rows,
            pltpu.VMEM((4, rows, width), F32), pltpu.VMEM((count, block, width), BF),
        ],
    )


def cross_body_self_head(c, three, s, mat_q, mat_o, gains, places, order):
    rows, width = three.shape
    window = c.k.shape[0]
    own = (slice(0, rows),)

    def program(e, core, store, grad, dq):
        def first():
            return norm_rows(e.three[...], *gain_rows(e.gains, 4)).astype(BF)

        attn_body(
            core, False, window, e.back_c, e.do_c, e.delta_c, e.dqh_c, first, e.q_c, e.k_c,
            e.v_c, e.lse_c, e.wq, e.qrow, e.kcol, grad, e.dwq, e.own, dq,
        )
        store(e.own, e.dwq)
        attn_head(
            core, True, grad[...], e.three, e.o, e.q, e.k, e.v, e.lse, e.wo, e.gains, 4,
            e.qrow, e.kcol, e.back, e.do, e.delta, e.dwo, e.halo, e.dqh, e.ng,
        )

    return fused(
        "cross_body_self_head",
        program,
        places.core,
        dict(qrow=places.qrow, kcol=places.kcol, gains=gains),
        dict(
            q_c=c.q,
            do_c=c.do,
            k_c=(c.k, (rows, width), ((own, own),)),
            v_c=(c.v, (rows, width), ((own, own),)),
            lse_c=c.lse,
            delta_c=c.delta,
            dqh_c=c.dqh,
            back_c=c.back,
            wq=mat_q,
            three=three,
            wo=mat_o,
            o=s.o,
            q=s.q,
            k=s.k,
            v=s.v,
            lse=s.lse,
        ),
        dict(
            own=shape_of(F32, 2, rows, width),
            dwq=shape_of(BF, width, width),
            **head_shapes(rows, window, width),
        ),
        8 * rows * width * width + 10 * rows * window * width,
        scratch=[pltpu.VMEM((rows, width), F32), pltpu.VMEM((rows, width), F32)],
        order=order,
    )


def own_body(name, kept, head, src, mat_q, causal, places, order):
    rows, width = src.shape
    window = kept.k.shape[0]
    own = (slice(0, rows),)

    def program(e, core, store, dq):
        attn_body(
            core, causal, window, e.back, e.do, e.delta, e.dqh, lambda: e.src[...], e.q, e.k,
            e.v, e.lse, e.wq, e.qrow, e.kcol, e.gq, e.dwq, e.own, dq,
        )

    return fused(
        name,
        program,
        places.core,
        dict(qrow=places.qrow, kcol=places.kcol),
        dict(
            q=kept.q,
            do=head.do,
            k=(kept.k, (rows, width), ((own, own),)),
            v=(kept.v, (rows, width), ((own, own),)),
            lse=kept.lse,
            delta=head.delta,
            dqh=head.dqh,
            back=head.back,
            wq=mat_q,
            src=src,
        ),
        dict(
            own=shape_of(F32, 2, rows, width),
            gq=shape_of(F32, rows, width),
            dwq=shape_of(BF, width, width),
        ),
        4 * rows * width * width + 10 * rows * rows * width,
        scratch=[pltpu.VMEM((rows, width), F32)],
        order=order,
    )


def both_kv(low, own_c, halo_c, mats_c, z, own_s, halo_s, mats_s, adds, grads, group, places):
    rows, width = low.shape
    per = 6 * width // group

    def program(e, core, store, scr, stack):
        total, dwk, dwv = kv_bwd(core, places.offsets, e.low, e.own_c, e.halo_c, e.wk_c, e.wv_c, (), scr)
        e.encoded[...] = total
        store(e.encoded)
        total, e.dwk[...], dwv_s = kv_bwd(
            core, places.offsets, e.z, e.own_s, e.halo_s, e.wk_s, e.wv_s, (e.add0, e.add1), scr
        )
        e.grad[...] = total.astype(BF)
        store(e.grad, e.dwk)
        lay_out(stack, (dwv_s, e.dwo_s, e.dwq_c, dwk, dwv, e.dwo_c))
        split_places(core, stack, e.kept, e.sent)

    return fused(
        "both_kv",
        program,
        places.core,
        dict(),
        dict(
            own_c=own_c,
            halo_c=halo_c,
            wk_c=mats_c[0],
            wv_c=mats_c[1],
            low=low,
            own_s=own_s,
            halo_s=halo_s,
            wk_s=mats_s[0],
            wv_s=mats_s[1],
            add0=adds[0],
            add1=adds[1],
            z=z,
            dwo_s=grads[0],
            dwq_c=grads[1],
            dwo_c=grads[2],
        ),
        dict(
            encoded=shape_of(F32, rows, width),
            grad=shape_of(BF, rows, width),
            dwk=shape_of(BF, width, width),
            sent=shape_of(BF, group // 2, per, width),
            kept=shape_of(BF, group // 2, per, width),
        ),
        16 * rows * width * width,
        scratch=[pltpu.VMEM((2, rows, width), F32), pltpu.VMEM((group, per, width), BF)],
    )


def enc_ffn_head(grad, one, two, kept, pack, mat_o, gains, places, order):
    rows, width = one.shape
    window = kept.k.shape[0]
    count, block = pack[0].shape[0], pack[1][1]

    def program(e, core, store, gh, hid_low, late_low, dpack):
        hid_low[...] = norm_rows(e.one[...], *gain_rows(e.gains, 0)).astype(BF)
        ffn_bwd(
            e.grad[...], e.two, e.gains, 2, e.pack, gh, e.late, e.ng2, hid_low, late_low, dpack
        )
        split_places(core, dpack, e.kept, e.sent)
        store(e.sent, e.kept, e.late, e.ng2)
        attn_head(
            core, False, gh[...], e.one, e.o, e.q, e.k, e.v, e.lse, e.wo, e.gains, 0,
            e.qrow, e.kcol, e.back, e.do, e.delta, e.dwo, e.halo, e.dqh, e.ng,
        )

    return fused(
        "enc_ffn_head",
        program,
        places.core,
        dict(qrow=places.qrow, kcol=places.kcol, gains=gains),
        dict(
            one=one,
            two=two,
            grad=grad,
            pack=pack,
            wo=mat_o,
            o=kept.o,
            q=kept.q,
            k=kept.k,
            v=kept.v,
            lse=kept.lse,
        ),
        dict(
            sent=shape_of(BF, count // 2, block, width),
            kept=shape_of(BF, count // 2, block, width),
            late=shape_of(F32, rows, width),
            ng2=shape_of(F32, 2, width),
            **head_shapes(rows, window, width),
        ),
        44 * rows * width * width + 10 * TILE * TILE * width,
        scratch=[
            pltpu.VMEM((rows, width), F32), pltpu.VMEM((rows, width), BF), pltpu.VMEM((rows, width), BF),
            pltpu.VMEM((count, block, width), BF),
        ],
        order=order,
    )


def enc_kv(x, own, halo, mats, adds, grads, norm, group, places, order):
    rows, width = x.shape
    per = 6 * width // group
    block = per + norm.shape[1]

    def program(e, core, store, scr, stack):
        total, dwk, dwv = kv_bwd(
            core, places.offsets, e.x, e.own, e.halo, e.wk, e.wv, (e.add0, e.add1), scr
        )
        lay_out(stack, (e.dwq_e, dwk, dwv, e.dwo_e, e.dwq_s, e.dwk_s))
        stack[:, per:, :] = e.norm[...]
        split_places(core, stack, e.kept, e.sent)
        store(e.sent, e.kept)
        e.grad[...] = total.astype(BF)

    return fused(
        "enc_kv",
        program,
        places.core,
        dict(),
        dict(
            own=own,
            halo=halo,
            wk=mats[0],
            wv=mats[1],
            x=x,
            dwq_e=grads[0],
            dwo_e=grads[1],
            dwq_s=grads[2],
            dwk_s=grads[3],
            norm=norm,
            add0=adds[0],
            add1=adds[1],
        ),
        dict(
            sent=shape_of(BF, group // 2, block, width),
            kept=shape_of(BF, group // 2, block, width),
            grad=shape_of(BF, rows, width),
        ),
        8 * rows * width * width,
        scratch=[pltpu.VMEM((2, rows, width), F32), pltpu.VMEM((group, block, width), BF)],
        order=order,
    )


def segments_at(bounds, places, total_len):
    found = jnp.sum((bounds[None, :] <= places[:, None]).astype(jnp.int32), axis=-1)
    return jnp.where((places >= 0) & (places < total_len), found, -1)


def row_squares(values):
    if values.ndim == 2:
        return jnp.sum(values * values, axis=1)
    return values * values


def owner_groups(rows_local, owner, per_group, count):
    group_ids = (owner * rows_local + jnp.arange(rows_local, dtype=jnp.int32)) // per_group
    return group_ids[:, None] == jnp.arange(count, dtype=jnp.int32)[None, :]


def group_sum(onehot, row_values):
    return jnp.sum(jnp.where(onehot, row_values[:, None], 0.0), axis=0)


def lamb_moments(master, grad_rows, first, second):
    first_new = beta_one * first + (1.0 - beta_one) * grad_rows
    second_new = beta_two * second + (1.0 - beta_two) * grad_rows * grad_rows
    update = (
        first_new
        / (1.0 - beta_one**STEP)
        / (jnp.sqrt(second_new / (1.0 - beta_two**STEP)) + lamb_eps)
        + weight_decay * master
    )
    return (first_new, second_new, update)


GROUP = ("lo", "y", "c")
CHIPS = ("lo", "y")
EVERY = ("hi", "lo", "y", "c")


def swap_hi(array):
    return lax.ppermute(array, "hi", [(0, 1), (1, 0)])


def shift_hi(array, distance):
    count = lax.axis_size("hi")
    route = [(i - distance, i) for i in range(count) if i - distance in range(count)]
    return lax.ppermute(array, "hi", route)


def halo_rows(rows_array):
    rows = rows_array.shape[0]
    if lax.axis_size("hi") == 2:
        return swap_core(jnp.where(lax.axis_index("c") == 0, rows_array[rows - HALO :], rows_array[:HALO]))
    left = shift_hi(rows_array[rows - HALO :], 1)
    right = shift_hi(rows_array[:HALO], -1)
    return jnp.concatenate((left, right), axis=0)


def halo_return(grads):
    if lax.axis_size("hi") == 2:
        return swap_core(grads)
    to_left = shift_hi(grads[:, :HALO], -1)
    to_right = shift_hi(grads[:, HALO:], 1)
    return jnp.concatenate((to_left, to_right), axis=1)


def trade(array):
    return lax.ppermute(array, ("hi", "c"), [(0, 0), (1, 2), (2, 1), (3, 3)])


def pack_up(rows):
    count, units = rows.shape
    return rows.reshape(count, 4, units // 4).swapaxes(0, 1).reshape(4 * count, units // 4)


def unpack_up(packed):
    count, width = packed.shape
    return packed.reshape(4, count // 4, width).swapaxes(0, 1).reshape(count // 4, 4 * width)


def swap_core(array):
    return lax.ppermute(array, "c", [(0, 1), (1, 0)])


def tie(array, other):
    bit = lax.slice(other, (0,) * other.ndim, (1,) * other.ndim).reshape(()) * 0
    return array + bit.astype(array.dtype)


def from_parity(mine, other):
    even = lax.axis_index("c") == 0
    full = jnp.stack((jnp.where(even, mine, other), jnp.where(even, other, mine)), axis=1)
    return full.reshape(-1, *mine.shape[1:])


def gather_plain(attn_shard, up_shard, down_shard, norm_shard):
    width = attn_shard.shape[1]
    group = lax.axis_size(GROUP)
    norm_count = norm_shard.shape[0]
    attn = lax.all_gather(attn_shard, EVERY, axis=0, tiled=True)
    down = lax.all_gather(down_shard, EVERY, axis=0, tiled=True).reshape(2, group, -1, width)
    up = lax.all_gather(up_shard, EVERY, axis=0, tiled=True)
    up = up.reshape(2, group, -1, 4, width).swapaxes(2, 3).reshape(2, group, -1, width)
    norms = jnp.pad(norm_shard[None, :], ((0, 0), (0, width - norm_count)))
    norms = lax.all_gather(norms, EVERY, axis=0, tiled=True)[:, :norm_count]
    ffn = jnp.concatenate((down, up), axis=2)
    attn = attn.reshape(2, group, -1, width)
    full = jnp.concatenate((attn[0], attn[1]), axis=1)
    return full, jnp.concatenate((ffn[0], ffn[1]), axis=1), norms.reshape(10, width).astype(F32)


def reduce_cores(kept, sent):
    return (kept.astype(F32) + swap_core(sent).astype(F32)).astype(BF)


def reduce_chips(pair):
    parts = lax.all_to_all(pair, CHIPS, split_axis=0, concat_axis=0, tiled=True)
    return jnp.sum(parts.astype(F32), axis=0)


def join_halves(zero, one):
    first = lax.axis_index("hi") == 0
    mine = jnp.where(first, zero, one)
    sent = jnp.where(first, one, zero).astype(BF)
    return mine + swap_hi(sent).astype(F32)


def reduce_plain(attn0, attn1, ffn0, ffn1, norm_local):
    group, _, width = ffn0.shape

    def scatter(rows):
        return lax.psum_scatter(rows, EVERY, scatter_dimension=0, tiled=True).astype(F32)

    attn = jnp.concatenate((attn0, attn1), axis=0).reshape(-1, width)
    ffn = jnp.stack((ffn0, ffn1)).reshape(2 * group, -1, width)
    up = ffn[:, 128:].reshape(2 * group, 4, 32, width).swapaxes(1, 2).reshape(-1, 4 * width)
    norms = lax.psum_scatter(
        norm_local.reshape(lax.axis_size(EVERY), -1), EVERY, scatter_dimension=0, tiled=True
    )
    return scatter(attn), scatter(up), scatter(ffn[:, :128].reshape(-1, width)), norms[0]


def shards(
    enc_in,
    dec_in,
    cotangent,
    lengths,
    attn_master,
    ffn_in_master,
    ffn_out_master,
    norm_master,
    attn_first,
    ffn_in_first,
    ffn_out_first,
    norm_first,
    attn_second,
    ffn_in_second,
    ffn_out_second,
    norm_second,
):
    micro, _, length_dev, width = enc_in.shape
    rows = micro * length_dev
    hidden_units = ffn_in_master.shape[1]
    high, low = lax.axis_index("hi"), lax.axis_index("lo")
    n_high = lax.axis_size("hi")
    owner = lax.axis_index(EVERY)
    masters = (attn_master, ffn_in_master, ffn_out_master, norm_master)
    group_info = ((width, 12), (width, 2), (hidden_units, 2), (width, 10))
    onehots = [
        owner_groups(master.shape[0], owner, info[0], info[1])
        for master, info in zip(masters, group_info)
    ]
    weight_local = jnp.concatenate(
        [group_sum(onehot, row_squares(master)) for onehot, master in zip(onehots, masters)]
    )

    plain = n_high != 2

    def regroup(*arrays):
        packed = jnp.stack([array[:, 0] for array in arrays], axis=1)
        packed = lax.all_to_all(packed, "lo", split_axis=0, concat_axis=0, tiled=True)
        packed = packed.swapaxes(0, 1).reshape(len(arrays), rows, width)
        return packed if plain else trade(packed)

    part = high if plain else lax.axis_index("c")
    core = jnp.stack((lax.axis_index("c"), jnp.where(part == 0, rows - HALO, 0))).astype(jnp.int32)
    attn_rows = attn_master.shape[0]
    norm_count = norm_master.shape[0]
    attn_low, up_low, down_low, norm_low = [master.astype(BF) for master in masters]
    if plain:
        full, late, gains = gather_plain(attn_low, up_low, down_low, norm_low)
        enc_rows, dec_rows, cot_rows = regroup(enc_in, dec_in, cotangent)
    else:
        first = high == 0
        norm_pad = jnp.pad(norm_low[None, :], ((0, 15), (0, width - norm_count)))
        mine = jnp.concatenate((attn_low, norm_pad), axis=0)
        other = swap_hi(mine)
        (enc_rows,) = regroup(enc_in)
        zero = jnp.where(first, mine, other)
        one = jnp.where(first, other, mine)
        early = (zero[:attn_rows], one[:attn_rows], zero[attn_rows : attn_rows + 1], one[attn_rows:-1])
        full = lax.all_gather(jnp.concatenate(early, axis=0), GROUP, axis=0, tiled=False)
        mine = tie(jnp.concatenate((down_low, pack_up(up_low)), axis=0), other)
        other = swap_hi(mine)
        both = jnp.concatenate((jnp.where(first, mine, other), jnp.where(first, other, mine)), axis=0)
        late = lax.all_gather(both, GROUP, axis=0, tiled=False)
        (dec_rows,) = regroup(tie(dec_in, enc_rows))
        (cot_rows,) = regroup(tie(cotangent, dec_rows))
        gains = full[:, 2 * attn_rows : 2 * attn_rows + 2, :norm_count].swapaxes(0, 1)
        gains = gains.reshape(10, width).astype(F32)
    enc_window = jnp.concatenate((enc_rows, halo_rows(enc_rows)), axis=0)
    dec_window = jnp.concatenate((dec_rows, halo_rows(dec_rows)), axis=0)
    group = full.shape[0]

    total_len = rows * n_high
    bounds = jnp.cumsum(lengths[:, 0, :], axis=-1)
    bounds = lax.dynamic_index_in_dim(bounds, low, 0, keepdims=False)
    bounds = bounds if plain else trade(bounds)
    base = part * rows
    own_pos = base + jnp.arange(rows, dtype=jnp.int32)
    step = jnp.arange(HALO, dtype=jnp.int32)
    if n_high == 2:
        halo_pos = jnp.where(part == 0, rows, rows - HALO) + step
    else:
        halo_pos = jnp.concatenate((base - HALO + step, base + rows + step))
    key_pos = jnp.concatenate((own_pos, halo_pos))
    key_seg = segments_at(bounds, key_pos, total_len)
    krow = jnp.stack((key_seg, key_pos), axis=0)
    kcol = jnp.stack((key_seg, key_pos), axis=1)
    places = types.SimpleNamespace(
        krow=krow,
        kcol=kcol,
        qrow=krow[:, :rows],
        qcol=kcol[:rows],
        offsets=None if n_high == 2 else (0, rows - HALO),
        core=core,
    )

    per = 6 * width // group
    mats = [square(full, 0, index) for index in range(6)] + [square(full, per, index) for index in range(6)]
    block = late.shape[1] // 2
    pack0, pack1 = rows_of(late, 0, block), rows_of(late, block, block)
    e = input_attention("enc_attention", enc_rows, enc_window, mats[0:4], False, places)
    s = input_attention("self_attention", dec_rows, dec_window, mats[4:8], True, places)
    two, low_rows = enc_ffn(e.resid, enc_rows, pack0, gains, places)
    low_window = jnp.concatenate((low_rows, halo_rows(low_rows)), axis=0)
    c = cross_and_ffn(s.resid, low_window, mats[8:12], pack1, dec_rows, cot_rows, gains, places)

    def restore(*arrays):
        outs = jnp.stack(arrays, axis=0).reshape(len(arrays), micro, length_dev, width).swapaxes(0, 1)
        return lax.all_to_all(outs, "lo", split_axis=0, concat_axis=0, tiled=True)

    def traded(array):
        return array if plain else trade(array)

    enc_out = restore(traded(low_rows))
    dec_out = traded(c.low)
    back_c = halo_return(c.halo)
    sh = cross_body_self_head(c, s.resid, s, mats[8], mats[7], gains, places, enc_out)
    back_s = halo_return(sh.halo)
    pair_f1 = c.kept if plain else reduce_cores(tie(c.kept, sh.ng), c.sent)
    sb = own_body("self_body", s, sh, dec_rows, mats[4], True, places, pair_f1)
    kv = both_kv(
        low_rows, sh.own, back_c, mats[9:11], dec_rows, sb.own, back_s, mats[5:7], (c.five, sb.gq),
        (sh.dwo, sh.dwq, c.dwo), group, places,
    )
    out_dec = traded(kv.grad)
    if plain:
        dec_out, pair_a1 = restore(dec_out), kv.kept
    else:
        part_f1 = reduce_chips(pair_f1)
        dec_out = restore(tie(dec_out, part_f1))
        pair_a1 = reduce_cores(kv.kept, kv.sent)
    eh = enc_ffn_head(kv.encoded, e.resid, two, e, pack0, mats[3], gains, places, pair_a1)
    back_e = halo_return(eh.halo)
    if plain:
        pair_f0 = eh.kept
    else:
        part_a1 = reduce_chips(pair_a1)
        pair_f0 = reduce_cores(tie(eh.kept, part_a1), eh.sent)
    eb = own_body("enc_body", e, eh, enc_rows, mats[0], False, places, dec_out)
    norm_local = jnp.concatenate((eh.ng, eh.ng2, sh.ng, c.ng, c.ng8), axis=0)
    norm_local = norm_local.reshape(n_high, group, norm_count)
    norm_block = jnp.pad(
        norm_local.swapaxes(0, 1).astype(BF), ((0, 0), (0, 16 - n_high), (0, width - norm_count))
    )
    ek = enc_kv(
        enc_rows, eb.own, back_e, mats[1:3], (eh.late, eb.gq), (eb.dwq, eh.dwo, sb.dwq, kv.dwk),
        norm_block, group, places, pair_f0,
    )
    out_enc = traded(ek.grad)
    if plain:
        attn_own, up_own, down_own, norm_own = reduce_plain(
            from_parity(ek.kept, ek.sent)[:, :per],
            from_parity(kv.kept, kv.sent),
            from_parity(eh.kept, eh.sent),
            from_parity(c.kept, c.sent),
            norm_local,
        )
        grads = restore(out_enc, out_dec)
    else:
        part_f0 = reduce_chips(pair_f0)
        part_a0 = reduce_chips(reduce_cores(ek.kept, ek.sent))
        grads = restore(tie(out_enc, part_a0), out_dec)
        ffn_own = join_halves(part_f0, part_f1)
        both = join_halves(part_a0, jnp.concatenate((part_a1, part_a0[attn_rows:]), axis=0))
        attn_own, up_own, down_own = both[:attn_rows], unpack_up(ffn_own[128:]), ffn_own[:128]
        norm_own = lax.dynamic_index_in_dim(both[attn_rows:], high, 0, keepdims=False)[:norm_count]

    owned = (attn_own, up_own, down_own, norm_own)
    firsts = (attn_first, ffn_in_first, ffn_out_first, norm_first)
    seconds = (attn_second, ffn_in_second, ffn_out_second, norm_second)
    moments = [
        lamb_moments(masters[index], owned[index], firsts[index], seconds[index])
        for index in range(4)
    ]
    update_local = jnp.concatenate(
        [group_sum(onehots[index], row_squares(moments[index][2])) for index in range(4)]
    )
    squares = jnp.stack((weight_local, update_local))
    squares = jnp.pad(squares, ((0, 6), (0, 128 - squares.shape[1])))
    count = lax.axis_size(EVERY)
    squares = jnp.broadcast_to(squares[None], (count,) + squares.shape)
    squares = jnp.sum(lax.all_to_all(squares, EVERY, split_axis=0, concat_axis=0, tiled=True), axis=0)
    norms = jnp.sqrt(squares[:2, :26])
    ratio = norms[0] / norms[1]
    bounds_at = (0, 12, 14, 16, 26)
    new_weights = []
    for index in range(4):
        row_ratio = jnp.sum(
            jnp.where(onehots[index], ratio[None, bounds_at[index] : bounds_at[index + 1]], 0.0), axis=1
        )
        if masters[index].ndim == 2:
            row_ratio = row_ratio[:, None]
        new_weights.append(masters[index] - learn_rate * row_ratio * moments[index][2])
    return (
        enc_out,
        dec_out,
        grads[:, 0][:, None].astype(F32),
        grads[:, 1][:, None].astype(F32),
        *owned,
        *new_weights,
        *[item[0] for item in moments],
        *[item[1] for item in moments],
        *[item.astype(BF) for item in new_weights],
        norms,
        ratio,
    )


def solution(mesh):
    count_seq, count_stream = mesh.shape["seq"], mesh.shape["stream"]

    def run(*args):
        micro = args[0].shape[0]
        split = Mesh(
            mesh.devices.reshape(count_seq // micro, micro, count_stream // 2, 2), ("hi", "lo", "y", "c")
        )
        tokens = P(None, ("y", "c"), ("hi", "lo"), None)
        wide = P(EVERY, None)
        flat = P(EVERY)
        owned = (wide, wide, wide, flat)
        return jax.shard_map(
            shards,
            mesh=split,
            in_specs=(tokens, tokens, tokens, P(None, ("y", "c"), None), *owned, *owned, *owned),
            out_specs=(tokens, tokens, tokens, tokens, *owned, *owned, *owned, *owned, *owned, P(), P()),
            check_vma=False,
        )(*args)

    return run
```

```python
import types

import jax
import jax.numpy as jnp
from jax import lax
from jax.experimental import pallas as pl
from jax.experimental.pallas import tpu as pltpu
from jax.sharding import Mesh
from jax.sharding import PartitionSpec as P

HEADS = 8
STEP = 5
HALO = 256
TILE = 256

norm_eps = 1e-05
beta_one = 0.5
beta_two = 0.5
lamb_eps = 1e-06
weight_decay = 0.01
learn_rate = 0.5
masked_score = -1e30

BF = jnp.bfloat16
F32 = jnp.float32
MIB = 1024 * 1024


def dot_nn(a, b):
    return lax.dot_general(a, b, (((1,), (0,)), ((), ())), preferred_element_type=F32)


def dot_nt(a, b):
    return lax.dot_general(a, b, (((1,), (1,)), ((), ())), preferred_element_type=F32)


def dot_tn(a, b):
    return lax.dot_general(a, b, (((0,), (0,)), ((), ())), preferred_element_type=F32)


def norm_parts(rows):
    centre = rows - jnp.mean(rows, axis=-1, keepdims=True)
    inv = lax.rsqrt(jnp.mean(centre * centre, axis=-1, keepdims=True) + norm_eps)
    return centre * inv, inv


def norm_rows(rows, gain, bias):
    return norm_parts(rows)[0] * gain + bias


def norm_back(rows, gain, grad):
    unit, inv = norm_parts(rows)
    lead = grad * gain
    back = inv * (
        lead
        - jnp.mean(lead, axis=-1, keepdims=True)
        - unit * jnp.mean(lead * unit, axis=-1, keepdims=True)
    )
    return (
        back,
        jnp.sum(grad * unit, axis=0, keepdims=True),
        jnp.sum(grad, axis=0, keepdims=True),
    )


gelu_a = 0.7978845608028654
gelu_b = 0.044715


def gelu(v):
    return 0.5 * v * (1.0 + jnp.tanh(gelu_a * (v + gelu_b * (v * v * v))))


def gelu_both(v):
    sq = v * v
    t = jnp.tanh(gelu_a * (v + gelu_b * (sq * v)))
    half = 0.5 * (1.0 + t)
    slope = half + 0.5 * v * (1.0 - t * t) * (gelu_a * (1.0 + 3.0 * gelu_b * sq))
    return v * half, slope


def lane_low(shape):
    return lax.broadcasted_iota(jnp.int32, shape, 1) < 64


def shape_of(dtype, *dims):
    return jax.ShapeDtypeStruct(dims, dtype)


class Fetched:
    def __init__(self, ref, copies):
        self.ref, self.copies, self.shape = ref, copies, ref.shape

    def __getitem__(self, index):
        for copy in self.copies:
            copy.wait()
        self.copies = ()
        return self.ref[index]


def square(array, start, index):
    places, _, width = array.shape
    per = 6 * width // places
    pieces = []
    row, end = index * width, index * width + width
    while row < end:
        place, at = divmod(row, per)
        take = min(per - at, end - row)
        spot = slice(row - index * width, row - index * width + take)
        pieces.append(((place, slice(start + at, start + at + take)), spot))
        row += take
    return (array, (width, width), tuple(pieces))


def fused(name, program, core, small, ins, outs, flops, scratch=(), order=None):
    big, sources = [], []
    for item in ins.values():
        array = item[0] if isinstance(item, tuple) else item
        known = [index for index, other in enumerate(big) if other is array]
        sources.append(known[0] if known else len(big))
        if not known:
            big.append(array)
    shapes = [item[1] if isinstance(item, tuple) else item.shape for item in ins.values()]
    pieces = [item[2] if isinstance(item, tuple) else None for item in ins.values()]
    kinds = [big[source].dtype for source in sources]
    counts = [len(item) if item else 1 for item in pieces]
    n_small, n_big, n_out, extra = len(small), len(big), len(outs), 0 if order is None else 1

    def body(core_ref, *refs):
        small_refs, refs = refs[:n_small], refs[n_small:]
        big_refs, refs = refs[:n_big], refs[n_big + extra :]
        out_refs, refs = refs[:n_out], refs[n_out:]
        in_bufs, refs = refs[: len(ins)], refs[len(ins) :]
        out_bufs, refs = refs[:n_out], refs[n_out:]
        user, (in_sem, out_sem) = refs[:-2], refs[-2:]
        env = types.SimpleNamespace(**dict(zip(small, small_refs)))
        used, fetched = 0, []
        for key, source, piece, buf in zip(ins, sources, pieces, in_bufs):
            src = big_refs[source]
            copies = []
            for item in piece or (None,):
                if item is None:
                    copy = pltpu.make_async_copy(src, buf, in_sem.at[used])
                else:
                    copy = pltpu.make_async_copy(src.at[item[0]], buf.at[item[1]], in_sem.at[used])
                copy.start()
                copies.append(copy)
                used += 1
            setattr(env, key, Fetched(buf, copies))
            fetched.append(getattr(env, key))
        for key, buf in zip(outs, out_bufs):
            setattr(env, key, buf)
        leaving = [None] * n_out

        def store(*bufs):
            for buf in bufs:
                (index,) = [place for place in range(n_out) if out_bufs[place] is buf]
                leaving[index] = pltpu.make_async_copy(buf, out_refs[index], out_sem.at[index])
                leaving[index].start()

        program(env, core_ref, store, *user)
        store(*[buf for buf, copy in zip(out_bufs, leaving) if copy is None])
        for copy in leaving:
            copy.wait()
        for item in fetched:
            for copy in item.copies:
                copy.wait()

    vmem = pl.BlockSpec(memory_space=pltpu.VMEM)
    anywhere = pl.BlockSpec(memory_space=pl.ANY)
    size = sum(array.size * array.dtype.itemsize for array in big)
    results = pl.pallas_call(
        body,
        in_specs=[pl.BlockSpec(memory_space=pltpu.SMEM)] + [vmem] * n_small + [anywhere] * (n_big + extra),
        out_specs=tuple([anywhere] * n_out),
        out_shape=tuple(outs.values()),
        scratch_shapes=[pltpu.VMEM(shape, dtype) for shape, dtype in zip(shapes, kinds)]
        + [pltpu.VMEM(out.shape, out.dtype) for out in outs.values()]
        + list(scratch)
        + [pltpu.SemaphoreType.DMA((sum(counts),)), pltpu.SemaphoreType.DMA((n_out,))],
        compiler_params=pltpu.CompilerParams(vmem_limit_bytes=56 * MIB),
        cost_estimate=pl.CostEstimate(flops=flops, bytes_accessed=size, transcendentals=0),
        name=name,
    )(core, *small.values(), *big, *(() if order is None else (order,)))
    return types.SimpleNamespace(**dict(zip(outs, results)))


def tiles_of(core, rows, window):
    if window == rows + HALO:
        near = pl.multiple_of(core[1], HALO)
        return ((near, 0), (pl.multiple_of(rows - TILE - core[1], HALO), None))
    return ((0, 0), (rows - TILE, 1))


def key_rows(ref, lanes, rows, halo):
    if halo is None:
        return ref[0:rows, lanes]
    if halo == 0:
        return ref[0 : rows + HALO, lanes]
    return jnp.concatenate((ref[0:rows, lanes], ref[rows + HALO : rows + 2 * HALO, lanes]), axis=0)


def key_lanes(ref, row, rows, halo):
    if halo is None:
        return ref[row : row + 1, 0:rows]
    if halo == 0:
        return ref[row : row + 1, 0 : rows + HALO]
    return jnp.concatenate(
        (ref[row : row + 1, 0:rows], ref[row : row + 1, rows + HALO : rows + 2 * HALO]), axis=1
    )


def halves(shape):
    low = lane_low(shape)
    return low, ~low


def keep(mask, values):
    return jnp.where(mask, values, jnp.zeros_like(values))


def gain_rows(gains, index):
    return gains[index : index + 1, :], gains[index + 1 : index + 2, :]


def attn_fwd(core, causal, low_src, base, kv_src, weights, qcol, krow, q_out, k_out, v_out, o_out, lse_out, res_out):
    rows, _ = q_out.shape
    window = k_out.shape[0]
    w_q, w_k, w_v, w_o = weights
    queries = dot_nn(low_src(), w_q[...])
    q_out[...] = (queries.astype(BF).astype(F32) * 0.125).astype(BF)
    k_out[...] = dot_nn(kv_src[...], w_k[...]).astype(BF)
    v_out[...] = dot_nn(kv_src[...], w_v[...]).astype(BF)
    for offset, halo in tiles_of(core, rows, window):
        spot = pl.ds(offset, TILE)
        allowed = qcol[spot, 0:1] == key_lanes(krow, 0, rows, halo)
        if causal:
            allowed = allowed & (key_lanes(krow, 1, rows, halo) <= qcol[spot, 1:2])
        lane = lax.broadcasted_iota(jnp.int32, (TILE, 128), 1)
        packed = jnp.zeros((TILE, 128), F32)
        for pair in range(HEADS // 2):
            lanes = slice(pair * 128, pair * 128 + 128)
            q2 = q_out[spot, lanes]
            k2 = key_rows(k_out, lanes, rows, halo)
            v2 = key_rows(v_out, lanes, rows, halo)
            mixed = None
            for half in range(2):
                scores = dot_nt(keep(halves(q2.shape)[half], q2), k2)
                scores = jnp.where(allowed, scores, masked_score)
                top = jnp.max(scores, axis=-1, keepdims=True)
                weights = jnp.exp(scores - top)
                total = jnp.sum(weights, axis=-1, keepdims=True)
                probs = (weights * (1.0 / total)).astype(BF)
                part = dot_nn(probs, keep(halves(v2.shape)[half], v2))
                mixed = part if mixed is None else mixed + part
                packed = jnp.where(lane == 2 * pair + half, top + jnp.log(total), packed)
            o_out[spot, lanes] = mixed.astype(BF)
        lse_out[:, spot] = jnp.transpose(packed)[0:HEADS, :]
    res_out[...] = base() + dot_nn(o_out[...], w_o[...])


def score_grads(q2, do2, k2, v2, allowed, lse, delta):
    sums = None
    for half in range(2):
        qh = keep(halves(q2.shape)[half], q2)
        doh = keep(halves(do2.shape)[half], do2)
        scores = jnp.where(allowed, dot_nt(k2, qh), masked_score)
        probs = jnp.exp(scores - lse[half])
        gscores = (probs * (dot_nt(v2, doh) - delta[half])).astype(BF)
        parts = (
            dot_tn(gscores, keep(halves(k2.shape)[half], k2)),
            dot_nn(gscores, qh),
            dot_nn(probs.astype(BF), doh),
        )
        sums = parts if sums is None else tuple(a + b for a, b in zip(sums, parts))
    return sums


def attn_head(
    core, causal, grad, resid, o_in, q_in, k_in, v_in, lse_in, w_o, gains, gain_at, qrow, kcol,
    back_out, do_out, delta_out, dwo_out, halo_out, dqh_out, ng_out,
):
    rows, width = do_out.shape
    window = k_in.shape[0]
    back, dgain, dbias = norm_back(resid[...], gain_rows(gains, gain_at)[0], grad)
    back_out[...] = back
    ng_out[0:1, :] = dgain
    ng_out[1:2, :] = dbias
    branch = back.astype(BF)
    do_out[...] = dot_nt(branch, w_o[...]).astype(BF)
    mixed = do_out[...].astype(F32) * o_in[...].astype(F32)
    high = mixed.astype(BF)
    rest = (mixed - high.astype(F32)).astype(BF)
    head = lax.broadcasted_iota(jnp.int32, (16, width), 1) // (width // HEADS)
    which = (head == lax.broadcasted_iota(jnp.int32, (16, width), 0)).astype(F32).astype(BF)
    delta_out[...] = (dot_nt(which, high) + dot_nt(which, rest))[0:HEADS, :]
    for offset, halo in tiles_of(core, rows, window):
        if halo is None:
            continue
        spot = pl.ds(offset, TILE)
        keys = slice(rows + halo * HALO, rows + halo * HALO + HALO)
        here = slice(halo * HALO, halo * HALO + HALO)
        allowed = kcol[keys, 0:1] == qrow[0:1, spot]
        if causal:
            allowed = allowed & (kcol[keys, 1:2] <= qrow[1:2, spot])
        for pair in range(HEADS // 2):
            lanes = slice(pair * 128, pair * 128 + 128)
            heads = (2 * pair, 2 * pair + 1)
            dq2, dk2, dv2 = score_grads(
                q_in[spot, lanes],
                do_out[spot, lanes],
                k_in[keys, lanes],
                v_in[keys, lanes],
                allowed,
                [lse_in[h : h + 1, spot] for h in heads],
                [delta_out[h : h + 1, spot] for h in heads],
            )
            dqh_out[here, lanes] = dq2
            halo_out[0, here, lanes] = dk2.astype(BF)
            halo_out[1, here, lanes] = dv2.astype(BF)
    dwo_out[...] = dot_tn(o_in[...], branch).astype(BF)


def attn_body(
    core, causal, window, back, do_in, delta, dqh, low_src, q_in, k_in, v_in, lse_in, w_q, qrow, kcol,
    gq_out, dwq_out, own_out, dq_scr,
):
    rows, width = gq_out.shape
    for tile in range(rows // TILE):
        spot = slice(tile * TILE, tile * TILE + TILE)
        allowed = kcol[0:rows, 0:1] == qrow[0:1, spot]
        if causal:
            allowed = allowed & (kcol[0:rows, 1:2] <= qrow[1:2, spot])
        for pair in range(HEADS // 2):
            lanes = slice(pair * 128, pair * 128 + 128)
            heads = (2 * pair, 2 * pair + 1)
            dq2, dk2, dv2 = score_grads(
                q_in[spot, lanes],
                do_in[spot, lanes],
                k_in[0:rows, lanes],
                v_in[0:rows, lanes],
                allowed,
                [lse_in[h : h + 1, spot] for h in heads],
                [delta[h : h + 1, spot] for h in heads],
            )
            dq_scr[spot, lanes] = dq2
            if tile == 0:
                own_out[0, :, lanes] = dk2
                own_out[1, :, lanes] = dv2
            else:
                own_out[0, :, lanes] += dk2
                own_out[1, :, lanes] += dv2
    for offset, halo in tiles_of(core, rows, window):
        if halo is not None:
            dq_scr[pl.ds(offset, TILE), :] += dqh[halo * HALO : halo * HALO + HALO, :]
    grad_q = (dq_scr[...] * 0.125).astype(BF)
    gq_out[...] = back[...] + dot_nt(grad_q, w_q[...])
    dwq_out[...] = dot_tn(low_src(), grad_q).astype(BF)


def split_places(core, source, kept, sent):
    for parity in range(2):

        @pl.when(core[0] == parity)
        def place():
            for chip in range(kept.shape[0]):
                kept[chip] = source[2 * chip + parity]
                sent[chip] = source[2 * chip + 1 - parity]


def kv_bwd(core, offsets, src, own, halo, w_k, w_v, adds, scr):
    scr[...] = own[...]
    for index in range(halo.shape[1] // HALO):
        spot = pl.ds(pl.multiple_of(core[1], HALO) if offsets is None else offsets[index], HALO)
        scr[:, spot, :] += halo[:, index * HALO : index * HALO + HALO, :].astype(F32)
    dk = scr[0].astype(BF)
    dv = scr[1].astype(BF)
    total = dot_nt(dk, w_k[...]) + dot_nt(dv, w_v[...])
    for ref in adds:
        total = total + ref[...]
    return total, dot_tn(src[...], dk).astype(BF), dot_tn(src[...], dv).astype(BF)


def lay_out(stack, mats):
    places, _, width = stack.shape
    per = 6 * width // places
    for slot, matrix in enumerate(mats):
        row, end = slot * width, slot * width + width
        while row < end:
            place, start = divmod(row, per)
            take = min(per - start, end - row)
            at = row - slot * width
            stack[place, start : start + take, :] = matrix[at : at + take, :]
            row += take


def pick(pack, place, rows):
    mine, other, core = pack
    chip = place // 2
    return jnp.where(core[0] == place % 2, mine[chip, rows, :], other[chip, rows, :])


def up_tile(pack, tile):
    spot = slice(128 + 32 * tile, 160 + 32 * tile)
    return jnp.concatenate([pick(pack, place, spot) for place in range(2 * pack[0].shape[0])], axis=0)


def down_tile(pack, tile):
    return jnp.concatenate([pick(pack, 4 * tile + step, slice(0, 128)) for step in range(4)], axis=0)


def ffn_fwd(resid, base, gains, gain_in, gain_out, pack, res_out, low_out, hid_low=None, pre=None):
    hidden = norm_rows(resid[...], *gain_rows(gains, gain_in))
    low = hidden.astype(BF)
    if hid_low is not None:
        hid_low[...] = low
    res_out[...] = hidden + base[...].astype(F32)
    for tile in range(4):
        values = dot_nn(low, up_tile(pack, tile))
        if pre is not None:
            pre[tile] = values
        res_out[...] += dot_nn(gelu(values).astype(BF), down_tile(pack, tile))
    low_out[...] = norm_rows(res_out[...], *gain_rows(gains, gain_out)).astype(BF)


def ffn_bwd(grad, res_late, gains, gain_out, pack, gh_out, late_out, ng_out, hid_low, late_low, dpack, pre=None):
    back, dgain, dbias = norm_back(res_late[...], gain_rows(gains, gain_out)[0], grad)
    late_out[...] = back
    gh_out[...] = back
    late_low[...] = back.astype(BF)
    ng_out[0:1, :] = dgain
    ng_out[1:2, :] = dbias
    places, _, width = dpack.shape
    for tile in range(4):
        activ, slope = gelu_both(dot_nn(hid_low[...], up_tile(pack, tile)) if pre is None else pre[tile])
        grad_down = dot_tn(activ.astype(BF), late_low[...]).astype(BF)
        dpack[4 * tile : 4 * tile + 4, 0:128, :] = grad_down.reshape(4, 128, width)
        grad_act = dot_nt(late_low[...], down_tile(pack, tile)).astype(BF).astype(F32)
        grad_pre = (grad_act * slope).astype(BF)
        grad_up = dot_tn(hid_low[...], grad_pre).astype(BF)
        dpack[:, 128 + 32 * tile : 160 + 32 * tile, :] = grad_up.reshape(places, 32, width)
        gh_out[...] += dot_nt(grad_pre, up_tile(pack, tile))


def kept_shapes(rows, window, width, with_o=True):
    outs = dict(
        q=shape_of(BF, rows, width),
        k=shape_of(BF, window, width),
        v=shape_of(BF, window, width),
        lse=shape_of(F32, HEADS, rows),
    )
    return dict(outs, o=shape_of(BF, rows, width)) if with_o else outs


def head_shapes(rows, window, width):
    return dict(
        back=shape_of(F32, rows, width),
        do=shape_of(BF, rows, width),
        delta=shape_of(F32, HEADS, rows),
        dwo=shape_of(BF, width, width),
        halo=shape_of(BF, 2, window - rows, width),
        dqh=shape_of(F32, window - rows, width),
        ng=shape_of(F32, 2, width),
    )


def weights_of(env):
    return env.wq, env.wk, env.wv, env.wo


def named_mats(mats):
    return dict(wq=mats[0], wk=mats[1], wv=mats[2], wo=mats[3])


def input_attention(name, x, window_rows, mats, causal, places):
    rows, width = x.shape
    window = window_rows.shape[0]

    def program(e, core, store):
        attn_fwd(
            core, causal, lambda: e.x[...], lambda: e.x[...].astype(F32), e.window, weights_of(e),
            e.qcol, e.krow, e.q, e.k, e.v, e.o, e.lse, e.resid,
        )

    return fused(
        name,
        program,
        places.core,
        dict(qcol=places.qcol, krow=places.krow),
        dict(x=x, window=window_rows, **named_mats(mats)),
        dict(kept_shapes(rows, window, width), resid=shape_of(F32, rows, width)),
        12 * rows * width * width + 8 * rows * window * width,
    )


def enc_ffn(one, x, pack, gains, places):
    rows, width = x.shape

    def program(e, core, store):
        ffn_fwd(e.one, e.x, e.gains, 0, 2, (e.mine, e.other, core), e.two, e.low)

    outs = fused(
        "enc_ffn",
        program,
        places.core,
        dict(gains=gains),
        dict(one=one, x=x, mine=pack[0], other=pack[1]),
        dict(low=shape_of(BF, rows, width), two=shape_of(F32, rows, width)),
        16 * rows * width * width,
    )
    return outs.two, outs.low


def cross_and_ffn(three, window_rows, mats, pack, z, cot, gains, places, order):
    rows, width = three.shape
    window = window_rows.shape[0]
    count, block = 2 * pack[0].shape[0], pack[0].shape[1]
    f32_rows, low_rows = pltpu.VMEM((rows, width), F32), pltpu.VMEM((rows, width), BF)

    def program(e, core, store, o, four, five, gh, hid_low, late_low, pre, dpack):
        def first():
            return norm_rows(e.three[...], *gain_rows(e.gains, 4))

        attn_fwd(
            core, False, lambda: first().astype(BF), first, e.window, weights_of(e),
            e.qcol, e.krow, e.q, e.k, e.v, o, e.lse, four,
        )
        store(e.q, e.k, e.v, e.lse)
        pack = (e.mine, e.other, core)
        ffn_fwd(four, e.z, e.gains, 6, 8, pack, five, e.low, hid_low, pre)
        store(e.low)
        ffn_bwd(
            e.cot[...].astype(F32), five, e.gains, 8, pack, gh, e.five, e.ng8,
            hid_low, late_low, dpack, pre,
        )
        split_places(core, dpack, e.kept, e.sent)
        store(e.sent, e.kept, e.five, e.ng8)
        attn_head(
            core, False, gh[...], four, o, e.q, e.k, e.v, e.lse, e.wo, e.gains, 6,
            e.qrow, e.kcol, e.back, e.do, e.delta, e.dwo, e.halo, e.dqh, e.ng,
        )

    return fused(
        "cross_and_ffn",
        program,
        places.core,
        dict(qcol=places.qcol, krow=places.krow, qrow=places.qrow, kcol=places.kcol, gains=gains),
        dict(three=three, wq=mats[0], window=window_rows, wk=mats[1], wv=mats[2], wo=mats[3], z=z, mine=pack[0], other=pack[1], cot=cot),
        dict(
            **kept_shapes(rows, window, width, False),
            low=shape_of(BF, rows, width),
            kept=shape_of(BF, count // 2, block, width),
            sent=shape_of(BF, count // 2, block, width),
            five=shape_of(F32, rows, width),
            ng8=shape_of(F32, 2, width),
            **head_shapes(rows, window, width),
        ),
        68 * rows * width * width + 8 * rows * window * width,
        scratch=[
            low_rows, f32_rows, f32_rows, f32_rows, low_rows, low_rows,
            pltpu.VMEM((4, rows, width), F32), pltpu.VMEM((count, block, width), BF),
        ],
        order=order,
    )


def cross_body_self_head(c, three, s, mat_q, mat_o, gains, places, order):
    rows, width = three.shape
    window = c.k.shape[0]
    own = (slice(0, rows),)

    def program(e, core, store, grad, dq):
        def first():
            return norm_rows(e.three[...], *gain_rows(e.gains, 4)).astype(BF)

        attn_body(
            core, False, window, e.back_c, e.do_c, e.delta_c, e.dqh_c, first, e.q_c, e.k_c,
            e.v_c, e.lse_c, e.wq, e.qrow, e.kcol, grad, e.dwq, e.own, dq,
        )
        store(e.own, e.dwq)
        attn_head(
            core, True, grad[...], e.three, e.o, e.q, e.k, e.v, e.lse, e.wo, e.gains, 4,
            e.qrow, e.kcol, e.back, e.do, e.delta, e.dwo, e.halo, e.dqh, e.ng,
        )

    return fused(
        "cross_body_self_head",
        program,
        places.core,
        dict(qrow=places.qrow, kcol=places.kcol, gains=gains),
        dict(
            q_c=c.q,
            do_c=c.do,
            k_c=(c.k, (rows, width), ((own, own),)),
            v_c=(c.v, (rows, width), ((own, own),)),
            lse_c=c.lse,
            delta_c=c.delta,
            dqh_c=c.dqh,
            back_c=c.back,
            wq=mat_q,
            three=three,
            wo=mat_o,
            o=s.o,
            q=s.q,
            k=s.k,
            v=s.v,
            lse=s.lse,
        ),
        dict(
            own=shape_of(F32, 2, rows, width),
            dwq=shape_of(BF, width, width),
            **head_shapes(rows, window, width),
        ),
        8 * rows * width * width + 10 * rows * window * width,
        scratch=[pltpu.VMEM((rows, width), F32), pltpu.VMEM((rows, width), F32)],
        order=order,
    )


def own_body(name, kept, head, src, mat_q, causal, places, order):
    rows, width = src.shape
    window = kept.k.shape[0]
    own = (slice(0, rows),)

    def program(e, core, store, dq):
        attn_body(
            core, causal, window, e.back, e.do, e.delta, e.dqh, lambda: e.src[...], e.q, e.k,
            e.v, e.lse, e.wq, e.qrow, e.kcol, e.gq, e.dwq, e.own, dq,
        )

    return fused(
        name,
        program,
        places.core,
        dict(qrow=places.qrow, kcol=places.kcol),
        dict(
            q=kept.q,
            do=head.do,
            k=(kept.k, (rows, width), ((own, own),)),
            v=(kept.v, (rows, width), ((own, own),)),
            lse=kept.lse,
            delta=head.delta,
            dqh=head.dqh,
            back=head.back,
            wq=mat_q,
            src=src,
        ),
        dict(
            own=shape_of(F32, 2, rows, width),
            gq=shape_of(F32, rows, width),
            dwq=shape_of(BF, width, width),
        ),
        4 * rows * width * width + 10 * rows * rows * width,
        scratch=[pltpu.VMEM((rows, width), F32)],
        order=order,
    )


def both_kv(low, own_c, halo_c, mats_c, z, own_s, halo_s, mats_s, adds, grads, group, places, order):
    rows, width = low.shape
    per = 6 * width // group

    def program(e, core, store, scr, stack):
        total, dwk, dwv = kv_bwd(core, places.offsets, e.low, e.own_c, e.halo_c, e.wk_c, e.wv_c, (), scr)
        e.encoded[...] = total
        store(e.encoded)
        total, e.dwk[...], dwv_s = kv_bwd(
            core, places.offsets, e.z, e.own_s, e.halo_s, e.wk_s, e.wv_s, (e.add0, e.add1), scr
        )
        e.grad[...] = total.astype(BF)
        store(e.grad, e.dwk)
        lay_out(stack, (dwv_s, e.dwo_s, e.dwq_c, dwk, dwv, e.dwo_c))
        split_places(core, stack, e.kept, e.sent)

    return fused(
        "both_kv",
        program,
        places.core,
        dict(),
        dict(
            own_c=own_c,
            halo_c=halo_c,
            wk_c=mats_c[0],
            wv_c=mats_c[1],
            low=low,
            own_s=own_s,
            halo_s=halo_s,
            wk_s=mats_s[0],
            wv_s=mats_s[1],
            add0=adds[0],
            add1=adds[1],
            z=z,
            dwo_s=grads[0],
            dwq_c=grads[1],
            dwo_c=grads[2],
        ),
        dict(
            encoded=shape_of(F32, rows, width),
            grad=shape_of(BF, rows, width),
            dwk=shape_of(BF, width, width),
            sent=shape_of(BF, group // 2, per, width),
            kept=shape_of(BF, group // 2, per, width),
        ),
        16 * rows * width * width,
        scratch=[pltpu.VMEM((2, rows, width), F32), pltpu.VMEM((group, per, width), BF)],
        order=order,
    )


def enc_ffn_head(grad, one, two, kept, pack, mat_o, gains, places, order):
    rows, width = one.shape
    window = kept.k.shape[0]
    count, block = 2 * pack[0].shape[0], pack[0].shape[1]

    def program(e, core, store, gh, hid_low, late_low, dpack):
        hid_low[...] = norm_rows(e.one[...], *gain_rows(e.gains, 0)).astype(BF)
        ffn_bwd(
            e.grad[...], e.two, e.gains, 2, (e.mine, e.other, core), gh, e.late, e.ng2, hid_low, late_low, dpack
        )
        split_places(core, dpack, e.kept, e.sent)
        store(e.sent, e.kept, e.late, e.ng2)
        attn_head(
            core, False, gh[...], e.one, e.o, e.q, e.k, e.v, e.lse, e.wo, e.gains, 0,
            e.qrow, e.kcol, e.back, e.do, e.delta, e.dwo, e.halo, e.dqh, e.ng,
        )

    return fused(
        "enc_ffn_head",
        program,
        places.core,
        dict(qrow=places.qrow, kcol=places.kcol, gains=gains),
        dict(
            one=one,
            two=two,
            grad=grad,
            mine=pack[0],
            other=pack[1],
            wo=mat_o,
            o=kept.o,
            q=kept.q,
            k=kept.k,
            v=kept.v,
            lse=kept.lse,
        ),
        dict(
            sent=shape_of(BF, count // 2, block, width),
            kept=shape_of(BF, count // 2, block, width),
            late=shape_of(F32, rows, width),
            ng2=shape_of(F32, 2, width),
            **head_shapes(rows, window, width),
        ),
        44 * rows * width * width + 10 * TILE * TILE * width,
        scratch=[
            pltpu.VMEM((rows, width), F32), pltpu.VMEM((rows, width), BF), pltpu.VMEM((rows, width), BF),
            pltpu.VMEM((count, block, width), BF),
        ],
        order=order,
    )


def enc_kv(x, own, halo, mats, adds, grads, norms, group, places, order):
    rows, width = x.shape
    per = 6 * width // group
    block = per + 16

    def program(e, core, store, scr, stack, lines):
        total, dwk, dwv = kv_bwd(
            core, places.offsets, e.x, e.own, e.halo, e.wk, e.wv, (e.add0, e.add1), scr
        )
        lay_out(stack, (e.dwq_e, dwk, dwv, e.dwo_e, e.dwq_s, e.dwk_s))
        lines[...] = jnp.zeros_like(lines)
        for index, item in enumerate((e.ng0, e.ng1, e.ng2, e.ng3, e.ng4)):
            lines[2 * index : 2 * index + 2, :] = item[...]
        for place in range(group):
            stack[place, per:, :] = lines[...].astype(BF)
        split_places(core, stack, e.kept, e.sent)
        store(e.sent, e.kept)
        e.grad[...] = total.astype(BF)

    return fused(
        "enc_kv",
        program,
        places.core,
        dict(),
        dict(
            own=own,
            halo=halo,
            wk=mats[0],
            wv=mats[1],
            x=x,
            dwq_e=grads[0],
            dwo_e=grads[1],
            dwq_s=grads[2],
            dwk_s=grads[3],
            ng0=norms[0],
            ng1=norms[1],
            ng2=norms[2],
            ng3=norms[3],
            ng4=norms[4],
            add0=adds[0],
            add1=adds[1],
        ),
        dict(
            sent=shape_of(BF, group // 2, block, width),
            kept=shape_of(BF, group // 2, block, width),
            grad=shape_of(BF, rows, width),
        ),
        8 * rows * width * width,
        scratch=[
            pltpu.VMEM((2, rows, width), F32), pltpu.VMEM((group, block, width), BF), pltpu.VMEM((16, width), F32),
        ],
        order=order,
    )


def segments_at(bounds, places, total_len):
    found = jnp.sum((bounds[None, :] <= places[:, None]).astype(jnp.int32), axis=-1)
    return jnp.where((places >= 0) & (places < total_len), found, -1)


def row_squares(values):
    if values.ndim == 2:
        return jnp.sum(values * values, axis=1)
    return values * values


def owner_groups(rows_local, owner, per_group, count):
    group_ids = (owner * rows_local + jnp.arange(rows_local, dtype=jnp.int32)) // per_group
    return group_ids[:, None] == jnp.arange(count, dtype=jnp.int32)[None, :]


def group_sum(onehot, row_values):
    return jnp.sum(jnp.where(onehot, row_values[:, None], 0.0), axis=0)


def lamb_moments(master, grad_rows, first, second):
    first_new = beta_one * first + (1.0 - beta_one) * grad_rows
    second_new = beta_two * second + (1.0 - beta_two) * grad_rows * grad_rows
    update = (
        first_new
        / (1.0 - beta_one**STEP)
        / (jnp.sqrt(second_new / (1.0 - beta_two**STEP)) + lamb_eps)
        + weight_decay * master
    )
    return (first_new, second_new, update)


GROUP = ("lo", "y", "c")
CHIPS = ("lo", "y")
EVERY = ("hi", "lo", "y", "c")


def swap_hi(array):
    return lax.ppermute(array, "hi", [(0, 1), (1, 0)])


def shift_hi(array, distance):
    count = lax.axis_size("hi")
    route = [(i - distance, i) for i in range(count) if i - distance in range(count)]
    return lax.ppermute(array, "hi", route)


def halo_rows(rows_array):
    rows = rows_array.shape[0]
    if lax.axis_size("hi") == 2:
        return swap_core(jnp.where(lax.axis_index("c") == 0, rows_array[rows - HALO :], rows_array[:HALO]))
    left = shift_hi(rows_array[rows - HALO :], 1)
    right = shift_hi(rows_array[:HALO], -1)
    return jnp.concatenate((left, right), axis=0)


def halo_return(grads):
    if lax.axis_size("hi") == 2:
        return swap_core(grads)
    to_left = shift_hi(grads[:, :HALO], -1)
    to_right = shift_hi(grads[:, HALO:], 1)
    return jnp.concatenate((to_left, to_right), axis=1)


def trade(array):
    return lax.ppermute(array, ("hi", "c"), [(0, 0), (1, 2), (2, 1), (3, 3)])


def pack_up(rows):
    count, units = rows.shape
    return rows.reshape(count, 4, units // 4).swapaxes(0, 1).reshape(4 * count, units // 4)


def unpack_up(packed):
    count, width = packed.shape
    return packed.reshape(4, count // 4, width).swapaxes(0, 1).reshape(count // 4, 4 * width)


def swap_core(array):
    return lax.ppermute(array, "c", [(0, 1), (1, 0)])


def tie(array, other):
    bit = lax.slice(other, (0,) * other.ndim, (1,) * other.ndim).reshape(()) * 0
    return array + bit.astype(array.dtype)


def spread_chips(shard):
    count = lax.axis_size(CHIPS)
    sent = jnp.broadcast_to(shard[None], (count,) + shard.shape)
    return lax.all_to_all(sent, CHIPS, split_axis=0, concat_axis=0, tiled=True)


def by_parity(full):
    even = lax.axis_index("c") == 0
    view = full.reshape(full.shape[0] // 2, 2, *full.shape[1:])
    return jnp.where(even, view[:, 0], view[:, 1]), jnp.where(even, view[:, 1], view[:, 0])


def from_parity(mine, other):
    even = lax.axis_index("c") == 0
    full = jnp.stack((jnp.where(even, mine, other), jnp.where(even, other, mine)), axis=1)
    return full.reshape(-1, *mine.shape[1:])


def gather_plain(attn_shard, up_shard, down_shard, norm_shard):
    width = attn_shard.shape[1]
    group = lax.axis_size(GROUP)
    norm_count = norm_shard.shape[0]
    attn = lax.all_gather(attn_shard, EVERY, axis=0, tiled=True)
    down = lax.all_gather(down_shard, EVERY, axis=0, tiled=True).reshape(2, group, -1, width)
    up = lax.all_gather(up_shard, EVERY, axis=0, tiled=True)
    up = up.reshape(2, group, -1, 4, width).swapaxes(2, 3).reshape(2, group, -1, width)
    norms = jnp.pad(norm_shard[None, :], ((0, 0), (0, width - norm_count)))
    norms = lax.all_gather(norms, EVERY, axis=0, tiled=True)[:, :norm_count]
    ffn = jnp.concatenate((down, up), axis=2)
    attn = attn.reshape(2, group, -1, width)
    full = jnp.concatenate((attn[0], attn[1]), axis=1)
    return full, by_parity(ffn[0]), by_parity(ffn[1]), norms.reshape(10, width).astype(F32)


def reduce_cores(kept, sent):
    return (kept.astype(F32) + swap_core(sent).astype(F32)).astype(BF)


def reduce_chips(pair):
    parts = lax.all_to_all(pair, CHIPS, split_axis=0, concat_axis=0, tiled=True)
    return jnp.sum(parts.astype(F32), axis=0)


def join_halves(zero, one):
    first = lax.axis_index("hi") == 0
    mine = jnp.where(first, zero, one)
    sent = jnp.where(first, one, zero).astype(BF)
    return mine + swap_hi(sent).astype(F32)


def reduce_plain(attn0, attn1, ffn0, ffn1, norm_local):
    group, _, width = ffn0.shape

    def scatter(rows):
        return lax.psum_scatter(rows, EVERY, scatter_dimension=0, tiled=True).astype(F32)

    attn = jnp.concatenate((attn0, attn1), axis=0).reshape(-1, width)
    ffn = jnp.stack((ffn0, ffn1)).reshape(2 * group, -1, width)
    up = ffn[:, 128:].reshape(2 * group, 4, 32, width).swapaxes(1, 2).reshape(-1, 4 * width)
    norms = lax.psum_scatter(
        norm_local.reshape(lax.axis_size(EVERY), -1), EVERY, scatter_dimension=0, tiled=True
    )
    return scatter(attn), scatter(up), scatter(ffn[:, :128].reshape(-1, width)), norms[0]


def shards(
    enc_in,
    dec_in,
    cotangent,
    lengths,
    attn_master,
    ffn_in_master,
    ffn_out_master,
    norm_master,
    attn_first,
    ffn_in_first,
    ffn_out_first,
    norm_first,
    attn_second,
    ffn_in_second,
    ffn_out_second,
    norm_second,
):
    micro, _, length_dev, width = enc_in.shape
    rows = micro * length_dev
    hidden_units = ffn_in_master.shape[1]
    high, low = lax.axis_index("hi"), lax.axis_index("lo")
    n_high = lax.axis_size("hi")
    owner = lax.axis_index(EVERY)
    masters = (attn_master, ffn_in_master, ffn_out_master, norm_master)
    group_info = ((width, 12), (width, 2), (hidden_units, 2), (width, 10))
    onehots = [
        owner_groups(master.shape[0], owner, info[0], info[1])
        for master, info in zip(masters, group_info)
    ]
    weight_local = jnp.concatenate(
        [group_sum(onehot, row_squares(master)) for onehot, master in zip(onehots, masters)]
    )

    plain = n_high != 2

    def regroup(*arrays):
        packed = jnp.stack([array[:, 0] for array in arrays], axis=1)
        packed = lax.all_to_all(packed, "lo", split_axis=0, concat_axis=0, tiled=True)
        packed = packed.swapaxes(0, 1).reshape(len(arrays), rows, width)
        return packed if plain else trade(packed)

    part = high if plain else lax.axis_index("c")
    core = jnp.stack((lax.axis_index("c"), jnp.where(part == 0, rows - HALO, 0))).astype(jnp.int32)
    attn_rows = attn_master.shape[0]
    norm_count = norm_master.shape[0]
    attn_low, up_low, down_low, norm_low = [master.astype(BF) for master in masters]
    if plain:
        full, pack0, pack1, gains = gather_plain(attn_low, up_low, down_low, norm_low)
        enc_rows, dec_rows, cot_rows = regroup(enc_in, dec_in, cotangent)
        enc_halo = halo_rows(enc_rows)
    else:
        first = high == 0
        norm_pad = jnp.pad(norm_low[None, :], ((0, 15), (0, width - norm_count)))
        mine = jnp.concatenate((attn_low, norm_pad), axis=0)
        other = swap_hi(mine)
        (enc_rows,) = regroup(enc_in)
        zero = jnp.where(first, mine, other)
        one = jnp.where(first, other, mine)
        early = (zero[:attn_rows], one[:attn_rows], zero[attn_rows : attn_rows + 1], one[attn_rows:-1])
        early = jnp.concatenate(early, axis=0)
        full = lax.all_gather(early, GROUP, axis=0, tiled=False)
        enc_halo = halo_rows(tie(enc_rows, early))
        mine = tie(jnp.concatenate((down_low, pack_up(up_low)), axis=0), early)
        other = swap_hi(mine)
        near = spread_chips(tie(jnp.where(first, mine, other), enc_halo))
        (dec_rows,) = regroup(tie(dec_in, near))
        far = spread_chips(tie(jnp.where(first, other, mine), dec_rows))
        (cot_rows,) = regroup(tie(cotangent, far))
        pack0, pack1 = (near, swap_core(near)), (far, swap_core(far))
        gains = full[:, 2 * attn_rows : 2 * attn_rows + 2, :norm_count].swapaxes(0, 1)
        gains = gains.reshape(10, width).astype(F32)
    enc_window = jnp.concatenate((enc_rows, enc_halo), axis=0)
    dec_window = jnp.concatenate((dec_rows, halo_rows(dec_rows)), axis=0)
    group = full.shape[0]

    total_len = rows * n_high
    bounds = jnp.cumsum(lengths[:, 0, :], axis=-1)
    bounds = lax.dynamic_index_in_dim(bounds, low, 0, keepdims=False)
    bounds = bounds if plain else trade(bounds)
    base = part * rows
    own_pos = base + jnp.arange(rows, dtype=jnp.int32)
    step = jnp.arange(HALO, dtype=jnp.int32)
    if n_high == 2:
        halo_pos = jnp.where(part == 0, rows, rows - HALO) + step
    else:
        halo_pos = jnp.concatenate((base - HALO + step, base + rows + step))
    key_pos = jnp.concatenate((own_pos, halo_pos))
    key_seg = segments_at(bounds, key_pos, total_len)
    krow = jnp.stack((key_seg, key_pos), axis=0)
    kcol = jnp.stack((key_seg, key_pos), axis=1)
    places = types.SimpleNamespace(
        krow=krow,
        kcol=kcol,
        qrow=krow[:, :rows],
        qcol=kcol[:rows],
        offsets=None if n_high == 2 else (0, rows - HALO),
        core=core,
    )

    per = 6 * width // group
    mats = [square(full, 0, index) for index in range(6)] + [square(full, per, index) for index in range(6)]
    e = input_attention("enc_attention", enc_rows, enc_window, mats[0:4], False, places)
    s = input_attention("self_attention", dec_rows, dec_window, mats[4:8], True, places)
    two, low_rows = enc_ffn(e.resid, enc_rows, pack0, gains, places)
    low_window = jnp.concatenate((low_rows, halo_rows(low_rows)), axis=0)

    def restore(*arrays):
        outs = jnp.stack(arrays, axis=0).reshape(len(arrays), micro, length_dev, width).swapaxes(0, 1)
        return lax.all_to_all(outs, "lo", split_axis=0, concat_axis=0, tiled=True)

    def traded(array):
        return array if plain else trade(array)

    enc_out = traded(low_rows)
    c = cross_and_ffn(s.resid, low_window, mats[8:12], pack1, dec_rows, cot_rows, gains, places, enc_out)

    dec_out = traded(c.low)
    back_c = halo_return(c.halo)
    sh = cross_body_self_head(c, s.resid, s, mats[8], mats[7], gains, places, None)
    back_s = halo_return(sh.halo)
    pair_f1 = c.kept if plain else reduce_cores(tie(c.kept, sh.ng), c.sent)
    sb = own_body("self_body", s, sh, dec_rows, mats[4], True, places, pair_f1)
    kv = both_kv(
        low_rows, sh.own, back_c, mats[9:11], dec_rows, sb.own, back_s, mats[5:7], (c.five, sb.gq),
        (sh.dwo, sh.dwq, c.dwo), group, places, dec_out,
    )
    out_dec = traded(kv.grad)
    if plain:
        pair_a1, pair_f0 = kv.kept, None
        outs = restore(enc_out, dec_out, out_dec)
    else:
        part_f1 = reduce_chips(pair_f1)
        pair_a1 = reduce_cores(kv.kept, kv.sent)
        part_a1 = reduce_chips(pair_a1)
        outs = restore(tie(enc_out, part_a1), dec_out, out_dec)
    eh = enc_ffn_head(kv.encoded, e.resid, two, e, pack0, mats[3], gains, places, pair_a1)
    back_e = halo_return(eh.halo)
    eb = own_body("enc_body", e, eh, enc_rows, mats[0], False, places, out_dec)
    if not plain:
        pair_f0 = reduce_cores(tie(eh.kept, part_a1), eh.sent)
    norm_grads = (eh.ng, eh.ng2, sh.ng, c.ng, c.ng8)
    ek = enc_kv(
        enc_rows, eb.own, back_e, mats[1:3], (eh.late, eb.gq), (eb.dwq, eh.dwo, sb.dwq, kv.dwk),
        norm_grads, group, places, pair_f0,
    )
    out_enc = traded(ek.grad)
    if plain:
        attn_own, up_own, down_own, norm_own = reduce_plain(
            from_parity(ek.kept, ek.sent)[:, :per],
            from_parity(kv.kept, kv.sent),
            from_parity(eh.kept, eh.sent),
            from_parity(c.kept, c.sent),
            jnp.concatenate(norm_grads, axis=0).reshape(n_high, group, norm_count),
        )
        enc_grad = restore(out_enc)
    else:
        part_f0 = reduce_chips(pair_f0)
        part_a0 = reduce_chips(reduce_cores(ek.kept, ek.sent))
        enc_grad = restore(tie(out_enc, part_a0))
        ffn_own = join_halves(part_f0, part_f1)
        both = join_halves(part_a0, jnp.concatenate((part_a1, part_a0[attn_rows:]), axis=0))
        attn_own, up_own, down_own = both[:attn_rows], unpack_up(ffn_own[128:]), ffn_own[:128]
        norm_own = lax.dynamic_slice_in_dim(both[attn_rows:].reshape(-1), owner * norm_count, norm_count)

    owned = (attn_own, up_own, down_own, norm_own)
    firsts = (attn_first, ffn_in_first, ffn_out_first, norm_first)
    seconds = (attn_second, ffn_in_second, ffn_out_second, norm_second)
    moments = [
        lamb_moments(masters[index], owned[index], firsts[index], seconds[index])
        for index in range(4)
    ]
    update_local = jnp.concatenate(
        [group_sum(onehots[index], row_squares(moments[index][2])) for index in range(4)]
    )
    squares = jnp.stack((weight_local, update_local))
    squares = jnp.pad(squares, ((0, 6), (0, 128 - squares.shape[1])))
    count = lax.axis_size(EVERY)
    squares = tie(squares, enc_grad)
    squares = jnp.broadcast_to(squares[None], (count,) + squares.shape)
    squares = jnp.sum(lax.all_to_all(squares, EVERY, split_axis=0, concat_axis=0, tiled=True), axis=0)
    norms = jnp.sqrt(squares[:2, :26])
    ratio = norms[0] / norms[1]
    bounds_at = (0, 12, 14, 16, 26)
    new_weights = []
    for index in range(4):
        row_ratio = jnp.sum(
            jnp.where(onehots[index], ratio[None, bounds_at[index] : bounds_at[index + 1]], 0.0), axis=1
        )
        if masters[index].ndim == 2:
            row_ratio = row_ratio[:, None]
        new_weights.append(masters[index] - learn_rate * row_ratio * moments[index][2])
    return (
        outs[:, 0][:, None],
        outs[:, 1][:, None],
        enc_grad.astype(F32),
        outs[:, 2][:, None].astype(F32),
        *owned,
        *new_weights,
        *[item[0] for item in moments],
        *[item[1] for item in moments],
        *[item.astype(BF) for item in new_weights],
        norms,
        ratio,
    )


def solution(mesh):
    count_seq, count_stream = mesh.shape["seq"], mesh.shape["stream"]

    def run(*args):
        micro = args[0].shape[0]
        split = Mesh(
            mesh.devices.reshape(count_seq // micro, micro, count_stream // 2, 2), ("hi", "lo", "y", "c")
        )
        tokens = P(None, ("y", "c"), ("hi", "lo"), None)
        wide = P(EVERY, None)
        flat = P(EVERY)
        owned = (wide, wide, wide, flat)
        return jax.shard_map(
            shards,
            mesh=split,
            in_specs=(tokens, tokens, tokens, P(None, ("y", "c"), None), *owned, *owned, *owned),
            out_specs=(tokens, tokens, tokens, tokens, *owned, *owned, *owned, *owned, *owned, P(), P()),
            check_vma=False,
        )(*args)

    return run
```

```python
import types

import jax
import jax.numpy as jnp
from jax import lax
from jax.experimental import pallas as pl
from jax.experimental.pallas import tpu as pltpu
from jax.sharding import Mesh
from jax.sharding import PartitionSpec as P

HEADS = 8
STEP = 5
HALO = 256
TILE = 256

norm_eps = 1e-05
beta_one = 0.5
beta_two = 0.5
lamb_eps = 1e-06
weight_decay = 0.01
learn_rate = 0.5
masked_score = -1e30

BF = jnp.bfloat16
F32 = jnp.float32
MIB = 1024 * 1024


def dot_nn(a, b):
    return lax.dot_general(a, b, (((1,), (0,)), ((), ())), preferred_element_type=F32)


def dot_nt(a, b):
    return lax.dot_general(a, b, (((1,), (1,)), ((), ())), preferred_element_type=F32)


def dot_tn(a, b):
    return lax.dot_general(a, b, (((0,), (0,)), ((), ())), preferred_element_type=F32)


def norm_parts(rows):
    centre = rows - jnp.mean(rows, axis=-1, keepdims=True)
    inv = lax.rsqrt(jnp.mean(centre * centre, axis=-1, keepdims=True) + norm_eps)
    return centre * inv, inv


def norm_rows(rows, gain, bias):
    return norm_parts(rows)[0] * gain + bias


def norm_back(rows, gain, grad):
    unit, inv = norm_parts(rows)
    lead = grad * gain
    back = inv * (
        lead
        - jnp.mean(lead, axis=-1, keepdims=True)
        - unit * jnp.mean(lead * unit, axis=-1, keepdims=True)
    )
    return (
        back,
        jnp.sum(grad * unit, axis=0, keepdims=True),
        jnp.sum(grad, axis=0, keepdims=True),
    )


gelu_a = 0.7978845608028654
gelu_b = 0.044715


def gelu(v):
    return 0.5 * v * (1.0 + jnp.tanh(gelu_a * (v + gelu_b * (v * v * v))))


def gelu_both(v):
    sq = v * v
    t = jnp.tanh(gelu_a * (v + gelu_b * (sq * v)))
    half = 0.5 * (1.0 + t)
    slope = half + 0.5 * v * (1.0 - t * t) * (gelu_a * (1.0 + 3.0 * gelu_b * sq))
    return v * half, slope


def lane_low(shape):
    return lax.broadcasted_iota(jnp.int32, shape, 1) < 64


def shape_of(dtype, *dims):
    return jax.ShapeDtypeStruct(dims, dtype)


class Fetched:
    def __init__(self, ref, copies):
        self.ref, self.copies, self.shape = ref, copies, ref.shape

    def __getitem__(self, index):
        for copy in self.copies:
            copy.wait()
        self.copies = ()
        return self.ref[index]


def square(array, start, index):
    places, _, width = array.shape
    per = 6 * width // places
    pieces = []
    row, end = index * width, index * width + width
    while row < end:
        place, at = divmod(row, per)
        take = min(per - at, end - row)
        spot = slice(row - index * width, row - index * width + take)
        pieces.append(((place, slice(start + at, start + at + take)), spot))
        row += take
    return (array, (width, width), tuple(pieces))


def rows_of(array, start, count):
    places, _, width = array.shape
    every = slice(0, places)
    return (array, (places, count, width), (((every, slice(start, start + count)), every),))


def fused(name, program, core, small, ins, outs, flops, scratch=(), order=None):
    big, sources = [], []
    for item in ins.values():
        array = item[0] if isinstance(item, tuple) else item
        known = [index for index, other in enumerate(big) if other is array]
        sources.append(known[0] if known else len(big))
        if not known:
            big.append(array)
    shapes = [item[1] if isinstance(item, tuple) else item.shape for item in ins.values()]
    pieces = [item[2] if isinstance(item, tuple) else None for item in ins.values()]
    kinds = [big[source].dtype for source in sources]
    counts = [len(item) if item else 1 for item in pieces]
    n_small, n_big, n_out, extra = len(small), len(big), len(outs), 0 if order is None else 1

    def body(core_ref, *refs):
        small_refs, refs = refs[:n_small], refs[n_small:]
        big_refs, refs = refs[:n_big], refs[n_big + extra :]
        out_refs, refs = refs[:n_out], refs[n_out:]
        in_bufs, refs = refs[: len(ins)], refs[len(ins) :]
        out_bufs, refs = refs[:n_out], refs[n_out:]
        user, (in_sem, out_sem) = refs[:-2], refs[-2:]
        env = types.SimpleNamespace(**dict(zip(small, small_refs)))
        used, fetched = 0, []
        for key, source, piece, buf in zip(ins, sources, pieces, in_bufs):
            src = big_refs[source]
            copies = []
            for item in piece or (None,):
                if item is None:
                    copy = pltpu.make_async_copy(src, buf, in_sem.at[used])
                else:
                    copy = pltpu.make_async_copy(src.at[item[0]], buf.at[item[1]], in_sem.at[used])
                copy.start()
                copies.append(copy)
                used += 1
            setattr(env, key, Fetched(buf, copies))
            fetched.append(getattr(env, key))
        for key, buf in zip(outs, out_bufs):
            setattr(env, key, buf)
        leaving = [None] * n_out

        def store(*bufs):
            for buf in bufs:
                (index,) = [place for place in range(n_out) if out_bufs[place] is buf]
                leaving[index] = pltpu.make_async_copy(buf, out_refs[index], out_sem.at[index])
                leaving[index].start()

        program(env, core_ref, store, *user)
        store(*[buf for buf, copy in zip(out_bufs, leaving) if copy is None])
        for copy in leaving:
            copy.wait()
        for item in fetched:
            for copy in item.copies:
                copy.wait()

    vmem = pl.BlockSpec(memory_space=pltpu.VMEM)
    anywhere = pl.BlockSpec(memory_space=pl.ANY)
    size = sum(array.size * array.dtype.itemsize for array in big)
    results = pl.pallas_call(
        body,
        in_specs=[pl.BlockSpec(memory_space=pltpu.SMEM)] + [vmem] * n_small + [anywhere] * (n_big + extra),
        out_specs=tuple([anywhere] * n_out),
        out_shape=tuple(outs.values()),
        scratch_shapes=[pltpu.VMEM(shape, dtype) for shape, dtype in zip(shapes, kinds)]
        + [pltpu.VMEM(out.shape, out.dtype) for out in outs.values()]
        + list(scratch)
        + [pltpu.SemaphoreType.DMA((sum(counts),)), pltpu.SemaphoreType.DMA((n_out,))],
        compiler_params=pltpu.CompilerParams(vmem_limit_bytes=56 * MIB),
        cost_estimate=pl.CostEstimate(flops=flops, bytes_accessed=size, transcendentals=0),
        name=name,
    )(core, *small.values(), *big, *(() if order is None else (order,)))
    return types.SimpleNamespace(**dict(zip(outs, results)))


def tiles_of(core, rows, window):
    if window == rows + HALO:
        near = pl.multiple_of(core[1], HALO)
        return ((near, 0), (pl.multiple_of(rows - TILE - core[1], HALO), None))
    return ((0, 0), (rows - TILE, 1))


def key_rows(ref, lanes, rows, halo):
    if halo is None:
        return ref[0:rows, lanes]
    if halo == 0:
        return ref[0 : rows + HALO, lanes]
    return jnp.concatenate((ref[0:rows, lanes], ref[rows + HALO : rows + 2 * HALO, lanes]), axis=0)


def key_lanes(ref, row, rows, halo):
    if halo is None:
        return ref[row : row + 1, 0:rows]
    if halo == 0:
        return ref[row : row + 1, 0 : rows + HALO]
    return jnp.concatenate(
        (ref[row : row + 1, 0:rows], ref[row : row + 1, rows + HALO : rows + 2 * HALO]), axis=1
    )


def halves(shape):
    low = lane_low(shape)
    return low, ~low


def keep(mask, values):
    return jnp.where(mask, values, jnp.zeros_like(values))


def gain_rows(gains, index):
    return gains[index : index + 1, :], gains[index + 1 : index + 2, :]


def attn_fwd(core, causal, low_src, base, kv_src, weights, qcol, krow, q_out, k_out, v_out, o_out, lse_out, res_out):
    rows, _ = q_out.shape
    window = k_out.shape[0]
    w_q, w_k, w_v, w_o = weights
    queries = dot_nn(low_src(), w_q[...])
    q_out[...] = (queries.astype(BF).astype(F32) * 0.125).astype(BF)
    k_out[...] = dot_nn(kv_src[...], w_k[...]).astype(BF)
    v_out[...] = dot_nn(kv_src[...], w_v[...]).astype(BF)
    for offset, halo in tiles_of(core, rows, window):
        spot = pl.ds(offset, TILE)
        allowed = qcol[spot, 0:1] == key_lanes(krow, 0, rows, halo)
        if causal:
            allowed = allowed & (key_lanes(krow, 1, rows, halo) <= qcol[spot, 1:2])
        lane = lax.broadcasted_iota(jnp.int32, (TILE, 128), 1)
        packed = jnp.zeros((TILE, 128), F32)
        for pair in range(HEADS // 2):
            lanes = slice(pair * 128, pair * 128 + 128)
            q2 = q_out[spot, lanes]
            k2 = key_rows(k_out, lanes, rows, halo)
            v2 = key_rows(v_out, lanes, rows, halo)
            mixed = None
            for half in range(2):
                scores = dot_nt(keep(halves(q2.shape)[half], q2), k2)
                scores = jnp.where(allowed, scores, masked_score)
                top = jnp.max(scores, axis=-1, keepdims=True)
                weights = jnp.exp(scores - top)
                total = jnp.sum(weights, axis=-1, keepdims=True)
                probs = (weights * (1.0 / total)).astype(BF)
                part = dot_nn(probs, keep(halves(v2.shape)[half], v2))
                mixed = part if mixed is None else mixed + part
                packed = jnp.where(lane == 2 * pair + half, top + jnp.log(total), packed)
            o_out[spot, lanes] = mixed.astype(BF)
        lse_out[:, spot] = jnp.transpose(packed)[0:HEADS, :]
    res_out[...] = base() + dot_nn(o_out[...], w_o[...])


def score_grads(q2, do2, k2, v2, allowed, lse, delta):
    sums = None
    for half in range(2):
        qh = keep(halves(q2.shape)[half], q2)
        doh = keep(halves(do2.shape)[half], do2)
        scores = jnp.where(allowed, dot_nt(k2, qh), masked_score)
        probs = jnp.exp(scores - lse[half])
        gscores = (probs * (dot_nt(v2, doh) - delta[half])).astype(BF)
        parts = (
            dot_tn(gscores, keep(halves(k2.shape)[half], k2)),
            dot_nn(gscores, qh),
            dot_nn(probs.astype(BF), doh),
        )
        sums = parts if sums is None else tuple(a + b for a, b in zip(sums, parts))
    return sums


def attn_head(
    core, causal, grad, resid, o_in, q_in, k_in, v_in, lse_in, weights, gains, gain_at, qrow, kcol, e,
):
    back_out, do_out, delta_out, dwo_out, halo_out, dqh_out, ng_out = e.back, e.do, e.delta, e.dwo, e.halo, e.dqh, e.ng
    w_k, w_v, w_o = weights
    rows, width = do_out.shape
    window = k_in.shape[0]
    back, dgain, dbias = norm_back(resid[...], gain_rows(gains, gain_at)[0], grad)
    back_out[...] = back
    ng_out[0:1, :] = dgain
    ng_out[1:2, :] = dbias
    branch = back.astype(BF)
    do_out[...] = dot_nt(branch, w_o[...]).astype(BF)
    mixed = do_out[...].astype(F32) * o_in[...].astype(F32)
    high = mixed.astype(BF)
    rest = (mixed - high.astype(F32)).astype(BF)
    head = lax.broadcasted_iota(jnp.int32, (16, width), 1) // (width // HEADS)
    which = (head == lax.broadcasted_iota(jnp.int32, (16, width), 0)).astype(F32).astype(BF)
    delta_out[...] = (dot_nt(which, high) + dot_nt(which, rest))[0:HEADS, :]
    for offset, halo in tiles_of(core, rows, window):
        if halo is None:
            continue
        spot = pl.ds(offset, TILE)
        keys = slice(rows + halo * HALO, rows + halo * HALO + HALO)
        here = slice(halo * HALO, halo * HALO + HALO)
        allowed = kcol[keys, 0:1] == qrow[0:1, spot]
        if causal:
            allowed = allowed & (kcol[keys, 1:2] <= qrow[1:2, spot])
        for pair in range(HEADS // 2):
            lanes = slice(pair * 128, pair * 128 + 128)
            heads = (2 * pair, 2 * pair + 1)
            dq2, dk2, dv2 = score_grads(
                q_in[spot, lanes],
                do_out[spot, lanes],
                k_in[keys, lanes],
                v_in[keys, lanes],
                allowed,
                [lse_in[h : h + 1, spot] for h in heads],
                [delta_out[h : h + 1, spot] for h in heads],
            )
            dqh_out[here, lanes] = dq2
            halo_out[0, here, lanes] = dk2.astype(BF)
            halo_out[1, here, lanes] = dv2.astype(BF)
    e.gxh[...] = (dot_nt(halo_out[0], w_k[...]) + dot_nt(halo_out[1], w_v[...])).astype(BF)
    dwo_out[...] = dot_tn(o_in[...], branch).astype(BF)


def attn_body(
    core, causal, window, back, do_in, delta, dqh, low_src, q_in, k_in, v_in, lse_in, w_q, qrow, kcol,
    gq_out, dwq_out, own_out, dq_scr,
):
    rows, width = gq_out.shape
    for tile in range(rows // TILE):
        spot = slice(tile * TILE, tile * TILE + TILE)
        allowed = kcol[0:rows, 0:1] == qrow[0:1, spot]
        if causal:
            allowed = allowed & (kcol[0:rows, 1:2] <= qrow[1:2, spot])
        for pair in range(HEADS // 2):
            lanes = slice(pair * 128, pair * 128 + 128)
            heads = (2 * pair, 2 * pair + 1)
            dq2, dk2, dv2 = score_grads(
                q_in[spot, lanes],
                do_in[spot, lanes],
                k_in[0:rows, lanes],
                v_in[0:rows, lanes],
                allowed,
                [lse_in[h : h + 1, spot] for h in heads],
                [delta[h : h + 1, spot] for h in heads],
            )
            dq_scr[spot, lanes] = dq2
            if tile == 0:
                own_out[0, :, lanes] = dk2
                own_out[1, :, lanes] = dv2
            else:
                own_out[0, :, lanes] += dk2
                own_out[1, :, lanes] += dv2
    for offset, halo in tiles_of(core, rows, window):
        if halo is not None:
            dq_scr[pl.ds(offset, TILE), :] += dqh[halo * HALO : halo * HALO + HALO, :]
    grad_q = (dq_scr[...] * 0.125).astype(BF)
    gq_out[...] = back[...] + dot_nt(grad_q, w_q[...])
    dwq_out[...] = dot_tn(low_src(), grad_q).astype(BF)


def split_places(core, source, kept, sent):
    for parity in range(2):

        @pl.when(core[0] == parity)
        def place():
            for chip in range(kept.shape[0]):
                kept[chip] = source[2 * chip + parity]
                sent[chip] = source[2 * chip + 1 - parity]


def kv_bwd(window_rows, own, halo, w_k, w_v):
    rows = own.shape[1]
    window = window_rows.shape[0]
    dk = own[0].astype(BF)
    dv = own[1].astype(BF)
    total = dot_nt(dk, w_k[...]) + dot_nt(dv, w_v[...])
    dwk = dot_tn(window_rows[0:rows, :], dk) + dot_tn(window_rows[rows:window, :], halo[0])
    dwv = dot_tn(window_rows[0:rows, :], dv) + dot_tn(window_rows[rows:window, :], halo[1])
    return total, dwk.astype(BF), dwv.astype(BF)


def lay_out(stack, mats):
    places, _, width = stack.shape
    per = 6 * width // places
    for slot, matrix in enumerate(mats):
        row, end = slot * width, slot * width + width
        while row < end:
            place, start = divmod(row, per)
            take = min(per - start, end - row)
            at = row - slot * width
            stack[place, start : start + take, :] = matrix[at : at + take, :]
            row += take


def up_tile(pack, tile):
    places, _, width = pack.shape
    return pack[:, 128 + 32 * tile : 160 + 32 * tile, :].reshape(places * 32, width)


def down_tile(pack, tile):
    return pack[4 * tile : 4 * tile + 4, 0:128, :].reshape(512, pack.shape[2])


def ffn_fwd(resid, base, gains, gain_in, gain_out, pack, res_out, low_out, hid_low=None, pre=None):
    hidden = norm_rows(resid[...], *gain_rows(gains, gain_in))
    low = hidden.astype(BF)
    if hid_low is not None:
        hid_low[...] = low
    res_out[...] = hidden + base[...].astype(F32)
    for tile in range(4):
        values = dot_nn(low, up_tile(pack, tile))
        if pre is not None:
            pre[tile] = values
        res_out[...] += dot_nn(gelu(values).astype(BF), down_tile(pack, tile))
    low_out[...] = norm_rows(res_out[...], *gain_rows(gains, gain_out)).astype(BF)


def ffn_bwd(grad, res_late, gains, gain_out, pack, gh_out, late_out, ng_out, hid_low, late_low, dpack, pre=None):
    back, dgain, dbias = norm_back(res_late[...], gain_rows(gains, gain_out)[0], grad)
    late_out[...] = back
    gh_out[...] = back
    late_low[...] = back.astype(BF)
    ng_out[0:1, :] = dgain
    ng_out[1:2, :] = dbias
    places, _, width = dpack.shape
    for tile in range(4):
        activ, slope = gelu_both(dot_nn(hid_low[...], up_tile(pack, tile)) if pre is None else pre[tile])
        grad_down = dot_tn(activ.astype(BF), late_low[...]).astype(BF)
        dpack[4 * tile : 4 * tile + 4, 0:128, :] = grad_down.reshape(4, 128, width)
        grad_act = dot_nt(late_low[...], down_tile(pack, tile)).astype(BF).astype(F32)
        grad_pre = (grad_act * slope).astype(BF)
        grad_up = dot_tn(hid_low[...], grad_pre).astype(BF)
        dpack[:, 128 + 32 * tile : 160 + 32 * tile, :] = grad_up.reshape(places, 32, width)
        gh_out[...] += dot_nt(grad_pre, up_tile(pack, tile))


def kept_shapes(rows, window, width, with_o=True):
    outs = dict(
        q=shape_of(BF, rows, width),
        k=shape_of(BF, window, width),
        v=shape_of(BF, window, width),
        lse=shape_of(F32, HEADS, rows),
    )
    return dict(outs, o=shape_of(BF, rows, width)) if with_o else outs


def head_shapes(rows, window, width):
    return dict(
        back=shape_of(F32, rows, width),
        do=shape_of(BF, rows, width),
        delta=shape_of(F32, HEADS, rows),
        dwo=shape_of(BF, width, width),
        halo=shape_of(BF, 2, window - rows, width),
        gxh=shape_of(BF, window - rows, width),
        dqh=shape_of(F32, window - rows, width),
        ng=shape_of(F32, 2, width),
    )


def weights_of(env):
    return env.wq, env.wk, env.wv, env.wo


def named_mats(mats):
    return dict(wq=mats[0], wk=mats[1], wv=mats[2], wo=mats[3])


def enc_forward(x, window_rows, mats, pack, gains, places):
    rows, width = x.shape
    window = window_rows.shape[0]

    def program(e, core, store):
        attn_fwd(
            core, False, lambda: e.x[...], lambda: e.x[...].astype(F32), e.window, weights_of(e),
            e.qcol, e.krow, e.q, e.k, e.v, e.o, e.lse, e.resid,
        )
        store(e.q, e.k, e.v, e.o, e.lse, e.resid)
        ffn_fwd(e.resid, e.x, e.gains, 0, 2, e.pack, e.two, e.low)

    return fused(
        "enc_forward",
        program,
        places.core,
        dict(qcol=places.qcol, krow=places.krow, gains=gains),
        dict(x=x, window=window_rows, **named_mats(mats), pack=pack),
        dict(
            kept_shapes(rows, window, width),
            resid=shape_of(F32, rows, width),
            two=shape_of(F32, rows, width),
            low=shape_of(BF, rows, width),
        ),
        28 * rows * width * width + 8 * rows * window * width,
    )


def self_forward(z, window_rows, mats, places):
    rows, width = z.shape
    window = window_rows.shape[0]

    def program(e, core, store):
        attn_fwd(
            core, True, lambda: e.z[...], lambda: e.z[...].astype(F32), e.window, weights_of(e),
            e.qcol, e.krow, e.q, e.k, e.v, e.o, e.lse, e.resid,
        )

    return fused(
        "self_forward",
        program,
        places.core,
        dict(qcol=places.qcol, krow=places.krow),
        dict(z=z, window=window_rows, **named_mats(mats)),
        dict(kept_shapes(rows, window, width), resid=shape_of(F32, rows, width)),
        12 * rows * width * width + 8 * rows * window * width,
    )


def cross_and_ffn(three, window_rows, mats, pack, z, cot, gains, places):
    rows, width = three.shape
    window = window_rows.shape[0]
    count, block = pack[0].shape[0], pack[1][1]
    f32_rows, low_rows = pltpu.VMEM((rows, width), F32), pltpu.VMEM((rows, width), BF)

    def program(e, core, store, o, four, five, gh, hid_low, late_low, pre, dpack):
        def first():
            return norm_rows(e.three[...], *gain_rows(e.gains, 4))

        attn_fwd(
            core, False, lambda: first().astype(BF), first, e.window, weights_of(e),
            e.qcol, e.krow, e.q, e.k, e.v, o, e.lse, four,
        )
        store(e.q, e.k, e.v, e.lse)
        ffn_fwd(four, e.z, e.gains, 6, 8, e.pack, five, e.low, hid_low, pre)
        store(e.low)
        ffn_bwd(
            e.cot[...].astype(F32), five, e.gains, 8, e.pack, gh, e.five, e.ng8,
            hid_low, late_low, dpack, pre,
        )
        split_places(core, dpack, e.kept, e.sent)
        store(e.sent, e.kept, e.five, e.ng8)
        attn_head(
            core, False, gh[...], four, o, e.q, e.k, e.v, e.lse, (e.wk, e.wv, e.wo), e.gains, 6, e.qrow, e.kcol, e,
        )

    return fused(
        "cross_and_ffn",
        program,
        places.core,
        dict(qcol=places.qcol, krow=places.krow, qrow=places.qrow, kcol=places.kcol, gains=gains),
        dict(three=three, wq=mats[0], window=window_rows, wk=mats[1], wv=mats[2], wo=mats[3], z=z, pack=pack, cot=cot),
        dict(
            **kept_shapes(rows, window, width, False),
            low=shape_of(BF, rows, width),
            kept=shape_of(BF, count // 2, block, width),
            sent=shape_of(BF, count // 2, block, width),
            five=shape_of(F32, rows, width),
            ng8=shape_of(F32, 2, width),
            **head_shapes(rows, window, width),
        ),
        68 * rows * width * width + 8 * rows * window * width,
        scratch=[
            low_rows, f32_rows, f32_rows, f32_rows, low_rows, low_rows,
            pltpu.VMEM((4, rows, width), F32), pltpu.VMEM((count, block, width), BF),
        ],
    )


def own_rows(array, rows):
    spot = (slice(0, rows),)
    return (array, (rows, array.shape[1]), ((spot, spot),))


def cross_body_self_head(c, low_window, three, s, cross_mats, self_mats, gains, places):
    rows, width = three.shape
    window = c.k.shape[0]

    def program(e, core, store, grad, dq, own):
        def first():
            return norm_rows(e.three[...], *gain_rows(e.gains, 4)).astype(BF)

        attn_body(
            core, False, window, e.back_c, e.do_c, e.delta_c, e.dqh_c, first, e.q_c, e.k_c,
            e.v_c, e.lse_c, e.wq_c, e.qrow, e.kcol, grad, e.dwq, own, dq,
        )
        e.gx[...], e.dwk[...], e.dwv[...] = kv_bwd(e.low_window, own, e.halo_c, e.wk_c, e.wv_c)
        store(e.dwq, e.gx, e.dwk, e.dwv)
        attn_head(
            core, True, grad[...], e.three, e.o, e.q, e.k, e.v, e.lse, (e.wk, e.wv, e.wo), e.gains, 4,
            e.qrow, e.kcol, e,
        )

    return fused(
        "cross_body_self_head",
        program,
        places.core,
        dict(qrow=places.qrow, kcol=places.kcol, gains=gains),
        dict(
            q_c=c.q,
            do_c=c.do,
            k_c=own_rows(c.k, rows),
            v_c=own_rows(c.v, rows),
            lse_c=c.lse,
            delta_c=c.delta,
            dqh_c=c.dqh,
            back_c=c.back,
            wq_c=cross_mats[0],
            three=three,
            low_window=low_window,
            halo_c=c.halo,
            wk_c=cross_mats[1],
            wv_c=cross_mats[2],
            wo=self_mats[3],
            o=s.o,
            q=s.q,
            k=s.k,
            v=s.v,
            lse=s.lse,
            wk=self_mats[1],
            wv=self_mats[2],
        ),
        dict(
            gx=shape_of(F32, rows, width),
            dwq=shape_of(BF, width, width),
            dwk=shape_of(BF, width, width),
            dwv=shape_of(BF, width, width),
            **head_shapes(rows, window, width),
        ),
        18 * rows * width * width + 10 * rows * window * width,
        scratch=[pltpu.VMEM((rows, width), F32), pltpu.VMEM((rows, width), F32), pltpu.VMEM((2, rows, width), F32)],
    )


def input_body(name, kept, head, src, window_rows, mats, causal, add, layout, grads, norms, group, places, order):
    rows, width = src.shape
    window = kept.k.shape[0]
    block = 6 * width // group + (16 if norms else 0)

    def program(e, core, store, dq, own, gq, stack, lines):
        others = (e.other0, e.other1, e.other2, e.other3, e.other4)
        attn_body(
            core, causal, window, e.back, e.do, e.delta, e.dqh, lambda: e.src[...], e.q, e.k,
            e.v, e.lse, e.wq, e.qrow, e.kcol, gq, e.dwq, own, dq,
        )
        total, dwk, dwv = kv_bwd(e.window, own, e.halo, e.wk, e.wv)
        e.dwk[...] = dwk
        parts = dict(q=e.dwq, k=dwk, v=dwv)
        lay_out(stack, [others[item] if isinstance(item, int) else parts[item] for item in layout])
        if norms:
            lines[...] = jnp.zeros_like(lines)
            for index, item in enumerate((e.ng0, e.ng1, e.ng2, e.ng3, e.ng4)):
                lines[2 * index : 2 * index + 2, :] = item[...]
            for place in range(group):
                stack[place, block - 16 :, :] = lines[...].astype(BF)
        split_places(core, stack, e.kept, e.sent)
        store(e.sent, e.kept)
        e.grad[...] = gq[...] + total + e.add[...]

    grads = tuple(grads) + (head.dwo,) * (5 - len(grads))
    ng = dict(ng0=norms[0], ng1=norms[1], ng2=norms[2], ng3=norms[3], ng4=norms[4]) if norms else {}
    return fused(
        name,
        program,
        places.core,
        dict(qrow=places.qrow, kcol=places.kcol),
        dict(
            q=kept.q,
            do=head.do,
            k=own_rows(kept.k, rows),
            v=own_rows(kept.v, rows),
            lse=kept.lse,
            delta=head.delta,
            dqh=head.dqh,
            back=head.back,
            wq=mats[0],
            src=src,
            window=window_rows,
            halo=head.halo,
            wk=mats[1],
            wv=mats[2],
            other0=grads[0],
            other1=grads[1],
            other2=grads[2],
            other3=grads[3],
            other4=grads[4],
            add=add,
            **ng,
        ),
        dict(
            sent=shape_of(BF, group // 2, block, width),
            kept=shape_of(BF, group // 2, block, width),
            dwq=shape_of(BF, width, width),
            dwk=shape_of(BF, width, width),
            grad=shape_of(F32, rows, width),
        ),
        14 * rows * width * width + 10 * rows * rows * width,
        scratch=[
            pltpu.VMEM((rows, width), F32), pltpu.VMEM((2, rows, width), F32), pltpu.VMEM((rows, width), F32),
            pltpu.VMEM((group, block, width), BF), pltpu.VMEM((16, width), F32),
        ],
        order=order,
    )


def enc_ffn_head(grad, one, two, kept, pack, mats, gains, places, order):
    rows, width = one.shape
    window = kept.k.shape[0]
    count, block = pack[0].shape[0], pack[1][1]

    def program(e, core, store, gh, hid_low, late_low, dpack):
        hid_low[...] = norm_rows(e.one[...], *gain_rows(e.gains, 0)).astype(BF)
        ffn_bwd(
            e.grad[...], e.two, e.gains, 2, e.pack, gh, e.late, e.ng2, hid_low, late_low, dpack
        )
        split_places(core, dpack, e.kept, e.sent)
        store(e.sent, e.kept, e.late, e.ng2)
        attn_head(
            core, False, gh[...], e.one, e.o, e.q, e.k, e.v, e.lse, (e.wk, e.wv, e.wo), e.gains, 0, e.qrow, e.kcol, e,
        )

    return fused(
        "enc_ffn_head",
        program,
        places.core,
        dict(qrow=places.qrow, kcol=places.kcol, gains=gains),
        dict(
            one=one,
            two=two,
            grad=grad,
            pack=pack,
            wo=mats[3],
            wk=mats[1],
            wv=mats[2],
            o=kept.o,
            q=kept.q,
            k=kept.k,
            v=kept.v,
            lse=kept.lse,
        ),
        dict(
            sent=shape_of(BF, count // 2, block, width),
            kept=shape_of(BF, count // 2, block, width),
            late=shape_of(F32, rows, width),
            ng2=shape_of(F32, 2, width),
            **head_shapes(rows, window, width),
        ),
        44 * rows * width * width + 10 * TILE * TILE * width,
        scratch=[
            pltpu.VMEM((rows, width), F32), pltpu.VMEM((rows, width), BF), pltpu.VMEM((rows, width), BF),
            pltpu.VMEM((count, block, width), BF),
        ],
        order=order,
    )


def segments_at(bounds, places, total_len):
    found = jnp.sum((bounds[None, :] <= places[:, None]).astype(jnp.int32), axis=-1)
    return jnp.where((places >= 0) & (places < total_len), found, -1)


def row_squares(values):
    if values.ndim == 2:
        return jnp.sum(values * values, axis=1)
    return values * values


def owner_groups(rows_local, owner, per_group, count):
    group_ids = (owner * rows_local + jnp.arange(rows_local, dtype=jnp.int32)) // per_group
    return group_ids[:, None] == jnp.arange(count, dtype=jnp.int32)[None, :]


def group_sum(onehot, row_values):
    return jnp.sum(jnp.where(onehot, row_values[:, None], 0.0), axis=0)


def lamb_moments(master, grad_rows, first, second):
    first_new = beta_one * first + (1.0 - beta_one) * grad_rows
    second_new = beta_two * second + (1.0 - beta_two) * grad_rows * grad_rows
    update = (
        first_new
        / (1.0 - beta_one**STEP)
        / (jnp.sqrt(second_new / (1.0 - beta_two**STEP)) + lamb_eps)
        + weight_decay * master
    )
    return (first_new, second_new, update)


GROUP = ("lo", "y", "c")
CHIPS = ("lo", "y")
EVERY = ("hi", "lo", "y", "c")


def swap_hi(array):
    return lax.ppermute(array, "hi", [(0, 1), (1, 0)])


def shift_hi(array, distance):
    count = lax.axis_size("hi")
    route = [(i - distance, i) for i in range(count) if i - distance in range(count)]
    return lax.ppermute(array, "hi", route)


def halo_rows(rows_array):
    rows = rows_array.shape[0]
    if lax.axis_size("hi") == 2:
        return swap_hi(jnp.where(lax.axis_index("hi") == 0, rows_array[rows - HALO :], rows_array[:HALO]))
    left = shift_hi(rows_array[rows - HALO :], 1)
    right = shift_hi(rows_array[:HALO], -1)
    return jnp.concatenate((left, right), axis=0)


def halo_return(grads, total):
    rest = total.shape[0] - HALO
    if lax.axis_size("hi") == 2:
        back = swap_hi(grads)
        last = lax.axis_index("hi") == 0
        return back, total + jnp.where(last, jnp.pad(back, ((rest, 0), (0, 0))), jnp.pad(back, ((0, rest), (0, 0))))
    back = jnp.concatenate((shift_hi(grads[HALO:], 1), shift_hi(grads[:HALO], -1)), axis=0)
    return back, total + jnp.pad(back[:HALO], ((0, rest), (0, 0))) + jnp.pad(back[HALO:], ((rest, 0), (0, 0)))


def pack_up(rows):
    count, units = rows.shape
    return rows.reshape(count, 4, units // 4).swapaxes(0, 1).reshape(4 * count, units // 4)


def unpack_up(packed):
    count, width = packed.shape
    return packed.reshape(4, count // 4, width).swapaxes(0, 1).reshape(count // 4, 4 * width)


def swap_core(array):
    return lax.ppermute(array, "c", [(0, 1), (1, 0)])


def tie(array, other):
    bit = lax.slice(other, (0,) * other.ndim, (1,) * other.ndim).reshape(()) * 0
    return array + bit.astype(array.dtype)


def from_parity(mine, other):
    even = lax.axis_index("c") == 0
    full = jnp.stack((jnp.where(even, mine, other), jnp.where(even, other, mine)), axis=1)
    return full.reshape(-1, *mine.shape[1:])


def gather_plain(attn_shard, up_shard, down_shard, norm_shard):
    width = attn_shard.shape[1]
    group = lax.axis_size(GROUP)
    norm_count = norm_shard.shape[0]
    attn = lax.all_gather(attn_shard, EVERY, axis=0, tiled=True)
    down = lax.all_gather(down_shard, EVERY, axis=0, tiled=True).reshape(2, group, -1, width)
    up = lax.all_gather(up_shard, EVERY, axis=0, tiled=True)
    up = up.reshape(2, group, -1, 4, width).swapaxes(2, 3).reshape(2, group, -1, width)
    norms = jnp.pad(norm_shard[None, :], ((0, 0), (0, width - norm_count)))
    norms = lax.all_gather(norms, EVERY, axis=0, tiled=True)[:, :norm_count]
    ffn = jnp.concatenate((down, up), axis=2)
    attn = attn.reshape(2, group, -1, width)
    full = jnp.concatenate((attn[0], attn[1], ffn[0]), axis=1)
    return full, ffn[1], norms.reshape(10, width).astype(F32)


def reduce_cores(kept, sent):
    return (kept.astype(F32) + swap_core(sent).astype(F32)).astype(BF)


def reduce_chips(pair):
    parts = lax.all_to_all(pair, CHIPS, split_axis=0, concat_axis=0, tiled=True)
    return jnp.sum(parts.astype(F32), axis=0)


def join_halves(zero, one):
    first = lax.axis_index("hi") == 0
    mine = jnp.where(first, zero, one)
    sent = jnp.where(first, one, zero).astype(BF)
    return mine + swap_hi(sent).astype(F32)


def reduce_plain(attn0, attn1, ffn0, ffn1, norm_local):
    group, _, width = ffn0.shape

    def scatter(rows):
        return lax.psum_scatter(rows, EVERY, scatter_dimension=0, tiled=True).astype(F32)

    attn = jnp.concatenate((attn0, attn1), axis=0).reshape(-1, width)
    ffn = jnp.stack((ffn0, ffn1)).reshape(2 * group, -1, width)
    up = ffn[:, 128:].reshape(2 * group, 4, 32, width).swapaxes(1, 2).reshape(-1, 4 * width)
    norms = lax.psum_scatter(
        norm_local.reshape(lax.axis_size(EVERY), -1), EVERY, scatter_dimension=0, tiled=True
    )
    return scatter(attn), scatter(up), scatter(ffn[:, :128].reshape(-1, width)), norms[0]


def shards(
    enc_in,
    dec_in,
    cotangent,
    lengths,
    attn_master,
    ffn_in_master,
    ffn_out_master,
    norm_master,
    attn_first,
    ffn_in_first,
    ffn_out_first,
    norm_first,
    attn_second,
    ffn_in_second,
    ffn_out_second,
    norm_second,
):
    micro, _, length_dev, width = enc_in.shape
    rows = micro * length_dev
    hidden_units = ffn_in_master.shape[1]
    high, low = lax.axis_index("hi"), lax.axis_index("lo")
    n_high = lax.axis_size("hi")
    owner = lax.axis_index(EVERY)
    masters = (attn_master, ffn_in_master, ffn_out_master, norm_master)
    group_info = ((width, 12), (width, 2), (hidden_units, 2), (width, 10))
    onehots = [
        owner_groups(master.shape[0], owner, info[0], info[1])
        for master, info in zip(masters, group_info)
    ]
    weight_local = jnp.concatenate(
        [group_sum(onehot, row_squares(master)) for onehot, master in zip(onehots, masters)]
    )

    plain = n_high != 2

    def regroup(*arrays):
        packed = jnp.stack([array[:, 0] for array in arrays], axis=1)
        packed = lax.all_to_all(packed, "lo", split_axis=0, concat_axis=0, tiled=True)
        packed = packed.swapaxes(0, 1).reshape(len(arrays), rows, width)
        return packed

    core = jnp.stack((lax.axis_index("c"), jnp.where(high == 0, rows - HALO, 0))).astype(jnp.int32)
    attn_rows = attn_master.shape[0]
    norm_count = norm_master.shape[0]
    attn_low, up_low, down_low, norm_low = [master.astype(BF) for master in masters]
    if plain:
        full, late, gains = gather_plain(attn_low, up_low, down_low, norm_low)
        enc_rows, dec_rows, cot_rows = regroup(enc_in, dec_in, cotangent)
    else:
        first = high == 0
        norm_pad = jnp.pad(norm_low[None, :], ((0, 15), (0, width - norm_count)))
        mine = jnp.concatenate((attn_low, down_low, pack_up(up_low), norm_pad), axis=0)
        other = swap_hi(mine)
        enc_rows, dec_rows, cot_rows = regroup(enc_in, dec_in, cotangent)
        zero = jnp.where(first, mine, other)
        one = jnp.where(first, other, mine)
        last = mine.shape[0] - 16
        early = (one[:attn_rows], zero[attn_rows : last + 1], one[last:-1])
        early = jnp.concatenate((tie(zero[:attn_rows], enc_rows), *early), axis=0)
        full = lax.all_gather(early, GROUP, axis=0, tiled=False)
        late = lax.all_gather(one[attn_rows:last], GROUP, axis=0, tiled=False)
        gains = full[:, attn_rows + last : attn_rows + last + 2, :norm_count].swapaxes(0, 1)
        gains = gains.reshape(10, width).astype(F32)
    enc_window = jnp.concatenate((enc_rows, halo_rows(enc_rows)), axis=0)
    dec_window = jnp.concatenate((dec_rows, halo_rows(dec_rows)), axis=0)
    group = full.shape[0]

    total_len = rows * n_high
    bounds = jnp.cumsum(lengths[:, 0, :], axis=-1)
    bounds = lax.dynamic_index_in_dim(bounds, low, 0, keepdims=False)
    base = high * rows
    own_pos = base + jnp.arange(rows, dtype=jnp.int32)
    step = jnp.arange(HALO, dtype=jnp.int32)
    if n_high == 2:
        halo_pos = jnp.where(high == 0, rows, rows - HALO) + step
    else:
        halo_pos = jnp.concatenate((base - HALO + step, base + rows + step))
    key_pos = jnp.concatenate((own_pos, halo_pos))
    key_seg = segments_at(bounds, key_pos, total_len)
    krow = jnp.stack((key_seg, key_pos), axis=0)
    kcol = jnp.stack((key_seg, key_pos), axis=1)
    places = types.SimpleNamespace(
        krow=krow,
        kcol=kcol,
        qrow=krow[:, :rows],
        qcol=kcol[:rows],
        core=core,
    )

    per = 6 * width // group
    mats = [square(full, 0, index) for index in range(6)] + [square(full, per, index) for index in range(6)]
    pack0, pack1 = rows_of(full, 2 * per, late.shape[1]), rows_of(late, 0, late.shape[1])
    e = enc_forward(enc_rows, enc_window, mats[0:4], pack0, gains, places)
    low_window = jnp.concatenate((e.low, halo_rows(e.low)), axis=0)
    s = self_forward(dec_rows, dec_window, mats[4:8], places)
    c = cross_and_ffn(s.resid, low_window, mats[8:12], pack1, dec_rows, cot_rows, gains, places)

    def restore(*arrays):
        outs = jnp.stack(arrays, axis=0).reshape(len(arrays), micro, length_dev, width).swapaxes(0, 1)
        return lax.all_to_all(outs, "lo", split_axis=0, concat_axis=0, tiled=True)

    sh = cross_body_self_head(c, low_window, s.resid, s, mats[8:12], mats[4:8], gains, places)
    back_c, grad_encoded = halo_return(c.gxh, sh.gx)
    pair_f1 = c.kept if plain else reduce_cores(tie(c.kept, sh.ng), c.sent)
    sb = input_body(
        "self_body", s, sh, dec_rows, dec_window, mats[4:8], True, c.five, ("v", 0, 1, 2, 3, 4),
        (sh.dwo, sh.dwq, sh.dwk, sh.dwv, c.dwo), (), group, places, pair_f1,
    )
    if plain:
        pair_a1, lows = sb.kept, restore(e.low, c.low)
    else:
        part_f1 = reduce_chips(pair_f1)
        lows = restore(tie(e.low, part_f1), c.low)
        pair_a1 = reduce_cores(sb.kept, sb.sent)
    eh = enc_ffn_head(grad_encoded, e.resid, e.two, e, pack0, mats[0:4], gains, places, pair_a1)
    if plain:
        pair_f0 = eh.kept
    else:
        part_a1 = reduce_chips(pair_a1)
        pair_f0 = reduce_cores(tie(eh.kept, part_a1), eh.sent)
    eb = input_body(
        "enc_body", e, eh, enc_rows, enc_window, mats[0:4], False, eh.late, ("q", "k", "v", 0, 1, 2),
        (eh.dwo, sb.dwq, sb.dwk), (eh.ng, eh.ng2, sh.ng, c.ng, c.ng8), group, places, pair_f0,
    )
    _, dec_grad = halo_return(sh.gxh, sb.grad)
    _, enc_grad = halo_return(eh.gxh, eb.grad)
    enc_grad, dec_grad = enc_grad.astype(BF), dec_grad.astype(BF)
    if plain:
        attn_own, up_own, down_own, norm_own = reduce_plain(
            from_parity(eb.kept, eb.sent)[:, :per],
            from_parity(sb.kept, sb.sent),
            from_parity(eh.kept, eh.sent),
            from_parity(c.kept, c.sent),
            jnp.concatenate((eh.ng, eh.ng2, sh.ng, c.ng, c.ng8), axis=0).reshape(n_high, group, norm_count),
        )
        grads = restore(enc_grad, dec_grad)
    else:
        part_f0 = reduce_chips(pair_f0)
        part_a0 = reduce_chips(reduce_cores(eb.kept, eb.sent))
        grads = restore(tie(enc_grad, part_a0), dec_grad)
        ffn_own = join_halves(part_f0, part_f1)
        both = join_halves(part_a0, jnp.concatenate((part_a1, part_a0[attn_rows:]), axis=0))
        attn_own, up_own, down_own = both[:attn_rows], unpack_up(ffn_own[128:]), ffn_own[:128]
        norm_own = lax.dynamic_slice_in_dim(both[attn_rows:].reshape(-1), owner * norm_count, norm_count)

    owned = (attn_own, up_own, down_own, norm_own)
    firsts = (attn_first, ffn_in_first, ffn_out_first, norm_first)
    seconds = (attn_second, ffn_in_second, ffn_out_second, norm_second)
    moments = [
        lamb_moments(masters[index], owned[index], firsts[index], seconds[index])
        for index in range(4)
    ]
    update_local = jnp.concatenate(
        [group_sum(onehots[index], row_squares(moments[index][2])) for index in range(4)]
    )
    squares = jnp.stack((weight_local, update_local))
    squares = jnp.pad(squares, ((0, 6), (0, 128 - squares.shape[1])))
    count = lax.axis_size(EVERY)
    squares = tie(squares, grads)
    squares = jnp.broadcast_to(squares[None], (count,) + squares.shape)
    squares = jnp.sum(lax.all_to_all(squares, EVERY, split_axis=0, concat_axis=0, tiled=True), axis=0)
    norms = jnp.sqrt(squares[:2, :26])
    ratio = norms[0] / norms[1]
    bounds_at = (0, 12, 14, 16, 26)
    new_weights = []
    for index in range(4):
        row_ratio = jnp.sum(
            jnp.where(onehots[index], ratio[None, bounds_at[index] : bounds_at[index + 1]], 0.0), axis=1
        )
        if masters[index].ndim == 2:
            row_ratio = row_ratio[:, None]
        new_weights.append(masters[index] - learn_rate * row_ratio * moments[index][2])
    return (
        lows[:, 0][:, None],
        lows[:, 1][:, None],
        grads[:, 0][:, None].astype(F32),
        grads[:, 1][:, None].astype(F32),
        *owned,
        *new_weights,
        *[item[0] for item in moments],
        *[item[1] for item in moments],
        *[item.astype(BF) for item in new_weights],
        norms,
        ratio,
    )


def solution(mesh):
    count_seq, count_stream = mesh.shape["seq"], mesh.shape["stream"]

    def run(*args):
        micro = args[0].shape[0]
        split = Mesh(
            mesh.devices.reshape(count_seq // micro, micro, count_stream // 2, 2), ("hi", "lo", "y", "c")
        )
        tokens = P(None, ("y", "c"), ("hi", "lo"), None)
        wide = P(EVERY, None)
        flat = P(EVERY)
        owned = (wide, wide, wide, flat)
        return jax.shard_map(
            shards,
            mesh=split,
            in_specs=(tokens, tokens, tokens, P(None, ("y", "c"), None), *owned, *owned, *owned),
            out_specs=(tokens, tokens, tokens, tokens, *owned, *owned, *owned, *owned, *owned, P(), P()),
            check_vma=False,
        )(*args)

    return run
```

```python
import types

import jax
import jax.numpy as jnp
from jax import lax
from jax.experimental import pallas as pl
from jax.experimental.pallas import tpu as pltpu
from jax.sharding import Mesh
from jax.sharding import PartitionSpec as P

HEADS = 8
STEP = 5
HALO = 256
TILE = 256

norm_eps = 1e-05
beta_one = 0.5
beta_two = 0.5
lamb_eps = 1e-06
weight_decay = 0.01
learn_rate = 0.5
masked_score = -1e30

BF = jnp.bfloat16
F32 = jnp.float32
MIB = 1024 * 1024


def dot_nn(a, b):
    return lax.dot_general(a, b, (((1,), (0,)), ((), ())), preferred_element_type=F32)


def dot_nt(a, b):
    return lax.dot_general(a, b, (((1,), (1,)), ((), ())), preferred_element_type=F32)


def dot_tn(a, b):
    return lax.dot_general(a, b, (((0,), (0,)), ((), ())), preferred_element_type=F32)


def norm_parts(rows):
    centre = rows - jnp.mean(rows, axis=-1, keepdims=True)
    inv = lax.rsqrt(jnp.mean(centre * centre, axis=-1, keepdims=True) + norm_eps)
    return centre * inv, inv


def norm_rows(rows, gain, bias):
    return norm_parts(rows)[0] * gain + bias


def norm_back(rows, gain, grad):
    unit, inv = norm_parts(rows)
    lead = grad * gain
    back = inv * (
        lead
        - jnp.mean(lead, axis=-1, keepdims=True)
        - unit * jnp.mean(lead * unit, axis=-1, keepdims=True)
    )
    return (
        back,
        jnp.sum(grad * unit, axis=0, keepdims=True),
        jnp.sum(grad, axis=0, keepdims=True),
    )


gelu_a = 0.7978845608028654
gelu_b = 0.044715


def gelu(v):
    return 0.5 * v * (1.0 + jnp.tanh(gelu_a * (v + gelu_b * (v * v * v))))


def gelu_both(v):
    sq = v * v
    t = jnp.tanh(gelu_a * (v + gelu_b * (sq * v)))
    half = 0.5 * (1.0 + t)
    slope = half + 0.5 * v * (1.0 - t * t) * (gelu_a * (1.0 + 3.0 * gelu_b * sq))
    return v * half, slope


def lane_low(shape):
    return lax.broadcasted_iota(jnp.int32, shape, 1) < 64


def shape_of(dtype, *dims):
    return jax.ShapeDtypeStruct(dims, dtype)


class Fetched:
    def __init__(self, ref, copies):
        self.ref, self.copies, self.shape = ref, copies, ref.shape

    def __getitem__(self, index):
        for copy in self.copies:
            copy.wait()
        self.copies = ()
        return self.ref[index]


def square(array, start, index):
    places, _, width = array.shape
    per = 6 * width // places
    pieces = []
    row, end = index * width, index * width + width
    while row < end:
        place, at = divmod(row, per)
        take = min(per - at, end - row)
        spot = slice(row - index * width, row - index * width + take)
        pieces.append(((place, slice(start + at, start + at + take)), spot))
        row += take
    return (array, (width, width), tuple(pieces))


def rows_of(array, start, count):
    places, _, width = array.shape
    every = slice(0, places)
    return (array, (places, count, width), (((every, slice(start, start + count)), every),))


def fused(name, program, core, small, ins, outs, flops, scratch=(), order=()):
    big, sources = [], []
    for item in ins.values():
        array = item[0] if isinstance(item, tuple) else item
        known = [index for index, other in enumerate(big) if other is array]
        sources.append(known[0] if known else len(big))
        if not known:
            big.append(array)
    shapes = [item[1] if isinstance(item, tuple) else item.shape for item in ins.values()]
    pieces = [item[2] if isinstance(item, tuple) else None for item in ins.values()]
    kinds = [big[source].dtype for source in sources]
    counts = [len(item) if item else 1 for item in pieces]
    n_small, n_big, n_out, extra = len(small), len(big), len(outs), len(order)

    def body(core_ref, *refs):
        small_refs, refs = refs[:n_small], refs[n_small:]
        big_refs, refs = refs[:n_big], refs[n_big + extra :]
        out_refs, refs = refs[:n_out], refs[n_out:]
        in_bufs, refs = refs[: len(ins)], refs[len(ins) :]
        out_bufs, refs = refs[:n_out], refs[n_out:]
        user, (in_sem, out_sem) = refs[:-2], refs[-2:]
        env = types.SimpleNamespace(**dict(zip(small, small_refs)))
        used, fetched = 0, []
        for key, source, piece, buf in zip(ins, sources, pieces, in_bufs):
            src = big_refs[source]
            copies = []
            for item in piece or (None,):
                if item is None:
                    copy = pltpu.make_async_copy(src, buf, in_sem.at[used])
                else:
                    copy = pltpu.make_async_copy(src.at[item[0]], buf.at[item[1]], in_sem.at[used])
                copy.start()
                copies.append(copy)
                used += 1
            setattr(env, key, Fetched(buf, copies))
            fetched.append(getattr(env, key))
        for key, buf in zip(outs, out_bufs):
            setattr(env, key, buf)
        leaving = [None] * n_out

        def store(*bufs):
            for buf in bufs:
                (index,) = [place for place in range(n_out) if out_bufs[place] is buf]
                leaving[index] = pltpu.make_async_copy(buf, out_refs[index], out_sem.at[index])
                leaving[index].start()

        program(env, core_ref, store, *user)
        store(*[buf for buf, copy in zip(out_bufs, leaving) if copy is None])
        for copy in leaving:
            copy.wait()
        for item in fetched:
            for copy in item.copies:
                copy.wait()

    vmem = pl.BlockSpec(memory_space=pltpu.VMEM)
    anywhere = pl.BlockSpec(memory_space=pl.ANY)
    size = sum(array.size * array.dtype.itemsize for array in big)
    results = pl.pallas_call(
        body,
        in_specs=[pl.BlockSpec(memory_space=pltpu.SMEM)] + [vmem] * n_small + [anywhere] * (n_big + extra),
        out_specs=tuple([anywhere] * n_out),
        out_shape=tuple(outs.values()),
        scratch_shapes=[pltpu.VMEM(shape, dtype) for shape, dtype in zip(shapes, kinds)]
        + [pltpu.VMEM(out.shape, out.dtype) for out in outs.values()]
        + list(scratch)
        + [pltpu.SemaphoreType.DMA((sum(counts),)), pltpu.SemaphoreType.DMA((n_out,))],
        compiler_params=pltpu.CompilerParams(vmem_limit_bytes=56 * MIB),
        cost_estimate=pl.CostEstimate(flops=flops, bytes_accessed=size, transcendentals=0),
        name=name,
    )(core, *small.values(), *big, *order)
    return types.SimpleNamespace(**dict(zip(outs, results)))


def tiles_of(core, rows, window):
    if window == rows + HALO:
        near = pl.multiple_of(core[1], HALO)
        return ((near, 0), (pl.multiple_of(rows - TILE - core[1], HALO), None))
    return ((0, 0), (rows - TILE, 1))


def key_rows(ref, lanes, rows, halo):
    if halo is None:
        return ref[0:rows, lanes]
    if halo == 0:
        return ref[0 : rows + HALO, lanes]
    return jnp.concatenate((ref[0:rows, lanes], ref[rows + HALO : rows + 2 * HALO, lanes]), axis=0)


def key_lanes(ref, row, rows, halo):
    if halo is None:
        return ref[row : row + 1, 0:rows]
    if halo == 0:
        return ref[row : row + 1, 0 : rows + HALO]
    return jnp.concatenate(
        (ref[row : row + 1, 0:rows], ref[row : row + 1, rows + HALO : rows + 2 * HALO]), axis=1
    )


def halves(shape):
    low = lane_low(shape)
    return low, ~low


def keep(mask, values):
    return jnp.where(mask, values, jnp.zeros_like(values))


def gain_rows(gains, index):
    return gains[index : index + 1, :], gains[index + 1 : index + 2, :]


def attn_fwd(core, causal, low_src, base, kv_src, weights, qcol, krow, q_out, k_out, v_out, o_out, lse_out, res_out):
    rows, _ = q_out.shape
    window = k_out.shape[0]
    w_q, w_k, w_v, w_o = weights
    queries = dot_nn(low_src(), w_q[...])
    q_out[...] = (queries.astype(BF).astype(F32) * 0.125).astype(BF)
    k_out[...] = dot_nn(kv_src[...], w_k[...]).astype(BF)
    v_out[...] = dot_nn(kv_src[...], w_v[...]).astype(BF)
    for offset, halo in tiles_of(core, rows, window):
        spot = pl.ds(offset, TILE)
        allowed = qcol[spot, 0:1] == key_lanes(krow, 0, rows, halo)
        if causal:
            allowed = allowed & (key_lanes(krow, 1, rows, halo) <= qcol[spot, 1:2])
        lane = lax.broadcasted_iota(jnp.int32, (TILE, 128), 1)
        packed = jnp.zeros((TILE, 128), F32)
        for pair in range(HEADS // 2):
            lanes = slice(pair * 128, pair * 128 + 128)
            q2 = q_out[spot, lanes]
            k2 = key_rows(k_out, lanes, rows, halo)
            v2 = key_rows(v_out, lanes, rows, halo)
            mixed = None
            for half in range(2):
                scores = dot_nt(keep(halves(q2.shape)[half], q2), k2)
                scores = jnp.where(allowed, scores, masked_score)
                top = jnp.max(scores, axis=-1, keepdims=True)
                weights = jnp.exp(scores - top)
                total = jnp.sum(weights, axis=-1, keepdims=True)
                probs = (weights * (1.0 / total)).astype(BF)
                part = dot_nn(probs, keep(halves(v2.shape)[half], v2))
                mixed = part if mixed is None else mixed + part
                packed = jnp.where(lane == 2 * pair + half, top + jnp.log(total), packed)
            o_out[spot, lanes] = mixed.astype(BF)
        lse_out[:, spot] = jnp.transpose(packed)[0:HEADS, :]
    res_out[...] = base() + dot_nn(o_out[...], w_o[...])


def score_grads(q2, do2, k2, v2, allowed, lse, delta):
    sums = None
    for half in range(2):
        qh = keep(halves(q2.shape)[half], q2)
        doh = keep(halves(do2.shape)[half], do2)
        scores = jnp.where(allowed, dot_nt(k2, qh), masked_score)
        probs = jnp.exp(scores - lse[half])
        gscores = (probs * (dot_nt(v2, doh) - delta[half])).astype(BF)
        parts = (
            dot_tn(gscores, keep(halves(k2.shape)[half], k2)),
            dot_nn(gscores, qh),
            dot_nn(probs.astype(BF), doh),
        )
        sums = parts if sums is None else tuple(a + b for a, b in zip(sums, parts))
    return sums


def attn_head(
    core, causal, grad, resid, o_in, q_in, k_in, v_in, lse_in, weights, gains, gain_at, qrow, kcol, e,
):
    back_out, do_out, delta_out, dwo_out, halo_out, dqh_out, ng_out = e.back, e.do, e.delta, e.dwo, e.halo, e.dqh, e.ng
    w_k, w_v, w_o = weights
    rows, width = do_out.shape
    window = k_in.shape[0]
    back, dgain, dbias = norm_back(resid[...], gain_rows(gains, gain_at)[0], grad)
    back_out[...] = back
    ng_out[0:1, :] = dgain
    ng_out[1:2, :] = dbias
    branch = back.astype(BF)
    do_out[...] = dot_nt(branch, w_o[...]).astype(BF)
    mixed = do_out[...].astype(F32) * o_in[...].astype(F32)
    high = mixed.astype(BF)
    rest = (mixed - high.astype(F32)).astype(BF)
    head = lax.broadcasted_iota(jnp.int32, (16, width), 1) // (width // HEADS)
    which = (head == lax.broadcasted_iota(jnp.int32, (16, width), 0)).astype(F32).astype(BF)
    delta_out[...] = (dot_nt(which, high) + dot_nt(which, rest))[0:HEADS, :]
    for offset, halo in tiles_of(core, rows, window):
        if halo is None:
            continue
        spot = pl.ds(offset, TILE)
        keys = slice(rows + halo * HALO, rows + halo * HALO + HALO)
        here = slice(halo * HALO, halo * HALO + HALO)
        allowed = kcol[keys, 0:1] == qrow[0:1, spot]
        if causal:
            allowed = allowed & (kcol[keys, 1:2] <= qrow[1:2, spot])
        for pair in range(HEADS // 2):
            lanes = slice(pair * 128, pair * 128 + 128)
            heads = (2 * pair, 2 * pair + 1)
            dq2, dk2, dv2 = score_grads(
                q_in[spot, lanes],
                do_out[spot, lanes],
                k_in[keys, lanes],
                v_in[keys, lanes],
                allowed,
                [lse_in[h : h + 1, spot] for h in heads],
                [delta_out[h : h + 1, spot] for h in heads],
            )
            dqh_out[here, lanes] = dq2
            halo_out[0, here, lanes] = dk2.astype(BF)
            halo_out[1, here, lanes] = dv2.astype(BF)
    e.gxh[...] = (dot_nt(halo_out[0], w_k[...]) + dot_nt(halo_out[1], w_v[...])).astype(BF)
    dwo_out[...] = dot_tn(o_in[...], branch).astype(BF)


def attn_body(
    core, causal, window, back, do_in, delta, dqh, low_src, q_in, k_in, v_in, lse_in, w_q, qrow, kcol,
    gq_out, dwq_out, own_out, dq_scr,
):
    rows, width = gq_out.shape
    for tile in range(rows // TILE):
        spot = slice(tile * TILE, tile * TILE + TILE)
        allowed = kcol[0:rows, 0:1] == qrow[0:1, spot]
        if causal:
            allowed = allowed & (kcol[0:rows, 1:2] <= qrow[1:2, spot])
        for pair in range(HEADS // 2):
            lanes = slice(pair * 128, pair * 128 + 128)
            heads = (2 * pair, 2 * pair + 1)
            dq2, dk2, dv2 = score_grads(
                q_in[spot, lanes],
                do_in[spot, lanes],
                k_in[0:rows, lanes],
                v_in[0:rows, lanes],
                allowed,
                [lse_in[h : h + 1, spot] for h in heads],
                [delta[h : h + 1, spot] for h in heads],
            )
            dq_scr[spot, lanes] = dq2
            if tile == 0:
                own_out[0, :, lanes] = dk2
                own_out[1, :, lanes] = dv2
            else:
                own_out[0, :, lanes] += dk2
                own_out[1, :, lanes] += dv2
    for offset, halo in tiles_of(core, rows, window):
        if halo is not None:
            dq_scr[pl.ds(offset, TILE), :] += dqh[halo * HALO : halo * HALO + HALO, :]
    grad_q = (dq_scr[...] * 0.125).astype(BF)
    gq_out[...] = back[...] + dot_nt(grad_q, w_q[...])
    dwq_out[...] = dot_tn(low_src(), grad_q).astype(BF)


def split_places(core, source, kept, sent):
    for parity in range(2):

        @pl.when(core[0] == parity)
        def place():
            for chip in range(kept.shape[0]):
                kept[chip] = source[2 * chip + parity]
                sent[chip] = source[2 * chip + 1 - parity]


def kv_bwd(window_rows, own, halo, w_k, w_v):
    rows = own.shape[1]
    window = window_rows.shape[0]
    dk = own[0].astype(BF)
    dv = own[1].astype(BF)
    total = dot_nt(dk, w_k[...]) + dot_nt(dv, w_v[...])
    dwk = dot_tn(window_rows[0:rows, :], dk) + dot_tn(window_rows[rows:window, :], halo[0])
    dwv = dot_tn(window_rows[0:rows, :], dv) + dot_tn(window_rows[rows:window, :], halo[1])
    return total, dwk.astype(BF), dwv.astype(BF)


def lay_out(stack, mats):
    places, _, width = stack.shape
    per = 6 * width // places
    for slot, matrix in enumerate(mats):
        row, end = slot * width, slot * width + width
        while row < end:
            place, start = divmod(row, per)
            take = min(per - start, end - row)
            at = row - slot * width
            stack[place, start : start + take, :] = matrix[at : at + take, :]
            row += take


def up_tile(pack, tile):
    places, _, width = pack.shape
    return pack[:, 128 + 32 * tile : 160 + 32 * tile, :].reshape(places * 32, width)


def down_tile(pack, tile):
    return pack[4 * tile : 4 * tile + 4, 0:128, :].reshape(512, pack.shape[2])


def ffn_fwd(resid, base, gains, gain_in, gain_out, pack, res_out, low_out, hid_low=None, pre=None):
    hidden = norm_rows(resid[...], *gain_rows(gains, gain_in))
    low = hidden.astype(BF)
    if hid_low is not None:
        hid_low[...] = low
    res_out[...] = hidden + base[...].astype(F32)
    for tile in range(4):
        values = dot_nn(low, up_tile(pack, tile))
        if pre is not None:
            pre[tile] = values
        res_out[...] += dot_nn(gelu(values).astype(BF), down_tile(pack, tile))
    low_out[...] = norm_rows(res_out[...], *gain_rows(gains, gain_out)).astype(BF)


def ffn_bwd(grad, res_late, gains, gain_out, pack, gh_out, late_out, ng_out, hid_low, late_low, dpack, pre=None):
    back, dgain, dbias = norm_back(res_late[...], gain_rows(gains, gain_out)[0], grad)
    late_out[...] = back
    gh_out[...] = back
    late_low[...] = back.astype(BF)
    ng_out[0:1, :] = dgain
    ng_out[1:2, :] = dbias
    places, _, width = dpack.shape
    for tile in range(4):
        activ, slope = gelu_both(dot_nn(hid_low[...], up_tile(pack, tile)) if pre is None else pre[tile])
        grad_down = dot_tn(activ.astype(BF), late_low[...]).astype(BF)
        dpack[4 * tile : 4 * tile + 4, 0:128, :] = grad_down.reshape(4, 128, width)
        grad_act = dot_nt(late_low[...], down_tile(pack, tile)).astype(BF).astype(F32)
        grad_pre = (grad_act * slope).astype(BF)
        grad_up = dot_tn(hid_low[...], grad_pre).astype(BF)
        dpack[:, 128 + 32 * tile : 160 + 32 * tile, :] = grad_up.reshape(places, 32, width)
        gh_out[...] += dot_nt(grad_pre, up_tile(pack, tile))


def kept_shapes(rows, window, width, with_o=True):
    outs = dict(
        q=shape_of(BF, rows, width),
        k=shape_of(BF, window, width),
        v=shape_of(BF, window, width),
        lse=shape_of(F32, HEADS, rows),
    )
    return dict(outs, o=shape_of(BF, rows, width)) if with_o else outs


def head_shapes(rows, window, width):
    return dict(
        back=shape_of(F32, rows, width),
        do=shape_of(BF, rows, width),
        delta=shape_of(F32, HEADS, rows),
        dwo=shape_of(BF, width, width),
        halo=shape_of(BF, 2, window - rows, width),
        gxh=shape_of(BF, window - rows, width),
        dqh=shape_of(F32, window - rows, width),
        ng=shape_of(F32, 2, width),
    )


def weights_of(env):
    return env.wq, env.wk, env.wv, env.wo


def named_mats(mats):
    return dict(wq=mats[0], wk=mats[1], wv=mats[2], wo=mats[3])


def enc_forward(x, window_rows, mats, pack, gains, places):
    rows, width = x.shape
    window = window_rows.shape[0]

    def program(e, core, store):
        attn_fwd(
            core, False, lambda: e.x[...], lambda: e.x[...].astype(F32), e.window, weights_of(e),
            e.qcol, e.krow, e.q, e.k, e.v, e.o, e.lse, e.resid,
        )
        store(e.q, e.k, e.v, e.o, e.lse, e.resid)
        ffn_fwd(e.resid, e.x, e.gains, 0, 2, e.pack, e.two, e.low)

    return fused(
        "enc_forward",
        program,
        places.core,
        dict(qcol=places.qcol, krow=places.krow, gains=gains),
        dict(x=x, window=window_rows, **named_mats(mats), pack=pack),
        dict(
            kept_shapes(rows, window, width),
            resid=shape_of(F32, rows, width),
            two=shape_of(F32, rows, width),
            low=shape_of(BF, rows, width),
        ),
        28 * rows * width * width + 8 * rows * window * width,
    )


def self_forward(z, window_rows, mats, places):
    rows, width = z.shape
    window = window_rows.shape[0]

    def program(e, core, store):
        attn_fwd(
            core, True, lambda: e.z[...], lambda: e.z[...].astype(F32), e.window, weights_of(e),
            e.qcol, e.krow, e.q, e.k, e.v, e.o, e.lse, e.resid,
        )

    return fused(
        "self_forward",
        program,
        places.core,
        dict(qcol=places.qcol, krow=places.krow),
        dict(z=z, window=window_rows, **named_mats(mats)),
        dict(kept_shapes(rows, window, width), resid=shape_of(F32, rows, width)),
        12 * rows * width * width + 8 * rows * window * width,
    )


def cross_and_ffn(three, window_rows, mats, pack, z, cot, gains, places):
    rows, width = three.shape
    window = window_rows.shape[0]
    count, block = pack[0].shape[0], pack[1][1]
    f32_rows, low_rows = pltpu.VMEM((rows, width), F32), pltpu.VMEM((rows, width), BF)

    def program(e, core, store, o, four, five, gh, hid_low, late_low, pre, dpack):
        def first():
            return norm_rows(e.three[...], *gain_rows(e.gains, 4))

        attn_fwd(
            core, False, lambda: first().astype(BF), first, e.window, weights_of(e),
            e.qcol, e.krow, e.q, e.k, e.v, o, e.lse, four,
        )
        store(e.q, e.k, e.v, e.lse)
        ffn_fwd(four, e.z, e.gains, 6, 8, e.pack, five, e.low, hid_low, pre)
        store(e.low)
        ffn_bwd(
            e.cot[...].astype(F32), five, e.gains, 8, e.pack, gh, e.five, e.ng8,
            hid_low, late_low, dpack, pre,
        )
        split_places(core, dpack, e.kept, e.sent)
        store(e.sent, e.kept, e.five, e.ng8)
        attn_head(
            core, False, gh[...], four, o, e.q, e.k, e.v, e.lse, (e.wk, e.wv, e.wo), e.gains, 6, e.qrow, e.kcol, e,
        )

    return fused(
        "cross_and_ffn",
        program,
        places.core,
        dict(qcol=places.qcol, krow=places.krow, qrow=places.qrow, kcol=places.kcol, gains=gains),
        dict(three=three, wq=mats[0], window=window_rows, wk=mats[1], wv=mats[2], wo=mats[3], z=z, pack=pack, cot=cot),
        dict(
            **kept_shapes(rows, window, width, False),
            low=shape_of(BF, rows, width),
            kept=shape_of(BF, count // 2, block, width),
            sent=shape_of(BF, count // 2, block, width),
            five=shape_of(F32, rows, width),
            ng8=shape_of(F32, 2, width),
            **head_shapes(rows, window, width),
        ),
        68 * rows * width * width + 8 * rows * window * width,
        scratch=[
            low_rows, f32_rows, f32_rows, f32_rows, low_rows, low_rows,
            pltpu.VMEM((4, rows, width), F32), pltpu.VMEM((count, block, width), BF),
        ],
    )


def own_rows(array, rows):
    spot = (slice(0, rows),)
    return (array, (rows, array.shape[1]), ((spot, spot),))


def cross_body_self_head(c, low_window, three, s, cross_mats, self_mats, gains, places):
    rows, width = three.shape
    window = c.k.shape[0]

    def program(e, core, store, grad, dq, own):
        def first():
            return norm_rows(e.three[...], *gain_rows(e.gains, 4)).astype(BF)

        attn_body(
            core, False, window, e.back_c, e.do_c, e.delta_c, e.dqh_c, first, e.q_c, e.k_c,
            e.v_c, e.lse_c, e.wq_c, e.qrow, e.kcol, grad, e.dwq, own, dq,
        )
        e.gx[...], e.dwk[...], e.dwv[...] = kv_bwd(e.low_window, own, e.halo_c, e.wk_c, e.wv_c)
        store(e.dwq, e.gx, e.dwk, e.dwv)
        attn_head(
            core, True, grad[...], e.three, e.o, e.q, e.k, e.v, e.lse, (e.wk, e.wv, e.wo), e.gains, 4,
            e.qrow, e.kcol, e,
        )

    return fused(
        "cross_body_self_head",
        program,
        places.core,
        dict(qrow=places.qrow, kcol=places.kcol, gains=gains),
        dict(
            q_c=c.q,
            do_c=c.do,
            k_c=own_rows(c.k, rows),
            v_c=own_rows(c.v, rows),
            lse_c=c.lse,
            delta_c=c.delta,
            dqh_c=c.dqh,
            back_c=c.back,
            wq_c=cross_mats[0],
            three=three,
            low_window=low_window,
            halo_c=c.halo,
            wk_c=cross_mats[1],
            wv_c=cross_mats[2],
            wo=self_mats[3],
            o=s.o,
            q=s.q,
            k=s.k,
            v=s.v,
            lse=s.lse,
            wk=self_mats[1],
            wv=self_mats[2],
        ),
        dict(
            gx=shape_of(F32, rows, width),
            dwq=shape_of(BF, width, width),
            dwk=shape_of(BF, width, width),
            dwv=shape_of(BF, width, width),
            **head_shapes(rows, window, width),
        ),
        18 * rows * width * width + 10 * rows * window * width,
        scratch=[pltpu.VMEM((rows, width), F32), pltpu.VMEM((rows, width), F32), pltpu.VMEM((2, rows, width), F32)],
    )


def input_body(name, kept, head, src, window_rows, mats, causal, add, layout, grads, norms, group, places, order):
    rows, width = src.shape
    window = kept.k.shape[0]
    block = 6 * width // group + (16 if norms else 0)

    def program(e, core, store, dq, own, gq, stack, lines):
        others = (e.other0, e.other1, e.other2, e.other3, e.other4)
        attn_body(
            core, causal, window, e.back, e.do, e.delta, e.dqh, lambda: e.src[...], e.q, e.k,
            e.v, e.lse, e.wq, e.qrow, e.kcol, gq, e.dwq, own, dq,
        )
        total, dwk, dwv = kv_bwd(e.window, own, e.halo, e.wk, e.wv)
        e.dwk[...] = dwk
        parts = dict(q=e.dwq, k=dwk, v=dwv)
        lay_out(stack, [others[item] if isinstance(item, int) else parts[item] for item in layout])
        if norms:
            lines[...] = jnp.zeros_like(lines)
            for index, item in enumerate((e.ng0, e.ng1, e.ng2, e.ng3, e.ng4)):
                lines[2 * index : 2 * index + 2, :] = item[...]
            for place in range(group):
                stack[place, block - 16 :, :] = lines[...].astype(BF)
        split_places(core, stack, e.kept, e.sent)
        store(e.sent, e.kept)
        e.grad[...] = gq[...] + total + e.add[...]

    grads = tuple(grads) + (head.dwo,) * (5 - len(grads))
    ng = dict(ng0=norms[0], ng1=norms[1], ng2=norms[2], ng3=norms[3], ng4=norms[4]) if norms else {}
    return fused(
        name,
        program,
        places.core,
        dict(qrow=places.qrow, kcol=places.kcol),
        dict(
            q=kept.q,
            do=head.do,
            k=own_rows(kept.k, rows),
            v=own_rows(kept.v, rows),
            lse=kept.lse,
            delta=head.delta,
            dqh=head.dqh,
            back=head.back,
            wq=mats[0],
            src=src,
            window=window_rows,
            halo=head.halo,
            wk=mats[1],
            wv=mats[2],
            other0=grads[0],
            other1=grads[1],
            other2=grads[2],
            other3=grads[3],
            other4=grads[4],
            add=add,
            **ng,
        ),
        dict(
            sent=shape_of(BF, group // 2, block, width),
            kept=shape_of(BF, group // 2, block, width),
            dwq=shape_of(BF, width, width),
            dwk=shape_of(BF, width, width),
            grad=shape_of(F32, rows, width),
        ),
        14 * rows * width * width + 10 * rows * rows * width,
        scratch=[
            pltpu.VMEM((rows, width), F32), pltpu.VMEM((2, rows, width), F32), pltpu.VMEM((rows, width), F32),
            pltpu.VMEM((group, block, width), BF), pltpu.VMEM((16, width), F32),
        ],
        order=order,
    )


def enc_ffn_head(grad, one, two, kept, pack, mats, gains, places, order):
    rows, width = one.shape
    window = kept.k.shape[0]
    count, block = pack[0].shape[0], pack[1][1]

    def program(e, core, store, gh, hid_low, late_low, dpack):
        hid_low[...] = norm_rows(e.one[...], *gain_rows(e.gains, 0)).astype(BF)
        ffn_bwd(
            e.grad[...], e.two, e.gains, 2, e.pack, gh, e.late, e.ng2, hid_low, late_low, dpack
        )
        split_places(core, dpack, e.kept, e.sent)
        store(e.sent, e.kept, e.late, e.ng2)
        attn_head(
            core, False, gh[...], e.one, e.o, e.q, e.k, e.v, e.lse, (e.wk, e.wv, e.wo), e.gains, 0, e.qrow, e.kcol, e,
        )

    return fused(
        "enc_ffn_head",
        program,
        places.core,
        dict(qrow=places.qrow, kcol=places.kcol, gains=gains),
        dict(
            one=one,
            two=two,
            grad=grad,
            pack=pack,
            wo=mats[3],
            wk=mats[1],
            wv=mats[2],
            o=kept.o,
            q=kept.q,
            k=kept.k,
            v=kept.v,
            lse=kept.lse,
        ),
        dict(
            sent=shape_of(BF, count // 2, block, width),
            kept=shape_of(BF, count // 2, block, width),
            late=shape_of(F32, rows, width),
            ng2=shape_of(F32, 2, width),
            **head_shapes(rows, window, width),
        ),
        44 * rows * width * width + 10 * TILE * TILE * width,
        scratch=[
            pltpu.VMEM((rows, width), F32), pltpu.VMEM((rows, width), BF), pltpu.VMEM((rows, width), BF),
            pltpu.VMEM((count, block, width), BF),
        ],
        order=order,
    )


def segments_at(bounds, places, total_len):
    found = jnp.sum((bounds[None, :] <= places[:, None]).astype(jnp.int32), axis=-1)
    return jnp.where((places >= 0) & (places < total_len), found, -1)


def row_squares(values):
    if values.ndim == 2:
        return jnp.sum(values * values, axis=1)
    return values * values


def owner_groups(rows_local, owner, per_group, count):
    group_ids = (owner * rows_local + jnp.arange(rows_local, dtype=jnp.int32)) // per_group
    return group_ids[:, None] == jnp.arange(count, dtype=jnp.int32)[None, :]


def group_sum(onehot, row_values):
    return jnp.sum(jnp.where(onehot, row_values[:, None], 0.0), axis=0)


def lamb_moments(master, grad_rows, first, second):
    first_new = beta_one * first + (1.0 - beta_one) * grad_rows
    second_new = beta_two * second + (1.0 - beta_two) * grad_rows * grad_rows
    update = (
        first_new
        / (1.0 - beta_one**STEP)
        / (jnp.sqrt(second_new / (1.0 - beta_two**STEP)) + lamb_eps)
        + weight_decay * master
    )
    return (first_new, second_new, update)


GROUP = ("lo", "y", "c")
CHIPS = ("lo", "y")
EVERY = ("hi", "lo", "y", "c")


def swap_hi(array):
    return lax.ppermute(array, "hi", [(0, 1), (1, 0)])


def shift_hi(array, distance):
    count = lax.axis_size("hi")
    route = [(i - distance, i) for i in range(count) if i - distance in range(count)]
    return lax.ppermute(array, "hi", route)


def halo_rows(rows_array):
    rows = rows_array.shape[0]
    if lax.axis_size("hi") == 2:
        return swap_hi(jnp.where(lax.axis_index("hi") == 0, rows_array[rows - HALO :], rows_array[:HALO]))
    left = shift_hi(rows_array[rows - HALO :], 1)
    right = shift_hi(rows_array[:HALO], -1)
    return jnp.concatenate((left, right), axis=0)


def halo_return(grads, total):
    rest = total.shape[0] - HALO
    if lax.axis_size("hi") == 2:
        back = swap_hi(grads)
        last = lax.axis_index("hi") == 0
        return back, total + jnp.where(last, jnp.pad(back, ((rest, 0), (0, 0))), jnp.pad(back, ((0, rest), (0, 0))))
    back = jnp.concatenate((shift_hi(grads[HALO:], 1), shift_hi(grads[:HALO], -1)), axis=0)
    return back, total + jnp.pad(back[:HALO], ((0, rest), (0, 0))) + jnp.pad(back[HALO:], ((rest, 0), (0, 0)))


def pack_up(rows):
    count, units = rows.shape
    return rows.reshape(count, 4, units // 4).swapaxes(0, 1).reshape(4 * count, units // 4)


def unpack_up(packed):
    count, width = packed.shape
    return packed.reshape(4, count // 4, width).swapaxes(0, 1).reshape(count // 4, 4 * width)


def swap_core(array):
    return lax.ppermute(array, "c", [(0, 1), (1, 0)])


def tie(array, other):
    bit = lax.slice(other, (0,) * other.ndim, (1,) * other.ndim).reshape(()) * 0
    return array + bit.astype(array.dtype)


def from_parity(mine, other):
    even = lax.axis_index("c") == 0
    full = jnp.stack((jnp.where(even, mine, other), jnp.where(even, other, mine)), axis=1)
    return full.reshape(-1, *mine.shape[1:])


def gather_plain(attn_shard, up_shard, down_shard, norm_shard):
    width = attn_shard.shape[1]
    group = lax.axis_size(GROUP)
    norm_count = norm_shard.shape[0]
    attn = lax.all_gather(attn_shard, EVERY, axis=0, tiled=True)
    down = lax.all_gather(down_shard, EVERY, axis=0, tiled=True).reshape(2, group, -1, width)
    up = lax.all_gather(up_shard, EVERY, axis=0, tiled=True)
    up = up.reshape(2, group, -1, 4, width).swapaxes(2, 3).reshape(2, group, -1, width)
    norms = jnp.pad(norm_shard[None, :], ((0, 0), (0, width - norm_count)))
    norms = lax.all_gather(norms, EVERY, axis=0, tiled=True)[:, :norm_count]
    ffn = jnp.concatenate((down, up), axis=2)
    attn = attn.reshape(2, group, -1, width)
    full = jnp.concatenate((attn[0], attn[1], ffn[0]), axis=1)
    return full, ffn[1], norms.reshape(10, width).astype(F32)


def reduce_cores(kept, sent):
    return (kept.astype(F32) + swap_core(sent).astype(F32)).astype(BF)


def reduce_chips(pair):
    parts = lax.all_to_all(pair, CHIPS, split_axis=0, concat_axis=0, tiled=True)
    return jnp.sum(parts.astype(F32), axis=0)


def join_halves(zero, one):
    first = lax.axis_index("hi") == 0
    mine = jnp.where(first, zero, one)
    sent = jnp.where(first, one, zero).astype(BF)
    return mine + swap_hi(sent).astype(F32)


def reduce_plain(attn0, attn1, ffn0, ffn1, norm_local):
    group, _, width = ffn0.shape

    def scatter(rows):
        return lax.psum_scatter(rows, EVERY, scatter_dimension=0, tiled=True).astype(F32)

    attn = jnp.concatenate((attn0, attn1), axis=0).reshape(-1, width)
    ffn = jnp.stack((ffn0, ffn1)).reshape(2 * group, -1, width)
    up = ffn[:, 128:].reshape(2 * group, 4, 32, width).swapaxes(1, 2).reshape(-1, 4 * width)
    norms = lax.psum_scatter(
        norm_local.reshape(lax.axis_size(EVERY), -1), EVERY, scatter_dimension=0, tiled=True
    )
    return scatter(attn), scatter(up), scatter(ffn[:, :128].reshape(-1, width)), norms[0]


def shards(
    enc_in,
    dec_in,
    cotangent,
    lengths,
    attn_master,
    ffn_in_master,
    ffn_out_master,
    norm_master,
    attn_first,
    ffn_in_first,
    ffn_out_first,
    norm_first,
    attn_second,
    ffn_in_second,
    ffn_out_second,
    norm_second,
):
    micro, _, length_dev, width = enc_in.shape
    rows = micro * length_dev
    hidden_units = ffn_in_master.shape[1]
    high, low = lax.axis_index("hi"), lax.axis_index("lo")
    n_high = lax.axis_size("hi")
    owner = lax.axis_index(EVERY)
    masters = (attn_master, ffn_in_master, ffn_out_master, norm_master)
    group_info = ((width, 12), (width, 2), (hidden_units, 2), (width, 10))
    onehots = [
        owner_groups(master.shape[0], owner, info[0], info[1])
        for master, info in zip(masters, group_info)
    ]
    weight_local = jnp.concatenate(
        [group_sum(onehot, row_squares(master)) for onehot, master in zip(onehots, masters)]
    )

    plain = n_high != 2

    def regroup(*arrays):
        packed = jnp.stack([array[:, 0] for array in arrays], axis=1)
        packed = lax.all_to_all(packed, "lo", split_axis=0, concat_axis=0, tiled=True)
        packed = packed.swapaxes(0, 1).reshape(len(arrays), rows, width)
        return packed

    core = jnp.stack((lax.axis_index("c"), jnp.where(high == 0, rows - HALO, 0))).astype(jnp.int32)
    attn_rows = attn_master.shape[0]
    norm_count = norm_master.shape[0]
    attn_low, up_low, down_low, norm_low = [master.astype(BF) for master in masters]
    if plain:
        full, late, gains = gather_plain(attn_low, up_low, down_low, norm_low)
        enc_rows, dec_rows, cot_rows = regroup(enc_in, dec_in, cotangent)
    else:
        first = high == 0
        norm_pad = jnp.pad(norm_low[None, :], ((0, 15), (0, width - norm_count)))
        mine = jnp.concatenate((attn_low, down_low, pack_up(up_low), norm_pad), axis=0)
        other = swap_hi(mine)
        enc_rows, dec_rows, cot_rows = regroup(enc_in, dec_in, cotangent)
        zero = jnp.where(first, mine, other)
        one = jnp.where(first, other, mine)
        last = mine.shape[0] - 16
        early = (one[:attn_rows], zero[attn_rows : last + 1], one[last:-1])
        early = jnp.concatenate((tie(zero[:attn_rows], enc_rows), *early), axis=0)
        full = lax.all_gather(early, GROUP, axis=0, tiled=False)
        late = lax.all_gather(one[attn_rows:last], GROUP, axis=0, tiled=False)
        gains = full[:, attn_rows + last : attn_rows + last + 2, :norm_count].swapaxes(0, 1)
        gains = gains.reshape(10, width).astype(F32)
    enc_window = jnp.concatenate((enc_rows, halo_rows(enc_rows)), axis=0)
    dec_window = jnp.concatenate((dec_rows, halo_rows(dec_rows)), axis=0)
    group = full.shape[0]

    total_len = rows * n_high
    bounds = jnp.cumsum(lengths[:, 0, :], axis=-1)
    bounds = lax.dynamic_index_in_dim(bounds, low, 0, keepdims=False)
    base = high * rows
    own_pos = base + jnp.arange(rows, dtype=jnp.int32)
    step = jnp.arange(HALO, dtype=jnp.int32)
    if n_high == 2:
        halo_pos = jnp.where(high == 0, rows, rows - HALO) + step
    else:
        halo_pos = jnp.concatenate((base - HALO + step, base + rows + step))
    key_pos = jnp.concatenate((own_pos, halo_pos))
    key_seg = segments_at(bounds, key_pos, total_len)
    krow = jnp.stack((key_seg, key_pos), axis=0)
    kcol = jnp.stack((key_seg, key_pos), axis=1)
    places = types.SimpleNamespace(
        krow=krow,
        kcol=kcol,
        qrow=krow[:, :rows],
        qcol=kcol[:rows],
        core=core,
    )

    per = 6 * width // group
    mats = [square(full, 0, index) for index in range(6)] + [square(full, per, index) for index in range(6)]
    pack0, pack1 = rows_of(full, 2 * per, late.shape[1]), rows_of(late, 0, late.shape[1])
    e = enc_forward(enc_rows, enc_window, mats[0:4], pack0, gains, places)
    low_window = jnp.concatenate((e.low, halo_rows(e.low)), axis=0)
    s = self_forward(dec_rows, dec_window, mats[4:8], places)
    c = cross_and_ffn(s.resid, low_window, mats[8:12], pack1, dec_rows, cot_rows, gains, places)

    def restore(*arrays):
        outs = jnp.stack(arrays, axis=0).reshape(len(arrays), micro, length_dev, width).swapaxes(0, 1)
        return lax.all_to_all(outs, "lo", split_axis=0, concat_axis=0, tiled=True)

    sh = cross_body_self_head(c, low_window, s.resid, s, mats[8:12], mats[4:8], gains, places)
    back_c, grad_encoded = halo_return(c.gxh, sh.gx)
    lows = restore(e.low, c.low)
    pair_f1 = c.kept if plain else reduce_cores(tie(tie(c.kept, sh.ng), lows), c.sent)
    sb = input_body(
        "self_body", s, sh, dec_rows, dec_window, mats[4:8], True, c.five, ("v", 0, 1, 2, 3, 4),
        (sh.dwo, sh.dwq, sh.dwk, sh.dwv, c.dwo), (), group, places, (pair_f1, back_c),
    )
    if plain:
        pair_a1 = sb.kept
    else:
        part_f1 = reduce_chips(pair_f1)
        pair_a1 = reduce_cores(sb.kept, sb.sent)
    back_s, dec_grad = halo_return(sh.gxh, sb.grad)
    eh = enc_ffn_head(grad_encoded, e.resid, e.two, e, pack0, mats[0:4], gains, places, (pair_a1, back_s))
    if plain:
        pair_f0 = eh.kept
    else:
        part_a1 = reduce_chips(pair_a1)
        pair_f0 = reduce_cores(tie(eh.kept, part_a1), eh.sent)
    eb = input_body(
        "enc_body", e, eh, enc_rows, enc_window, mats[0:4], False, eh.late, ("q", "k", "v", 0, 1, 2),
        (eh.dwo, sb.dwq, sb.dwk), (eh.ng, eh.ng2, sh.ng, c.ng, c.ng8), group, places, (pair_f0,),
    )
    back_e, enc_grad = halo_return(eh.gxh, eb.grad)
    enc_grad, dec_grad = enc_grad.astype(BF), dec_grad.astype(BF)
    if plain:
        attn_own, up_own, down_own, norm_own = reduce_plain(
            from_parity(eb.kept, eb.sent)[:, :per],
            from_parity(sb.kept, sb.sent),
            from_parity(eh.kept, eh.sent),
            from_parity(c.kept, c.sent),
            jnp.concatenate((eh.ng, eh.ng2, sh.ng, c.ng, c.ng8), axis=0).reshape(n_high, group, norm_count),
        )
        grads = restore(enc_grad, dec_grad)
    else:
        part_f0 = reduce_chips(pair_f0)
        part_a0 = reduce_chips(reduce_cores(tie(eb.kept, back_e), eb.sent))
        grads = restore(tie(enc_grad, part_a0), dec_grad)
        ffn_own = join_halves(part_f0, part_f1)
        both = join_halves(part_a0, jnp.concatenate((part_a1, part_a0[attn_rows:]), axis=0))
        attn_own, up_own, down_own = both[:attn_rows], unpack_up(ffn_own[128:]), ffn_own[:128]
        norm_own = lax.dynamic_slice_in_dim(both[attn_rows:].reshape(-1), owner * norm_count, norm_count)

    owned = (attn_own, up_own, down_own, norm_own)
    firsts = (attn_first, ffn_in_first, ffn_out_first, norm_first)
    seconds = (attn_second, ffn_in_second, ffn_out_second, norm_second)
    moments = [
        lamb_moments(masters[index], owned[index], firsts[index], seconds[index])
        for index in range(4)
    ]
    update_local = jnp.concatenate(
        [group_sum(onehots[index], row_squares(moments[index][2])) for index in range(4)]
    )
    squares = jnp.stack((weight_local, update_local))
    squares = jnp.pad(squares, ((0, 6), (0, 128 - squares.shape[1])))
    count = lax.axis_size(EVERY)
    squares = tie(squares, grads)
    squares = jnp.broadcast_to(squares[None], (count,) + squares.shape)
    squares = jnp.sum(lax.all_to_all(squares, EVERY, split_axis=0, concat_axis=0, tiled=True), axis=0)
    norms = jnp.sqrt(squares[:2, :26])
    ratio = norms[0] / norms[1]
    bounds_at = (0, 12, 14, 16, 26)
    new_weights = []
    for index in range(4):
        row_ratio = jnp.sum(
            jnp.where(onehots[index], ratio[None, bounds_at[index] : bounds_at[index + 1]], 0.0), axis=1
        )
        if masters[index].ndim == 2:
            row_ratio = row_ratio[:, None]
        new_weights.append(masters[index] - learn_rate * row_ratio * moments[index][2])
    return (
        lows[:, 0][:, None],
        lows[:, 1][:, None],
        grads[:, 0][:, None].astype(F32),
        grads[:, 1][:, None].astype(F32),
        *owned,
        *new_weights,
        *[item[0] for item in moments],
        *[item[1] for item in moments],
        *[item.astype(BF) for item in new_weights],
        norms,
        ratio,
    )


def solution(mesh):
    count_seq, count_stream = mesh.shape["seq"], mesh.shape["stream"]

    def run(*args):
        micro = args[0].shape[0]
        split = Mesh(
            mesh.devices.reshape(count_seq // micro, micro, count_stream // 2, 2), ("hi", "lo", "y", "c")
        )
        tokens = P(None, ("y", "c"), ("hi", "lo"), None)
        wide = P(EVERY, None)
        flat = P(EVERY)
        owned = (wide, wide, wide, flat)
        return jax.shard_map(
            shards,
            mesh=split,
            in_specs=(tokens, tokens, tokens, P(None, ("y", "c"), None), *owned, *owned, *owned),
            out_specs=(tokens, tokens, tokens, tokens, *owned, *owned, *owned, *owned, *owned, P(), P()),
            check_vma=False,
        )(*args)

    return run
```

```python
import types

import jax
import jax.numpy as jnp
from jax import lax
from jax.experimental import pallas as pl
from jax.experimental.pallas import tpu as pltpu
from jax.sharding import Mesh
from jax.sharding import PartitionSpec as P

HEADS = 8
STEP = 5
HALO = 256
TILE = 256

norm_eps = 1e-05
beta_one = 0.5
beta_two = 0.5
lamb_eps = 1e-06
weight_decay = 0.01
learn_rate = 0.5
masked_score = -1e30

BF = jnp.bfloat16
F32 = jnp.float32
MIB = 1024 * 1024


def dot_nn(a, b):
    return lax.dot_general(a, b, (((1,), (0,)), ((), ())), preferred_element_type=F32)


def dot_nt(a, b):
    return lax.dot_general(a, b, (((1,), (1,)), ((), ())), preferred_element_type=F32)


def dot_tn(a, b):
    return lax.dot_general(a, b, (((0,), (0,)), ((), ())), preferred_element_type=F32)


def norm_parts(rows):
    centre = rows - jnp.mean(rows, axis=-1, keepdims=True)
    inv = lax.rsqrt(jnp.mean(centre * centre, axis=-1, keepdims=True) + norm_eps)
    return centre * inv, inv


def norm_rows(rows, gain, bias):
    return norm_parts(rows)[0] * gain + bias


def norm_back(rows, gain, grad):
    unit, inv = norm_parts(rows)
    lead = grad * gain
    back = inv * (
        lead
        - jnp.mean(lead, axis=-1, keepdims=True)
        - unit * jnp.mean(lead * unit, axis=-1, keepdims=True)
    )
    return (
        back,
        jnp.sum(grad * unit, axis=0, keepdims=True),
        jnp.sum(grad, axis=0, keepdims=True),
    )


gelu_a = 0.7978845608028654
gelu_b = 0.044715


def gelu(v):
    return 0.5 * v * (1.0 + jnp.tanh(gelu_a * (v + gelu_b * (v * v * v))))


def gelu_both(v):
    sq = v * v
    t = jnp.tanh(gelu_a * (v + gelu_b * (sq * v)))
    half = 0.5 * (1.0 + t)
    slope = half + 0.5 * v * (1.0 - t * t) * (gelu_a * (1.0 + 3.0 * gelu_b * sq))
    return v * half, slope


def lane_low(shape):
    return lax.broadcasted_iota(jnp.int32, shape, 1) < 64


def shape_of(dtype, *dims):
    return jax.ShapeDtypeStruct(dims, dtype)


class Fetched:
    def __init__(self, ref, copies):
        self.ref, self.copies, self.shape = ref, copies, ref.shape

    def __getitem__(self, index):
        for copy in self.copies:
            copy.wait()
        self.copies = ()
        return self.ref[index]


def square(array, start, index):
    places, _, width = array.shape
    per = 6 * width // places
    pieces = []
    row, end = index * width, index * width + width
    while row < end:
        place, at = divmod(row, per)
        take = min(per - at, end - row)
        spot = slice(row - index * width, row - index * width + take)
        pieces.append(((place, slice(start + at, start + at + take)), spot))
        row += take
    return (array, (width, width), tuple(pieces))


def rows_of(array, start, count):
    places, _, width = array.shape
    every = slice(0, places)
    return (array, (places, count, width), (((every, slice(start, start + count)), every),))


def fused(name, program, core, small, ins, outs, flops, scratch=(), order=()):
    big, sources = [], []
    for item in ins.values():
        array = item[0] if isinstance(item, tuple) else item
        known = [index for index, other in enumerate(big) if other is array]
        sources.append(known[0] if known else len(big))
        if not known:
            big.append(array)
    shapes = [item[1] if isinstance(item, tuple) else item.shape for item in ins.values()]
    pieces = [item[2] if isinstance(item, tuple) else None for item in ins.values()]
    kinds = [big[source].dtype for source in sources]
    counts = [len(item) if item else 1 for item in pieces]
    n_small, n_big, n_out, extra = len(small), len(big), len(outs), len(order)

    def body(core_ref, *refs):
        small_refs, refs = refs[:n_small], refs[n_small:]
        big_refs, refs = refs[:n_big], refs[n_big + extra :]
        out_refs, refs = refs[:n_out], refs[n_out:]
        in_bufs, refs = refs[: len(ins)], refs[len(ins) :]
        out_bufs, refs = refs[:n_out], refs[n_out:]
        user, (in_sem, out_sem) = refs[:-2], refs[-2:]
        env = types.SimpleNamespace(**dict(zip(small, small_refs)))
        used, fetched = 0, []
        for key, source, piece, buf in zip(ins, sources, pieces, in_bufs):
            src = big_refs[source]
            copies = []
            for item in piece or (None,):
                if item is None:
                    copy = pltpu.make_async_copy(src, buf, in_sem.at[used])
                else:
                    copy = pltpu.make_async_copy(src.at[item[0]], buf.at[item[1]], in_sem.at[used])
                copy.start()
                copies.append(copy)
                used += 1
            setattr(env, key, Fetched(buf, copies))
            fetched.append(getattr(env, key))
        for key, buf in zip(outs, out_bufs):
            setattr(env, key, buf)
        leaving = [None] * n_out

        def store(*bufs):
            for buf in bufs:
                (index,) = [place for place in range(n_out) if out_bufs[place] is buf]
                leaving[index] = pltpu.make_async_copy(buf, out_refs[index], out_sem.at[index])
                leaving[index].start()

        program(env, core_ref, store, *user)
        store(*[buf for buf, copy in zip(out_bufs, leaving) if copy is None])
        for copy in leaving:
            copy.wait()
        for item in fetched:
            for copy in item.copies:
                copy.wait()

    vmem = pl.BlockSpec(memory_space=pltpu.VMEM)
    anywhere = pl.BlockSpec(memory_space=pl.ANY)
    size = sum(array.size * array.dtype.itemsize for array in big)
    results = pl.pallas_call(
        body,
        in_specs=[pl.BlockSpec(memory_space=pltpu.SMEM)] + [vmem] * n_small + [anywhere] * (n_big + extra),
        out_specs=tuple([anywhere] * n_out),
        out_shape=tuple(outs.values()),
        scratch_shapes=[pltpu.VMEM(shape, dtype) for shape, dtype in zip(shapes, kinds)]
        + [pltpu.VMEM(out.shape, out.dtype) for out in outs.values()]
        + list(scratch)
        + [pltpu.SemaphoreType.DMA((sum(counts),)), pltpu.SemaphoreType.DMA((n_out,))],
        compiler_params=pltpu.CompilerParams(vmem_limit_bytes=56 * MIB),
        cost_estimate=pl.CostEstimate(flops=flops, bytes_accessed=size, transcendentals=0),
        name=name,
    )(core, *small.values(), *big, *order)
    return types.SimpleNamespace(**dict(zip(outs, results)))


def tiles_of(core, rows, window):
    if window == rows + HALO:
        near = pl.multiple_of(core[1], HALO)
        return ((near, 0), (pl.multiple_of(rows - TILE - core[1], HALO), None))
    return ((0, 0), (rows - TILE, 1))


def key_rows(ref, lanes, rows, halo):
    if halo is None:
        return ref[0:rows, lanes]
    if halo == 0:
        return ref[0 : rows + HALO, lanes]
    return jnp.concatenate((ref[0:rows, lanes], ref[rows + HALO : rows + 2 * HALO, lanes]), axis=0)


def key_lanes(ref, row, rows, halo):
    if halo is None:
        return ref[row : row + 1, 0:rows]
    if halo == 0:
        return ref[row : row + 1, 0 : rows + HALO]
    return jnp.concatenate(
        (ref[row : row + 1, 0:rows], ref[row : row + 1, rows + HALO : rows + 2 * HALO]), axis=1
    )


def halves(shape):
    low = lane_low(shape)
    return low, ~low


def keep(mask, values):
    return jnp.where(mask, values, jnp.zeros_like(values))


def gain_rows(gains, index):
    return gains[index : index + 1, :], gains[index + 1 : index + 2, :]


def attn_fwd(core, causal, low_src, base, kv_src, weights, qcol, krow, q_out, k_out, v_out, o_out, lse_out, res_out):
    rows, _ = q_out.shape
    window = k_out.shape[0]
    w_q, w_k, w_v, w_o = weights
    queries = dot_nn(low_src(), w_q[...])
    q_out[...] = (queries.astype(BF).astype(F32) * 0.125).astype(BF)
    k_out[...] = dot_nn(kv_src[...], w_k[...]).astype(BF)
    v_out[...] = dot_nn(kv_src[...], w_v[...]).astype(BF)
    for offset, halo in tiles_of(core, rows, window):
        spot = pl.ds(offset, TILE)
        allowed = qcol[spot, 0:1] == key_lanes(krow, 0, rows, halo)
        if causal:
            allowed = allowed & (key_lanes(krow, 1, rows, halo) <= qcol[spot, 1:2])
        lane = lax.broadcasted_iota(jnp.int32, (TILE, 128), 1)
        packed = jnp.zeros((TILE, 128), F32)
        for pair in range(HEADS // 2):
            lanes = slice(pair * 128, pair * 128 + 128)
            q2 = q_out[spot, lanes]
            k2 = key_rows(k_out, lanes, rows, halo)
            v2 = key_rows(v_out, lanes, rows, halo)
            mixed = None
            for half in range(2):
                scores = dot_nt(keep(halves(q2.shape)[half], q2), k2)
                scores = jnp.where(allowed, scores, masked_score)
                top = jnp.max(scores, axis=-1, keepdims=True)
                weights = jnp.exp(scores - top)
                total = jnp.sum(weights, axis=-1, keepdims=True)
                probs = (weights * (1.0 / total)).astype(BF)
                part = dot_nn(probs, keep(halves(v2.shape)[half], v2))
                mixed = part if mixed is None else mixed + part
                packed = jnp.where(lane == 2 * pair + half, top + jnp.log(total), packed)
            o_out[spot, lanes] = mixed.astype(BF)
        lse_out[:, spot] = jnp.transpose(packed)[0:HEADS, :]
    res_out[...] = base() + dot_nn(o_out[...], w_o[...])


def score_grads(q2, do2, k2, v2, allowed, lse, delta):
    sums = None
    for half in range(2):
        qh = keep(halves(q2.shape)[half], q2)
        doh = keep(halves(do2.shape)[half], do2)
        scores = jnp.where(allowed, dot_nt(k2, qh), masked_score)
        probs = jnp.exp(scores - lse[half])
        gscores = (probs * (dot_nt(v2, doh) - delta[half])).astype(BF)
        parts = (
            dot_tn(gscores, keep(halves(k2.shape)[half], k2)),
            dot_nn(gscores, qh),
            dot_nn(probs.astype(BF), doh),
        )
        sums = parts if sums is None else tuple(a + b for a, b in zip(sums, parts))
    return sums


def attn_head(
    core, causal, grad, resid, o_in, q_in, k_in, v_in, lse_in, weights, gains, gain_at, qrow, kcol, e,
):
    back_out, do_out, delta_out, dwo_out, halo_out, dqh_out, ng_out = e.back, e.do, e.delta, e.dwo, e.halo, e.dqh, e.ng
    w_k, w_v, w_o = weights
    rows, width = do_out.shape
    window = k_in.shape[0]
    back, dgain, dbias = norm_back(resid[...], gain_rows(gains, gain_at)[0], grad)
    back_out[...] = back
    ng_out[0:1, :] = dgain
    ng_out[1:2, :] = dbias
    branch = back.astype(BF)
    do_out[...] = dot_nt(branch, w_o[...]).astype(BF)
    mixed = do_out[...].astype(F32) * o_in[...].astype(F32)
    high = mixed.astype(BF)
    rest = (mixed - high.astype(F32)).astype(BF)
    head = lax.broadcasted_iota(jnp.int32, (16, width), 1) // (width // HEADS)
    which = (head == lax.broadcasted_iota(jnp.int32, (16, width), 0)).astype(F32).astype(BF)
    delta_out[...] = (dot_nt(which, high) + dot_nt(which, rest))[0:HEADS, :]
    for offset, halo in tiles_of(core, rows, window):
        if halo is None:
            continue
        spot = pl.ds(offset, TILE)
        keys = slice(rows + halo * HALO, rows + halo * HALO + HALO)
        here = slice(halo * HALO, halo * HALO + HALO)
        allowed = kcol[keys, 0:1] == qrow[0:1, spot]
        if causal:
            allowed = allowed & (kcol[keys, 1:2] <= qrow[1:2, spot])
        for pair in range(HEADS // 2):
            lanes = slice(pair * 128, pair * 128 + 128)
            heads = (2 * pair, 2 * pair + 1)
            dq2, dk2, dv2 = score_grads(
                q_in[spot, lanes],
                do_out[spot, lanes],
                k_in[keys, lanes],
                v_in[keys, lanes],
                allowed,
                [lse_in[h : h + 1, spot] for h in heads],
                [delta_out[h : h + 1, spot] for h in heads],
            )
            dqh_out[here, lanes] = dq2
            halo_out[0, here, lanes] = dk2.astype(BF)
            halo_out[1, here, lanes] = dv2.astype(BF)
    e.gxh[...] = (dot_nt(halo_out[0], w_k[...]) + dot_nt(halo_out[1], w_v[...])).astype(BF)
    dwo_out[...] = dot_tn(o_in[...], branch).astype(BF)


def attn_body(
    core, causal, window, back, do_in, delta, dqh, low_src, q_in, k_in, v_in, lse_in, w_q, qrow, kcol,
    gq_out, dwq_out, own_out, dq_scr,
):
    rows, width = gq_out.shape
    for tile in range(rows // TILE):
        spot = slice(tile * TILE, tile * TILE + TILE)
        allowed = kcol[0:rows, 0:1] == qrow[0:1, spot]
        if causal:
            allowed = allowed & (kcol[0:rows, 1:2] <= qrow[1:2, spot])
        for pair in range(HEADS // 2):
            lanes = slice(pair * 128, pair * 128 + 128)
            heads = (2 * pair, 2 * pair + 1)
            dq2, dk2, dv2 = score_grads(
                q_in[spot, lanes],
                do_in[spot, lanes],
                k_in[0:rows, lanes],
                v_in[0:rows, lanes],
                allowed,
                [lse_in[h : h + 1, spot] for h in heads],
                [delta[h : h + 1, spot] for h in heads],
            )
            dq_scr[spot, lanes] = dq2
            if tile == 0:
                own_out[0, :, lanes] = dk2
                own_out[1, :, lanes] = dv2
            else:
                own_out[0, :, lanes] += dk2
                own_out[1, :, lanes] += dv2
    for offset, halo in tiles_of(core, rows, window):
        if halo is not None:
            dq_scr[pl.ds(offset, TILE), :] += dqh[halo * HALO : halo * HALO + HALO, :]
    grad_q = (dq_scr[...] * 0.125).astype(BF)
    gq_out[...] = back[...] + dot_nt(grad_q, w_q[...])
    dwq_out[...] = dot_tn(low_src(), grad_q).astype(BF)


def split_places(core, source, kept, sent):
    for parity in range(2):

        @pl.when(core[0] == parity)
        def place():
            for chip in range(kept.shape[0]):
                kept[chip] = source[2 * chip + parity]
                sent[chip] = source[2 * chip + 1 - parity]


def kv_bwd(window_rows, own, halo, w_k, w_v):
    rows = own.shape[1]
    window = window_rows.shape[0]
    dk = own[0].astype(BF)
    dv = own[1].astype(BF)
    total = dot_nt(dk, w_k[...]) + dot_nt(dv, w_v[...])
    dwk = dot_tn(window_rows[0:rows, :], dk) + dot_tn(window_rows[rows:window, :], halo[0])
    dwv = dot_tn(window_rows[0:rows, :], dv) + dot_tn(window_rows[rows:window, :], halo[1])
    return total, dwk.astype(BF), dwv.astype(BF)


def lay_out(stack, mats):
    places, _, width = stack.shape
    per = 6 * width // places
    for slot, matrix in enumerate(mats):
        row, end = slot * width, slot * width + width
        while row < end:
            place, start = divmod(row, per)
            take = min(per - start, end - row)
            at = row - slot * width
            stack[place, start : start + take, :] = matrix[at : at + take, :]
            row += take


def up_tile(pack, tile):
    places, _, width = pack.shape
    return pack[:, 128 + 32 * tile : 160 + 32 * tile, :].reshape(places * 32, width)


def down_tile(pack, tile):
    return pack[4 * tile : 4 * tile + 4, 0:128, :].reshape(512, pack.shape[2])


def ffn_fwd(resid, base, gains, gain_in, gain_out, pack, res_out, low_out, hid_low=None, pre=None):
    hidden = norm_rows(resid[...], *gain_rows(gains, gain_in))
    low = hidden.astype(BF)
    if hid_low is not None:
        hid_low[...] = low
    res_out[...] = hidden + base[...].astype(F32)
    for tile in range(4):
        values = dot_nn(low, up_tile(pack, tile))
        if pre is not None:
            pre[tile] = values
        res_out[...] += dot_nn(gelu(values).astype(BF), down_tile(pack, tile))
    low_out[...] = norm_rows(res_out[...], *gain_rows(gains, gain_out)).astype(BF)


def ffn_bwd(grad, res_late, gains, gain_out, pack, gh_out, late_out, ng_out, hid_low, late_low, dpack, pre=None):
    back, dgain, dbias = norm_back(res_late[...], gain_rows(gains, gain_out)[0], grad)
    late_out[...] = back
    gh_out[...] = back
    late_low[...] = back.astype(BF)
    ng_out[0:1, :] = dgain
    ng_out[1:2, :] = dbias
    places, _, width = dpack.shape
    for tile in range(4):
        activ, slope = gelu_both(dot_nn(hid_low[...], up_tile(pack, tile)) if pre is None else pre[tile])
        grad_down = dot_tn(activ.astype(BF), late_low[...]).astype(BF)
        dpack[4 * tile : 4 * tile + 4, 0:128, :] = grad_down.reshape(4, 128, width)
        grad_act = dot_nt(late_low[...], down_tile(pack, tile)).astype(BF).astype(F32)
        grad_pre = (grad_act * slope).astype(BF)
        grad_up = dot_tn(hid_low[...], grad_pre).astype(BF)
        dpack[:, 128 + 32 * tile : 160 + 32 * tile, :] = grad_up.reshape(places, 32, width)
        gh_out[...] += dot_nt(grad_pre, up_tile(pack, tile))


def kept_shapes(rows, window, width, with_o=True):
    outs = dict(
        q=shape_of(BF, rows, width),
        k=shape_of(BF, window, width),
        v=shape_of(BF, window, width),
        lse=shape_of(F32, HEADS, rows),
    )
    return dict(outs, o=shape_of(BF, rows, width)) if with_o else outs


def head_shapes(rows, window, width):
    return dict(
        back=shape_of(F32, rows, width),
        do=shape_of(BF, rows, width),
        delta=shape_of(F32, HEADS, rows),
        dwo=shape_of(BF, width, width),
        halo=shape_of(BF, 2, window - rows, width),
        gxh=shape_of(BF, window - rows, width),
        dqh=shape_of(F32, window - rows, width),
        ng=shape_of(F32, 2, width),
    )


def weights_of(env):
    return env.wq, env.wk, env.wv, env.wo


def named_mats(mats):
    return dict(wq=mats[0], wk=mats[1], wv=mats[2], wo=mats[3])


def enc_forward(x, window_rows, mats, pack, gains, places):
    rows, width = x.shape
    window = window_rows.shape[0]

    def program(e, core, store):
        attn_fwd(
            core, False, lambda: e.x[...], lambda: e.x[...].astype(F32), e.window, weights_of(e),
            e.qcol, e.krow, e.q, e.k, e.v, e.o, e.lse, e.resid,
        )
        store(e.q, e.k, e.v, e.o, e.lse, e.resid)
        ffn_fwd(e.resid, e.x, e.gains, 0, 2, e.pack, e.two, e.low)

    return fused(
        "enc_forward",
        program,
        places.core,
        dict(qcol=places.qcol, krow=places.krow, gains=gains),
        dict(x=x, window=window_rows, **named_mats(mats), pack=pack),
        dict(
            kept_shapes(rows, window, width),
            resid=shape_of(F32, rows, width),
            two=shape_of(F32, rows, width),
            low=shape_of(BF, rows, width),
        ),
        28 * rows * width * width + 8 * rows * window * width,
    )


def self_forward(z, window_rows, mats, places):
    rows, width = z.shape
    window = window_rows.shape[0]

    def program(e, core, store):
        attn_fwd(
            core, True, lambda: e.z[...], lambda: e.z[...].astype(F32), e.window, weights_of(e),
            e.qcol, e.krow, e.q, e.k, e.v, e.o, e.lse, e.resid,
        )

    return fused(
        "self_forward",
        program,
        places.core,
        dict(qcol=places.qcol, krow=places.krow),
        dict(z=z, window=window_rows, **named_mats(mats)),
        dict(kept_shapes(rows, window, width), resid=shape_of(F32, rows, width)),
        12 * rows * width * width + 8 * rows * window * width,
    )


def cross_and_ffn(three, window_rows, mats, pack, z, cot, gains, places):
    rows, width = three.shape
    window = window_rows.shape[0]
    count, block = pack[0].shape[0], pack[1][1]
    f32_rows, low_rows = pltpu.VMEM((rows, width), F32), pltpu.VMEM((rows, width), BF)

    def program(e, core, store, o, four, five, gh, hid_low, late_low, pre, dpack):
        def first():
            return norm_rows(e.three[...], *gain_rows(e.gains, 4))

        attn_fwd(
            core, False, lambda: first().astype(BF), first, e.window, weights_of(e),
            e.qcol, e.krow, e.q, e.k, e.v, o, e.lse, four,
        )
        store(e.q, e.k, e.v, e.lse)
        ffn_fwd(four, e.z, e.gains, 6, 8, e.pack, five, e.low, hid_low, pre)
        store(e.low)
        ffn_bwd(
            e.cot[...].astype(F32), five, e.gains, 8, e.pack, gh, e.five, e.ng8,
            hid_low, late_low, dpack, pre,
        )
        split_places(core, dpack, e.kept, e.sent)
        store(e.sent, e.kept, e.five, e.ng8)
        attn_head(
            core, False, gh[...], four, o, e.q, e.k, e.v, e.lse, (e.wk, e.wv, e.wo), e.gains, 6, e.qrow, e.kcol, e,
        )

    return fused(
        "cross_and_ffn",
        program,
        places.core,
        dict(qcol=places.qcol, krow=places.krow, qrow=places.qrow, kcol=places.kcol, gains=gains),
        dict(three=three, wq=mats[0], window=window_rows, wk=mats[1], wv=mats[2], wo=mats[3], z=z, pack=pack, cot=cot),
        dict(
            **kept_shapes(rows, window, width, False),
            low=shape_of(BF, rows, width),
            kept=shape_of(BF, count // 2, block, width),
            sent=shape_of(BF, count // 2, block, width),
            five=shape_of(F32, rows, width),
            ng8=shape_of(F32, 2, width),
            **head_shapes(rows, window, width),
        ),
        68 * rows * width * width + 8 * rows * window * width,
        scratch=[
            low_rows, f32_rows, f32_rows, f32_rows, low_rows, low_rows,
            pltpu.VMEM((4, rows, width), F32), pltpu.VMEM((count, block, width), BF),
        ],
    )


def own_rows(array, rows):
    spot = (slice(0, rows),)
    return (array, (rows, array.shape[1]), ((spot, spot),))


def cross_body_self_head(c, low_window, three, s, cross_mats, self_mats, gains, places):
    rows, width = three.shape
    window = c.k.shape[0]

    def program(e, core, store, grad, dq, own):
        def first():
            return norm_rows(e.three[...], *gain_rows(e.gains, 4)).astype(BF)

        attn_body(
            core, False, window, e.back_c, e.do_c, e.delta_c, e.dqh_c, first, e.q_c, e.k_c,
            e.v_c, e.lse_c, e.wq_c, e.qrow, e.kcol, grad, e.dwq, own, dq,
        )
        e.gx[...], e.dwk[...], e.dwv[...] = kv_bwd(e.low_window, own, e.halo_c, e.wk_c, e.wv_c)
        store(e.dwq, e.gx, e.dwk, e.dwv)
        attn_head(
            core, True, grad[...], e.three, e.o, e.q, e.k, e.v, e.lse, (e.wk, e.wv, e.wo), e.gains, 4,
            e.qrow, e.kcol, e,
        )

    return fused(
        "cross_body_self_head",
        program,
        places.core,
        dict(qrow=places.qrow, kcol=places.kcol, gains=gains),
        dict(
            q_c=c.q,
            do_c=c.do,
            k_c=own_rows(c.k, rows),
            v_c=own_rows(c.v, rows),
            lse_c=c.lse,
            delta_c=c.delta,
            dqh_c=c.dqh,
            back_c=c.back,
            wq_c=cross_mats[0],
            three=three,
            low_window=low_window,
            halo_c=c.halo,
            wk_c=cross_mats[1],
            wv_c=cross_mats[2],
            wo=self_mats[3],
            o=s.o,
            q=s.q,
            k=s.k,
            v=s.v,
            lse=s.lse,
            wk=self_mats[1],
            wv=self_mats[2],
        ),
        dict(
            gx=shape_of(F32, rows, width),
            dwq=shape_of(BF, width, width),
            dwk=shape_of(BF, width, width),
            dwv=shape_of(BF, width, width),
            **head_shapes(rows, window, width),
        ),
        18 * rows * width * width + 10 * rows * window * width,
        scratch=[pltpu.VMEM((rows, width), F32), pltpu.VMEM((rows, width), F32), pltpu.VMEM((2, rows, width), F32)],
    )


def input_body(name, kept, head, src, window_rows, mats, causal, add, layout, grads, norms, group, places, order):
    rows, width = src.shape
    window = kept.k.shape[0]
    block = 6 * width // group + (16 if norms else 0)

    def program(e, core, store, dq, own, gq, stack, lines):
        others = (e.other0, e.other1, e.other2, e.other3, e.other4)
        attn_body(
            core, causal, window, e.back, e.do, e.delta, e.dqh, lambda: e.src[...], e.q, e.k,
            e.v, e.lse, e.wq, e.qrow, e.kcol, gq, e.dwq, own, dq,
        )
        total, dwk, dwv = kv_bwd(e.window, own, e.halo, e.wk, e.wv)
        e.dwk[...] = dwk
        parts = dict(q=e.dwq, k=dwk, v=dwv)
        lay_out(stack, [others[item] if isinstance(item, int) else parts[item] for item in layout])
        if norms:
            lines[...] = jnp.zeros_like(lines)
            for index, item in enumerate((e.ng0, e.ng1, e.ng2, e.ng3, e.ng4)):
                lines[2 * index : 2 * index + 2, :] = item[...]
            for place in range(group):
                stack[place, block - 16 :, :] = lines[...].astype(BF)
        split_places(core, stack, e.kept, e.sent)
        store(e.sent, e.kept)
        e.grad[...] = gq[...] + total + e.add[...]

    grads = tuple(grads) + (head.dwo,) * (5 - len(grads))
    ng = dict(ng0=norms[0], ng1=norms[1], ng2=norms[2], ng3=norms[3], ng4=norms[4]) if norms else {}
    return fused(
        name,
        program,
        places.core,
        dict(qrow=places.qrow, kcol=places.kcol),
        dict(
            q=kept.q,
            do=head.do,
            k=own_rows(kept.k, rows),
            v=own_rows(kept.v, rows),
            lse=kept.lse,
            delta=head.delta,
            dqh=head.dqh,
            back=head.back,
            wq=mats[0],
            src=src,
            window=window_rows,
            halo=head.halo,
            wk=mats[1],
            wv=mats[2],
            other0=grads[0],
            other1=grads[1],
            other2=grads[2],
            other3=grads[3],
            other4=grads[4],
            add=add,
            **ng,
        ),
        dict(
            sent=shape_of(BF, group // 2, block, width),
            kept=shape_of(BF, group // 2, block, width),
            dwq=shape_of(BF, width, width),
            dwk=shape_of(BF, width, width),
            grad=shape_of(F32, rows, width),
        ),
        14 * rows * width * width + 10 * rows * rows * width,
        scratch=[
            pltpu.VMEM((rows, width), F32), pltpu.VMEM((2, rows, width), F32), pltpu.VMEM((rows, width), F32),
            pltpu.VMEM((group, block, width), BF), pltpu.VMEM((16, width), F32),
        ],
        order=order,
    )


def enc_ffn_head(grad, one, two, kept, pack, mats, gains, places, order):
    rows, width = one.shape
    window = kept.k.shape[0]
    count, block = pack[0].shape[0], pack[1][1]

    def program(e, core, store, gh, hid_low, late_low, dpack):
        hid_low[...] = norm_rows(e.one[...], *gain_rows(e.gains, 0)).astype(BF)
        ffn_bwd(
            e.grad[...], e.two, e.gains, 2, e.pack, gh, e.late, e.ng2, hid_low, late_low, dpack
        )
        split_places(core, dpack, e.kept, e.sent)
        store(e.sent, e.kept, e.late, e.ng2)
        attn_head(
            core, False, gh[...], e.one, e.o, e.q, e.k, e.v, e.lse, (e.wk, e.wv, e.wo), e.gains, 0, e.qrow, e.kcol, e,
        )

    return fused(
        "enc_ffn_head",
        program,
        places.core,
        dict(qrow=places.qrow, kcol=places.kcol, gains=gains),
        dict(
            one=one,
            two=two,
            grad=grad,
            pack=pack,
            wo=mats[3],
            wk=mats[1],
            wv=mats[2],
            o=kept.o,
            q=kept.q,
            k=kept.k,
            v=kept.v,
            lse=kept.lse,
        ),
        dict(
            sent=shape_of(BF, count // 2, block, width),
            kept=shape_of(BF, count // 2, block, width),
            late=shape_of(F32, rows, width),
            ng2=shape_of(F32, 2, width),
            **head_shapes(rows, window, width),
        ),
        44 * rows * width * width + 10 * TILE * TILE * width,
        scratch=[
            pltpu.VMEM((rows, width), F32), pltpu.VMEM((rows, width), BF), pltpu.VMEM((rows, width), BF),
            pltpu.VMEM((count, block, width), BF),
        ],
        order=order,
    )


def segments_at(bounds, places, total_len):
    found = jnp.sum((bounds[None, :] <= places[:, None]).astype(jnp.int32), axis=-1)
    return jnp.where((places >= 0) & (places < total_len), found, -1)


def row_squares(values):
    if values.ndim == 2:
        return jnp.sum(values * values, axis=1)
    return values * values


def owner_groups(rows_local, owner, per_group, count):
    group_ids = (owner * rows_local + jnp.arange(rows_local, dtype=jnp.int32)) // per_group
    return group_ids[:, None] == jnp.arange(count, dtype=jnp.int32)[None, :]


def group_sum(onehot, row_values):
    return jnp.sum(jnp.where(onehot, row_values[:, None], 0.0), axis=0)


def lamb_moments(master, grad_rows, first, second):
    first_new = beta_one * first + (1.0 - beta_one) * grad_rows
    second_new = beta_two * second + (1.0 - beta_two) * grad_rows * grad_rows
    update = (
        first_new
        / (1.0 - beta_one**STEP)
        / (jnp.sqrt(second_new / (1.0 - beta_two**STEP)) + lamb_eps)
        + weight_decay * master
    )
    return (first_new, second_new, update)


GROUP = ("lo", "y", "c")
CHIPS = ("lo", "y")
EVERY = ("hi", "lo", "y", "c")


def swap_hi(array):
    return lax.ppermute(array, "hi", [(0, 1), (1, 0)])


def shift_hi(array, distance):
    count = lax.axis_size("hi")
    route = [(i - distance, i) for i in range(count) if i - distance in range(count)]
    return lax.ppermute(array, "hi", route)


def halo_rows(rows_array):
    rows = rows_array.shape[0]
    if lax.axis_size("hi") == 2:
        return swap_hi(jnp.where(lax.axis_index("hi") == 0, rows_array[rows - HALO :], rows_array[:HALO]))
    left = shift_hi(rows_array[rows - HALO :], 1)
    right = shift_hi(rows_array[:HALO], -1)
    return jnp.concatenate((left, right), axis=0)


def halo_return(grads, total):
    rest = total.shape[0] - HALO
    if lax.axis_size("hi") == 2:
        back = swap_hi(grads)
        last = lax.axis_index("hi") == 0
        return back, total + jnp.where(last, jnp.pad(back, ((rest, 0), (0, 0))), jnp.pad(back, ((0, rest), (0, 0))))
    back = jnp.concatenate((shift_hi(grads[HALO:], 1), shift_hi(grads[:HALO], -1)), axis=0)
    return back, total + jnp.pad(back[:HALO], ((0, rest), (0, 0))) + jnp.pad(back[HALO:], ((rest, 0), (0, 0)))


def pack_up(rows):
    count, units = rows.shape
    return rows.reshape(count, 4, units // 4).swapaxes(0, 1).reshape(4 * count, units // 4)


def unpack_up(packed):
    count, width = packed.shape
    return packed.reshape(4, count // 4, width).swapaxes(0, 1).reshape(count // 4, 4 * width)


def swap_core(array):
    return lax.ppermute(array, "c", [(0, 1), (1, 0)])


def tie(array, other):
    bit = lax.slice(other, (0,) * other.ndim, (1,) * other.ndim).reshape(()) * 0
    return array + bit.astype(array.dtype)


def from_parity(mine, other):
    even = lax.axis_index("c") == 0
    full = jnp.stack((jnp.where(even, mine, other), jnp.where(even, other, mine)), axis=1)
    return full.reshape(-1, *mine.shape[1:])


def gather_plain(attn_shard, up_shard, down_shard, norm_shard):
    width = attn_shard.shape[1]
    group = lax.axis_size(GROUP)
    norm_count = norm_shard.shape[0]
    attn = lax.all_gather(attn_shard, EVERY, axis=0, tiled=True)
    down = lax.all_gather(down_shard, EVERY, axis=0, tiled=True).reshape(2, group, -1, width)
    up = lax.all_gather(up_shard, EVERY, axis=0, tiled=True)
    up = up.reshape(2, group, -1, 4, width).swapaxes(2, 3).reshape(2, group, -1, width)
    norms = jnp.pad(norm_shard[None, :], ((0, 0), (0, width - norm_count)))
    norms = lax.all_gather(norms, EVERY, axis=0, tiled=True)[:, :norm_count]
    ffn = jnp.concatenate((down, up), axis=2)
    attn = attn.reshape(2, group, -1, width)
    full = jnp.concatenate((attn[0], attn[1], ffn[0]), axis=1)
    return full, ffn[1], norms.reshape(10, width).astype(F32)


def reduce_cores(kept, sent):
    return (kept.astype(F32) + swap_core(sent).astype(F32)).astype(BF)


def reduce_chips(pair):
    parts = lax.all_to_all(pair, CHIPS, split_axis=0, concat_axis=0, tiled=True)
    return jnp.sum(parts.astype(F32), axis=0)


def join_halves(zero, one):
    first = lax.axis_index("hi") == 0
    mine = jnp.where(first, zero, one)
    sent = jnp.where(first, one, zero).astype(BF)
    return mine + swap_hi(sent).astype(F32)


def reduce_plain(attn0, attn1, ffn0, ffn1, norm_local):
    group, _, width = ffn0.shape

    def scatter(rows):
        return lax.psum_scatter(rows, EVERY, scatter_dimension=0, tiled=True).astype(F32)

    attn = jnp.concatenate((attn0, attn1), axis=0).reshape(-1, width)
    ffn = jnp.stack((ffn0, ffn1)).reshape(2 * group, -1, width)
    up = ffn[:, 128:].reshape(2 * group, 4, 32, width).swapaxes(1, 2).reshape(-1, 4 * width)
    norms = lax.psum_scatter(
        norm_local.reshape(lax.axis_size(EVERY), -1), EVERY, scatter_dimension=0, tiled=True
    )
    return scatter(attn), scatter(up), scatter(ffn[:, :128].reshape(-1, width)), norms[0]


def shards(
    enc_in,
    dec_in,
    cotangent,
    lengths,
    attn_master,
    ffn_in_master,
    ffn_out_master,
    norm_master,
    attn_first,
    ffn_in_first,
    ffn_out_first,
    norm_first,
    attn_second,
    ffn_in_second,
    ffn_out_second,
    norm_second,
):
    micro, _, length_dev, width = enc_in.shape
    rows = micro * length_dev
    hidden_units = ffn_in_master.shape[1]
    high, low = lax.axis_index("hi"), lax.axis_index("lo")
    n_high = lax.axis_size("hi")
    owner = lax.axis_index(EVERY)
    masters = (attn_master, ffn_in_master, ffn_out_master, norm_master)
    group_info = ((width, 12), (width, 2), (hidden_units, 2), (width, 10))
    onehots = [
        owner_groups(master.shape[0], owner, info[0], info[1])
        for master, info in zip(masters, group_info)
    ]
    weight_local = jnp.concatenate(
        [group_sum(onehot, row_squares(master)) for onehot, master in zip(onehots, masters)]
    )

    plain = n_high != 2

    def regroup(*arrays):
        packed = jnp.stack([array[:, 0] for array in arrays], axis=1)
        packed = lax.all_to_all(packed, "lo", split_axis=0, concat_axis=0, tiled=True)
        packed = packed.swapaxes(0, 1).reshape(len(arrays), rows, width)
        return packed

    core = jnp.stack((lax.axis_index("c"), jnp.where(high == 0, rows - HALO, 0))).astype(jnp.int32)
    attn_rows = attn_master.shape[0]
    norm_count = norm_master.shape[0]
    attn_low, up_low, down_low, norm_low = [master.astype(BF) for master in masters]
    if plain:
        full, late, gains = gather_plain(attn_low, up_low, down_low, norm_low)
        enc_rows, dec_rows, cot_rows = regroup(enc_in, dec_in, cotangent)
    else:
        first = high == 0
        norm_pad = jnp.pad(norm_low[None, :], ((0, 15), (0, width - norm_count)))
        mine = jnp.concatenate((attn_low, down_low, pack_up(up_low), norm_pad), axis=0)
        other = swap_hi(mine)
        enc_rows, dec_rows, cot_rows = regroup(enc_in, dec_in, cotangent)
        zero = jnp.where(first, mine, other)
        one = jnp.where(first, other, mine)
        last = mine.shape[0] - 16
        early = (one[:attn_rows], zero[attn_rows : last + 1], one[last:-1])
        early = jnp.concatenate((tie(zero[:attn_rows], enc_rows), *early), axis=0)
        full = lax.all_gather(early, GROUP, axis=0, tiled=False)
        late = lax.all_gather(one[attn_rows:last], GROUP, axis=0, tiled=False)
        gains = full[:, attn_rows + last : attn_rows + last + 2, :norm_count].swapaxes(0, 1)
        gains = gains.reshape(10, width).astype(F32)
    enc_window = jnp.concatenate((enc_rows, halo_rows(enc_rows)), axis=0)
    dec_window = jnp.concatenate((dec_rows, halo_rows(dec_rows)), axis=0)
    group = full.shape[0]

    total_len = rows * n_high
    bounds = jnp.cumsum(lengths[:, 0, :], axis=-1)
    bounds = lax.dynamic_index_in_dim(bounds, low, 0, keepdims=False)
    base = high * rows
    own_pos = base + jnp.arange(rows, dtype=jnp.int32)
    step = jnp.arange(HALO, dtype=jnp.int32)
    if n_high == 2:
        halo_pos = jnp.where(high == 0, rows, rows - HALO) + step
    else:
        halo_pos = jnp.concatenate((base - HALO + step, base + rows + step))
    key_pos = jnp.concatenate((own_pos, halo_pos))
    key_seg = segments_at(bounds, key_pos, total_len)
    krow = jnp.stack((key_seg, key_pos), axis=0)
    kcol = jnp.stack((key_seg, key_pos), axis=1)
    places = types.SimpleNamespace(
        krow=krow,
        kcol=kcol,
        qrow=krow[:, :rows],
        qcol=kcol[:rows],
        core=core,
    )

    per = 6 * width // group
    mats = [square(full, 0, index) for index in range(6)] + [square(full, per, index) for index in range(6)]
    pack0, pack1 = rows_of(full, 2 * per, late.shape[1]), rows_of(late, 0, late.shape[1])
    e = enc_forward(enc_rows, enc_window, mats[0:4], pack0, gains, places)
    low_window = jnp.concatenate((e.low, halo_rows(e.low)), axis=0)
    s = self_forward(dec_rows, dec_window, mats[4:8], places)
    c = cross_and_ffn(s.resid, low_window, mats[8:12], pack1, dec_rows, cot_rows, gains, places)

    def restore(*arrays):
        outs = jnp.stack(arrays, axis=0).reshape(len(arrays), micro, length_dev, width).swapaxes(0, 1)
        return lax.all_to_all(outs, "lo", split_axis=0, concat_axis=0, tiled=True)

    sh = cross_body_self_head(c, low_window, s.resid, s, mats[8:12], mats[4:8], gains, places)
    back_c, grad_encoded = halo_return(c.gxh, sh.gx)
    lows = restore(e.low, c.low)
    pair_f1 = c.kept if plain else reduce_cores(tie(tie(c.kept, sh.ng), lows), c.sent)
    sb = input_body(
        "self_body", s, sh, dec_rows, dec_window, mats[4:8], True, c.five, ("v", 0, 1, 2, 3, 4),
        (sh.dwo, sh.dwq, sh.dwk, sh.dwv, c.dwo), (), group, places, (pair_f1, back_c),
    )
    if plain:
        pair_a1 = sb.kept
    else:
        part_f1 = reduce_chips(pair_f1)
        pair_a1 = reduce_cores(tie(sb.kept, part_f1), sb.sent)
    _, dec_grad = halo_return(sh.gxh, sb.grad)
    eh = enc_ffn_head(grad_encoded, e.resid, e.two, e, pack0, mats[0:4], gains, places, (pair_a1,))
    if plain:
        pair_f0 = eh.kept
    else:
        part_a1 = reduce_chips(pair_a1)
        pair_f0 = reduce_cores(tie(eh.kept, part_a1), eh.sent)
    eb = input_body(
        "enc_body", e, eh, enc_rows, enc_window, mats[0:4], False, eh.late, ("q", "k", "v", 0, 1, 2),
        (eh.dwo, sb.dwq, sb.dwk), (eh.ng, eh.ng2, sh.ng, c.ng, c.ng8), group, places, (pair_f0,),
    )
    _, enc_grad = halo_return(eh.gxh, eb.grad)
    enc_grad, dec_grad = enc_grad.astype(BF), dec_grad.astype(BF)
    if plain:
        attn_own, up_own, down_own, norm_own = reduce_plain(
            from_parity(eb.kept, eb.sent)[:, :per],
            from_parity(sb.kept, sb.sent),
            from_parity(eh.kept, eh.sent),
            from_parity(c.kept, c.sent),
            jnp.concatenate((eh.ng, eh.ng2, sh.ng, c.ng, c.ng8), axis=0).reshape(n_high, group, norm_count),
        )
        grads = restore(enc_grad, dec_grad)
    else:
        part_f0 = reduce_chips(pair_f0)
        part_a0 = reduce_chips(reduce_cores(eb.kept, eb.sent))
        grads = restore(tie(enc_grad, part_a0), dec_grad)
        ffn_own = join_halves(part_f0, part_f1)
        both = join_halves(part_a0, jnp.concatenate((part_a1, part_a0[attn_rows:]), axis=0))
        attn_own, up_own, down_own = both[:attn_rows], unpack_up(ffn_own[128:]), ffn_own[:128]
        norm_own = lax.dynamic_slice_in_dim(both[attn_rows:].reshape(-1), owner * norm_count, norm_count)

    owned = (attn_own, up_own, down_own, norm_own)
    firsts = (attn_first, ffn_in_first, ffn_out_first, norm_first)
    seconds = (attn_second, ffn_in_second, ffn_out_second, norm_second)
    moments = [
        lamb_moments(masters[index], owned[index], firsts[index], seconds[index])
        for index in range(4)
    ]
    update_local = jnp.concatenate(
        [group_sum(onehots[index], row_squares(moments[index][2])) for index in range(4)]
    )
    squares = jnp.stack((weight_local, update_local))
    squares = jnp.pad(squares, ((0, 6), (0, 128 - squares.shape[1])))
    count = lax.axis_size(EVERY)
    squares = tie(squares, grads)
    squares = jnp.broadcast_to(squares[None], (count,) + squares.shape)
    squares = jnp.sum(lax.all_to_all(squares, EVERY, split_axis=0, concat_axis=0, tiled=True), axis=0)
    norms = jnp.sqrt(squares[:2, :26])
    ratio = norms[0] / norms[1]
    bounds_at = (0, 12, 14, 16, 26)
    new_weights = []
    for index in range(4):
        row_ratio = jnp.sum(
            jnp.where(onehots[index], ratio[None, bounds_at[index] : bounds_at[index + 1]], 0.0), axis=1
        )
        if masters[index].ndim == 2:
            row_ratio = row_ratio[:, None]
        new_weights.append(masters[index] - learn_rate * row_ratio * moments[index][2])
    return (
        lows[:, 0][:, None],
        lows[:, 1][:, None],
        grads[:, 0][:, None].astype(F32),
        grads[:, 1][:, None].astype(F32),
        *owned,
        *new_weights,
        *[item[0] for item in moments],
        *[item[1] for item in moments],
        *[item.astype(BF) for item in new_weights],
        norms,
        ratio,
    )


def solution(mesh):
    count_seq, count_stream = mesh.shape["seq"], mesh.shape["stream"]

    def run(*args):
        micro = args[0].shape[0]
        split = Mesh(
            mesh.devices.reshape(count_seq // micro, micro, count_stream // 2, 2), ("hi", "lo", "y", "c")
        )
        tokens = P(None, ("y", "c"), ("hi", "lo"), None)
        wide = P(EVERY, None)
        flat = P(EVERY)
        owned = (wide, wide, wide, flat)
        return jax.shard_map(
            shards,
            mesh=split,
            in_specs=(tokens, tokens, tokens, P(None, ("y", "c"), None), *owned, *owned, *owned),
            out_specs=(tokens, tokens, tokens, tokens, *owned, *owned, *owned, *owned, *owned, P(), P()),
            check_vma=False,
        )(*args)

    return run
```

```python
import types

import jax
import jax.numpy as jnp
from jax import lax
from jax.experimental import pallas as pl
from jax.experimental.pallas import tpu as pltpu
from jax.sharding import Mesh
from jax.sharding import PartitionSpec as P

HEADS = 8
STEP = 5
HALO = 256
TILE = 256

norm_eps = 1e-05
beta_one = 0.5
beta_two = 0.5
lamb_eps = 1e-06
weight_decay = 0.01
learn_rate = 0.5
masked_score = -1e30

BF = jnp.bfloat16
F32 = jnp.float32
MIB = 1024 * 1024


def dot_nn(a, b):
    return lax.dot_general(a, b, (((1,), (0,)), ((), ())), preferred_element_type=F32)


def dot_nt(a, b):
    return lax.dot_general(a, b, (((1,), (1,)), ((), ())), preferred_element_type=F32)


def dot_tn(a, b):
    return lax.dot_general(a, b, (((0,), (0,)), ((), ())), preferred_element_type=F32)


def norm_parts(rows):
    centre = rows - jnp.mean(rows, axis=-1, keepdims=True)
    inv = lax.rsqrt(jnp.mean(centre * centre, axis=-1, keepdims=True) + norm_eps)
    return centre * inv, inv


def norm_rows(rows, gain, bias):
    return norm_parts(rows)[0] * gain + bias


def norm_back(rows, gain, grad):
    unit, inv = norm_parts(rows)
    lead = grad * gain
    back = inv * (
        lead
        - jnp.mean(lead, axis=-1, keepdims=True)
        - unit * jnp.mean(lead * unit, axis=-1, keepdims=True)
    )
    return (
        back,
        jnp.sum(grad * unit, axis=0, keepdims=True),
        jnp.sum(grad, axis=0, keepdims=True),
    )


gelu_a = 0.7978845608028654
gelu_b = 0.044715


def gelu(v):
    return 0.5 * v * (1.0 + jnp.tanh(gelu_a * (v + gelu_b * (v * v * v))))


def gelu_both(v):
    sq = v * v
    t = jnp.tanh(gelu_a * (v + gelu_b * (sq * v)))
    half = 0.5 * (1.0 + t)
    slope = half + 0.5 * v * (1.0 - t * t) * (gelu_a * (1.0 + 3.0 * gelu_b * sq))
    return v * half, slope


def lane_low(shape):
    return lax.broadcasted_iota(jnp.int32, shape, 1) < 64


def shape_of(dtype, *dims):
    return jax.ShapeDtypeStruct(dims, dtype)


class Fetched:
    def __init__(self, ref, copies):
        self.ref, self.copies, self.shape = ref, copies, ref.shape

    def __getitem__(self, index):
        for copy in self.copies:
            copy.wait()
        self.copies = ()
        return self.ref[index]


def square(array, start, index):
    places, _, width = array.shape
    per = 6 * width // places
    pieces = []
    row, end = index * width, index * width + width
    while row < end:
        place, at = divmod(row, per)
        take = min(per - at, end - row)
        spot = slice(row - index * width, row - index * width + take)
        pieces.append(((place, slice(start + at, start + at + take)), spot))
        row += take
    return (array, (width, width), tuple(pieces))


def rows_of(array, start, count):
    places, _, width = array.shape
    every = slice(0, places)
    return (array, (places, count, width), (((every, slice(start, start + count)), every),))


def fused(name, program, core, small, ins, outs, flops, scratch=(), order=()):
    big, sources = [], []
    for item in ins.values():
        array = item[0] if isinstance(item, tuple) else item
        known = [index for index, other in enumerate(big) if other is array]
        sources.append(known[0] if known else len(big))
        if not known:
            big.append(array)
    shapes = [item[1] if isinstance(item, tuple) else item.shape for item in ins.values()]
    pieces = [item[2] if isinstance(item, tuple) else None for item in ins.values()]
    kinds = [big[source].dtype for source in sources]
    counts = [len(item) if item else 1 for item in pieces]
    n_small, n_big, n_out, extra = len(small), len(big), len(outs), len(order)

    def body(core_ref, *refs):
        small_refs, refs = refs[:n_small], refs[n_small:]
        big_refs, refs = refs[:n_big], refs[n_big + extra :]
        out_refs, refs = refs[:n_out], refs[n_out:]
        in_bufs, refs = refs[: len(ins)], refs[len(ins) :]
        out_bufs, refs = refs[:n_out], refs[n_out:]
        user, (in_sem, out_sem) = refs[:-2], refs[-2:]
        env = types.SimpleNamespace(**dict(zip(small, small_refs)))
        used, fetched = 0, []
        for key, source, piece, buf in zip(ins, sources, pieces, in_bufs):
            src = big_refs[source]
            copies = []
            for item in piece or (None,):
                if item is None:
                    copy = pltpu.make_async_copy(src, buf, in_sem.at[used])
                else:
                    copy = pltpu.make_async_copy(src.at[item[0]], buf.at[item[1]], in_sem.at[used])
                copy.start()
                copies.append(copy)
                used += 1
            setattr(env, key, Fetched(buf, copies))
            fetched.append(getattr(env, key))
        for key, buf in zip(outs, out_bufs):
            setattr(env, key, buf)
        leaving = [None] * n_out

        def store(*bufs):
            for buf in bufs:
                (index,) = [place for place in range(n_out) if out_bufs[place] is buf]
                leaving[index] = pltpu.make_async_copy(buf, out_refs[index], out_sem.at[index])
                leaving[index].start()

        program(env, core_ref, store, *user)
        store(*[buf for buf, copy in zip(out_bufs, leaving) if copy is None])
        for copy in leaving:
            copy.wait()
        for item in fetched:
            for copy in item.copies:
                copy.wait()

    vmem = pl.BlockSpec(memory_space=pltpu.VMEM)
    anywhere = pl.BlockSpec(memory_space=pl.ANY)
    size = sum(array.size * array.dtype.itemsize for array in big)
    results = pl.pallas_call(
        body,
        in_specs=[pl.BlockSpec(memory_space=pltpu.SMEM)] + [vmem] * n_small + [anywhere] * (n_big + extra),
        out_specs=tuple([anywhere] * n_out),
        out_shape=tuple(outs.values()),
        scratch_shapes=[pltpu.VMEM(shape, dtype) for shape, dtype in zip(shapes, kinds)]
        + [pltpu.VMEM(out.shape, out.dtype) for out in outs.values()]
        + list(scratch)
        + [pltpu.SemaphoreType.DMA((sum(counts),)), pltpu.SemaphoreType.DMA((n_out,))],
        compiler_params=pltpu.CompilerParams(vmem_limit_bytes=56 * MIB),
        cost_estimate=pl.CostEstimate(flops=flops, bytes_accessed=size, transcendentals=0),
        name=name,
    )(core, *small.values(), *big, *order)
    return types.SimpleNamespace(**dict(zip(outs, results)))


def tiles_of(core, rows, window):
    if window == rows + HALO:
        near = pl.multiple_of(core[1], HALO)
        return ((near, 0), (pl.multiple_of(rows - TILE - core[1], HALO), None))
    return ((0, 0), (rows - TILE, 1))


def key_rows(ref, lanes, rows, halo):
    if halo is None:
        return ref[0:rows, lanes]
    if halo == 0:
        return ref[0 : rows + HALO, lanes]
    return jnp.concatenate((ref[0:rows, lanes], ref[rows + HALO : rows + 2 * HALO, lanes]), axis=0)


def key_lanes(ref, row, rows, halo):
    if halo is None:
        return ref[row : row + 1, 0:rows]
    if halo == 0:
        return ref[row : row + 1, 0 : rows + HALO]
    return jnp.concatenate(
        (ref[row : row + 1, 0:rows], ref[row : row + 1, rows + HALO : rows + 2 * HALO]), axis=1
    )


def halves(shape):
    low = lane_low(shape)
    return low, ~low


def keep(mask, values):
    return jnp.where(mask, values, jnp.zeros_like(values))


def gain_rows(gains, index):
    return gains[index : index + 1, :], gains[index + 1 : index + 2, :]


def attn_fwd(core, causal, low_src, base, kv_src, weights, qcol, krow, q_out, k_out, v_out, o_out, lse_out, res_out):
    rows, _ = q_out.shape
    window = k_out.shape[0]
    w_q, w_k, w_v, w_o = weights
    queries = dot_nn(low_src(), w_q[...])
    q_out[...] = (queries.astype(BF).astype(F32) * 0.125).astype(BF)
    k_out[...] = dot_nn(kv_src[...], w_k[...]).astype(BF)
    v_out[...] = dot_nn(kv_src[...], w_v[...]).astype(BF)
    for offset, halo in tiles_of(core, rows, window):
        spot = pl.ds(offset, TILE)
        allowed = qcol[spot, 0:1] == key_lanes(krow, 0, rows, halo)
        if causal:
            allowed = allowed & (key_lanes(krow, 1, rows, halo) <= qcol[spot, 1:2])
        lane = lax.broadcasted_iota(jnp.int32, (TILE, 128), 1)
        packed = jnp.zeros((TILE, 128), F32)
        for pair in range(HEADS // 2):
            lanes = slice(pair * 128, pair * 128 + 128)
            q2 = q_out[spot, lanes]
            k2 = key_rows(k_out, lanes, rows, halo)
            v2 = key_rows(v_out, lanes, rows, halo)
            mixed = None
            for half in range(2):
                scores = dot_nt(keep(halves(q2.shape)[half], q2), k2)
                scores = jnp.where(allowed, scores, masked_score)
                top = jnp.max(scores, axis=-1, keepdims=True)
                weights = jnp.exp(scores - top)
                total = jnp.sum(weights, axis=-1, keepdims=True)
                probs = (weights * (1.0 / total)).astype(BF)
                part = dot_nn(probs, keep(halves(v2.shape)[half], v2))
                mixed = part if mixed is None else mixed + part
                packed = jnp.where(lane == 2 * pair + half, top + jnp.log(total), packed)
            o_out[spot, lanes] = mixed.astype(BF)
        lse_out[:, spot] = jnp.transpose(packed)[0:HEADS, :]
    res_out[...] = base() + dot_nn(o_out[...], w_o[...])


def score_grads(q2, do2, k2, v2, allowed, lse, delta):
    sums = None
    for half in range(2):
        qh = keep(halves(q2.shape)[half], q2)
        doh = keep(halves(do2.shape)[half], do2)
        scores = jnp.where(allowed, dot_nt(k2, qh), masked_score)
        probs = jnp.exp(scores - lse[half])
        gscores = (probs * (dot_nt(v2, doh) - delta[half])).astype(BF)
        parts = (
            dot_tn(gscores, keep(halves(k2.shape)[half], k2)),
            dot_nn(gscores, qh),
            dot_nn(probs.astype(BF), doh),
        )
        sums = parts if sums is None else tuple(a + b for a, b in zip(sums, parts))
    return sums


def attn_head(
    core, causal, grad, resid, o_in, q_in, k_in, v_in, lse_in, weights, gains, gain_at, qrow, kcol, e,
):
    back_out, do_out, delta_out, dwo_out, halo_out, dqh_out, ng_out = e.back, e.do, e.delta, e.dwo, e.halo, e.dqh, e.ng
    w_k, w_v, w_o = weights
    rows, width = do_out.shape
    window = k_in.shape[0]
    back, dgain, dbias = norm_back(resid[...], gain_rows(gains, gain_at)[0], grad)
    back_out[...] = back
    ng_out[0:1, :] = dgain
    ng_out[1:2, :] = dbias
    branch = back.astype(BF)
    do_out[...] = dot_nt(branch, w_o[...]).astype(BF)
    mixed = do_out[...].astype(F32) * o_in[...].astype(F32)
    high = mixed.astype(BF)
    rest = (mixed - high.astype(F32)).astype(BF)
    head = lax.broadcasted_iota(jnp.int32, (16, width), 1) // (width // HEADS)
    which = (head == lax.broadcasted_iota(jnp.int32, (16, width), 0)).astype(F32).astype(BF)
    delta_out[...] = (dot_nt(which, high) + dot_nt(which, rest))[0:HEADS, :]
    for offset, halo in tiles_of(core, rows, window):
        if halo is None:
            continue
        spot = pl.ds(offset, TILE)
        keys = slice(rows + halo * HALO, rows + halo * HALO + HALO)
        here = slice(halo * HALO, halo * HALO + HALO)
        allowed = kcol[keys, 0:1] == qrow[0:1, spot]
        if causal:
            allowed = allowed & (kcol[keys, 1:2] <= qrow[1:2, spot])
        for pair in range(HEADS // 2):
            lanes = slice(pair * 128, pair * 128 + 128)
            heads = (2 * pair, 2 * pair + 1)
            dq2, dk2, dv2 = score_grads(
                q_in[spot, lanes],
                do_out[spot, lanes],
                k_in[keys, lanes],
                v_in[keys, lanes],
                allowed,
                [lse_in[h : h + 1, spot] for h in heads],
                [delta_out[h : h + 1, spot] for h in heads],
            )
            dqh_out[here, lanes] = dq2
            halo_out[0, here, lanes] = dk2.astype(BF)
            halo_out[1, here, lanes] = dv2.astype(BF)
    e.gxh[...] = (dot_nt(halo_out[0], w_k[...]) + dot_nt(halo_out[1], w_v[...])).astype(BF)
    dwo_out[...] = dot_tn(o_in[...], branch).astype(BF)


def attn_body(
    core, causal, window, back, do_in, delta, dqh, low_src, q_in, k_in, v_in, lse_in, w_q, qrow, kcol,
    gq_out, dwq_out, own_out, dq_scr,
):
    rows, width = gq_out.shape
    for tile in range(rows // TILE):
        spot = slice(tile * TILE, tile * TILE + TILE)
        allowed = kcol[0:rows, 0:1] == qrow[0:1, spot]
        if causal:
            allowed = allowed & (kcol[0:rows, 1:2] <= qrow[1:2, spot])
        for pair in range(HEADS // 2):
            lanes = slice(pair * 128, pair * 128 + 128)
            heads = (2 * pair, 2 * pair + 1)
            dq2, dk2, dv2 = score_grads(
                q_in[spot, lanes],
                do_in[spot, lanes],
                k_in[0:rows, lanes],
                v_in[0:rows, lanes],
                allowed,
                [lse_in[h : h + 1, spot] for h in heads],
                [delta[h : h + 1, spot] for h in heads],
            )
            dq_scr[spot, lanes] = dq2
            if tile == 0:
                own_out[0, :, lanes] = dk2
                own_out[1, :, lanes] = dv2
            else:
                own_out[0, :, lanes] += dk2
                own_out[1, :, lanes] += dv2
    for offset, halo in tiles_of(core, rows, window):
        if halo is not None:
            dq_scr[pl.ds(offset, TILE), :] += dqh[halo * HALO : halo * HALO + HALO, :]
    grad_q = (dq_scr[...] * 0.125).astype(BF)
    gq_out[...] = back[...] + dot_nt(grad_q, w_q[...])
    dwq_out[...] = dot_tn(low_src(), grad_q).astype(BF)


def split_places(core, source, kept, sent):
    for parity in range(2):

        @pl.when(core[0] == parity)
        def place():
            for chip in range(kept.shape[0]):
                kept[chip] = source[2 * chip + parity]
                sent[chip] = source[2 * chip + 1 - parity]


def kv_bwd(window_rows, own, halo, w_k, w_v):
    rows = own.shape[1]
    window = window_rows.shape[0]
    dk = own[0].astype(BF)
    dv = own[1].astype(BF)
    total = dot_nt(dk, w_k[...]) + dot_nt(dv, w_v[...])
    dwk = dot_tn(window_rows[0:rows, :], dk) + dot_tn(window_rows[rows:window, :], halo[0])
    dwv = dot_tn(window_rows[0:rows, :], dv) + dot_tn(window_rows[rows:window, :], halo[1])
    return total, dwk.astype(BF), dwv.astype(BF)


def lay_out(stack, mats):
    places, _, width = stack.shape
    per = 6 * width // places
    for slot, matrix in enumerate(mats):
        row, end = slot * width, slot * width + width
        while row < end:
            place, start = divmod(row, per)
            take = min(per - start, end - row)
            at = row - slot * width
            stack[place, start : start + take, :] = matrix[at : at + take, :]
            row += take


def up_tile(pack, tile):
    places, _, width = pack.shape
    return pack[:, 128 + 32 * tile : 160 + 32 * tile, :].reshape(places * 32, width)


def down_tile(pack, tile):
    return pack[4 * tile : 4 * tile + 4, 0:128, :].reshape(512, pack.shape[2])


def ffn_fwd(resid, base, gains, gain_in, gain_out, pack, res_out, low_out, hid_low=None, pre=None):
    hidden = norm_rows(resid[...], *gain_rows(gains, gain_in))
    low = hidden.astype(BF)
    if hid_low is not None:
        hid_low[...] = low
    res_out[...] = hidden + base[...].astype(F32)
    for tile in range(4):
        values = dot_nn(low, up_tile(pack, tile))
        if pre is not None:
            pre[tile] = values
        res_out[...] += dot_nn(gelu(values).astype(BF), down_tile(pack, tile))
    low_out[...] = norm_rows(res_out[...], *gain_rows(gains, gain_out)).astype(BF)


def ffn_bwd(grad, res_late, gains, gain_out, pack, gh_out, late_out, ng_out, hid_low, late_low, dpack, pre=None):
    back, dgain, dbias = norm_back(res_late[...], gain_rows(gains, gain_out)[0], grad)
    late_out[...] = back
    gh_out[...] = back
    late_low[...] = back.astype(BF)
    ng_out[0:1, :] = dgain
    ng_out[1:2, :] = dbias
    places, _, width = dpack.shape
    for tile in range(4):
        activ, slope = gelu_both(dot_nn(hid_low[...], up_tile(pack, tile)) if pre is None else pre[tile])
        grad_down = dot_tn(activ.astype(BF), late_low[...]).astype(BF)
        dpack[4 * tile : 4 * tile + 4, 0:128, :] = grad_down.reshape(4, 128, width)
        grad_act = dot_nt(late_low[...], down_tile(pack, tile)).astype(BF).astype(F32)
        grad_pre = (grad_act * slope).astype(BF)
        grad_up = dot_tn(hid_low[...], grad_pre).astype(BF)
        dpack[:, 128 + 32 * tile : 160 + 32 * tile, :] = grad_up.reshape(places, 32, width)
        gh_out[...] += dot_nt(grad_pre, up_tile(pack, tile))


def kept_shapes(rows, window, width, with_o=True):
    outs = dict(
        q=shape_of(BF, rows, width),
        k=shape_of(BF, window, width),
        v=shape_of(BF, window, width),
        lse=shape_of(F32, HEADS, rows),
    )
    return dict(outs, o=shape_of(BF, rows, width)) if with_o else outs


def head_shapes(rows, window, width):
    return dict(
        back=shape_of(F32, rows, width),
        do=shape_of(BF, rows, width),
        delta=shape_of(F32, HEADS, rows),
        dwo=shape_of(BF, width, width),
        halo=shape_of(BF, 2, window - rows, width),
        gxh=shape_of(BF, window - rows, width),
        dqh=shape_of(F32, window - rows, width),
        ng=shape_of(F32, 2, width),
    )


def weights_of(env):
    return env.wq, env.wk, env.wv, env.wo


def named_mats(mats):
    return dict(wq=mats[0], wk=mats[1], wv=mats[2], wo=mats[3])


def enc_forward(x, window_rows, mats, pack, gains, places):
    rows, width = x.shape
    window = window_rows.shape[0]

    def program(e, core, store):
        attn_fwd(
            core, False, lambda: e.x[...], lambda: e.x[...].astype(F32), e.window, weights_of(e),
            e.qcol, e.krow, e.q, e.k, e.v, e.o, e.lse, e.resid,
        )
        store(e.q, e.k, e.v, e.o, e.lse, e.resid)
        ffn_fwd(e.resid, e.x, e.gains, 0, 2, e.pack, e.two, e.low)

    return fused(
        "enc_forward",
        program,
        places.core,
        dict(qcol=places.qcol, krow=places.krow, gains=gains),
        dict(x=x, window=window_rows, **named_mats(mats), pack=pack),
        dict(
            kept_shapes(rows, window, width),
            resid=shape_of(F32, rows, width),
            two=shape_of(F32, rows, width),
            low=shape_of(BF, rows, width),
        ),
        28 * rows * width * width + 8 * rows * window * width,
    )


def self_forward(z, window_rows, mats, places):
    rows, width = z.shape
    window = window_rows.shape[0]

    def program(e, core, store):
        attn_fwd(
            core, True, lambda: e.z[...], lambda: e.z[...].astype(F32), e.window, weights_of(e),
            e.qcol, e.krow, e.q, e.k, e.v, e.o, e.lse, e.resid,
        )

    return fused(
        "self_forward",
        program,
        places.core,
        dict(qcol=places.qcol, krow=places.krow),
        dict(z=z, window=window_rows, **named_mats(mats)),
        dict(kept_shapes(rows, window, width), resid=shape_of(F32, rows, width)),
        12 * rows * width * width + 8 * rows * window * width,
    )


def cross_and_ffn(three, window_rows, mats, pack, z, cot, gains, places):
    rows, width = three.shape
    window = window_rows.shape[0]
    count, block = pack[0].shape[0], pack[1][1]
    f32_rows, low_rows = pltpu.VMEM((rows, width), F32), pltpu.VMEM((rows, width), BF)

    def program(e, core, store, o, four, five, gh, hid_low, late_low, pre, dpack):
        def first():
            return norm_rows(e.three[...], *gain_rows(e.gains, 4))

        attn_fwd(
            core, False, lambda: first().astype(BF), first, e.window, weights_of(e),
            e.qcol, e.krow, e.q, e.k, e.v, o, e.lse, four,
        )
        store(e.q, e.k, e.v, e.lse)
        ffn_fwd(four, e.z, e.gains, 6, 8, e.pack, five, e.low, hid_low, pre)
        store(e.low)
        ffn_bwd(
            e.cot[...].astype(F32), five, e.gains, 8, e.pack, gh, e.five, e.ng8,
            hid_low, late_low, dpack, pre,
        )
        split_places(core, dpack, e.kept, e.sent)
        store(e.sent, e.kept, e.five, e.ng8)
        attn_head(
            core, False, gh[...], four, o, e.q, e.k, e.v, e.lse, (e.wk, e.wv, e.wo), e.gains, 6, e.qrow, e.kcol, e,
        )

    return fused(
        "cross_and_ffn",
        program,
        places.core,
        dict(qcol=places.qcol, krow=places.krow, qrow=places.qrow, kcol=places.kcol, gains=gains),
        dict(three=three, wq=mats[0], window=window_rows, wk=mats[1], wv=mats[2], wo=mats[3], z=z, pack=pack, cot=cot),
        dict(
            **kept_shapes(rows, window, width, False),
            low=shape_of(BF, rows, width),
            kept=shape_of(BF, count // 2, block, width),
            sent=shape_of(BF, count // 2, block, width),
            five=shape_of(F32, rows, width),
            ng8=shape_of(F32, 2, width),
            **head_shapes(rows, window, width),
        ),
        68 * rows * width * width + 8 * rows * window * width,
        scratch=[
            low_rows, f32_rows, f32_rows, f32_rows, low_rows, low_rows,
            pltpu.VMEM((4, rows, width), F32), pltpu.VMEM((count, block, width), BF),
        ],
    )


def own_rows(array, rows):
    spot = (slice(0, rows),)
    return (array, (rows, array.shape[1]), ((spot, spot),))


def cross_body_self_head(c, low_window, three, s, cross_mats, self_mats, gains, places):
    rows, width = three.shape
    window = c.k.shape[0]

    def program(e, core, store, grad, dq, own):
        def first():
            return norm_rows(e.three[...], *gain_rows(e.gains, 4)).astype(BF)

        attn_body(
            core, False, window, e.back_c, e.do_c, e.delta_c, e.dqh_c, first, e.q_c, e.k_c,
            e.v_c, e.lse_c, e.wq_c, e.qrow, e.kcol, grad, e.dwq, own, dq,
        )
        e.gx[...], e.dwk[...], e.dwv[...] = kv_bwd(e.low_window, own, e.halo_c, e.wk_c, e.wv_c)
        store(e.dwq, e.gx, e.dwk, e.dwv)
        attn_head(
            core, True, grad[...], e.three, e.o, e.q, e.k, e.v, e.lse, (e.wk, e.wv, e.wo), e.gains, 4,
            e.qrow, e.kcol, e,
        )

    return fused(
        "cross_body_self_head",
        program,
        places.core,
        dict(qrow=places.qrow, kcol=places.kcol, gains=gains),
        dict(
            q_c=c.q,
            do_c=c.do,
            k_c=own_rows(c.k, rows),
            v_c=own_rows(c.v, rows),
            lse_c=c.lse,
            delta_c=c.delta,
            dqh_c=c.dqh,
            back_c=c.back,
            wq_c=cross_mats[0],
            three=three,
            low_window=low_window,
            halo_c=c.halo,
            wk_c=cross_mats[1],
            wv_c=cross_mats[2],
            wo=self_mats[3],
            o=s.o,
            q=s.q,
            k=s.k,
            v=s.v,
            lse=s.lse,
            wk=self_mats[1],
            wv=self_mats[2],
        ),
        dict(
            gx=shape_of(F32, rows, width),
            dwq=shape_of(BF, width, width),
            dwk=shape_of(BF, width, width),
            dwv=shape_of(BF, width, width),
            **head_shapes(rows, window, width),
        ),
        18 * rows * width * width + 10 * rows * window * width,
        scratch=[pltpu.VMEM((rows, width), F32), pltpu.VMEM((rows, width), F32), pltpu.VMEM((2, rows, width), F32)],
    )


def input_body(name, kept, head, src, window_rows, mats, causal, add, layout, grads, norms, group, places, order):
    rows, width = src.shape
    window = kept.k.shape[0]
    block = 6 * width // group + (16 if norms else 0)

    def program(e, core, store, dq, own, gq, stack, lines):
        others = (e.other0, e.other1, e.other2, e.other3, e.other4)
        attn_body(
            core, causal, window, e.back, e.do, e.delta, e.dqh, lambda: e.src[...], e.q, e.k,
            e.v, e.lse, e.wq, e.qrow, e.kcol, gq, e.dwq, own, dq,
        )
        total, dwk, dwv = kv_bwd(e.window, own, e.halo, e.wk, e.wv)
        e.dwk[...] = dwk
        parts = dict(q=e.dwq, k=dwk, v=dwv)
        lay_out(stack, [others[item] if isinstance(item, int) else parts[item] for item in layout])
        if norms:
            lines[...] = jnp.zeros_like(lines)
            for index, item in enumerate((e.ng0, e.ng1, e.ng2, e.ng3, e.ng4)):
                lines[2 * index : 2 * index + 2, :] = item[...]
            for place in range(group):
                stack[place, block - 16 :, :] = lines[...].astype(BF)
        split_places(core, stack, e.kept, e.sent)
        store(e.sent, e.kept)
        e.grad[...] = gq[...] + total + e.add[...]

    grads = tuple(grads) + (head.dwo,) * (5 - len(grads))
    ng = dict(ng0=norms[0], ng1=norms[1], ng2=norms[2], ng3=norms[3], ng4=norms[4]) if norms else {}
    return fused(
        name,
        program,
        places.core,
        dict(qrow=places.qrow, kcol=places.kcol),
        dict(
            q=kept.q,
            do=head.do,
            k=own_rows(kept.k, rows),
            v=own_rows(kept.v, rows),
            lse=kept.lse,
            delta=head.delta,
            dqh=head.dqh,
            back=head.back,
            wq=mats[0],
            src=src,
            window=window_rows,
            halo=head.halo,
            wk=mats[1],
            wv=mats[2],
            other0=grads[0],
            other1=grads[1],
            other2=grads[2],
            other3=grads[3],
            other4=grads[4],
            add=add,
            **ng,
        ),
        dict(
            sent=shape_of(BF, group // 2, block, width),
            kept=shape_of(BF, group // 2, block, width),
            dwq=shape_of(BF, width, width),
            dwk=shape_of(BF, width, width),
            grad=shape_of(F32, rows, width),
        ),
        14 * rows * width * width + 10 * rows * rows * width,
        scratch=[
            pltpu.VMEM((rows, width), F32), pltpu.VMEM((2, rows, width), F32), pltpu.VMEM((rows, width), F32),
            pltpu.VMEM((group, block, width), BF), pltpu.VMEM((16, width), F32),
        ],
        order=order,
    )


def enc_ffn_head(grad, one, two, kept, pack, mats, gains, places, order):
    rows, width = one.shape
    window = kept.k.shape[0]
    count, block = pack[0].shape[0], pack[1][1]

    def program(e, core, store, gh, hid_low, late_low, dpack):
        hid_low[...] = norm_rows(e.one[...], *gain_rows(e.gains, 0)).astype(BF)
        ffn_bwd(
            e.grad[...], e.two, e.gains, 2, e.pack, gh, e.late, e.ng2, hid_low, late_low, dpack
        )
        split_places(core, dpack, e.kept, e.sent)
        store(e.sent, e.kept, e.late, e.ng2)
        attn_head(
            core, False, gh[...], e.one, e.o, e.q, e.k, e.v, e.lse, (e.wk, e.wv, e.wo), e.gains, 0, e.qrow, e.kcol, e,
        )

    return fused(
        "enc_ffn_head",
        program,
        places.core,
        dict(qrow=places.qrow, kcol=places.kcol, gains=gains),
        dict(
            one=one,
            two=two,
            grad=grad,
            pack=pack,
            wo=mats[3],
            wk=mats[1],
            wv=mats[2],
            o=kept.o,
            q=kept.q,
            k=kept.k,
            v=kept.v,
            lse=kept.lse,
        ),
        dict(
            sent=shape_of(BF, count // 2, block, width),
            kept=shape_of(BF, count // 2, block, width),
            late=shape_of(F32, rows, width),
            ng2=shape_of(F32, 2, width),
            **head_shapes(rows, window, width),
        ),
        44 * rows * width * width + 10 * TILE * TILE * width,
        scratch=[
            pltpu.VMEM((rows, width), F32), pltpu.VMEM((rows, width), BF), pltpu.VMEM((rows, width), BF),
            pltpu.VMEM((count, block, width), BF),
        ],
        order=order,
    )


def segments_at(bounds, places, total_len):
    found = jnp.sum((bounds[None, :] <= places[:, None]).astype(jnp.int32), axis=-1)
    return jnp.where((places >= 0) & (places < total_len), found, -1)


def row_squares(values):
    if values.ndim == 2:
        return jnp.sum(values * values, axis=1)
    return values * values


def owner_groups(rows_local, owner, per_group, count):
    group_ids = (owner * rows_local + jnp.arange(rows_local, dtype=jnp.int32)) // per_group
    return group_ids[:, None] == jnp.arange(count, dtype=jnp.int32)[None, :]


def group_sum(onehot, row_values):
    return jnp.sum(jnp.where(onehot, row_values[:, None], 0.0), axis=0)


def lamb_moments(master, grad_rows, first, second):
    first_new = beta_one * first + (1.0 - beta_one) * grad_rows
    second_new = beta_two * second + (1.0 - beta_two) * grad_rows * grad_rows
    update = (
        first_new
        / (1.0 - beta_one**STEP)
        / (jnp.sqrt(second_new / (1.0 - beta_two**STEP)) + lamb_eps)
        + weight_decay * master
    )
    return (first_new, second_new, update)


GROUP = ("lo", "y", "c")
CHIPS = ("lo", "y")
EVERY = ("hi", "lo", "y", "c")


def swap_hi(array):
    return lax.ppermute(array, "hi", [(0, 1), (1, 0)])


def shift_hi(array, distance):
    count = lax.axis_size("hi")
    route = [(i - distance, i) for i in range(count) if i - distance in range(count)]
    return lax.ppermute(array, "hi", route)


def halo_rows(rows_array):
    rows = rows_array.shape[0]
    if lax.axis_size("hi") == 2:
        return swap_hi(jnp.where(lax.axis_index("hi") == 0, rows_array[rows - HALO :], rows_array[:HALO]))
    left = shift_hi(rows_array[rows - HALO :], 1)
    right = shift_hi(rows_array[:HALO], -1)
    return jnp.concatenate((left, right), axis=0)


def halo_return(grads, total):
    rest = total.shape[0] - HALO
    if lax.axis_size("hi") == 2:
        back = swap_hi(grads)
        last = lax.axis_index("hi") == 0
        return back, total + jnp.where(last, jnp.pad(back, ((rest, 0), (0, 0))), jnp.pad(back, ((0, rest), (0, 0))))
    back = jnp.concatenate((shift_hi(grads[HALO:], 1), shift_hi(grads[:HALO], -1)), axis=0)
    return back, total + jnp.pad(back[:HALO], ((0, rest), (0, 0))) + jnp.pad(back[HALO:], ((rest, 0), (0, 0)))


def pack_up(rows):
    count, units = rows.shape
    return rows.reshape(count, 4, units // 4).swapaxes(0, 1).reshape(4 * count, units // 4)


def unpack_up(packed):
    count, width = packed.shape
    return packed.reshape(4, count // 4, width).swapaxes(0, 1).reshape(count // 4, 4 * width)


def swap_core(array):
    return lax.ppermute(array, "c", [(0, 1), (1, 0)])


def tie(array, other):
    bit = lax.slice(other, (0,) * other.ndim, (1,) * other.ndim).reshape(()) * 0
    return array + bit.astype(array.dtype)


def from_parity(mine, other):
    even = lax.axis_index("c") == 0
    full = jnp.stack((jnp.where(even, mine, other), jnp.where(even, other, mine)), axis=1)
    return full.reshape(-1, *mine.shape[1:])


def gather_plain(attn_shard, up_shard, down_shard, norm_shard):
    width = attn_shard.shape[1]
    group = lax.axis_size(GROUP)
    norm_count = norm_shard.shape[0]
    attn = lax.all_gather(attn_shard, EVERY, axis=0, tiled=True)
    down = lax.all_gather(down_shard, EVERY, axis=0, tiled=True).reshape(2, group, -1, width)
    up = lax.all_gather(up_shard, EVERY, axis=0, tiled=True)
    up = up.reshape(2, group, -1, 4, width).swapaxes(2, 3).reshape(2, group, -1, width)
    norms = jnp.pad(norm_shard[None, :], ((0, 0), (0, width - norm_count)))
    norms = lax.all_gather(norms, EVERY, axis=0, tiled=True)[:, :norm_count]
    ffn = jnp.concatenate((down, up), axis=2)
    attn = attn.reshape(2, group, -1, width)
    full = jnp.concatenate((attn[0], attn[1], ffn[0]), axis=1)
    return full, ffn[1], norms.reshape(10, width).astype(F32)


def reduce_cores(kept, sent):
    return (kept.astype(F32) + swap_core(sent).astype(F32)).astype(BF)


def reduce_chips(pair):
    parts = lax.all_to_all(pair, CHIPS, split_axis=0, concat_axis=0, tiled=True)
    return jnp.sum(parts.astype(F32), axis=0)


def join_halves(zero, one):
    first = lax.axis_index("hi") == 0
    mine = jnp.where(first, zero, one)
    sent = jnp.where(first, one, zero).astype(BF)
    return mine + swap_hi(sent).astype(F32)


def reduce_plain(attn0, attn1, ffn0, ffn1, norm_local):
    group, _, width = ffn0.shape

    def scatter(rows):
        return lax.psum_scatter(rows, EVERY, scatter_dimension=0, tiled=True).astype(F32)

    attn = jnp.concatenate((attn0, attn1), axis=0).reshape(-1, width)
    ffn = jnp.stack((ffn0, ffn1)).reshape(2 * group, -1, width)
    up = ffn[:, 128:].reshape(2 * group, 4, 32, width).swapaxes(1, 2).reshape(-1, 4 * width)
    norms = lax.psum_scatter(
        norm_local.reshape(lax.axis_size(EVERY), -1), EVERY, scatter_dimension=0, tiled=True
    )
    return scatter(attn), scatter(up), scatter(ffn[:, :128].reshape(-1, width)), norms[0]


def shards(
    enc_in,
    dec_in,
    cotangent,
    lengths,
    attn_master,
    ffn_in_master,
    ffn_out_master,
    norm_master,
    attn_first,
    ffn_in_first,
    ffn_out_first,
    norm_first,
    attn_second,
    ffn_in_second,
    ffn_out_second,
    norm_second,
):
    micro, _, length_dev, width = enc_in.shape
    rows = micro * length_dev
    hidden_units = ffn_in_master.shape[1]
    high, low = lax.axis_index("hi"), lax.axis_index("lo")
    n_high = lax.axis_size("hi")
    owner = lax.axis_index(EVERY)
    masters = (attn_master, ffn_in_master, ffn_out_master, norm_master)
    group_info = ((width, 12), (width, 2), (hidden_units, 2), (width, 10))
    onehots = [
        owner_groups(master.shape[0], owner, info[0], info[1])
        for master, info in zip(masters, group_info)
    ]
    weight_local = jnp.concatenate(
        [group_sum(onehot, row_squares(master)) for onehot, master in zip(onehots, masters)]
    )

    plain = n_high != 2

    def regroup(*arrays):
        packed = jnp.stack([array[:, 0] for array in arrays], axis=1)
        packed = lax.all_to_all(packed, "lo", split_axis=0, concat_axis=0, tiled=True)
        packed = packed.swapaxes(0, 1).reshape(len(arrays), rows, width)
        return packed

    core = jnp.stack((lax.axis_index("c"), jnp.where(high == 0, rows - HALO, 0))).astype(jnp.int32)
    attn_rows = attn_master.shape[0]
    norm_count = norm_master.shape[0]
    attn_low, up_low, down_low, norm_low = [master.astype(BF) for master in masters]
    if plain:
        full, late, gains = gather_plain(attn_low, up_low, down_low, norm_low)
        enc_rows, dec_rows, cot_rows = regroup(enc_in, dec_in, cotangent)
    else:
        first = high == 0
        norm_pad = jnp.pad(norm_low[None, :], ((0, 15), (0, width - norm_count)))
        mine = jnp.concatenate((attn_low, down_low, pack_up(up_low), norm_pad), axis=0)
        other = swap_hi(mine)
        enc_rows, dec_rows, cot_rows = regroup(enc_in, dec_in, cotangent)
        zero = jnp.where(first, mine, other)
        one = jnp.where(first, other, mine)
        last = mine.shape[0] - 16
        early = (one[:attn_rows], zero[attn_rows : last + 1], one[last:-1])
        early = jnp.concatenate((tie(zero[:attn_rows], enc_rows), *early), axis=0)
        full = lax.all_gather(early, GROUP, axis=0, tiled=False)
        late = lax.all_gather(one[attn_rows:last], GROUP, axis=0, tiled=False)
        gains = full[:, attn_rows + last : attn_rows + last + 2, :norm_count].swapaxes(0, 1)
        gains = gains.reshape(10, width).astype(F32)
    enc_window = jnp.concatenate((enc_rows, halo_rows(enc_rows)), axis=0)
    dec_window = jnp.concatenate((dec_rows, halo_rows(dec_rows)), axis=0)
    group = full.shape[0]

    total_len = rows * n_high
    bounds = jnp.cumsum(lengths[:, 0, :], axis=-1)
    bounds = lax.dynamic_index_in_dim(bounds, low, 0, keepdims=False)
    base = high * rows
    own_pos = base + jnp.arange(rows, dtype=jnp.int32)
    step = jnp.arange(HALO, dtype=jnp.int32)
    if n_high == 2:
        halo_pos = jnp.where(high == 0, rows, rows - HALO) + step
    else:
        halo_pos = jnp.concatenate((base - HALO + step, base + rows + step))
    key_pos = jnp.concatenate((own_pos, halo_pos))
    key_seg = segments_at(bounds, key_pos, total_len)
    krow = jnp.stack((key_seg, key_pos), axis=0)
    kcol = jnp.stack((key_seg, key_pos), axis=1)
    places = types.SimpleNamespace(
        krow=krow,
        kcol=kcol,
        qrow=krow[:, :rows],
        qcol=kcol[:rows],
        core=core,
    )

    per = 6 * width // group
    mats = [square(full, 0, index) for index in range(6)] + [square(full, per, index) for index in range(6)]
    pack0, pack1 = rows_of(full, 2 * per, late.shape[1]), rows_of(late, 0, late.shape[1])
    e = enc_forward(enc_rows, enc_window, mats[0:4], pack0, gains, places)
    low_window = jnp.concatenate((e.low, halo_rows(e.low)), axis=0)
    s = self_forward(dec_rows, dec_window, mats[4:8], places)
    c = cross_and_ffn(s.resid, low_window, mats[8:12], pack1, dec_rows, cot_rows, gains, places)

    def restore(*arrays):
        outs = jnp.stack(arrays, axis=0).reshape(len(arrays), micro, length_dev, width).swapaxes(0, 1)
        return lax.all_to_all(outs, "lo", split_axis=0, concat_axis=0, tiled=True)

    sh = cross_body_self_head(c, low_window, s.resid, s, mats[8:12], mats[4:8], gains, places)
    back_c, grad_encoded = halo_return(c.gxh, sh.gx)
    lows = restore(e.low, c.low)
    pair_f1 = c.kept if plain else reduce_cores(tie(tie(tie(c.kept, sh.ng), lows), back_c), c.sent)
    sb = input_body(
        "self_body", s, sh, dec_rows, dec_window, mats[4:8], True, c.five, ("v", 0, 1, 2, 3, 4),
        (sh.dwo, sh.dwq, sh.dwk, sh.dwv, c.dwo), (), group, places, (pair_f1, back_c),
    )
    back_s, dec_grad = halo_return(sh.gxh, sb.grad)
    if plain:
        pair_a1 = sb.kept
    else:
        part_f1 = reduce_chips(pair_f1)
        pair_a1 = reduce_cores(tie(tie(sb.kept, part_f1), back_s), sb.sent)
    eh = enc_ffn_head(grad_encoded, e.resid, e.two, e, pack0, mats[0:4], gains, places, (pair_a1,))
    if plain:
        pair_f0 = eh.kept
    else:
        part_a1 = reduce_chips(pair_a1)
        pair_f0 = reduce_cores(tie(eh.kept, part_a1), eh.sent)
    eb = input_body(
        "enc_body", e, eh, enc_rows, enc_window, mats[0:4], False, eh.late, ("q", "k", "v", 0, 1, 2),
        (eh.dwo, sb.dwq, sb.dwk), (eh.ng, eh.ng2, sh.ng, c.ng, c.ng8), group, places, (pair_f0,),
    )
    _, enc_grad = halo_return(eh.gxh, eb.grad)
    enc_grad, dec_grad = enc_grad.astype(BF), dec_grad.astype(BF)
    if plain:
        attn_own, up_own, down_own, norm_own = reduce_plain(
            from_parity(eb.kept, eb.sent)[:, :per],
            from_parity(sb.kept, sb.sent),
            from_parity(eh.kept, eh.sent),
            from_parity(c.kept, c.sent),
            jnp.concatenate((eh.ng, eh.ng2, sh.ng, c.ng, c.ng8), axis=0).reshape(n_high, group, norm_count),
        )
        grads = restore(enc_grad, dec_grad)
    else:
        part_f0 = reduce_chips(pair_f0)
        part_a0 = reduce_chips(reduce_cores(eb.kept, eb.sent))
        grads = restore(tie(enc_grad, part_a0), dec_grad)
        ffn_own = join_halves(part_f0, part_f1)
        both = join_halves(part_a0, jnp.concatenate((part_a1, part_a0[attn_rows:]), axis=0))
        attn_own, up_own, down_own = both[:attn_rows], unpack_up(ffn_own[128:]), ffn_own[:128]
        norm_own = lax.dynamic_slice_in_dim(both[attn_rows:].reshape(-1), owner * norm_count, norm_count)

    owned = (attn_own, up_own, down_own, norm_own)
    firsts = (attn_first, ffn_in_first, ffn_out_first, norm_first)
    seconds = (attn_second, ffn_in_second, ffn_out_second, norm_second)
    moments = [
        lamb_moments(masters[index], owned[index], firsts[index], seconds[index])
        for index in range(4)
    ]
    update_local = jnp.concatenate(
        [group_sum(onehots[index], row_squares(moments[index][2])) for index in range(4)]
    )
    squares = jnp.stack((weight_local, update_local))
    squares = jnp.pad(squares, ((0, 6), (0, 128 - squares.shape[1])))
    count = lax.axis_size(EVERY)
    squares = tie(squares, grads)
    squares = jnp.broadcast_to(squares[None], (count,) + squares.shape)
    squares = jnp.sum(lax.all_to_all(squares, EVERY, split_axis=0, concat_axis=0, tiled=True), axis=0)
    norms = jnp.sqrt(squares[:2, :26])
    ratio = norms[0] / norms[1]
    bounds_at = (0, 12, 14, 16, 26)
    new_weights = []
    for index in range(4):
        row_ratio = jnp.sum(
            jnp.where(onehots[index], ratio[None, bounds_at[index] : bounds_at[index + 1]], 0.0), axis=1
        )
        if masters[index].ndim == 2:
            row_ratio = row_ratio[:, None]
        new_weights.append(masters[index] - learn_rate * row_ratio * moments[index][2])
    return (
        lows[:, 0][:, None],
        lows[:, 1][:, None],
        grads[:, 0][:, None].astype(F32),
        grads[:, 1][:, None].astype(F32),
        *owned,
        *new_weights,
        *[item[0] for item in moments],
        *[item[1] for item in moments],
        *[item.astype(BF) for item in new_weights],
        norms,
        ratio,
    )


def solution(mesh):
    count_seq, count_stream = mesh.shape["seq"], mesh.shape["stream"]

    def run(*args):
        micro = args[0].shape[0]
        split = Mesh(
            mesh.devices.reshape(count_seq // micro, micro, count_stream // 2, 2), ("hi", "lo", "y", "c")
        )
        tokens = P(None, ("y", "c"), ("hi", "lo"), None)
        wide = P(EVERY, None)
        flat = P(EVERY)
        owned = (wide, wide, wide, flat)
        return jax.shard_map(
            shards,
            mesh=split,
            in_specs=(tokens, tokens, tokens, P(None, ("y", "c"), None), *owned, *owned, *owned),
            out_specs=(tokens, tokens, tokens, tokens, *owned, *owned, *owned, *owned, *owned, P(), P()),
            check_vma=False,
        )(*args)

    return run
```

```python
import types

import jax
import jax.numpy as jnp
from jax import lax
from jax.experimental import pallas as pl
from jax.experimental.pallas import tpu as pltpu
from jax.sharding import Mesh
from jax.sharding import PartitionSpec as P

HEADS = 8
STEP = 5
HALO = 256
TILE = 256

norm_eps = 1e-05
beta_one = 0.5
beta_two = 0.5
lamb_eps = 1e-06
weight_decay = 0.01
learn_rate = 0.5
masked_score = -1e30

BF = jnp.bfloat16
F32 = jnp.float32
MIB = 1024 * 1024


def dot_nn(a, b):
    return lax.dot_general(a, b, (((1,), (0,)), ((), ())), preferred_element_type=F32)


def dot_nt(a, b):
    return lax.dot_general(a, b, (((1,), (1,)), ((), ())), preferred_element_type=F32)


def dot_tn(a, b):
    return lax.dot_general(a, b, (((0,), (0,)), ((), ())), preferred_element_type=F32)


def norm_parts(rows):
    centre = rows - jnp.mean(rows, axis=-1, keepdims=True)
    inv = lax.rsqrt(jnp.mean(centre * centre, axis=-1, keepdims=True) + norm_eps)
    return centre * inv, inv


def norm_rows(rows, gain, bias):
    return norm_parts(rows)[0] * gain + bias


def norm_back(rows, gain, grad):
    unit, inv = norm_parts(rows)
    lead = grad * gain
    back = inv * (
        lead
        - jnp.mean(lead, axis=-1, keepdims=True)
        - unit * jnp.mean(lead * unit, axis=-1, keepdims=True)
    )
    return (
        back,
        jnp.sum(grad * unit, axis=0, keepdims=True),
        jnp.sum(grad, axis=0, keepdims=True),
    )


gelu_a = 0.7978845608028654
gelu_b = 0.044715


def gelu(v):
    return 0.5 * v * (1.0 + jnp.tanh(gelu_a * (v + gelu_b * (v * v * v))))


def gelu_both(v):
    sq = v * v
    t = jnp.tanh(gelu_a * (v + gelu_b * (sq * v)))
    half = 0.5 * (1.0 + t)
    slope = half + 0.5 * v * (1.0 - t * t) * (gelu_a * (1.0 + 3.0 * gelu_b * sq))
    return v * half, slope


def lane_low(shape):
    return lax.broadcasted_iota(jnp.int32, shape, 1) < 64


def shape_of(dtype, *dims):
    return jax.ShapeDtypeStruct(dims, dtype)


class Fetched:
    def __init__(self, ref, copies):
        self.ref, self.copies, self.shape = ref, copies, ref.shape

    def __getitem__(self, index):
        for copy in self.copies:
            copy.wait()
        self.copies = ()
        return self.ref[index]


def square(array, start, index):
    places, _, width = array.shape
    per = 6 * width // places
    pieces = []
    row, end = index * width, index * width + width
    while row < end:
        place, at = divmod(row, per)
        take = min(per - at, end - row)
        spot = slice(row - index * width, row - index * width + take)
        pieces.append(((place, slice(start + at, start + at + take)), spot))
        row += take
    return (array, (width, width), tuple(pieces))


def rows_of(array, start, count):
    places, _, width = array.shape
    every = slice(0, places)
    return (array, (places, count, width), (((every, slice(start, start + count)), every),))


def fused(name, program, core, small, ins, outs, flops, scratch=(), order=()):
    big, sources = [], []
    for item in ins.values():
        array = item[0] if isinstance(item, tuple) else item
        known = [index for index, other in enumerate(big) if other is array]
        sources.append(known[0] if known else len(big))
        if not known:
            big.append(array)
    shapes = [item[1] if isinstance(item, tuple) else item.shape for item in ins.values()]
    pieces = [item[2] if isinstance(item, tuple) else None for item in ins.values()]
    kinds = [big[source].dtype for source in sources]
    counts = [len(item) if item else 1 for item in pieces]
    n_small, n_big, n_out, extra = len(small), len(big), len(outs), len(order)

    def body(core_ref, *refs):
        small_refs, refs = refs[:n_small], refs[n_small:]
        big_refs, refs = refs[:n_big], refs[n_big + extra :]
        out_refs, refs = refs[:n_out], refs[n_out:]
        in_bufs, refs = refs[: len(ins)], refs[len(ins) :]
        out_bufs, refs = refs[:n_out], refs[n_out:]
        user, (in_sem, out_sem) = refs[:-2], refs[-2:]
        env = types.SimpleNamespace(**dict(zip(small, small_refs)))
        used, fetched = 0, []
        for key, source, piece, buf in zip(ins, sources, pieces, in_bufs):
            src = big_refs[source]
            copies = []
            for item in piece or (None,):
                if item is None:
                    copy = pltpu.make_async_copy(src, buf, in_sem.at[used])
                else:
                    copy = pltpu.make_async_copy(src.at[item[0]], buf.at[item[1]], in_sem.at[used])
                copy.start()
                copies.append(copy)
                used += 1
            setattr(env, key, Fetched(buf, copies))
            fetched.append(getattr(env, key))
        for key, buf in zip(outs, out_bufs):
            setattr(env, key, buf)
        leaving = [None] * n_out

        def store(*bufs):
            for buf in bufs:
                (index,) = [place for place in range(n_out) if out_bufs[place] is buf]
                leaving[index] = pltpu.make_async_copy(buf, out_refs[index], out_sem.at[index])
                leaving[index].start()

        program(env, core_ref, store, *user)
        store(*[buf for buf, copy in zip(out_bufs, leaving) if copy is None])
        for copy in leaving:
            copy.wait()
        for item in fetched:
            for copy in item.copies:
                copy.wait()

    vmem = pl.BlockSpec(memory_space=pltpu.VMEM)
    anywhere = pl.BlockSpec(memory_space=pl.ANY)
    size = sum(array.size * array.dtype.itemsize for array in big)
    results = pl.pallas_call(
        body,
        in_specs=[pl.BlockSpec(memory_space=pltpu.SMEM)] + [vmem] * n_small + [anywhere] * (n_big + extra),
        out_specs=tuple([anywhere] * n_out),
        out_shape=tuple(outs.values()),
        scratch_shapes=[pltpu.VMEM(shape, dtype) for shape, dtype in zip(shapes, kinds)]
        + [pltpu.VMEM(out.shape, out.dtype) for out in outs.values()]
        + list(scratch)
        + [pltpu.SemaphoreType.DMA((sum(counts),)), pltpu.SemaphoreType.DMA((n_out,))],
        compiler_params=pltpu.CompilerParams(vmem_limit_bytes=56 * MIB),
        cost_estimate=pl.CostEstimate(flops=flops, bytes_accessed=size, transcendentals=0),
        name=name,
    )(core, *small.values(), *big, *order)
    return types.SimpleNamespace(**dict(zip(outs, results)))


def tiles_of(core, rows, window):
    if window == rows + HALO:
        near = pl.multiple_of(core[1], HALO)
        return ((near, 0), (pl.multiple_of(rows - TILE - core[1], HALO), None))
    return ((0, 0), (rows - TILE, 1))


def key_rows(ref, lanes, rows, halo):
    if halo is None:
        return ref[0:rows, lanes]
    if halo == 0:
        return ref[0 : rows + HALO, lanes]
    return jnp.concatenate((ref[0:rows, lanes], ref[rows + HALO : rows + 2 * HALO, lanes]), axis=0)


def key_lanes(ref, row, rows, halo):
    if halo is None:
        return ref[row : row + 1, 0:rows]
    if halo == 0:
        return ref[row : row + 1, 0 : rows + HALO]
    return jnp.concatenate(
        (ref[row : row + 1, 0:rows], ref[row : row + 1, rows + HALO : rows + 2 * HALO]), axis=1
    )


def halves(shape):
    low = lane_low(shape)
    return low, ~low


def keep(mask, values):
    return jnp.where(mask, values, jnp.zeros_like(values))


def gain_rows(gains, index):
    return gains[index : index + 1, :], gains[index + 1 : index + 2, :]


def attn_fwd(core, causal, low_src, base, kv_src, weights, qcol, krow, q_out, k_out, v_out, o_out, lse_out, res_out):
    rows, _ = q_out.shape
    window = k_out.shape[0]
    w_q, w_k, w_v, w_o = weights
    queries = dot_nn(low_src(), w_q[...])
    q_out[...] = (queries.astype(BF).astype(F32) * 0.125).astype(BF)
    k_out[...] = dot_nn(kv_src[...], w_k[...]).astype(BF)
    v_out[...] = dot_nn(kv_src[...], w_v[...]).astype(BF)
    for offset, halo in tiles_of(core, rows, window):
        spot = pl.ds(offset, TILE)
        allowed = qcol[spot, 0:1] == key_lanes(krow, 0, rows, halo)
        if causal:
            allowed = allowed & (key_lanes(krow, 1, rows, halo) <= qcol[spot, 1:2])
        lane = lax.broadcasted_iota(jnp.int32, (TILE, 128), 1)
        packed = jnp.zeros((TILE, 128), F32)
        for pair in range(HEADS // 2):
            lanes = slice(pair * 128, pair * 128 + 128)
            q2 = q_out[spot, lanes]
            k2 = key_rows(k_out, lanes, rows, halo)
            v2 = key_rows(v_out, lanes, rows, halo)
            mixed = None
            for half in range(2):
                scores = dot_nt(keep(halves(q2.shape)[half], q2), k2)
                scores = jnp.where(allowed, scores, masked_score)
                top = jnp.max(scores, axis=-1, keepdims=True)
                weights = jnp.exp(scores - top)
                total = jnp.sum(weights, axis=-1, keepdims=True)
                probs = (weights * (1.0 / total)).astype(BF)
                part = dot_nn(probs, keep(halves(v2.shape)[half], v2))
                mixed = part if mixed is None else mixed + part
                packed = jnp.where(lane == 2 * pair + half, top + jnp.log(total), packed)
            o_out[spot, lanes] = mixed.astype(BF)
        lse_out[:, spot] = jnp.transpose(packed)[0:HEADS, :]
    res_out[...] = base() + dot_nn(o_out[...], w_o[...])


def score_grads(q2, do2, k2, v2, allowed, lse, delta):
    sums = None
    for half in range(2):
        qh = keep(halves(q2.shape)[half], q2)
        doh = keep(halves(do2.shape)[half], do2)
        scores = jnp.where(allowed, dot_nt(k2, qh), masked_score)
        probs = jnp.exp(scores - lse[half])
        gscores = (probs * (dot_nt(v2, doh) - delta[half])).astype(BF)
        parts = (
            dot_tn(gscores, keep(halves(k2.shape)[half], k2)),
            dot_nn(gscores, qh),
            dot_nn(probs.astype(BF), doh),
        )
        sums = parts if sums is None else tuple(a + b for a, b in zip(sums, parts))
    return sums


def attn_head(
    core, causal, grad, resid, o_in, q_in, k_in, v_in, lse_in, weights, gains, gain_at, qrow, kcol, e,
):
    back_out, do_out, delta_out, dwo_out, halo_out, dqh_out, ng_out = e.back, e.do, e.delta, e.dwo, e.halo, e.dqh, e.ng
    w_k, w_v, w_o = weights
    rows, width = do_out.shape
    window = k_in.shape[0]
    back, dgain, dbias = norm_back(resid[...], gain_rows(gains, gain_at)[0], grad)
    back_out[...] = back
    ng_out[0:1, :] = dgain
    ng_out[1:2, :] = dbias
    branch = back.astype(BF)
    do_out[...] = dot_nt(branch, w_o[...]).astype(BF)
    mixed = do_out[...].astype(F32) * o_in[...].astype(F32)
    high = mixed.astype(BF)
    rest = (mixed - high.astype(F32)).astype(BF)
    head = lax.broadcasted_iota(jnp.int32, (16, width), 1) // (width // HEADS)
    which = (head == lax.broadcasted_iota(jnp.int32, (16, width), 0)).astype(F32).astype(BF)
    delta_out[...] = (dot_nt(which, high) + dot_nt(which, rest))[0:HEADS, :]
    for offset, halo in tiles_of(core, rows, window):
        if halo is None:
            continue
        spot = pl.ds(offset, TILE)
        keys = slice(rows + halo * HALO, rows + halo * HALO + HALO)
        here = slice(halo * HALO, halo * HALO + HALO)
        allowed = kcol[keys, 0:1] == qrow[0:1, spot]
        if causal:
            allowed = allowed & (kcol[keys, 1:2] <= qrow[1:2, spot])
        for pair in range(HEADS // 2):
            lanes = slice(pair * 128, pair * 128 + 128)
            heads = (2 * pair, 2 * pair + 1)
            dq2, dk2, dv2 = score_grads(
                q_in[spot, lanes],
                do_out[spot, lanes],
                k_in[keys, lanes],
                v_in[keys, lanes],
                allowed,
                [lse_in[h : h + 1, spot] for h in heads],
                [delta_out[h : h + 1, spot] for h in heads],
            )
            dqh_out[here, lanes] = dq2
            halo_out[0, here, lanes] = dk2.astype(BF)
            halo_out[1, here, lanes] = dv2.astype(BF)
    e.gxh[...] = (dot_nt(halo_out[0], w_k[...]) + dot_nt(halo_out[1], w_v[...])).astype(BF)
    dwo_out[...] = dot_tn(o_in[...], branch).astype(BF)


def attn_body(
    core, causal, window, back, do_in, delta, dqh, low_src, q_in, k_in, v_in, lse_in, w_q, qrow, kcol,
    gq_out, dwq_out, own_out, dq_scr,
):
    rows, width = gq_out.shape
    for tile in range(rows // TILE):
        spot = slice(tile * TILE, tile * TILE + TILE)
        allowed = kcol[0:rows, 0:1] == qrow[0:1, spot]
        if causal:
            allowed = allowed & (kcol[0:rows, 1:2] <= qrow[1:2, spot])
        for pair in range(HEADS // 2):
            lanes = slice(pair * 128, pair * 128 + 128)
            heads = (2 * pair, 2 * pair + 1)
            dq2, dk2, dv2 = score_grads(
                q_in[spot, lanes],
                do_in[spot, lanes],
                k_in[0:rows, lanes],
                v_in[0:rows, lanes],
                allowed,
                [lse_in[h : h + 1, spot] for h in heads],
                [delta[h : h + 1, spot] for h in heads],
            )
            dq_scr[spot, lanes] = dq2
            if tile == 0:
                own_out[0, :, lanes] = dk2
                own_out[1, :, lanes] = dv2
            else:
                own_out[0, :, lanes] += dk2
                own_out[1, :, lanes] += dv2
    for offset, halo in tiles_of(core, rows, window):
        if halo is not None:
            dq_scr[pl.ds(offset, TILE), :] += dqh[halo * HALO : halo * HALO + HALO, :]
    grad_q = (dq_scr[...] * 0.125).astype(BF)
    gq_out[...] = back[...] + dot_nt(grad_q, w_q[...])
    dwq_out[...] = dot_tn(low_src(), grad_q).astype(BF)


def split_places(core, source, kept, sent):
    for parity in range(2):

        @pl.when(core[0] == parity)
        def place():
            for chip in range(kept.shape[0]):
                kept[chip] = source[2 * chip + parity]
                sent[chip] = source[2 * chip + 1 - parity]


def kv_bwd(window_rows, own, halo, w_k, w_v):
    rows = own.shape[1]
    window = window_rows.shape[0]
    dk = own[0].astype(BF)
    dv = own[1].astype(BF)
    total = dot_nt(dk, w_k[...]) + dot_nt(dv, w_v[...])
    dwk = dot_tn(window_rows[0:rows, :], dk) + dot_tn(window_rows[rows:window, :], halo[0])
    dwv = dot_tn(window_rows[0:rows, :], dv) + dot_tn(window_rows[rows:window, :], halo[1])
    return total, dwk.astype(BF), dwv.astype(BF)


def lay_out(stack, mats):
    places, _, width = stack.shape
    per = 6 * width // places
    for slot, matrix in enumerate(mats):
        row, end = slot * width, slot * width + width
        while row < end:
            place, start = divmod(row, per)
            take = min(per - start, end - row)
            at = row - slot * width
            stack[place, start : start + take, :] = matrix[at : at + take, :]
            row += take


def up_tile(pack, tile):
    places, _, width = pack.shape
    return pack[:, 128 + 32 * tile : 160 + 32 * tile, :].reshape(places * 32, width)


def down_tile(pack, tile):
    return pack[4 * tile : 4 * tile + 4, 0:128, :].reshape(512, pack.shape[2])


def ffn_fwd(resid, base, gains, gain_in, gain_out, pack, res_out, low_out, hid_low=None, pre=None):
    hidden = norm_rows(resid[...], *gain_rows(gains, gain_in))
    low = hidden.astype(BF)
    if hid_low is not None:
        hid_low[...] = low
    res_out[...] = hidden + base[...].astype(F32)
    for tile in range(4):
        values = dot_nn(low, up_tile(pack, tile))
        if pre is not None:
            pre[tile] = values
        res_out[...] += dot_nn(gelu(values).astype(BF), down_tile(pack, tile))
    low_out[...] = norm_rows(res_out[...], *gain_rows(gains, gain_out)).astype(BF)


def ffn_bwd(grad, res_late, gains, gain_out, pack, gh_out, late_out, ng_out, hid_low, late_low, dpack, pre=None):
    back, dgain, dbias = norm_back(res_late[...], gain_rows(gains, gain_out)[0], grad)
    late_out[...] = back
    gh_out[...] = back
    late_low[...] = back.astype(BF)
    ng_out[0:1, :] = dgain
    ng_out[1:2, :] = dbias
    places, _, width = dpack.shape
    for tile in range(4):
        activ, slope = gelu_both(dot_nn(hid_low[...], up_tile(pack, tile)) if pre is None else pre[tile])
        grad_down = dot_tn(activ.astype(BF), late_low[...]).astype(BF)
        dpack[4 * tile : 4 * tile + 4, 0:128, :] = grad_down.reshape(4, 128, width)
        grad_act = dot_nt(late_low[...], down_tile(pack, tile)).astype(BF).astype(F32)
        grad_pre = (grad_act * slope).astype(BF)
        grad_up = dot_tn(hid_low[...], grad_pre).astype(BF)
        dpack[:, 128 + 32 * tile : 160 + 32 * tile, :] = grad_up.reshape(places, 32, width)
        gh_out[...] += dot_nt(grad_pre, up_tile(pack, tile))


def kept_shapes(rows, window, width, with_o=True):
    outs = dict(
        q=shape_of(BF, rows, width),
        k=shape_of(BF, window, width),
        v=shape_of(BF, window, width),
        lse=shape_of(F32, HEADS, rows),
    )
    return dict(outs, o=shape_of(BF, rows, width)) if with_o else outs


def head_shapes(rows, window, width):
    return dict(
        back=shape_of(F32, rows, width),
        do=shape_of(BF, rows, width),
        delta=shape_of(F32, HEADS, rows),
        dwo=shape_of(BF, width, width),
        halo=shape_of(BF, 2, window - rows, width),
        gxh=shape_of(BF, window - rows, width),
        dqh=shape_of(F32, window - rows, width),
        ng=shape_of(F32, 2, width),
    )


def weights_of(env):
    return env.wq, env.wk, env.wv, env.wo


def named_mats(mats):
    return dict(wq=mats[0], wk=mats[1], wv=mats[2], wo=mats[3])


def enc_forward(x, window_rows, mats, pack, gains, places):
    rows, width = x.shape
    window = window_rows.shape[0]

    def program(e, core, store):
        attn_fwd(
            core, False, lambda: e.x[...], lambda: e.x[...].astype(F32), e.window, weights_of(e),
            e.qcol, e.krow, e.q, e.k, e.v, e.o, e.lse, e.resid,
        )
        store(e.q, e.k, e.v, e.o, e.lse, e.resid)
        ffn_fwd(e.resid, e.x, e.gains, 0, 2, e.pack, e.two, e.low)

    return fused(
        "enc_forward",
        program,
        places.core,
        dict(qcol=places.qcol, krow=places.krow, gains=gains),
        dict(x=x, window=window_rows, **named_mats(mats), pack=pack),
        dict(
            kept_shapes(rows, window, width),
            resid=shape_of(F32, rows, width),
            two=shape_of(F32, rows, width),
            low=shape_of(BF, rows, width),
        ),
        28 * rows * width * width + 8 * rows * window * width,
    )


def self_forward(z, window_rows, mats, places):
    rows, width = z.shape
    window = window_rows.shape[0]

    def program(e, core, store):
        attn_fwd(
            core, True, lambda: e.z[...], lambda: e.z[...].astype(F32), e.window, weights_of(e),
            e.qcol, e.krow, e.q, e.k, e.v, e.o, e.lse, e.resid,
        )

    return fused(
        "self_forward",
        program,
        places.core,
        dict(qcol=places.qcol, krow=places.krow),
        dict(z=z, window=window_rows, **named_mats(mats)),
        dict(kept_shapes(rows, window, width), resid=shape_of(F32, rows, width)),
        12 * rows * width * width + 8 * rows * window * width,
    )


def cross_and_ffn(three, window_rows, mats, pack, z, cot, gains, places):
    rows, width = three.shape
    window = window_rows.shape[0]
    count, block = pack[0].shape[0], pack[1][1]
    f32_rows, low_rows = pltpu.VMEM((rows, width), F32), pltpu.VMEM((rows, width), BF)

    def program(e, core, store, o, four, five, gh, hid_low, late_low, pre, dpack):
        def first():
            return norm_rows(e.three[...], *gain_rows(e.gains, 4))

        attn_fwd(
            core, False, lambda: first().astype(BF), first, e.window, weights_of(e),
            e.qcol, e.krow, e.q, e.k, e.v, o, e.lse, four,
        )
        store(e.q, e.k, e.v, e.lse)
        ffn_fwd(four, e.z, e.gains, 6, 8, e.pack, five, e.low, hid_low, pre)
        store(e.low)
        ffn_bwd(
            e.cot[...].astype(F32), five, e.gains, 8, e.pack, gh, e.five, e.ng8,
            hid_low, late_low, dpack, pre,
        )
        split_places(core, dpack, e.kept, e.sent)
        store(e.sent, e.kept, e.five, e.ng8)
        attn_head(
            core, False, gh[...], four, o, e.q, e.k, e.v, e.lse, (e.wk, e.wv, e.wo), e.gains, 6, e.qrow, e.kcol, e,
        )

    return fused(
        "cross_and_ffn",
        program,
        places.core,
        dict(qcol=places.qcol, krow=places.krow, qrow=places.qrow, kcol=places.kcol, gains=gains),
        dict(three=three, wq=mats[0], window=window_rows, wk=mats[1], wv=mats[2], wo=mats[3], z=z, pack=pack, cot=cot),
        dict(
            **kept_shapes(rows, window, width, False),
            low=shape_of(BF, rows, width),
            kept=shape_of(BF, count // 2, block, width),
            sent=shape_of(BF, count // 2, block, width),
            five=shape_of(F32, rows, width),
            ng8=shape_of(F32, 2, width),
            **head_shapes(rows, window, width),
        ),
        68 * rows * width * width + 8 * rows * window * width,
        scratch=[
            low_rows, f32_rows, f32_rows, f32_rows, low_rows, low_rows,
            pltpu.VMEM((4, rows, width), F32), pltpu.VMEM((count, block, width), BF),
        ],
    )


def own_rows(array, rows):
    spot = (slice(0, rows),)
    return (array, (rows, array.shape[1]), ((spot, spot),))


def cross_body_self_head(c, low_window, three, s, cross_mats, self_mats, gains, places):
    rows, width = three.shape
    window = c.k.shape[0]

    def program(e, core, store, grad, dq, own):
        def first():
            return norm_rows(e.three[...], *gain_rows(e.gains, 4)).astype(BF)

        attn_body(
            core, False, window, e.back_c, e.do_c, e.delta_c, e.dqh_c, first, e.q_c, e.k_c,
            e.v_c, e.lse_c, e.wq_c, e.qrow, e.kcol, grad, e.dwq, own, dq,
        )
        e.gx[...], e.dwk[...], e.dwv[...] = kv_bwd(e.low_window, own, e.halo_c, e.wk_c, e.wv_c)
        store(e.dwq, e.gx, e.dwk, e.dwv)
        attn_head(
            core, True, grad[...], e.three, e.o, e.q, e.k, e.v, e.lse, (e.wk, e.wv, e.wo), e.gains, 4,
            e.qrow, e.kcol, e,
        )

    return fused(
        "cross_body_self_head",
        program,
        places.core,
        dict(qrow=places.qrow, kcol=places.kcol, gains=gains),
        dict(
            q_c=c.q,
            do_c=c.do,
            k_c=own_rows(c.k, rows),
            v_c=own_rows(c.v, rows),
            lse_c=c.lse,
            delta_c=c.delta,
            dqh_c=c.dqh,
            back_c=c.back,
            wq_c=cross_mats[0],
            three=three,
            low_window=low_window,
            halo_c=c.halo,
            wk_c=cross_mats[1],
            wv_c=cross_mats[2],
            wo=self_mats[3],
            o=s.o,
            q=s.q,
            k=s.k,
            v=s.v,
            lse=s.lse,
            wk=self_mats[1],
            wv=self_mats[2],
        ),
        dict(
            gx=shape_of(F32, rows, width),
            dwq=shape_of(BF, width, width),
            dwk=shape_of(BF, width, width),
            dwv=shape_of(BF, width, width),
            **head_shapes(rows, window, width),
        ),
        18 * rows * width * width + 10 * rows * window * width,
        scratch=[pltpu.VMEM((rows, width), F32), pltpu.VMEM((rows, width), F32), pltpu.VMEM((2, rows, width), F32)],
    )


def input_body(name, kept, head, src, window_rows, mats, causal, add, layout, grads, norms, group, places, order):
    rows, width = src.shape
    window = kept.k.shape[0]
    block = 6 * width // group + (16 if norms else 0)

    def program(e, core, store, dq, own, gq, stack, lines):
        others = (e.other0, e.other1, e.other2, e.other3, e.other4)
        attn_body(
            core, causal, window, e.back, e.do, e.delta, e.dqh, lambda: e.src[...], e.q, e.k,
            e.v, e.lse, e.wq, e.qrow, e.kcol, gq, e.dwq, own, dq,
        )
        total, dwk, dwv = kv_bwd(e.window, own, e.halo, e.wk, e.wv)
        e.dwk[...] = dwk
        parts = dict(q=e.dwq, k=dwk, v=dwv)
        lay_out(stack, [others[item] if isinstance(item, int) else parts[item] for item in layout])
        if norms:
            lines[...] = jnp.zeros_like(lines)
            for index, item in enumerate((e.ng0, e.ng1, e.ng2, e.ng3, e.ng4)):
                lines[2 * index : 2 * index + 2, :] = item[...]
            for place in range(group):
                stack[place, block - 16 :, :] = lines[...].astype(BF)
        split_places(core, stack, e.kept, e.sent)
        store(e.sent, e.kept)
        e.grad[...] = gq[...] + total + e.add[...]

    grads = tuple(grads) + (head.dwo,) * (5 - len(grads))
    ng = dict(ng0=norms[0], ng1=norms[1], ng2=norms[2], ng3=norms[3], ng4=norms[4]) if norms else {}
    return fused(
        name,
        program,
        places.core,
        dict(qrow=places.qrow, kcol=places.kcol),
        dict(
            q=kept.q,
            do=head.do,
            k=own_rows(kept.k, rows),
            v=own_rows(kept.v, rows),
            lse=kept.lse,
            delta=head.delta,
            dqh=head.dqh,
            back=head.back,
            wq=mats[0],
            src=src,
            window=window_rows,
            halo=head.halo,
            wk=mats[1],
            wv=mats[2],
            other0=grads[0],
            other1=grads[1],
            other2=grads[2],
            other3=grads[3],
            other4=grads[4],
            add=add,
            **ng,
        ),
        dict(
            sent=shape_of(BF, group // 2, block, width),
            kept=shape_of(BF, group // 2, block, width),
            dwq=shape_of(BF, width, width),
            dwk=shape_of(BF, width, width),
            grad=shape_of(F32, rows, width),
        ),
        14 * rows * width * width + 10 * rows * rows * width,
        scratch=[
            pltpu.VMEM((rows, width), F32), pltpu.VMEM((2, rows, width), F32), pltpu.VMEM((rows, width), F32),
            pltpu.VMEM((group, block, width), BF), pltpu.VMEM((16, width), F32),
        ],
        order=order,
    )


def enc_ffn_head(grad, one, two, kept, pack, mats, gains, places, order):
    rows, width = one.shape
    window = kept.k.shape[0]
    count, block = pack[0].shape[0], pack[1][1]

    def program(e, core, store, gh, hid_low, late_low, dpack):
        hid_low[...] = norm_rows(e.one[...], *gain_rows(e.gains, 0)).astype(BF)
        ffn_bwd(
            e.grad[...], e.two, e.gains, 2, e.pack, gh, e.late, e.ng2, hid_low, late_low, dpack
        )
        split_places(core, dpack, e.kept, e.sent)
        store(e.sent, e.kept, e.late, e.ng2)
        attn_head(
            core, False, gh[...], e.one, e.o, e.q, e.k, e.v, e.lse, (e.wk, e.wv, e.wo), e.gains, 0, e.qrow, e.kcol, e,
        )

    return fused(
        "enc_ffn_head",
        program,
        places.core,
        dict(qrow=places.qrow, kcol=places.kcol, gains=gains),
        dict(
            one=one,
            two=two,
            grad=grad,
            pack=pack,
            wo=mats[3],
            wk=mats[1],
            wv=mats[2],
            o=kept.o,
            q=kept.q,
            k=kept.k,
            v=kept.v,
            lse=kept.lse,
        ),
        dict(
            sent=shape_of(BF, count // 2, block, width),
            kept=shape_of(BF, count // 2, block, width),
            late=shape_of(F32, rows, width),
            ng2=shape_of(F32, 2, width),
            **head_shapes(rows, window, width),
        ),
        44 * rows * width * width + 10 * TILE * TILE * width,
        scratch=[
            pltpu.VMEM((rows, width), F32), pltpu.VMEM((rows, width), BF), pltpu.VMEM((rows, width), BF),
            pltpu.VMEM((count, block, width), BF),
        ],
        order=order,
    )


def segments_at(bounds, places, total_len):
    found = jnp.sum((bounds[None, :] <= places[:, None]).astype(jnp.int32), axis=-1)
    return jnp.where((places >= 0) & (places < total_len), found, -1)


def row_squares(values):
    if values.ndim == 2:
        return jnp.sum(values * values, axis=1)
    return values * values


def owner_groups(rows_local, owner, per_group, count):
    group_ids = (owner * rows_local + jnp.arange(rows_local, dtype=jnp.int32)) // per_group
    return group_ids[:, None] == jnp.arange(count, dtype=jnp.int32)[None, :]


def group_sum(onehot, row_values):
    return jnp.sum(jnp.where(onehot, row_values[:, None], 0.0), axis=0)


def lamb_moments(master, grad_rows, first, second):
    first_new = beta_one * first + (1.0 - beta_one) * grad_rows
    second_new = beta_two * second + (1.0 - beta_two) * grad_rows * grad_rows
    update = (
        first_new
        / (1.0 - beta_one**STEP)
        / (jnp.sqrt(second_new / (1.0 - beta_two**STEP)) + lamb_eps)
        + weight_decay * master
    )
    return (first_new, second_new, update)


GROUP = ("lo", "y", "c")
CHIPS = ("lo", "y")
EVERY = ("hi", "lo", "y", "c")


def swap_hi(array):
    return lax.ppermute(array, "hi", [(0, 1), (1, 0)])


def shift_hi(array, distance):
    count = lax.axis_size("hi")
    route = [(i - distance, i) for i in range(count) if i - distance in range(count)]
    return lax.ppermute(array, "hi", route)


def halo_rows(rows_array):
    rows = rows_array.shape[0]
    if lax.axis_size("hi") == 2:
        return swap_hi(jnp.where(lax.axis_index("hi") == 0, rows_array[rows - HALO :], rows_array[:HALO]))
    left = shift_hi(rows_array[rows - HALO :], 1)
    right = shift_hi(rows_array[:HALO], -1)
    return jnp.concatenate((left, right), axis=0)


def halo_return(grads, total):
    rest = total.shape[0] - HALO
    if lax.axis_size("hi") == 2:
        back = swap_hi(grads)
        last = lax.axis_index("hi") == 0
        return back, total + jnp.where(last, jnp.pad(back, ((rest, 0), (0, 0))), jnp.pad(back, ((0, rest), (0, 0))))
    back = jnp.concatenate((shift_hi(grads[HALO:], 1), shift_hi(grads[:HALO], -1)), axis=0)
    return back, total + jnp.pad(back[:HALO], ((0, rest), (0, 0))) + jnp.pad(back[HALO:], ((rest, 0), (0, 0)))


def pack_up(rows):
    count, units = rows.shape
    return rows.reshape(count, 4, units // 4).swapaxes(0, 1).reshape(4 * count, units // 4)


def unpack_up(packed):
    count, width = packed.shape
    return packed.reshape(4, count // 4, width).swapaxes(0, 1).reshape(count // 4, 4 * width)


def swap_core(array):
    return lax.ppermute(array, "c", [(0, 1), (1, 0)])


def tie(array, other):
    bit = lax.slice(other, (0,) * other.ndim, (1,) * other.ndim).reshape(()) * 0
    return array + bit.astype(array.dtype)


def from_parity(mine, other):
    even = lax.axis_index("c") == 0
    full = jnp.stack((jnp.where(even, mine, other), jnp.where(even, other, mine)), axis=1)
    return full.reshape(-1, *mine.shape[1:])


def gather_plain(attn_shard, up_shard, down_shard, norm_shard):
    width = attn_shard.shape[1]
    group = lax.axis_size(GROUP)
    norm_count = norm_shard.shape[0]
    attn = lax.all_gather(attn_shard, EVERY, axis=0, tiled=True)
    down = lax.all_gather(down_shard, EVERY, axis=0, tiled=True).reshape(2, group, -1, width)
    up = lax.all_gather(up_shard, EVERY, axis=0, tiled=True)
    up = up.reshape(2, group, -1, 4, width).swapaxes(2, 3).reshape(2, group, -1, width)
    norms = jnp.pad(norm_shard[None, :], ((0, 0), (0, width - norm_count)))
    norms = lax.all_gather(norms, EVERY, axis=0, tiled=True)[:, :norm_count]
    ffn = jnp.concatenate((down, up), axis=2)
    attn = attn.reshape(2, group, -1, width)
    full = jnp.concatenate((attn[0], attn[1], ffn[0]), axis=1)
    return full, ffn[1], norms.reshape(10, width).astype(F32)


def reduce_cores(kept, sent):
    return (kept.astype(F32) + swap_core(sent).astype(F32)).astype(BF)


def reduce_chips(pair):
    parts = lax.all_to_all(pair, CHIPS, split_axis=0, concat_axis=0, tiled=True)
    return jnp.sum(parts.astype(F32), axis=0)


def join_halves(zero, one):
    first = lax.axis_index("hi") == 0
    mine = jnp.where(first, zero, one)
    sent = jnp.where(first, one, zero).astype(BF)
    return mine + swap_hi(sent).astype(F32)


def reduce_plain(attn0, attn1, ffn0, ffn1, norm_local):
    group, _, width = ffn0.shape

    def scatter(rows):
        return lax.psum_scatter(rows, EVERY, scatter_dimension=0, tiled=True).astype(F32)

    attn = jnp.concatenate((attn0, attn1), axis=0).reshape(-1, width)
    ffn = jnp.stack((ffn0, ffn1)).reshape(2 * group, -1, width)
    up = ffn[:, 128:].reshape(2 * group, 4, 32, width).swapaxes(1, 2).reshape(-1, 4 * width)
    norms = lax.psum_scatter(
        norm_local.reshape(lax.axis_size(EVERY), -1), EVERY, scatter_dimension=0, tiled=True
    )
    return scatter(attn), scatter(up), scatter(ffn[:, :128].reshape(-1, width)), norms[0]


def shards(
    enc_in,
    dec_in,
    cotangent,
    lengths,
    attn_master,
    ffn_in_master,
    ffn_out_master,
    norm_master,
    attn_first,
    ffn_in_first,
    ffn_out_first,
    norm_first,
    attn_second,
    ffn_in_second,
    ffn_out_second,
    norm_second,
):
    micro, _, length_dev, width = enc_in.shape
    rows = micro * length_dev
    hidden_units = ffn_in_master.shape[1]
    high, low = lax.axis_index("hi"), lax.axis_index("lo")
    n_high = lax.axis_size("hi")
    owner = lax.axis_index(EVERY)
    masters = (attn_master, ffn_in_master, ffn_out_master, norm_master)
    group_info = ((width, 12), (width, 2), (hidden_units, 2), (width, 10))
    onehots = [
        owner_groups(master.shape[0], owner, info[0], info[1])
        for master, info in zip(masters, group_info)
    ]
    weight_local = jnp.concatenate(
        [group_sum(onehot, row_squares(master)) for onehot, master in zip(onehots, masters)]
    )

    plain = n_high != 2

    def regroup(*arrays):
        packed = jnp.stack([array[:, 0] for array in arrays], axis=1)
        packed = lax.all_to_all(packed, "lo", split_axis=0, concat_axis=0, tiled=True)
        packed = packed.swapaxes(0, 1).reshape(len(arrays), rows, width)
        return packed

    core = jnp.stack((lax.axis_index("c"), jnp.where(high == 0, rows - HALO, 0))).astype(jnp.int32)
    attn_rows = attn_master.shape[0]
    norm_count = norm_master.shape[0]
    attn_low, up_low, down_low, norm_low = [master.astype(BF) for master in masters]
    if plain:
        full, late, gains = gather_plain(attn_low, up_low, down_low, norm_low)
        enc_rows, dec_rows, cot_rows = regroup(enc_in, dec_in, cotangent)
    else:
        first = high == 0
        norm_pad = jnp.pad(norm_low[None, :], ((0, 15), (0, width - norm_count)))
        mine = jnp.concatenate((attn_low, down_low, pack_up(up_low), norm_pad), axis=0)
        other = swap_hi(mine)
        enc_rows, dec_rows, cot_rows = regroup(enc_in, dec_in, cotangent)
        zero = jnp.where(first, mine, other)
        one = jnp.where(first, other, mine)
        last = mine.shape[0] - 16
        early = (one[:attn_rows], zero[attn_rows : last + 1], one[last:-1])
        early = jnp.concatenate((tie(zero[:attn_rows], enc_rows), *early), axis=0)
        full = lax.all_gather(early, GROUP, axis=0, tiled=False)
        late = lax.all_gather(one[attn_rows:last], GROUP, axis=0, tiled=False)
        gains = full[:, attn_rows + last : attn_rows + last + 2, :norm_count].swapaxes(0, 1)
        gains = gains.reshape(10, width).astype(F32)
    enc_window = jnp.concatenate((enc_rows, halo_rows(enc_rows)), axis=0)
    dec_window = jnp.concatenate((dec_rows, halo_rows(dec_rows)), axis=0)
    group = full.shape[0]

    total_len = rows * n_high
    bounds = jnp.cumsum(lengths[:, 0, :], axis=-1)
    bounds = lax.dynamic_index_in_dim(bounds, low, 0, keepdims=False)
    base = high * rows
    own_pos = base + jnp.arange(rows, dtype=jnp.int32)
    step = jnp.arange(HALO, dtype=jnp.int32)
    if n_high == 2:
        halo_pos = jnp.where(high == 0, rows, rows - HALO) + step
    else:
        halo_pos = jnp.concatenate((base - HALO + step, base + rows + step))
    key_pos = jnp.concatenate((own_pos, halo_pos))
    key_seg = segments_at(bounds, key_pos, total_len)
    krow = jnp.stack((key_seg, key_pos), axis=0)
    kcol = jnp.stack((key_seg, key_pos), axis=1)
    places = types.SimpleNamespace(
        krow=krow,
        kcol=kcol,
        qrow=krow[:, :rows],
        qcol=kcol[:rows],
        core=core,
    )

    per = 6 * width // group
    mats = [square(full, 0, index) for index in range(6)] + [square(full, per, index) for index in range(6)]
    pack0, pack1 = rows_of(full, 2 * per, late.shape[1]), rows_of(late, 0, late.shape[1])
    e = enc_forward(enc_rows, enc_window, mats[0:4], pack0, gains, places)
    low_window = jnp.concatenate((e.low, halo_rows(e.low)), axis=0)
    s = self_forward(dec_rows, dec_window, mats[4:8], places)
    c = cross_and_ffn(s.resid, low_window, mats[8:12], pack1, dec_rows, cot_rows, gains, places)

    def restore(*arrays):
        outs = jnp.stack(arrays, axis=0).reshape(len(arrays), micro, length_dev, width).swapaxes(0, 1)
        return lax.all_to_all(outs, "lo", split_axis=0, concat_axis=0, tiled=True)

    sh = cross_body_self_head(c, low_window, s.resid, s, mats[8:12], mats[4:8], gains, places)
    back_c, grad_encoded = halo_return(c.gxh, sh.gx)
    lows = restore(e.low, c.low)
    pair_f1 = c.kept if plain else reduce_cores(tie(tie(tie(c.kept, sh.ng), lows), back_c), c.sent)
    sb = input_body(
        "self_body", s, sh, dec_rows, dec_window, mats[4:8], True, c.five, ("v", 0, 1, 2, 3, 4),
        (sh.dwo, sh.dwq, sh.dwk, sh.dwv, c.dwo), (), group, places, (pair_f1, back_c),
    )
    back_s, dec_grad = halo_return(sh.gxh, sb.grad)
    if plain:
        pair_a1 = sb.kept
    else:
        part_f1 = reduce_chips(pair_f1)
        pair_a1 = reduce_cores(tie(sb.kept, part_f1), sb.sent)
    eh = enc_ffn_head(grad_encoded, e.resid, e.two, e, pack0, mats[0:4], gains, places, (pair_a1,))
    if plain:
        pair_f0 = eh.kept
    else:
        part_a1 = reduce_chips(pair_a1)
        pair_f0 = reduce_cores(tie(tie(eh.kept, part_a1), back_s), eh.sent)
    eb = input_body(
        "enc_body", e, eh, enc_rows, enc_window, mats[0:4], False, eh.late, ("q", "k", "v", 0, 1, 2),
        (eh.dwo, sb.dwq, sb.dwk), (eh.ng, eh.ng2, sh.ng, c.ng, c.ng8), group, places, (pair_f0,),
    )
    _, enc_grad = halo_return(eh.gxh, eb.grad)
    enc_grad, dec_grad = enc_grad.astype(BF), dec_grad.astype(BF)
    if plain:
        attn_own, up_own, down_own, norm_own = reduce_plain(
            from_parity(eb.kept, eb.sent)[:, :per],
            from_parity(sb.kept, sb.sent),
            from_parity(eh.kept, eh.sent),
            from_parity(c.kept, c.sent),
            jnp.concatenate((eh.ng, eh.ng2, sh.ng, c.ng, c.ng8), axis=0).reshape(n_high, group, norm_count),
        )
        grads = restore(enc_grad, dec_grad)
    else:
        part_f0 = reduce_chips(pair_f0)
        part_a0 = reduce_chips(reduce_cores(eb.kept, eb.sent))
        grads = restore(tie(enc_grad, part_a0), dec_grad)
        ffn_own = join_halves(part_f0, part_f1)
        both = join_halves(part_a0, jnp.concatenate((part_a1, part_a0[attn_rows:]), axis=0))
        attn_own, up_own, down_own = both[:attn_rows], unpack_up(ffn_own[128:]), ffn_own[:128]
        norm_own = lax.dynamic_slice_in_dim(both[attn_rows:].reshape(-1), owner * norm_count, norm_count)

    owned = (attn_own, up_own, down_own, norm_own)
    firsts = (attn_first, ffn_in_first, ffn_out_first, norm_first)
    seconds = (attn_second, ffn_in_second, ffn_out_second, norm_second)
    moments = [
        lamb_moments(masters[index], owned[index], firsts[index], seconds[index])
        for index in range(4)
    ]
    update_local = jnp.concatenate(
        [group_sum(onehots[index], row_squares(moments[index][2])) for index in range(4)]
    )
    squares = jnp.stack((weight_local, update_local))
    squares = jnp.pad(squares, ((0, 6), (0, 128 - squares.shape[1])))
    count = lax.axis_size(EVERY)
    squares = tie(squares, grads)
    squares = jnp.broadcast_to(squares[None], (count,) + squares.shape)
    squares = jnp.sum(lax.all_to_all(squares, EVERY, split_axis=0, concat_axis=0, tiled=True), axis=0)
    norms = jnp.sqrt(squares[:2, :26])
    ratio = norms[0] / norms[1]
    bounds_at = (0, 12, 14, 16, 26)
    new_weights = []
    for index in range(4):
        row_ratio = jnp.sum(
            jnp.where(onehots[index], ratio[None, bounds_at[index] : bounds_at[index + 1]], 0.0), axis=1
        )
        if masters[index].ndim == 2:
            row_ratio = row_ratio[:, None]
        new_weights.append(masters[index] - learn_rate * row_ratio * moments[index][2])
    return (
        lows[:, 0][:, None],
        lows[:, 1][:, None],
        grads[:, 0][:, None].astype(F32),
        grads[:, 1][:, None].astype(F32),
        *owned,
        *new_weights,
        *[item[0] for item in moments],
        *[item[1] for item in moments],
        *[item.astype(BF) for item in new_weights],
        norms,
        ratio,
    )


def solution(mesh):
    count_seq, count_stream = mesh.shape["seq"], mesh.shape["stream"]

    def run(*args):
        micro = args[0].shape[0]
        split = Mesh(
            mesh.devices.reshape(count_seq // micro, micro, count_stream // 2, 2), ("hi", "lo", "y", "c")
        )
        tokens = P(None, ("y", "c"), ("hi", "lo"), None)
        wide = P(EVERY, None)
        flat = P(EVERY)
        owned = (wide, wide, wide, flat)
        return jax.shard_map(
            shards,
            mesh=split,
            in_specs=(tokens, tokens, tokens, P(None, ("y", "c"), None), *owned, *owned, *owned),
            out_specs=(tokens, tokens, tokens, tokens, *owned, *owned, *owned, *owned, *owned, P(), P()),
            check_vma=False,
        )(*args)

    return run
```
